32 devices in a mesh: bucket: 8 (over y, x, core), seq: 4 (over z).
Axes of the slice: x: 2, y: 2, z: 4, core: 2. Of those that a mesh axis runs over, the one named last changes fastest.
Arguments:
- tokens: bfloat16 [8192, 1536], P(('bucket', 'seq')), may hold values from -6 to 6
- condition: float32 [32, 1536], P('bucket'), may hold values from -6 to 6
- captions: bfloat16 [32, 256, 4096], P('bucket', 'seq'), may hold values from -6 to 6
- caption_lengths: int32 [32], P('bucket'), may hold values from 1 to 256, as said below
- null_flags: int32 [32], P('bucket'), may hold values 0 or 1
- slot_buckets: int32 [8], P('bucket'), may hold values from 0 to 2, as said below
- null_caption: bfloat16 [256, 4096], replicated, may hold values from -6 to 6
- modulation: bfloat16 [1536, 6144], P('bucket'), may hold values from -0.15625 to 0.15625
- projection: bfloat16 [1536, 4608], P('bucket'), may hold values from -0.15625 to 0.15625
- text_weight: bfloat16 [4096, 3072], P('bucket'), may hold values from -0.09375 to 0.09375
- output_weight: bfloat16 [1536, 1536], P('bucket'), may hold values from -0.15625 to 0.15625
- gate_up: bfloat16 [1536, 8192], P('bucket'), may hold values from -0.15625 to 0.15625
- down_weight: bfloat16 [4096, 1536], P('bucket'), may hold values from -0.09375 to 0.09375
- norm_gains: float32 [4, 1536], replicated, may hold values from 0.25 to 1.75
- head_gains: float32 [3, 1536], replicated, may hold values from 0.25 to 1.75
- cross_gates: float32 [24], replicated, may hold values from -1.5 to 1.5
- cotangent: bfloat16 [8192, 1536], P(('bucket', 'seq')), may hold values from -6 to 6
Outputs:
- mixed: bfloat16 [8192, 1536], P(('bucket', 'seq'))
- grad_tokens: float32 [8192, 1536], P(('bucket', 'seq'))
- grad_captions: float32 [32, 256, 4096], P('bucket', 'seq')
- grad_null: float32 [256, 4096], P(('bucket', 'seq'))
- grad_modulation: float32 [1536, 6144], P(('bucket', 'seq'))
- grad_projection: float32 [1536, 4608], P(('bucket', 'seq'))
- grad_text_weight: float32 [4096, 3072], P(('bucket', 'seq'))
- grad_output_weight: float32 [1536, 1536], P(('bucket', 'seq'))
- grad_gate_up: float32 [1536, 8192], P(('bucket', 'seq'))
- grad_down_weight: float32 [4096, 1536], P(('bucket', 'seq'))
- grad_norm_gains: float32 [4, 1536], P(None, ('bucket', 'seq'))
- grad_head_gains: float32 [3, 1536], P(None, ('bucket', 'seq'))
- grad_cross_gates: float32 [24], replicated
The draws below stay inside these ranges and needn't reach their ends.
Inputs may be any that keep to these rules, and one draw needn't show every extreme that they name: `slot_buckets`: A slot of bucket u holds 4 / 2**u clips; about four sevenths of the slots are of bucket 2, two sevenths of bucket 1, the rest of bucket 0, and every bucket has a slot. `caption_lengths`: only the first 4 / 2**u clip places of a slot of bucket u are read. In every draw the first clip place of some slot has length 256.
All inputs are finite; a program needn't handle non-finite values. No bound on the sum of `null_flags` on one device may be relied on, other than what follows from the above.
Results may differ from the reference program's by a relative error of at most 0.017.
Values may be sent and summed in bfloat16 or wider, within the bound.
A program may use at most 576 MiB of HBM per device.

```python
import jax
import jax.numpy as jnp
from jax import lax

H = 24
HD = 64
D = 1536
FF = 4096
TD = 4096
CAP = 256
SLOT = 1024
TOKENS = 8192
CLIPS = 32
N_BUCKET = 8


def draw_slot_buckets(key, part):
    key = jax.random.fold_in(key, 11)
    longest = max(1, 4 * N_BUCKET // 7)
    between = max(1, 2 * N_BUCKET // 7)
    index = jnp.arange(N_BUCKET, dtype=jnp.int32)
    pattern = jnp.where(index < longest, 2, jnp.where(index < longest + between, 1, 0)).astype(jnp.int32)
    return pattern[jax.random.permutation(key, N_BUCKET)]


def draw_caption_lengths(key, part):
    key = jax.random.fold_in(key, 12)
    first_key, second_key = jax.random.split(key)
    lengths = jax.random.randint(first_key, (4 * N_BUCKET,), 1, CAP + 1, dtype=jnp.int32)
    chosen = jax.random.randint(second_key, (), 0, N_BUCKET, dtype=jnp.int32)
    return jnp.where(jnp.arange(4 * N_BUCKET, dtype=jnp.int32) == 4 * chosen, CAP, lengths).astype(jnp.int32)


def set_ends(values, rng, least, largest):
    shape = values.shape
    spot = [jax.random.randint(jax.random.fold_in(rng, axis), (), 0, shape[axis]) for axis in range(len(shape))]
    values = values.at[tuple(spot)].set(least)
    longest = shape.index(max(shape))
    spot[longest] = (spot[longest] + 1) % shape[longest]
    return values.at[tuple(spot)].set(largest)


def block_levels(key, extent, shards, low, largest):
    def one(dim, parts):
        draws = jax.random.uniform(jax.random.fold_in(jax.random.fold_in(key, 6), dim), (parts,), jnp.float32, low / len(shards), largest / len(shards))
        return jnp.repeat(jnp.exp(draws), extent[dim] // parts).reshape((-1,) + (1,) * (len(extent) - dim - 1))

    level = one(*shards[0])
    for cut in shards[1:]:
        level = level * one(*cut)
    return level


def normal_values(own_key, shape, scale, bound, pieces=(), held_as=jnp.bfloat16):
    values = jax.random.normal(own_key, shape, jnp.float32) * scale
    if len(pieces) > 0:
        values = block_levels(own_key, shape, pieces, -0.22, 0.18) * values
    return jnp.clip(values, min=-bound, max=bound).astype(held_as)


def setup_inputs(seed: int = 0) -> dict:
    streams_of = jax.random.split(jax.random.key(seed), 18)
    tokens = normal_values(streams_of[0], (TOKENS, D), 1.0, 6.0, ((0, 32),))
    condition = normal_values(streams_of[1], (CLIPS, D), 1.0, 6.0, ((0, 8),), jnp.float32)
    captions = normal_values(streams_of[2], (CLIPS, CAP, TD), 1.0, 6.0, ((0, 8), (1, 4)))
    caption_lengths = draw_caption_lengths(jax.random.fold_in(streams_of[17], 71), 0)
    null_flags = set_ends((jax.random.randint(streams_of[4], (CLIPS,), 0, 4) < 1).astype(jnp.int32), jax.random.fold_in(streams_of[4], 1), 0, 1)
    slot_buckets = draw_slot_buckets(jax.random.fold_in(streams_of[17], 71), 0)
    null_caption = normal_values(streams_of[6], (CAP, TD), 1.0, 6.0)
    modulation = normal_values(streams_of[7], (D, 4 * D), D ** -0.5, 0.15625, ((0, 8),))
    projection = normal_values(streams_of[8], (D, 3 * D), D ** -0.5, 0.15625, ((0, 8),))
    text_weight = normal_values(streams_of[9], (TD, 2 * D), TD ** -0.5, 0.09375, ((0, 8),))
    output_weight = normal_values(streams_of[10], (D, D), D ** -0.5, 0.15625, ((0, 8),))
    gate_up = normal_values(streams_of[11], (D, 2 * FF), D ** -0.5, 0.15625, ((0, 8),))
    down_weight = normal_values(streams_of[12], (FF, D), FF ** -0.5, 0.09375, ((0, 8),))
    norm_gains = jnp.clip(1.0 + 0.15 * jax.random.normal(streams_of[13], (4, D), jnp.float32), 0.25, 1.75)
    head_gains = jnp.clip(1.0 + 0.15 * jax.random.normal(streams_of[14], (3, D), jnp.float32), 0.25, 1.75)
    cross_gates = jnp.clip(jax.random.uniform(streams_of[15], (H,), jnp.float32, -1.5, 1.5), -1.5, 1.5)
    cotangent = normal_values(streams_of[16], (TOKENS, D), 1.0, 6.0, ((0, 32),))
    return {"tokens": tokens, "condition": condition, "captions": captions, "caption_lengths": caption_lengths, "null_flags": null_flags, "slot_buckets": slot_buckets, "null_caption": null_caption, "modulation": modulation, "projection": projection, "text_weight": text_weight, "output_weight": output_weight, "gate_up": gate_up, "down_weight": down_weight, "norm_gains": norm_gains, "head_gains": head_gains, "cross_gates": cross_gates, "cotangent": cotangent}


@jax.custom_vjp
def low(v):
    return lax.optimization_barrier(v.astype(jnp.bfloat16)).astype(jnp.float32)

@jax.custom_vjp
def low_back(v):
    return v

def low_keep(v):
    return (low(v), None)

def low_pass(kept, grad):
    return (grad,)

def back_keep(v):
    return (v, None)

def back_low(kept, grad):
    return (low(grad),)
low.defvjp(low_keep, low_pass)
low_back.defvjp(back_keep, back_low)
EPSILON = 1e-06
NEGATIVE = -1e+30
HIGHEST = lax.Precision.HIGHEST

def matmul(leading, trailing):
    return jnp.dot(leading, trailing, precision=HIGHEST, preferred_element_type=jnp.float32)

def rms_norm(values, norm_gain):
    return values * lax.rsqrt(lax.optimization_barrier(jnp.mean(values * values, axis=-1, keepdims=True)) + EPSILON) * norm_gain

def rotate(values, angles):
    count = values.shape[0]
    half = angles.shape[1]
    shaped = values.reshape(count, -1, 2 * half)
    first_half = shaped[..., :half]
    second_half = shaped[..., half:]
    cosine = jnp.cos(angles)[:, None, :]
    sine = jnp.sin(angles)[:, None, :]
    turned = jnp.concatenate([first_half * cosine - second_half * sine, first_half * sine + second_half * cosine], axis=-1)
    return turned.reshape(count, -1)

def slot_forward(inputs, weights):
    tokens, condition, captions, lengths, nulls, bucket = inputs
    null_caption, modulation, projection, text_weight, output_weight, gate_up, down_weight, norm_gains, head_gains, cross_gates = weights
    positions = jnp.arange(SLOT, dtype=jnp.int32)
    clip_length = jnp.where(bucket == 0, SLOT // 4, jnp.where(bucket == 1, SLOT // 2, SLOT)).astype(jnp.int32)
    clip = positions // clip_length
    inside = positions - clip * clip_length
    modulated = matmul(low(jax.nn.silu(condition)), modulation)[clip]
    scale_attn = modulated[:, :D]
    gate_attn = modulated[:, D:2 * D]
    scale_ffn = modulated[:, 2 * D:3 * D]
    gate_ffn = modulated[:, 3 * D:]
    normed = low(rms_norm(tokens, norm_gains[0]) * (1.0 + scale_attn))
    projected = low_back(matmul(normed, projection))
    query_norm = rms_norm(projected[:, :D], head_gains[0])
    key_norm = rms_norm(projected[:, D:2 * D], head_gains[1])
    frequency = 10000.0 ** (-jnp.arange(HD // 2, dtype=jnp.float32) / (HD // 2))
    angles = inside.astype(jnp.float32)[:, None] * frequency[None, :]
    query_rot = low(rotate(query_norm, angles)).reshape(SLOT, H, HD)
    key_rot = low(rotate(key_norm, angles)).reshape(SLOT, H, HD)
    values = low(projected[:, 2 * D:]).reshape(SLOT, H, HD)
    query_cross = low(query_norm).reshape(SLOT, H, HD)
    words = jnp.where(nulls[:, None, None] == 1, null_caption[None], captions).reshape(4 * CAP, TD)
    text_pairs = low_back(matmul(words, text_weight))
    text_keys = low(rms_norm(text_pairs[:, :D], head_gains[2])).reshape(4 * CAP, H, HD)
    text_values = low(text_pairs[:, D:]).reshape(4 * CAP, H, HD)
    caption_index = jnp.arange(4 * CAP, dtype=jnp.int32)
    caption_clip = caption_index // CAP
    caption_live = caption_index - caption_clip * CAP < jnp.repeat(lengths, CAP)
    tanh_gates = jnp.tanh(cross_gates)
    scaling = HD ** (-0.5)

    def block(operands):
        block_query, block_cross, block_clip = operands
        scores = low_back(jnp.einsum('qhd,khd->hqk', block_query, key_rot, precision=HIGHEST) * scaling)
        scores = jnp.where((block_clip[:, None] == clip[None, :])[None], scores, NEGATIVE)
        shares = low(jax.nn.softmax(scores, axis=-1))
        self_out = low_back(jnp.einsum('hqk,khd->qhd', shares, values, precision=HIGHEST))
        cross_scores = low_back(jnp.einsum('qhd,khd->hqk', block_cross, text_keys, precision=HIGHEST) * scaling)
        allowed = (block_clip[:, None] == caption_clip[None, :]) & caption_live[None, :]
        cross_scores = jnp.where(allowed[None], cross_scores, NEGATIVE)
        cross_shares = low(jax.nn.softmax(cross_scores, axis=-1))
        cross_out = low_back(jnp.einsum('hqk,khd->qhd', cross_shares, text_values, precision=HIGHEST))
        return low(self_out + tanh_gates[None, :, None] * cross_out)
    block_rows = min(512, SLOT)
    combined = lax.map(jax.checkpoint(block), (query_rot.reshape(SLOT // block_rows, block_rows, H, HD), query_cross.reshape(SLOT // block_rows, block_rows, H, HD), clip.reshape(SLOT // block_rows, block_rows)))
    combined = combined.reshape(SLOT, D)
    attended = low_back(matmul(combined, output_weight))
    middle = tokens + jnp.tanh(gate_attn) * rms_norm(attended, norm_gains[1])
    normed_ffn = low(rms_norm(middle, norm_gains[2]) * (1.0 + scale_ffn))
    gate_values = low_back(matmul(normed_ffn, gate_up))
    hidden = low(jax.nn.silu(gate_values[:, :FF]) * gate_values[:, FF:])
    lowered = low_back(matmul(hidden, down_weight))
    return middle + jnp.tanh(gate_ffn) * rms_norm(lowered, norm_gains[3])

def reference(tokens, condition, captions, caption_lengths, null_flags, slot_buckets, null_caption, modulation, projection, text_weight, output_weight, gate_up, down_weight, norm_gains, head_gains, cross_gates, cotangent):
    wide = jnp.float32

    def forward(tokens_in, captions_in, null_in, modulation_in, projection_in, text_in, output_in, gate_in, down_in, norm_in, head_in, cross_in):
        weights = (null_in, modulation_in, projection_in, text_in, output_in, gate_in, down_in, norm_in, head_in, cross_in)

        def one_slot(inputs):
            return slot_forward(inputs, weights)
        outputs = lax.map(jax.checkpoint(one_slot), (tokens_in.reshape(N_BUCKET, SLOT, D), condition.astype(wide).reshape(N_BUCKET, 4, D), captions_in.reshape(N_BUCKET, 4, CAP, TD), caption_lengths.reshape(N_BUCKET, 4), null_flags.reshape(N_BUCKET, 4), slot_buckets))
        return outputs.reshape(TOKENS, D)
    mixed, pullback = jax.vjp(forward, tokens.astype(wide), captions.astype(wide), null_caption.astype(wide), modulation.astype(wide), projection.astype(wide), text_weight.astype(wide), output_weight.astype(wide), gate_up.astype(wide), down_weight.astype(wide), norm_gains.astype(wide), head_gains.astype(wide), cross_gates.astype(wide))
    grads = pullback(cotangent.astype(wide))
    return (mixed.astype(jnp.bfloat16), grads[0], grads[1], grads[2], grads[3], grads[4], grads[5], grads[6], grads[7], grads[8], grads[9], grads[10], grads[11])
```

```python
from functools import partial

import jax
import jax.numpy as jnp
from jax import lax
from jax.experimental import pallas as pl
from jax.experimental.pallas import tpu as pltpu
from jax.sharding import PartitionSpec as P

EPSILON = 1e-06
NEGATIVE = -1e30
HIGHEST = lax.Precision.HIGHEST
wide = jnp.float32
narrow = jnp.bfloat16
VMEM_LIMIT = 50 * 2**20


def rms_norm(values, norm_gain):
    return (
        values * lax.rsqrt(jnp.mean(values * values, axis=-1, keepdims=True) + EPSILON) * norm_gain
    )


def dense(leading, trailing):
    return jnp.dot(leading, trailing, preferred_element_type=wide)


def contract_rows(leading, trailing):
    return lax.dot_general(
        leading, trailing, (((0,), (0,)), ((), ())), preferred_element_type=wide
    )


def contract_cols(leading, trailing):
    return lax.dot_general(
        leading, trailing, (((1,), (1,)), ((), ())), preferred_element_type=wide
    )


def pre_attention(tokens_in, modulated, norm_gains):
    model_width = tokens_in.shape[1]
    return rms_norm(tokens_in, norm_gains[0]) * (1.0 + modulated[:, :model_width])


def text_heads(text_pairs, gain):
    model_width = text_pairs.shape[1] // 2
    return (rms_norm(text_pairs[:, :model_width], gain), text_pairs[:, model_width:])


def post_attention(attended, tokens_in, modulated, norm_gains):
    model_width = tokens_in.shape[1]
    middle = tokens_in + jnp.tanh(modulated[:, model_width : 2 * model_width]) * rms_norm(
        attended, norm_gains[1]
    )
    normed_ffn = rms_norm(middle, norm_gains[2]) * (
        1.0 + modulated[:, 2 * model_width : 3 * model_width]
    )
    return (middle, normed_ffn)


def swiglu(gate_values):
    hidden_width = gate_values.shape[1] // 2
    return jax.nn.silu(gate_values[:, :hidden_width]) * gate_values[:, hidden_width:]


def finish(lowered, middle, modulated, norm_gains):
    model_width = middle.shape[1]
    return middle + jnp.tanh(modulated[:, 3 * model_width :]) * rms_norm(lowered, norm_gains[3])


def flip(values, bits):
    count = lax.axis_size("bucket")
    return lax.ppermute(values, "bucket", [(i, i ^ bits) for i in range(count)])


def plane_orders():
    count = lax.axis_size("bucket")
    outer = [1 << i for i in range(1, count.bit_length() - 1)]
    return outer + [1], outer[::-1] + [1]


def plane_gather(values, order):
    blocks = [values]
    for bit in order:
        blocks = blocks + [flip(block, bit) for block in blocks]
    return jnp.concatenate(blocks, axis=0)


def plane_scatter(values, order):
    total = values
    for bit in order[::-1]:
        half = total.shape[0] // 2
        arrived = flip(total[half:].astype(narrow), bit)
        total = total[:half].astype(wide) + arrived.astype(wide)
    return total


def ring_gather(values):
    count = lax.axis_size("seq")
    index = lax.axis_index("seq")
    out = jnp.zeros((count,) + values.shape, values.dtype)
    block = values
    for step in range(count):
        if step > 0:
            block = lax.ppermute(block, "seq", [(i, (i + 1) % count) for i in range(count)])
        out = lax.dynamic_update_index_in_dim(out, block, lax.rem(index - step + count, count), 0)
    return out


def ring_scatter(values):
    count = lax.axis_size("seq")
    index = lax.axis_index("seq")

    def part(step):
        return lax.dynamic_index_in_dim(
            values, lax.rem(index - 1 - step + 2 * count, count), 0, keepdims=False
        ).astype(wide)

    total = part(0)
    for step in range(1, count):
        moved = lax.ppermute(
            total.astype(narrow), "seq", [(i, (i + 1) % count) for i in range(count)]
        )
        total = part(step) + moved.astype(wide)
    return total


def clip_span(bucket, slot_rows, block, block_rows):
    length = jnp.where(
        bucket == 0, slot_rows // 4, jnp.where(bucket == 1, slot_rows // 2, slot_rows)
    )
    clip = lax.div(jnp.int32(block * block_rows), length)
    return clip, clip * length, length


def dot_nt(leading, trailing):
    return contract_cols(leading, trailing)


def attend_kernel(
    blocks, bucket, lengths, gates, q, k, vt, qc, tk, tvt, out, total, cross_total
):
    head = pl.program_id(0)
    rows = q.shape[1]
    block_rows = rows // blocks
    key_index = lax.broadcasted_iota(jnp.int32, (rows, block_rows), 0)
    cap_index = lax.broadcasted_iota(jnp.int32, (tk.shape[2], block_rows), 0)
    for block in range(blocks):
        clip, first, length = clip_span(bucket[0], rows, block, block_rows)
        here = slice(block * block_rows, (block + 1) * block_rows)
        scores = dot_nt(k[0], q[0, here])
        scores = jnp.where(
            (key_index >= first) & (key_index < first + length), scores, NEGATIVE
        )
        peak = jnp.max(scores, axis=0, keepdims=True)
        shares = jnp.exp(scores - peak)
        mass = jnp.sum(shares, axis=0, keepdims=True)
        self_out = dense(vt[0], shares.astype(narrow)) / mass
        total[0, :, here] = peak + jnp.log(mass)
        scores = dot_nt(tk[0, clip], qc[0, here])
        scores = jnp.where(cap_index < lengths[clip], scores, NEGATIVE)
        peak = jnp.max(scores, axis=0, keepdims=True)
        shares = jnp.exp(scores - peak)
        mass = jnp.sum(shares, axis=0, keepdims=True)
        cross_out = dense(tvt[0, clip], shares.astype(narrow)) / mass
        cross_total[0, :, here] = peak + jnp.log(mass)
        out[0, :, here] = (self_out + gates[head] * cross_out).astype(narrow)


def attend_back_kernel(
    blocks, scaling, bucket, lengths, gates, q, k, kt, v, qc, tk, tkt, tv, go, total, cross_total,
    dq, dqc, dk, dv, dtk, dtv, dgate,
):
    head = pl.program_id(0)
    rows = q.shape[1]
    block_rows = rows // blocks
    gate = gates[head]
    key_index = lax.broadcasted_iota(jnp.int32, (rows, block_rows), 0)
    cap_index = lax.broadcasted_iota(jnp.int32, (tk.shape[2], block_rows), 0)
    dk[...] = jnp.zeros_like(dk)
    dv[...] = jnp.zeros_like(dv)
    dtk[...] = jnp.zeros_like(dtk)
    dtv[...] = jnp.zeros_like(dtv)
    for block in range(blocks):
        clip, first, length = clip_span(bucket[0], rows, block, block_rows)
        here = slice(block * block_rows, (block + 1) * block_rows)
        grad = go[0, here]
        scores = dot_nt(k[0], q[0, here])
        scores = jnp.where(
            (key_index >= first) & (key_index < first + length), scores, NEGATIVE
        )
        shares = jnp.exp(scores - total[0, :, here])
        grad_shares = dot_nt(v[0], grad)
        row = jnp.sum(grad_shares * shares, axis=0, keepdims=True)
        grad_scores = (shares * (grad_shares - row)).astype(narrow)
        dv[0] += dense(shares.astype(narrow), grad)
        dk[0] += dense(grad_scores, q[0, here])
        dq[0, :, here] = dense(kt[0], grad_scores) * scaling
        scores = dot_nt(tk[0, clip], qc[0, here])
        scores = jnp.where(cap_index < lengths[clip], scores, NEGATIVE)
        shares = jnp.exp(scores - cross_total[0, :, here])
        grad_shares = dot_nt(tv[0, clip], grad)
        row = jnp.sum(grad_shares * shares, axis=0, keepdims=True)
        grad_scores = (gate * (shares * (grad_shares - row))).astype(narrow)
        dtv[0, clip] += gate * dense(shares.astype(narrow), grad)
        dtk[0, clip] += dense(grad_scores, qc[0, here])
        dqc[0, :, here] = dense(tkt[0, clip], grad_scores) * scaling
        dgate[0, :, here] = row


def head_spec(shape):
    rest = len(shape) - 1
    return pl.BlockSpec((1,) + tuple(shape[1:]), lambda h: (h,) + (0,) * rest)


def call_heads(kernel, scalars, arrays, outs, flops, name):
    heads = arrays[0].shape[0]
    return pl.pallas_call(
        kernel,
        grid=(heads,),
        in_specs=[pl.BlockSpec(memory_space=pltpu.SMEM)] * len(scalars)
        + [head_spec(a.shape) for a in arrays],
        out_specs=[head_spec(o.shape) for o in outs],
        out_shape=outs,
        compiler_params=pltpu.CompilerParams(vmem_limit_bytes=VMEM_LIMIT),
        cost_estimate=pl.CostEstimate(flops=flops, bytes_accessed=16 * 2**20, transcendentals=0),
        name=name,
    )(*scalars, *arrays)


def turn(values, cosine, sine):
    half = cosine.shape[-1]
    first, second = values[..., :half], values[..., half:]
    return jnp.concatenate(
        [first * cosine - second * sine, first * sine + second * cosine], axis=-1
    )


def per_device(
    tokens,
    condition,
    captions,
    caption_lengths,
    null_flags,
    slot_buckets,
    null_caption,
    modulation,
    projection,
    text_weight,
    output_weight,
    gate_up,
    down_weight,
    norm_gains,
    head_gains,
    cross_gates,
    cotangent,
):
    count_s, count_b = lax.axis_size("seq"), lax.axis_size("bucket")
    s, b = lax.axis_index("seq"), lax.axis_index("bucket")
    assert count_s % 4 == 0
    local, width = tokens.shape
    heads = cross_gates.shape[0]
    size = width // heads
    own_heads = heads // count_s
    own = width // count_s
    rows = local * count_s
    places, cap_local, text_width = captions.shape
    cap_rows = places * cap_local
    hidden_width = down_weight.shape[0]
    scaling = size ** (-0.5)
    bucket = slot_buckets[0]
    clip_length = jnp.where(
        bucket == 0, rows // 4, jnp.where(bucket == 1, rows // 2, rows)
    ).astype(jnp.int32)
    order_a, order_b = plane_orders()
    halves = ((slice(0, local // 2), order_a), (slice(local // 2, local), order_b))

    own_projection = lax.dynamic_index_in_dim(
        projection.reshape(-1, 3, count_s, own), s, 2, keepdims=False
    ).reshape(-1, 3 * own)
    own_projection = lax.all_gather(own_projection, "bucket", axis=0, tiled=True)
    full_output = lax.all_gather(output_weight, "bucket", axis=0, tiled=True)

    silu_cond = jax.nn.silu(condition).astype(narrow)
    cond_columns = lax.all_to_all(silu_cond, "bucket", 1, 0, tiled=True)
    mod_width = modulation.shape[1] // count_s
    mod_part = dense(cond_columns, lax.dynamic_slice_in_dim(modulation, s * mod_width, mod_width, 1))
    mod_part = lax.all_to_all(mod_part, "bucket", 0, 0, tiled=True)
    mod_part = jnp.sum(mod_part.reshape(count_b, places, mod_width), axis=0)
    clip_of = (jnp.arange(count_s, dtype=jnp.int32) * local) // clip_length
    chosen = clip_of[:, None] == jnp.arange(places, dtype=jnp.int32)[None, :]
    mod_rows = jnp.sum(jnp.where(chosen[:, :, None], mod_part[None], 0.0), axis=1)
    modulated = lax.all_to_all(mod_rows, "seq", 0, 1, tiled=True)

    tokens_in = tokens.astype(wide)
    normed_full, pre_pull = jax.vjp(pre_attention, tokens_in, modulated, norm_gains)
    normed = ring_gather(normed_full.astype(narrow)).reshape(rows, width)

    null_rows = lax.dynamic_slice_in_dim(null_caption, s * cap_local, cap_local, 0)
    is_null = null_flags[:, None, None] == 1
    words_own = jnp.where(is_null, null_rows[None], captions).reshape(cap_rows, text_width)
    text_rows = text_weight.shape[0]
    block_ids = [0]
    for bit in order_a:
        block_ids = block_ids + [k | bit for k in block_ids]
    ids_b = [0]
    for bit in order_b:
        ids_b = ids_b + [k | bit for k in ids_b]
    from_a_to_b = [block_ids.index(k) for k in ids_b]

    def word_block(k):
        piece = lax.dynamic_slice_in_dim(words_own, jnp.bitwise_xor(b, k) * text_rows, text_rows, 1)
        return flip(piece, k) if k else piece

    words = jnp.concatenate([word_block(k) for k in block_ids], axis=0)
    pairs_a = dense(words, text_weight[:, :width])
    pairs_b = dense(words, text_weight[:, width:])
    pairs_b = jnp.concatenate(
        [pairs_b[i * cap_rows : (i + 1) * cap_rows] for i in from_a_to_b], axis=0
    )
    text_pairs = jnp.concatenate(
        [
            plane_scatter(pairs_a.astype(narrow), order_a),
            plane_scatter(pairs_b.astype(narrow), order_b),
        ],
        axis=1,
    )
    text_outs, text_pull = jax.vjp(text_heads, text_pairs, head_gains[2])
    text_kv = jnp.stack([o.astype(narrow).reshape(cap_rows, count_s, own) for o in text_outs])
    text_kv = lax.all_to_all(text_kv.transpose(2, 0, 1, 3), "seq", 0, 0, tiled=True)
    text_kv = text_kv.reshape(count_s, 2, places, cap_local, own_heads, size)
    text_kv = text_kv.transpose(1, 4, 2, 0, 3, 5).reshape(
        2, own_heads, places, count_s * cap_local, size
    )
    text_keys, text_values = text_kv[0], text_kv[1]

    projected = dense(normed, own_projection)
    gain_q = lax.dynamic_slice_in_dim(head_gains[0], s * own, own, 0)
    gain_k = lax.dynamic_slice_in_dim(head_gains[1], s * own, own, 0)
    raw_q, raw_k, raw_v = (projected[:, i * own : (i + 1) * own] for i in range(3))
    squares = jnp.stack([jnp.sum(raw_q * raw_q, axis=1), jnp.sum(raw_k * raw_k, axis=1)])
    rate = lax.rsqrt(lax.psum(squares, "seq") / width + EPSILON)
    hat_q = raw_q * rate[0][:, None]
    hat_k = raw_k * rate[1][:, None]
    inside = lax.rem(jnp.arange(rows, dtype=jnp.int32), clip_length)
    half = size // 2
    frequency = 10000.0 ** (-jnp.arange(half, dtype=wide) / half)
    angles = inside.astype(wide)[:, None] * frequency[None, :]
    cosine, sine = jnp.cos(angles), jnp.sin(angles)

    def to_heads(values):
        return values.reshape(rows, own_heads, size).transpose(1, 0, 2)

    def from_heads(values):
        return values.transpose(1, 0, 2).reshape(rows, own)

    norm_q = to_heads(hat_q * gain_q)
    query = turn(norm_q, cosine, sine).astype(narrow)
    query_cross = norm_q.astype(narrow)
    key = turn(to_heads(hat_k * gain_k), cosine, sine).astype(narrow)
    value = to_heads(raw_v.astype(narrow))
    scaled = (query * scaling).astype(narrow)
    scaled_cross = (query_cross * scaling).astype(narrow)

    tanh_gates = jnp.tanh(cross_gates)
    own_gates = lax.dynamic_slice_in_dim(tanh_gates, s * own_heads, own_heads, 0)
    scalars = (slot_buckets, caption_lengths, own_gates)
    span = rows + count_s * cap_local
    products = own_heads * rows * span * size * 2
    row_shape = jax.ShapeDtypeStruct((own_heads, 1, rows), wide)
    combined, total, cross_total = call_heads(
        partial(attend_kernel, count_s),
        scalars,
        (
            scaled,
            key,
            value.transpose(0, 2, 1),
            scaled_cross,
            text_keys,
            text_values.transpose(0, 1, 3, 2),
        ),
        (jax.ShapeDtypeStruct((own_heads, size, rows), narrow), row_shape, row_shape),
        2 * products,
        "attend",
    )
    combined = combined.reshape(own, rows).T
    combined = lax.all_to_all(combined, "seq", 0, 1, tiled=True)

    attended = dense(combined, full_output)
    (middle, ffn_full), post_pull = jax.vjp(
        post_attention, attended, tokens_in, modulated, norm_gains
    )
    normed_ffn = ffn_full.astype(narrow)

    own_hidden = hidden_width
    gate_rows = gate_up.shape[0]
    own_gate_up = lax.all_to_all(
        gate_up.reshape(gate_rows, 2, count_b, own_hidden), "bucket", 2, 0, tiled=True
    ).reshape(count_b * gate_rows, 2 * own_hidden)
    gathered, hiddens, pulls, lows = [], [], [], []
    for part, order in halves:
        plane = plane_gather(normed_ffn[part], order)
        hidden_full, pull = jax.vjp(swiglu, dense(plane, own_gate_up))
        hidden = hidden_full.astype(narrow)
        lows.append(plane_scatter(dense(hidden, down_weight), order))
        gathered.append(plane)
        hiddens.append(hidden)
        pulls.append(pull)
    lowered = jnp.concatenate(lows, axis=0)
    mixed, finish_pull = jax.vjp(finish, lowered, middle, modulated, norm_gains)
    grad_lowered, grad_middle, grad_modulated_last, grad_norm_last = finish_pull(
        cotangent.astype(wide)
    )
    grad_lowered_low = grad_lowered.astype(narrow)
    grad_normed_ffn, grad_down, grad_gate_up = [], 0.0, 0.0
    for (part, order), plane, hidden, pull in zip(halves, gathered, hiddens, pulls, strict=True):
        upstream = plane_gather(grad_lowered_low[part], order)
        (grad_gate_values,) = pull(contract_cols(upstream, down_weight))
        grad_gate_low = grad_gate_values.astype(narrow)
        grad_normed_ffn.append(plane_scatter(contract_cols(grad_gate_low, own_gate_up), order))
        grad_down = grad_down + contract_rows(hidden, upstream)
        grad_gate_up = grad_gate_up + contract_rows(plane, grad_gate_low)
    grad_normed_ffn = jnp.concatenate(grad_normed_ffn, axis=0)
    down_share = lax.psum_scatter(
        grad_down.astype(narrow), "seq", scatter_dimension=0, tiled=True
    ).astype(wide)
    gate_share = lax.psum_scatter(
        grad_gate_up.astype(narrow).reshape(count_b, gate_rows, 2 * own_hidden),
        "seq",
        scatter_dimension=1,
        tiled=True,
    )
    share_rows = gate_rows // count_s
    gate_share = lax.all_to_all(gate_share, "bucket", 0, 0, tiled=True)
    gate_share = (
        gate_share.reshape(count_b, share_rows, 2, own_hidden)
        .transpose(1, 2, 0, 3)
        .reshape(share_rows, 2 * count_b * own_hidden)
        .astype(wide)
    )

    grad_attended, grad_tokens_post, grad_modulated_post, grad_norm_post = post_pull(
        (grad_middle, grad_normed_ffn)
    )
    grad_attended_low = grad_attended.astype(narrow)
    grad_combined = contract_cols(grad_attended_low, full_output).astype(narrow)
    grad_output = contract_rows(combined, grad_attended_low).astype(narrow)
    output_share = lax.psum_scatter(
        grad_output, ("bucket", "seq"), scatter_dimension=0, tiled=True
    ).astype(wide)
    grad_heads = to_heads(lax.all_to_all(grad_combined, "seq", 1, 0, tiled=True))
    head_rows = jax.ShapeDtypeStruct((own_heads, rows, size), wide)
    head_columns = jax.ShapeDtypeStruct((own_heads, size, rows), wide)
    text_shape = jax.ShapeDtypeStruct(text_keys.shape, wide)
    grad_query, grad_cross, grad_key, grad_value, grad_text_keys, grad_text_values, grad_gates = (
        call_heads(
            partial(attend_back_kernel, count_s, scaling),
            scalars,
            (
                scaled,
                key,
                key.transpose(0, 2, 1),
                value,
                scaled_cross,
                text_keys,
                text_keys.transpose(0, 1, 3, 2),
                text_values,
                grad_heads,
                total,
                cross_total,
            ),
            (
                head_columns,
                head_columns,
                head_rows,
                head_rows,
                text_shape,
                text_shape,
                row_shape,
            ),
            5 * products,
            "attend_back",
        )
    )

    grad_kv = jnp.stack([grad_text_keys, grad_text_values]).astype(narrow)
    grad_kv = grad_kv.reshape(2, own_heads, places, count_s, cap_local, size)
    grad_kv = grad_kv.transpose(3, 0, 2, 4, 1, 5).reshape(count_s, 2, cap_rows, own)
    grad_kv = lax.all_to_all(grad_kv, "seq", 0, 0, tiled=True)
    grad_kv = grad_kv.transpose(1, 2, 0, 3).reshape(2, cap_rows, width).astype(wide)
    grad_pairs, grad_gain_text = text_pull((grad_kv[0], grad_kv[1]))
    grad_pairs_low = grad_pairs.astype(narrow)
    plane_a = plane_gather(grad_pairs_low[:, :width], order_a)
    plane_b = plane_gather(grad_pairs_low[:, width:], order_b)
    plane_b = jnp.concatenate(
        [
            plane_b[ids_b.index(k) * cap_rows : (ids_b.index(k) + 1) * cap_rows]
            for k in block_ids
        ],
        axis=0,
    )
    grad_text = jnp.concatenate(
        [contract_rows(words, plane_a), contract_rows(words, plane_b)], axis=1
    )
    text_share = lax.psum_scatter(
        grad_text.astype(narrow), "seq", scatter_dimension=0, tiled=True
    ).astype(wide)
    grad_words = (
        contract_cols(plane_a, text_weight[:, :width])
        + contract_cols(plane_b, text_weight[:, width:])
    ).astype(narrow)
    pieces = []
    for i, k in enumerate(block_ids):
        piece = grad_words[i * cap_rows : (i + 1) * cap_rows]
        pieces.append(flip(piece, k) if k else piece)
    pieces = jnp.stack([pieces[block_ids.index(k)] for k in range(count_b)])
    grad_words = jnp.concatenate(
        [
            lax.dynamic_index_in_dim(pieces, jnp.bitwise_xor(b, j), 0, keepdims=False)
            for j in range(count_b)
        ],
        axis=1,
    ).reshape(places, cap_local, text_width)
    grad_captions = jnp.where(is_null, 0.0, grad_words.astype(wide))
    null_local = jnp.sum(jnp.where(is_null, grad_words.astype(wide), 0.0), axis=0).astype(narrow)
    null_share = lax.all_to_all(null_local, "bucket", 0, 0, tiled=True)
    null_share = jnp.sum(null_share.reshape(count_b, -1, text_width).astype(wide), axis=0)
    null_share = lax.ppermute(
        null_share,
        ("bucket", "seq"),
        [(i * count_s + j, j * count_b + i) for i in range(count_b) for j in range(count_s)],
    )

    back_q = turn(grad_query.transpose(0, 2, 1), cosine, -sine) + grad_cross.transpose(0, 2, 1)
    back_q = from_heads(back_q)
    back_k = from_heads(turn(grad_key * 1.0, cosine, -sine))
    back_v = from_heads(grad_value)
    scaled_q, scaled_k = back_q * gain_q, back_k * gain_k
    means = jnp.stack([jnp.sum(scaled_q * hat_q, axis=1), jnp.sum(scaled_k * hat_k, axis=1)])
    means = lax.psum(means, "seq") / width
    grad_projected = jnp.concatenate(
        [
            rate[0][:, None] * (scaled_q - hat_q * means[0][:, None]),
            rate[1][:, None] * (scaled_k - hat_k * means[1][:, None]),
            back_v,
        ],
        axis=1,
    ).astype(narrow)
    grad_projection = contract_rows(normed, grad_projected).astype(narrow)
    proj_share = lax.psum_scatter(grad_projection, "bucket", scatter_dimension=0, tiled=True)
    proj_share = lax.all_to_all(
        proj_share.reshape(count_s, -1, 3 * own), "seq", 0, 0, tiled=True
    )
    proj_share = (
        proj_share.reshape(count_s, -1, 3, own)
        .transpose(1, 2, 0, 3)
        .reshape(-1, 3 * width)
        .astype(wide)
    )
    grad_normed = ring_scatter(
        contract_cols(grad_projected, own_projection).reshape(count_s, local, width)
    )
    grad_tokens_pre, grad_modulated_pre, grad_norm_pre = pre_pull(grad_normed)
    grad_tokens = grad_tokens_pre + grad_tokens_post

    grad_modulated = grad_modulated_pre + grad_modulated_post + grad_modulated_last
    my_clip = (s * local) // clip_length
    placed = jnp.where(
        jnp.arange(places, dtype=jnp.int32)[:, None] == my_clip, grad_modulated, 0.0
    )
    placed = lax.all_gather(lax.psum(placed, "seq"), "bucket", axis=0, tiled=True)
    mod_rows_out = silu_cond.shape[1] // (count_s * count_b)
    cond_own = lax.dynamic_slice_in_dim(cond_columns, s * mod_rows_out, mod_rows_out, 1)
    mod_share = lax.dot_general(
        cond_own.astype(wide), placed, (((0,), (0,)), ((), ())), precision=HIGHEST
    )

    def place(values):
        return lax.dynamic_update_slice_in_dim(jnp.zeros((width,), wide), values, s * own, 0)

    gate_sums = lax.dynamic_update_slice_in_dim(
        jnp.zeros((heads,), wide),
        jnp.sum(grad_gates, axis=(1, 2)) * (1.0 - own_gates * own_gates),
        s * own_heads,
        0,
    )
    small = jnp.concatenate(
        [
            grad_norm_pre + grad_norm_post + grad_norm_last,
            jnp.stack(
                [
                    place(jnp.sum(back_q * hat_q, axis=0)),
                    place(jnp.sum(back_k * hat_k, axis=0)),
                    grad_gain_text,
                    jnp.pad(gate_sums, (0, width - heads)),
                ]
            ),
        ],
        axis=0,
    )
    small = lax.psum(small, ("bucket", "seq"))
    share = width // (count_b * count_s)
    own_small = lax.dynamic_slice_in_dim(small, (b * count_s + s) * share, share, 1)
    return (
        mixed.astype(narrow),
        grad_tokens,
        grad_captions,
        null_share,
        mod_share,
        proj_share,
        text_share,
        output_share,
        gate_share,
        down_share,
        own_small[:4],
        own_small[4:7],
        small[7, :heads],
    )


def solution(mesh):
    whole = P(("bucket", "seq"), None)
    shard = P("bucket", None)
    return jax.shard_map(
        per_device,
        mesh=mesh,
        in_specs=(
            whole,
            shard,
            P("bucket", "seq", None),
            P("bucket"),
            P("bucket"),
            P("bucket"),
            P(),
            shard,
            shard,
            shard,
            shard,
            shard,
            shard,
            P(),
            P(),
            P(),
            whole,
        ),
        out_specs=(
            whole,
            whole,
            P("bucket", "seq", None),
            whole,
            whole,
            whole,
            whole,
            whole,
            whole,
            whole,
            P(None, ("bucket", "seq")),
            P(None, ("bucket", "seq")),
            P(),
        ),
        check_vma=False,
    )
```

```python
from functools import partial

import jax
import jax.numpy as jnp
from jax import lax
from jax.experimental import pallas as pl
from jax.experimental.pallas import tpu as pltpu
from jax.sharding import PartitionSpec as P

EPSILON = 1e-06
NEGATIVE = -1e30
HIGHEST = lax.Precision.HIGHEST
wide = jnp.float32
narrow = jnp.bfloat16
VMEM_LIMIT = 50 * 2**20


def rms_norm(values, norm_gain):
    return (
        values * lax.rsqrt(jnp.mean(values * values, axis=-1, keepdims=True) + EPSILON) * norm_gain
    )


def dense(leading, trailing):
    return jnp.dot(leading, trailing, preferred_element_type=wide)


def contract_rows(leading, trailing):
    return lax.dot_general(
        leading, trailing, (((0,), (0,)), ((), ())), preferred_element_type=wide
    )


def contract_cols(leading, trailing):
    return lax.dot_general(
        leading, trailing, (((1,), (1,)), ((), ())), preferred_element_type=wide
    )


def pre_attention(tokens_in, modulated, norm_gains):
    model_width = tokens_in.shape[1]
    return rms_norm(tokens_in, norm_gains[0]) * (1.0 + modulated[:, :model_width])


def text_heads(text_pairs, gain):
    model_width = text_pairs.shape[1] // 2
    return (rms_norm(text_pairs[:, :model_width], gain), text_pairs[:, model_width:])


def post_attention(attended, tokens_in, modulated, norm_gains):
    model_width = tokens_in.shape[1]
    middle = tokens_in + jnp.tanh(modulated[:, model_width : 2 * model_width]) * rms_norm(
        attended, norm_gains[1]
    )
    normed_ffn = rms_norm(middle, norm_gains[2]) * (
        1.0 + modulated[:, 2 * model_width : 3 * model_width]
    )
    return (middle, normed_ffn)


def swiglu(gate_values):
    hidden_width = gate_values.shape[1] // 2
    return jax.nn.silu(gate_values[:, :hidden_width]) * gate_values[:, hidden_width:]


def finish(lowered, middle, modulated, norm_gains):
    model_width = middle.shape[1]
    return middle + jnp.tanh(modulated[:, 3 * model_width :]) * rms_norm(lowered, norm_gains[3])


MESH = pl.DeviceIdType.MESH


class Transfers:
    def __init__(self, send, arrive):
        self.send, self.arrive, self.used = send, arrive, 0
        self.open = []

    def start(self, source, target, device):
        copy = pltpu.make_async_remote_copy(
            src_ref=source,
            dst_ref=target,
            send_sem=self.send.at[self.used],
            recv_sem=self.arrive.at[self.used],
            device_id=device,
            device_id_type=MESH,
        )
        self.used += 1
        copy.start()
        self.open.append(copy)
        return copy

    def finish(self):
        for copy in self.open:
            copy.wait_send()


def meet(devices):
    barrier = pltpu.get_barrier_semaphore()
    for device in devices:
        pl.semaphore_signal(barrier, inc=1, device_id=device, device_id_type=MESH)
    pl.semaphore_wait(barrier, len(devices))


def partner(bits):
    return {"bucket": jnp.bitwise_xor(lax.axis_index("bucket"), bits)}


def outer_bits(count):
    return [1 << i for i in range(1, count.bit_length() - 1)]


def block_index(k, count):
    return (k >> 1) + (k & 1) * (count // 2)


def last_bit(block, order):
    return [bit for bit in order if block & bit][-1]


class PlaneExchange:
    def __init__(
        self, count, links, gathered, partial=None, arrived_core=None, arrived_outer=None, natural=False
    ):
        self.count, self.links, self.natural = count, links, natural
        self.index = lax.axis_index("bucket")
        self.gathered, self.partial = gathered, partial
        self.arrived_core, self.arrived_outer = arrived_core, arrived_outer
        bits = outer_bits(count)
        self.orders = (bits, bits[::-1])
        self.outer = [k for k in range(0, count, 2)]
        self.rows = gathered.shape[1] // 2
        self.coming, self.slots = {}, {}
        self.blocks = [0]

    def part(self, ref, block, half):
        return ref.at[block, pl.ds(half * self.rows, self.rows)]

    def place(self, block):
        return jnp.bitwise_xor(self.index, block) if self.natural else block_index(block, self.count)

    def onward(self, half, block, bit):
        source = self.place(block)
        target = source if self.natural else self.place(block | bit)
        self.coming[half, block | bit] = self.links.start(
            self.part(self.gathered, source, half),
            self.part(self.gathered, target, half),
            partner(bit),
        )

    def forward(self, half, block):
        order = self.orders[half]
        later = order if block == 0 else order[order.index(last_bit(block, order)) + 1 :]
        for bit in later:
            self.onward(half, block, bit)

    def forward_core(self, half, block):
        self.onward(half, block, 1)

    def arrive(self, block):
        for half in range(2):
            self.coming[half, block].wait_recv()

    def begin(self):
        for step in range(len(self.orders[0])):
            for half in range(2):
                self.onward(half, 0, self.orders[half][step])
        for half in range(2):
            self.forward_core(half, 0)

    def run_gather(self, compute, scatter=None):
        self.begin()
        compute([0])
        levels = len(self.orders[0])
        self.arrive(1)
        compute([block_index(1, self.count)])
        if scatter is not None:
            self.send_core(1)
        for level in range(1, levels + 1):
            here = [k for k in self.outer if bin(k).count("1") == level]
            steps = [(half, k) for k in here for half in range(2)]
            steps.sort(key=lambda s: [self.orders[s[0]].index(bit) for bit in self.orders[s[0]] if s[1] & bit][::-1])
            for half, k in steps:
                self.coming[half, k].wait_recv()
                self.forward(half, k)
                self.forward_core(half, k)
            if level == 2 and scatter is not None:
                next(scatter)
            compute([block_index(k, self.count) for k in here])
            for k in here:
                self.arrive(k | 1)
            compute([block_index(k | 1, self.count) for k in here])
            for k in here:
                if scatter is not None:
                    self.send_core(k | 1)

    def send_core(self, block):
        place = block_index(block, self.count)
        target = self.arrived_core.at[block >> 1]
        self.slots["core", block & ~1] = self.links.start(self.partial.at[place], target, partner(1))

    def total(self, half, block, slots):
        rows = pl.ds(half * self.rows, self.rows)
        value = self.partial[block >> 1, rows].astype(wide)
        value = value + self.arrived_core[block >> 1, rows].astype(wide)
        for slot in slots:
            value = value + self.arrived_outer[half, slot].astype(wide)
        return value

    def scatter(self, finish):
        slot_of = {}
        waiting = {(half, k): [] for half in range(2) for k in self.outer}
        core_seen = set()
        left = [list(self.outer), list(self.outer)]
        for step in range(len(self.orders[0])):
            jobs = []
            for half in range(2):
                bit = self.orders[half][::-1][step]
                jobs.append([(half, bit, k) for k in left[half] if k & bit])
                left[half] = [k for k in left[half] if not k & bit]
            for pair in zip(*jobs, strict=True):
                for half, bit, k in pair:
                    if k not in core_seen:
                        self.slots["core", k].wait_recv()
                        core_seen.add(k)
                    for copy, _ in waiting[half, k]:
                        copy.wait_recv()
                    rows = pl.ds(half * self.rows, self.rows)
                    total = self.total(half, k, [slot for _, slot in waiting[half, k]])
                    self.partial[k >> 1, rows] = total.astype(narrow)
                    slot = slot_of.setdefault((half, bit, k ^ bit), len([1 for h, *_ in slot_of if h == half]))
                    copy = self.links.start(
                        self.partial.at[k >> 1, rows], self.arrived_outer.at[half, slot], partner(bit)
                    )
                    waiting[half, k ^ bit].append((copy, slot))
                yield
        if 0 not in core_seen:
            self.slots["core", 0].wait_recv()
        for half in range(2):
            for copy, _ in waiting[half, 0]:
                copy.wait_recv()
            finish(half, self.total(half, 0, [slot for _, slot in waiting[half, 0]]))


def plane_partners(count):
    return [partner(bit) for bit in outer_bits(count) + [1]]


def plane_copies(count):
    outer = count // 2
    return 2 * (outer - 1) + 2 * outer, outer + 2 * (outer - 1)


def spans(blocks):
    runs = []
    for block in sorted(blocks):
        if runs and runs[-1][1] == block:
            runs[-1][1] = block + 1
        else:
            runs.append([block, block + 1])
    return runs


def each(blocks, body):
    for first, end in spans(blocks):
        if end - first == 1:
            body(first)
        else:
            lax.fori_loop(first, end, lambda i, _: (body(i), 0)[1], 0)


def ffn_kernel(
    count, x, gate_up, down, lowered, plane_out, values_out, hidden_out,
    plane, partial, core, outer, values, hidden, send, arrive, local,
):
    links = Transfers(send, arrive)
    meet(plane_partners(count))
    units = down.shape[0]
    wide_block = 256
    plane[0] = x[...]
    saved = pltpu.make_async_copy(plane, plane_out, local.at[0])

    def compute(blocks):
        def one(place):
            for start in range(0, units, wide_block):
                columns = slice(start, start + wide_block)
                after = slice(units + start, units + start + wide_block)
                gate = dense(plane[place], gate_up[:, columns])
                up = dense(plane[place], gate_up[:, after])
                values[place, :, columns] = gate
                values[place, :, after] = up
                hidden[place, :, columns] = (jax.nn.silu(gate) * up).astype(narrow)
            partial[place] = dense(hidden[place], down[...]).astype(narrow)

        each(blocks, one)

    exchange = PlaneExchange(count, links, plane, partial, core, outer)
    def finish(half, total):
        lowered[pl.ds(half * exchange.rows, exchange.rows)] = total

    sums = exchange.scatter(finish)
    exchange.run_gather(compute, sums)
    saved.start()
    kept = pltpu.make_async_copy(values, values_out, local.at[1])
    kept.start()
    held = pltpu.make_async_copy(hidden, hidden_out, local.at[2])
    held.start()

    for _ in sums:
        pass
    saved.wait()
    kept.wait()
    held.wait()
    links.finish()


def plane_scratch(count, rows, width):
    outer = count // 2
    return [
        pltpu.VMEM((count, rows, width), narrow),
        pltpu.VMEM((count, rows, width), narrow),
        pltpu.VMEM((outer, rows, width), narrow),
        pltpu.VMEM((2, outer - 1, rows // 2, width), narrow),
    ]


def ffn_forward(count, x, gate_up, down):
    rows, width = x.shape
    units = down.shape[0]
    copies = sum(plane_copies(count))
    vmem, anywhere = pl.BlockSpec(memory_space=pltpu.VMEM), pl.BlockSpec(memory_space=pl.ANY)
    return pl.pallas_call(
        partial(ffn_kernel, count),
        in_specs=[vmem] * 3,
        out_specs=[vmem] + [anywhere] * 3,
        out_shape=[
            jax.ShapeDtypeStruct((rows, width), wide),
            jax.ShapeDtypeStruct((count, rows, width), narrow),
            jax.ShapeDtypeStruct((count, rows, 2 * units), wide),
            jax.ShapeDtypeStruct((count, rows, units), narrow),
        ],
        scratch_shapes=plane_scratch(count, rows, width)
        + [
            pltpu.VMEM((count, rows, 2 * units), wide),
            pltpu.VMEM((count, rows, units), narrow),
            pltpu.SemaphoreType.DMA((copies,)),
            pltpu.SemaphoreType.DMA((copies,)),
            pltpu.SemaphoreType.DMA((3,)),
        ],
        compiler_params=pltpu.CompilerParams(
            collective_id=1, has_side_effects=True, vmem_limit_bytes=60 * 2**20
        ),
        name="ffn_forward",
    )(x, gate_up, down)

def ffn_back_kernel(
    count, g, gate_up, down, values_in, x_in, hidden_in, grad_normed, grad_gate_up, grad_down,
    plane, partial, core, outer, values, grads, taken, send, arrive, local,
):
    links = Transfers(send, arrive)
    fetch = pltpu.make_async_copy(values_in, values, local.at[2])
    fetch.start()
    meet(plane_partners(count))
    units, width = down.shape
    wide_block = 256
    plane[0] = g[...]
    fetched = []

    def compute(places):
        if not fetched:
            fetch.wait()
            fetched.append(True)

        def one(place):
            for start in range(0, units, wide_block):
                columns = slice(start, start + wide_block)
                after = slice(units + start, units + start + wide_block)
                back = contract_cols(plane[place], down[columns])
                gate, up = values[place, :, columns], values[place, :, after]
                sigma = jax.nn.sigmoid(gate)
                grads[place, :, columns] = (
                    back * up * (sigma * (1.0 + gate * (1.0 - sigma)))
                ).astype(narrow)
                grads[place, :, after] = (back * (gate * sigma)).astype(narrow)
            partial[place] = contract_cols(grads[place], gate_up[...]).astype(narrow)

        each(places, one)

    exchange = PlaneExchange(count, links, plane, partial, core, outer)

    def finish(half, total):
        grad_normed[pl.ds(half * exchange.rows, exchange.rows)] = total

    sums = exchange.scatter(finish)
    exchange.run_gather(compute, sums)

    jobs = [(x_in, grads, grad_gate_up, i) for i in range(width // wide_block)]
    jobs += [(hidden_in, plane, grad_down, i) for i in range(units // wide_block)]

    def take(number):
        source, _, _, i = jobs[number]
        columns = pl.ds(i * wide_block, wide_block)
        return pltpu.make_async_copy(
            source.at[:, :, columns], taken.at[number % 2], local.at[number % 2]
        )

    def work(number):
        if number + 1 < len(jobs):
            take(number + 1).start()
        take(number).wait()
        _, upstream, out, i = jobs[number]
        for start in range(0, upstream.shape[2], 512):
            columns = slice(start, start + 512)
            out[i * wide_block : (i + 1) * wide_block, columns] = contract_rows(
                flat(taken[number % 2]), flat(upstream[:, :, columns])
            ).astype(narrow)

    take(0).start()
    done = 0
    for _ in sums:
        for number in range(done, min(done + 3, len(jobs))):
            work(number)
            done += 1
    for number in range(done, len(jobs)):
        work(number)
    links.finish()


def ffn_backward(count, g, gate_up, down, values, x, hidden):
    rows, width = g.shape
    units = down.shape[0]
    copies = sum(plane_copies(count))
    vmem, anywhere = pl.BlockSpec(memory_space=pltpu.VMEM), pl.BlockSpec(memory_space=pl.ANY)
    return pl.pallas_call(
        partial(ffn_back_kernel, count),
        in_specs=[vmem] * 3 + [anywhere] * 3,
        out_specs=[vmem] * 3,
        out_shape=[
            jax.ShapeDtypeStruct((rows, width), wide),
            jax.ShapeDtypeStruct((width, 2 * units), narrow),
            jax.ShapeDtypeStruct((units, width), narrow),
        ],
        scratch_shapes=plane_scratch(count, rows, width)
        + [
            pltpu.VMEM((count, rows, 2 * units), wide),
            pltpu.VMEM((count, rows, 2 * units), narrow),
            pltpu.VMEM((2, count, rows, 256), narrow),
            pltpu.SemaphoreType.DMA((copies,)),
            pltpu.SemaphoreType.DMA((copies,)),
            pltpu.SemaphoreType.DMA((3,)),
        ],
        compiler_params=pltpu.CompilerParams(
            collective_id=2, has_side_effects=True, vmem_limit_bytes=62 * 2**20
        ),
        name="ffn_backward",
    )(g, gate_up, down, values, x, hidden)


def seq_device(index):
    return {"seq": index}


def mod_kernel(
    count, depth, pieces, columns, shard, words, got, mods, gathered, spread, product, back, send,
    arrive,
):
    links = Transfers(send, arrive)
    b, s = lax.axis_index("bucket"), lax.axis_index("seq")
    others = [partner(k) for k in range(1, count)]
    along = [seq_device(lax.rem(s + step, depth)) for step in range(1, depth)]
    meet(others + along)
    first = [
        links.start(pieces.at[jnp.bitwise_xor(b, k)], got.at[k], others[k - 1])
        for k in range(1, count)
    ]
    got[0] = pieces[b]
    gathered[b] = shard[...]
    exchange = PlaneExchange(count, links, gathered, natural=True)
    for copy in first:
        copy.wait_recv()
    for k in range(count):
        product[k] = dense(got[k].astype(narrow), columns[...])
    second = [links.start(product.at[k], back.at[k - 1], others[k - 1]) for k in range(1, count)]
    feature = spread.shape[2]

    def features(target):
        return words.at[:, pl.ds(pl.multiple_of(target * feature, 128), feature)]

    far = [
        links.start(features(jnp.bitwise_xor(b, k)), spread.at[b], others[k - 1])
        for k in range(1, count)
    ]
    spread[b] = words[:, pl.ds(pl.multiple_of(b * feature, 128), feature)]
    total = product[0]
    for k, copy in enumerate(second):
        copy.wait_recv()
        total = total + back[k]
    mods[s] = total
    third = [links.start(mods.at[s], mods.at[s], device) for device in along]
    exchange.run_gather(lambda places: None)
    for copy in third + far:
        copy.wait_recv()
    links.finish()


def modulate(count, depth, pieces, columns, shard, words):
    vmem = pl.BlockSpec(memory_space=pltpu.VMEM)
    places, width = pieces.shape[1], columns.shape[1]
    copies = 3 * (count - 1) + depth - 1 + plane_copies(count)[0]
    return pl.pallas_call(
        partial(mod_kernel, count, depth),
        in_specs=[vmem] * 4,
        out_specs=[vmem] * 4,
        out_shape=[
            jax.ShapeDtypeStruct(pieces.shape, wide),
            jax.ShapeDtypeStruct((depth, places, width), wide),
            jax.ShapeDtypeStruct((count,) + shard.shape, narrow),
            jax.ShapeDtypeStruct((count, words.shape[0], words.shape[1] // count), narrow),
        ],
        scratch_shapes=[
            pltpu.VMEM((count, places, width), wide),
            pltpu.VMEM((count - 1, places, width), wide),
            pltpu.SemaphoreType.DMA((copies,)),
            pltpu.SemaphoreType.DMA((copies,)),
        ],
        compiler_params=pltpu.CompilerParams(
            collective_id=3, has_side_effects=True, vmem_limit_bytes=32 * 2**20
        ),
        name="modulate",
    )(pieces, columns, shard, words)


def small_kernel(count, depth, values, out, along, send, arrive):
    links = Transfers(send, arrive)
    s = lax.axis_index("seq")
    others = [partner(k) for k in range(1, count)]
    line = [seq_device(lax.rem(s + step, depth)) for step in range(1, depth)]
    meet(others + line)
    first = [links.start(values, along.at[i], device) for i, device in enumerate(line)]
    total = values[...]
    for i, copy in enumerate(first):
        copy.wait_recv()
        total = total + along[i]
    out[0] = total
    second = [links.start(out.at[0], out.at[k], others[k - 1]) for k in range(1, count)]
    for copy in second:
        copy.wait_recv()
    links.finish()


def gather_small(count, depth, values, collective_id):
    vmem = pl.BlockSpec(memory_space=pltpu.VMEM)
    copies = count - 1 + depth - 1
    return pl.pallas_call(
        partial(small_kernel, count, depth),
        in_specs=[vmem],
        out_specs=vmem,
        out_shape=jax.ShapeDtypeStruct((count,) + values.shape, wide),
        scratch_shapes=[
            pltpu.VMEM((depth - 1,) + values.shape, wide),
            pltpu.SemaphoreType.DMA((copies,)),
            pltpu.SemaphoreType.DMA((copies,)),
        ],
        compiler_params=pltpu.CompilerParams(
            collective_id=collective_id, has_side_effects=True, vmem_limit_bytes=32 * 2**20
        ),
        name="gather_small",
    )(values)


class Ring:
    def __init__(self, depth, links):
        self.depth, self.links = depth, links
        self.index = lax.axis_index("seq")
        self.right = seq_device(lax.rem(self.index + 1, depth))
        self.left = seq_device(lax.rem(self.index + depth - 1, depth))

    def source(self, step):
        return lax.rem(self.index - step + 2 * self.depth, self.depth)


def start_kernel(
    count, depth, words, text, x, projection, pairs, normed, q, k, v,
    plane, partial, core, outer, send, arrive,
):
    links = Transfers(send, arrive)
    ring = Ring(depth, links)
    b = lax.axis_index("bucket")
    meet(plane_partners(count) + [ring.left, ring.right])
    own = q.shape[2]
    normed[ring.index] = x[...]
    moving = [links.start(x, normed.at[ring.index], ring.right)]

    def project(step):
        place = ring.source(step)
        for i, out in enumerate((q, k, v)):
            out[place] = dense(normed[place], projection[:, i * own : (i + 1) * own])

    def ring_step(step):
        moving[-1].wait_recv()
        place = ring.source(step)
        if step < depth - 1:
            moving.append(links.start(normed.at[place], normed.at[place], ring.right))
        project(step)

    exchange = PlaneExchange(count, links, plane, partial, core, outer)
    width = text.shape[1]

    def pair(block):
        source = words[jnp.bitwise_xor(b, block)]
        place = block_index(block, count)
        for first in range(0, width, 512):
            columns = slice(first, first + 512)
            partial[place, :, columns] = dense(source, text[:, columns]).astype(narrow)
        if block & 1:
            exchange.send_core(block)

    def finish(half, total):
        pairs[pl.ds(half * exchange.rows, exchange.rows)] = total

    sums = exchange.scatter(finish)
    order = sorted(exchange.outer, key=lambda block: (bin(block).count("1"), block))
    order = order[1:] + order[:1]
    levels = len(exchange.orders[0])
    for i, block in enumerate(order):
        pair(block | 1)
        pair(block)
        if i + 1 == levels:
            next(sums)
    project(0)
    step = 1
    for _ in sums:
        if step < depth:
            ring_step(step)
            step += 1
    while step < depth:
        ring_step(step)
        step += 1
    links.finish()


def start_exchange(count, depth, words, text, x, projection):
    vmem = pl.BlockSpec(memory_space=pltpu.VMEM)
    rows, width = x.shape
    own = projection.shape[1] // 3
    cap_rows, pair_width = words.shape[1], text.shape[1]
    copies = plane_copies(count)[1] + depth - 1
    raw = jax.ShapeDtypeStruct((depth, rows, own), wide)
    return pl.pallas_call(
        partial(start_kernel, count, depth),
        in_specs=[vmem] * 4,
        out_specs=[vmem] * 5,
        out_shape=[
            jax.ShapeDtypeStruct((cap_rows, pair_width), wide),
            jax.ShapeDtypeStruct((depth, rows, width), narrow),
            raw,
            raw,
            raw,
        ],
        scratch_shapes=[pltpu.VMEM((1, cap_rows, 128), narrow)]
        + plane_scratch(count, cap_rows, pair_width)[1:]
        + [pltpu.SemaphoreType.DMA((copies,)), pltpu.SemaphoreType.DMA((copies,))],
        compiler_params=pltpu.CompilerParams(
            collective_id=4, has_side_effects=True, vmem_limit_bytes=60 * 2**20
        ),
        name="start_exchange",
    )(words, text, x, projection)


def end_kernel(
    count, depth, pairs, text, words, grads, projection, normed, grad_words, share,
    plane, back, send_sum, ring_in, total, send_low, low_in, send, arrive,
):
    links = Transfers(send, arrive)
    ring = Ring(depth, links)
    b = lax.axis_index("bucket")
    others = [partner(k) for k in range(1, count)]
    meet(others + [ring.left, ring.right])
    plane[0] = pairs[...]
    exchange = PlaneExchange(count, links, plane, plane, plane, plane)
    feature = text.shape[0]
    width = text.shape[1]
    moving = []

    def round_step(step):
        value = contract_cols(grads[ring.source(step + 1)], projection[...])
        if step > 0:
            moving[-1].wait_recv()
            value = value + ring_in[step - 1].astype(wide)
        if step < depth - 1:
            send_sum[step] = value.astype(narrow)
            moving.append(links.start(send_sum.at[step], ring_in.at[step], ring.right))
        else:
            normed[...] = value

    steps = [0]

    def advance():
        if steps[0] < depth:
            round_step(steps[0])
            steps[0] += 1

    arriving = []
    blocks = [None] * count
    for block in range(count):
        blocks[block_index(block, count)] = block

    def compute(places):
        for place in places:
            block = blocks[place]
            for first in range(0, width, 512):
                columns = slice(first, first + 512)
                part = dense(words[jnp.bitwise_xor(b, block)], plane[place, :, columns])
                if place == 0:
                    total[:, columns] = part
                else:
                    total[:, columns] += part
            value = contract_cols(plane[place], text[...]).astype(narrow)
            if block == 0:
                grad_words[b] = value
            else:
                back[place - 1] = value
                arriving.append(
                    links.start(back.at[place - 1], grad_words.at[b], others[block - 1])
                )
        advance()

    exchange.run_gather(compute)
    while steps[0] < depth:
        advance()
    low_rows = feature // depth
    going = []
    for step in range(depth):
        rows = pl.ds(pl.multiple_of(ring.source(step + 1) * low_rows, low_rows), low_rows)
        value = total[rows]
        if step > 0:
            going[-1].wait_recv()
            value = value + low_in[step - 1].astype(wide)
        if step < depth - 1:
            send_low[step] = value.astype(narrow)
            going.append(links.start(send_low.at[step], low_in.at[step], ring.right))
        else:
            share[...] = value
    for copy in arriving:
        copy.wait_recv()
    links.finish()


def end_exchange(count, depth, pairs, text, words, grads, projection):
    vmem = pl.BlockSpec(memory_space=pltpu.VMEM)
    cap_rows, pair_width = pairs.shape
    feature = text.shape[0]
    rows, width = grads.shape[1], projection.shape[0]
    copies = plane_copies(count)[0] + count - 1 + 2 * (depth - 1)
    quarter = (depth - 1, feature // depth, pair_width)
    return pl.pallas_call(
        partial(end_kernel, count, depth),
        in_specs=[vmem] * 5,
        out_specs=[vmem] * 3,
        out_shape=[
            jax.ShapeDtypeStruct((rows, width), wide),
            jax.ShapeDtypeStruct((count, cap_rows, feature), narrow),
            jax.ShapeDtypeStruct((feature // depth, pair_width), wide),
        ],
        scratch_shapes=[
            pltpu.VMEM((count, cap_rows, pair_width), narrow),
            pltpu.VMEM((count - 1, cap_rows, feature), narrow),
            pltpu.VMEM((depth - 1, rows, width), narrow),
            pltpu.VMEM((depth - 1, rows, width), narrow),
            pltpu.VMEM((feature, pair_width), wide),
            pltpu.VMEM(quarter, narrow),
            pltpu.VMEM(quarter, narrow),
            pltpu.SemaphoreType.DMA((copies,)),
            pltpu.SemaphoreType.DMA((copies,)),
        ],
        compiler_params=pltpu.CompilerParams(
            collective_id=5, has_side_effects=True, vmem_limit_bytes=60 * 2**20
        ),
        name="end_exchange",
    )(pairs, text, words, grads, projection)


def head_lanes(values, head, size):
    lane = lax.broadcasted_iota(jnp.int32, values.shape, 1)
    return jnp.where((lane >= head * size) & (lane < (head + 1) * size), values, 0)


def swap_halves(values, size):
    half = size // 2
    lanes = values.shape[1]
    if lanes % 128 == 0:
        lane = lax.broadcasted_iota(jnp.int32, values.shape, 1)
        ahead = pltpu.roll(values, lanes - half, 1)
        behind = pltpu.roll(values, half, 1)
        return jnp.where(lax.rem(lane, size) < half, ahead, behind)
    parts = []
    for start in range(0, lanes, size):
        parts.append(values[:, start + half : start + size])
        parts.append(values[:, start : start + half])
    return jnp.concatenate(parts, axis=1)


def turn(values, cosine, signed_sine, size):
    return values * cosine + swap_halves(values, size) * signed_sine


def flat(values):
    return values.reshape(-1, values.shape[-1])


def scalar_spec():
    return pl.BlockSpec(memory_space=pltpu.SMEM)


def row_sums(values):
    ones = jnp.ones((8, values.shape[1]), wide)
    return lax.dot_general(
        ones, values, (((1,), (1,)), ((), ())), precision=HIGHEST, preferred_element_type=wide
    )[:1]


def loop(count, body):
    if count == 1:
        body(0)
    else:
        lax.fori_loop(0, count, lambda i, _: (body(i), 0)[1], 0)


def lane_block(index, lanes):
    if isinstance(index, int):
        return pl.ds(index * lanes, lanes)
    return pl.ds(pl.multiple_of(index * lanes, 128), lanes)


def block_rows_of(index, rows):
    if isinstance(index, int):
        return pl.ds(index * rows, rows)
    return pl.ds(pl.multiple_of(index * rows, 128), rows)


def forward_kernel(
    count, depth, size, lanes, spans, lengths, gates, raw_q, raw_k, raw_v, gain_q, gain_k, cosine,
    sine, text_own, gate_up, combined, q, k, v, qc, total, cross_total, rates, text, gathered,
    stat, stat_in, self_out, staged, send, arrive, local,
):
    links = Transfers(send, arrive)
    b, s = lax.axis_index("bucket"), lax.axis_index("seq")
    others = [partner(k) for k in range(1, count)]
    turns = [lax.rem(s + step, depth) for step in range(1, depth)]
    along = [seq_device(place) for place in turns]
    meet(others + along)
    block_rows, own = raw_q.shape[1:]
    rows = depth * block_rows
    width = own * depth
    grid, heads = own // lanes, lanes // size
    scaling = size ** (-0.5)
    for i, raw in enumerate((raw_q, raw_k)):
        for block in range(depth):
            place = i * depth + block
            stat[place : place + 1] = row_sums(raw[block] * raw[block])
    stats = [links.start(stat, stat_in.at[i], device) for i, device in enumerate(along)]
    words = [
        links.start(text_own.at[place], text.at[s], device)
        for place, device in zip(turns, along, strict=True)
    ]
    text[s] = text_own[s]
    gate_rows, units = gate_up.shape[0], gathered.shape[1] // 2
    half_width = gate_up.shape[1] // 2
    here = pl.ds(pl.multiple_of(b * gate_rows, 16), gate_rows)
    weights, kept = [], []
    for block in range(count):
        target = jnp.bitwise_xor(b, block)
        for half in range(2):
            source = gate_up.at[
                :, pl.ds(pl.multiple_of(half * half_width + target * units, 128), units)
            ]
            landing = gathered.at[here, pl.ds(half * units, units)]
            if block:
                weights.append(links.start(source, landing, others[block - 1]))
            else:
                copy = pltpu.make_async_copy(source, landing, local.at[half])
                copy.start()
                kept.append(copy)
    for block in range(depth):
        v[block_rows_of(block, block_rows)] = raw_v[block].astype(narrow)
    squares = stat[...]
    for i, copy in enumerate(stats):
        copy.wait_recv()
        squares = squares + stat_in[i]
    rates[...] = lax.rsqrt(squares / width + EPSILON)
    columns = rates[...].T
    for block in range(depth):
        at = block_rows_of(block, block_rows)
        cos, sin = cosine[at], sine[at]
        for group in range(grid):
            span = lane_block(group, lanes)
            norm_q = raw_q[block, :, span] * columns[:, block : block + 1] * gain_q[:, span]
            norm_k = (
                raw_k[block, :, span]
                * columns[:, depth + block : depth + block + 1]
                * gain_k[:, span]
            )
            turned = turn(norm_q, cos, sin, size).astype(narrow).astype(wide)
            q[at, span] = (turned * scaling).astype(narrow)
            qc[at, span] = (norm_q.astype(narrow).astype(wide) * scaling).astype(narrow)
            k[at, span] = turn(norm_k, cos, sin, size).astype(narrow)
    key_index = lax.broadcasted_iota(jnp.int32, (rows, block_rows), 0)

    def attend_self(group):
        span = lane_block(group, lanes)
        value_t = v[:, span].astype(wide).T.astype(narrow)
        for block in range(depth):
            at = block_rows_of(block, block_rows)
            allowed = (key_index >= spans[0, block]) & (key_index < spans[1, block])
            outs = []
            for head in range(heads):
                scores = contract_cols(k[:, span], head_lanes(q[at, span], head, size))
                scores = jnp.where(allowed, scores, NEGATIVE)
                peak = jnp.max(scores, axis=0, keepdims=True)
                shares = jnp.exp(scores - peak)
                mass = jnp.sum(shares, axis=0, keepdims=True)
                part = slice(head * size, (head + 1) * size)
                outs.append(dense(value_t[part], shares.astype(narrow)) / mass)
                total[group, head : head + 1, at] = peak + jnp.log(mass)
            self_out[at, span] = jnp.concatenate(outs, axis=0).T

    loop(grid, attend_self)
    for copy in words:
        copy.wait_recv()
    cap = text.shape[0] * text.shape[3]
    cap_index = lax.broadcasted_iota(jnp.int32, (cap, block_rows), 0)
    results = []
    for step in range(depth):
        block = lax.rem(s + 1 + step, depth)
        at = block_rows_of(block, block_rows)
        clip = spans[2, block]
        live = cap_index < lengths[clip]

        def attend_cross(group):
            span = lane_block(group, lanes)
            text_key = flat(text[:, 0, clip, :, span])
            value_t = flat(text[:, 1, clip, :, span]).astype(wide).T.astype(narrow)
            outs = []
            for head in range(heads):
                scores = contract_cols(text_key, head_lanes(qc[at, span], head, size))
                scores = jnp.where(live, scores, NEGATIVE)
                peak = jnp.max(scores, axis=0, keepdims=True)
                shares = jnp.exp(scores - peak)
                mass = jnp.sum(shares, axis=0, keepdims=True)
                part = slice(head * size, (head + 1) * size)
                gate = gates[group * heads + head]
                outs.append(dense(value_t[part], shares.astype(narrow)) * (gate / mass))
                cross_total[group, head : head + 1, at] = peak + jnp.log(mass)
            staged[step, :, span] = (
                self_out[at, span] + jnp.concatenate(outs, axis=0).T
            ).astype(narrow)

        loop(grid, attend_cross)
        if step < depth - 1:
            results.append(links.start(staged.at[step], combined.at[s], along[step]))
        else:
            combined[s] = staged[step]
    for copy in results + weights:
        copy.wait_recv()
    for copy in kept:
        copy.wait()
    links.finish()


def attention_forward(
    count, depth, size, lanes, scalars, raws, gains, angles, text_own, gate_up
):
    block_rows, own = raws[0].shape[1:]
    rows = depth * block_rows
    grid, heads = own // lanes, lanes // size
    vmem, anywhere = pl.BlockSpec(memory_space=pltpu.VMEM), pl.BlockSpec(memory_space=pl.ANY)
    units = gate_up.shape[1] // (2 * count)
    copies = 3 * (depth - 1) + 2 * (count - 1)
    row_block = jax.ShapeDtypeStruct((rows, own), narrow)
    totals = jax.ShapeDtypeStruct((grid, heads, rows), wide)
    return pl.pallas_call(
        partial(forward_kernel, count, depth, size, lanes),
        in_specs=[scalar_spec()] * 3 + [vmem] * 8 + [anywhere],
        out_specs=[vmem] * 10,
        out_shape=[
            jax.ShapeDtypeStruct((depth, block_rows, own), narrow),
            row_block,
            row_block,
            row_block,
            row_block,
            totals,
            totals,
            jax.ShapeDtypeStruct((2 * depth, block_rows), wide),
            jax.ShapeDtypeStruct(text_own.shape, narrow),
            jax.ShapeDtypeStruct((count * gate_up.shape[0], 2 * units), narrow),
        ],
        scratch_shapes=[
            pltpu.VMEM((2 * depth, block_rows), wide),
            pltpu.VMEM((depth - 1, 2 * depth, block_rows), wide),
            pltpu.VMEM((rows, own), wide),
            pltpu.VMEM((depth, block_rows, own), narrow),
            pltpu.SemaphoreType.DMA((copies,)),
            pltpu.SemaphoreType.DMA((copies,)),
            pltpu.SemaphoreType.DMA((2,)),
        ],
        compiler_params=pltpu.CompilerParams(
            collective_id=8, has_side_effects=True, vmem_limit_bytes=60 * 2**20
        ),
        name="attention_forward",
    )(*scalars, *raws, *gains, *angles, text_own, gate_up)


def backward_kernel(
    count, depth, size, lanes, spans, lengths, gates, upstream, weight, q, k, v, qc, raw_q, raw_k,
    rates, gain_q, gain_k, cosine, sine, text, total, cross_total, small, projected, gain_sums,
    dgate, grad_text, small_out, go, send_go, dqc, back_q, back_k, parts, send_text, stat,
    stat_in, along_in, sum_k, sum_v, send, arrive,
):
    links = Transfers(send, arrive)
    s = lax.axis_index("seq")
    others = [partner(k) for k in range(1, count)]
    turns = [lax.rem(s + step, depth) for step in range(1, depth)]
    along = [seq_device(place) for place in turns]
    meet(others + along)
    block_rows, own = upstream.shape[0], q.shape[1]
    rows = depth * block_rows
    width = own * depth
    grid, heads = own // lanes, lanes // size
    scaling = size ** (-0.5)
    smalls = [links.start(small, along_in.at[i], device) for i, device in enumerate(along)]

    def grad_out(place):
        at = pl.ds(pl.multiple_of(place * own, 64), own)
        return contract_cols(upstream[...], weight[at]).astype(narrow)

    arriving = []
    for i, (place, device) in enumerate(zip(turns, along, strict=True)):
        send_go[i] = grad_out(place)
        arriving.append(links.start(send_go.at[i], go.at[s], device))
    go[s] = grad_out(s)

    cap_local = text.shape[3]
    cap = text.shape[0] * cap_local
    places = text.shape[2]
    cap_index = lax.broadcasted_iota(jnp.int32, (cap, block_rows), 0)
    clips = []
    for step in range(depth):
        block = lax.rem(s - step + depth, depth)
        if step:
            arriving[step - 1].wait_recv()
        at = block_rows_of(block, block_rows)
        clip = spans[2, block]
        clips.append(clip)
        live = cap_index < lengths[clip]

        def back_cross(group):
            span = lane_block(group, lanes)
            text_key = flat(text[:, 0, clip, :, span])
            text_value = flat(text[:, 1, clip, :, span])
            key_t = text_key.astype(wide).T.astype(narrow)
            grads = []
            for head in range(heads):
                gate = gates[group * heads + head]
                query = head_lanes(qc[at, span], head, size)
                grad = head_lanes(go[block, :, span], head, size)
                scores = contract_cols(text_key, query)
                scores = jnp.where(live, scores, NEGATIVE)
                shares = jnp.exp(scores - cross_total[group, head : head + 1, at])
                grad_shares = contract_cols(text_value, grad)
                row = jnp.sum(grad_shares * shares, axis=0, keepdims=True)
                grad_scores = (gate * (shares * (grad_shares - row))).astype(narrow)
                grad_key = dense(grad_scores, query)
                grad_value = gate * dense(shares.astype(narrow), grad)
                if head == 0:
                    parts[step, 0, :, span] = grad_key
                    parts[step, 1, :, span] = grad_value
                else:
                    parts[step, 0, :, span] += grad_key
                    parts[step, 1, :, span] += grad_value
                part = slice(head * size, (head + 1) * size)
                grads.append(dense(key_t[part], grad_scores) * scaling)
                if step == 0:
                    dgate[group, head : head + 1] = row
                else:
                    dgate[group, head : head + 1] += row
            dqc[at, span] = jnp.concatenate(grads, axis=0).T

        loop(grid, back_cross)
    for which in range(2):
        for place in range(places):
            for target in range(depth):
                at = pl.ds(target * cap_local, cap_local)
                value = jnp.zeros((cap_local, own), wide)
                for step in range(depth):
                    value = value + jnp.where(
                        clips[step] == place, parts[step, which, at], 0.0
                    )
                send_text[target, which, place] = value.astype(narrow)
    words = [
        links.start(send_text.at[place], grad_text.at[s], device)
        for place, device in zip(turns, along, strict=True)
    ]
    grad_text[s] = send_text[s]
    sums = small[...]
    for i, copy in enumerate(smalls):
        copy.wait_recv()
        sums = sums + along_in[i]
    small_out[0] = sums
    spread = [links.start(small_out.at[0], small_out.at[k], others[k - 1]) for k in range(1, count)]

    key_index = lax.broadcasted_iota(jnp.int32, (rows, block_rows), 0)

    def back_self(group):
        span = lane_block(group, lanes)
        key_t = k[:, span].astype(wide).T.astype(narrow)
        for block in range(depth):
            at = block_rows_of(block, block_rows)
            allowed = (key_index >= spans[0, block]) & (key_index < spans[1, block])
            grads = []
            for head in range(heads):
                query = head_lanes(q[at, span], head, size)
                grad = head_lanes(go[block, :, span], head, size)
                scores = contract_cols(k[:, span], query)
                scores = jnp.where(allowed, scores, NEGATIVE)
                shares = jnp.exp(scores - total[group, head : head + 1, at])
                grad_shares = contract_cols(v[:, span], grad)
                row = jnp.sum(grad_shares * shares, axis=0, keepdims=True)
                grad_scores = (shares * (grad_shares - row)).astype(narrow)
                if block == 0 and head == 0:
                    sum_v[...] = dense(shares.astype(narrow), grad)
                    sum_k[...] = dense(grad_scores, query)
                else:
                    sum_v[...] += dense(shares.astype(narrow), grad)
                    sum_k[...] += dense(grad_scores, query)
                part = slice(head * size, (head + 1) * size)
                grads.append(dense(key_t[part], grad_scores) * scaling)
            back = jnp.concatenate(grads, axis=0).T
            back_q[at, span] = turn(back, cosine[at], -sine[at], size) + dqc[at, span]
        back_k[:, span] = turn(sum_k[...], cosine[...], -sine[...], size)
        for block in range(depth):
            at = block_rows_of(block, block_rows)
            if isinstance(group, int):
                to = pl.ds(2 * own + group * lanes, lanes)
            else:
                to = pl.ds(pl.multiple_of(2 * own + group * lanes, 128), lanes)
            projected[block, :, to] = sum_v[at].astype(narrow)

    loop(grid, back_self)
    columns = rates[...].T
    pairs = ((raw_q, back_q, gain_q), (raw_k, back_k, gain_k))
    for i, (raw, back, gain) in enumerate(pairs):
        gains = jnp.zeros((1, own), wide)
        for block in range(depth):
            place = i * depth + block
            at = block_rows_of(block, block_rows)
            hat = raw[block] * columns[:, place : place + 1]
            gains = gains + jnp.sum(back[at] * hat, axis=0, keepdims=True)
            stat[place : place + 1] = row_sums(back[at] * gain[...] * hat)
        gain_sums[i : i + 1] = gains
    stats = [links.start(stat, stat_in.at[i], device) for i, device in enumerate(along)]
    means = stat[...]
    for i, copy in enumerate(stats):
        copy.wait_recv()
        means = means + stat_in[i]
    means = (means / width).T
    for i, (raw, back, gain) in enumerate(pairs):
        for block in range(depth):
            place = slice(i * depth + block, i * depth + block + 1)
            at = block_rows_of(block, block_rows)
            rate = columns[:, place]
            hat = raw[block] * rate
            projected[block, :, i * own : (i + 1) * own] = (
                rate * (back[at] * gain[...] - hat * means[:, place])
            ).astype(narrow)
    for copy in words + spread:
        copy.wait_recv()
    links.finish()


def attention_backward(
    count, depth, size, lanes, scalars, upstream, weight, saved, raws, rates, gains, angles, text,
    totals, small,
):
    block_rows, own = raws[0].shape[1:]
    rows = depth * block_rows
    grid, heads = own // lanes, lanes // size
    vmem = pl.BlockSpec(memory_space=pltpu.VMEM)
    copies = 4 * (depth - 1) + count - 1
    cap = text.shape[0] * text.shape[3]
    args = (*scalars, upstream, weight, *saved, *raws, rates, *gains, *angles, text, *totals, small)
    return pl.pallas_call(
        partial(backward_kernel, count, depth, size, lanes),
        in_specs=[scalar_spec()] * 3 + [vmem] * (len(args) - 3),
        out_specs=[vmem] * 5,
        out_shape=[
            jax.ShapeDtypeStruct((depth, block_rows, 3 * own), narrow),
            jax.ShapeDtypeStruct((2, own), wide),
            jax.ShapeDtypeStruct((grid, heads, block_rows), wide),
            jax.ShapeDtypeStruct(text.shape, narrow),
            jax.ShapeDtypeStruct((count,) + small.shape, wide),
        ],
        scratch_shapes=[
            pltpu.VMEM((depth, block_rows, own), narrow),
            pltpu.VMEM((depth - 1, block_rows, own), narrow),
            pltpu.VMEM((rows, own), wide),
            pltpu.VMEM((rows, own), wide),
            pltpu.VMEM((rows, own), wide),
            pltpu.VMEM((depth, 2, cap, own), wide),
            pltpu.VMEM(text.shape, narrow),
            pltpu.VMEM((2 * depth, block_rows), wide),
            pltpu.VMEM((depth - 1, 2 * depth, block_rows), wide),
            pltpu.VMEM((depth - 1,) + small.shape, wide),
            pltpu.VMEM((rows, lanes), wide),
            pltpu.VMEM((rows, lanes), wide),
            pltpu.SemaphoreType.DMA((copies,)),
            pltpu.SemaphoreType.DMA((copies,)),
        ],
        compiler_params=pltpu.CompilerParams(
            collective_id=9, has_side_effects=True, vmem_limit_bytes=60 * 2**20
        ),
        name="attention_backward",
    )(*args)


def per_device(
    tokens,
    condition,
    captions,
    caption_lengths,
    null_flags,
    slot_buckets,
    null_caption,
    modulation,
    projection,
    text_weight,
    output_weight,
    gate_up,
    down_weight,
    norm_gains,
    head_gains,
    cross_gates,
    cotangent,
):
    count_s, count_b = lax.axis_size("seq"), lax.axis_size("bucket")
    s, b = lax.axis_index("seq"), lax.axis_index("bucket")
    assert count_s % 4 == 0
    local, width = tokens.shape
    heads = cross_gates.shape[0]
    size = width // heads
    own_heads = heads // count_s
    own = width // count_s
    rows = local * count_s
    places, cap_local, text_width = captions.shape
    cap_rows = places * cap_local
    bucket = slot_buckets[0]
    clip_length = jnp.where(
        bucket == 0, rows // 4, jnp.where(bucket == 1, rows // 2, rows)
    ).astype(jnp.int32)

    own_hidden = down_weight.shape[0]
    gate_rows = gate_up.shape[0]
    text_rows = text_weight.shape[0]
    null_rows = lax.dynamic_slice_in_dim(null_caption, s * cap_local, cap_local, 0)
    is_null = null_flags[:, None, None] == 1
    words_own = jnp.where(is_null, null_rows[None], captions).reshape(cap_rows, text_width)
    own_projection = jnp.concatenate(
        [
            lax.dynamic_slice_in_dim(projection, i * width + s * own, own, 1)
            for i in range(3)
        ],
        axis=1,
    )

    silu_cond = jax.nn.silu(condition).astype(narrow)
    mod_width = modulation.shape[1] // count_s
    pieces = silu_cond.astype(wide).reshape(places, count_b, -1).transpose(1, 0, 2)
    cond_columns, mods, own_projection, words = modulate(
        count_b,
        count_s,
        pieces,
        lax.dynamic_slice_in_dim(modulation, s * mod_width, mod_width, 1),
        own_projection,
        words_own,
    )
    own_projection = own_projection.reshape(width, 3 * own)
    my_clip = (s * local) // clip_length
    modulated = lax.dynamic_index_in_dim(mods, my_clip, 1, keepdims=False).reshape(1, 4 * width)

    tokens_in = tokens.astype(wide)
    normed_full, pre_pull = jax.vjp(pre_attention, tokens_in, modulated, norm_gains)
    normed_low = normed_full.astype(narrow)
    text_pairs, normed, raw_q, raw_k, raw_v = start_exchange(
        count_b, count_s, words, text_weight, normed_low, own_projection
    )
    text_outs, text_pull = jax.vjp(text_heads, text_pairs, head_gains[2])
    text_own = jnp.stack([o.astype(narrow).reshape(cap_rows, count_s, own) for o in text_outs])
    text_own = text_own.transpose(2, 0, 1, 3).reshape(count_s, 2, places, cap_local, own)

    gains = [lax.dynamic_slice_in_dim(head_gains[i : i + 1], s * own, own, 1) for i in range(2)]
    inside = lax.rem(jnp.arange(rows, dtype=jnp.int32), clip_length)
    half = size // 2
    frequency = 10000.0 ** (-jnp.arange(half, dtype=wide) / half)
    angles = inside.astype(wide)[:, None] * frequency[None, :]
    lanes = 128 if own % 128 == 0 else own
    block_heads = lanes // size
    cosine = jnp.tile(jnp.cos(angles), (1, 2 * block_heads))
    sine = jnp.tile(
        jnp.concatenate([-jnp.sin(angles), jnp.sin(angles)], axis=1), (1, block_heads)
    )
    tanh_gates = jnp.tanh(cross_gates)
    own_gates = lax.dynamic_slice_in_dim(tanh_gates, s * own_heads, own_heads, 0)
    clip_of = (jnp.arange(count_s, dtype=jnp.int32) * local) // clip_length
    spans = jnp.stack([clip_of * clip_length, (clip_of + 1) * clip_length, clip_of])
    scalars = (spans, caption_lengths, own_gates)
    full_output, text_own = lax.optimization_barrier((output_weight, text_own))
    full_output = lax.all_gather(full_output, "bucket", axis=0, tiled=True)
    combined, *saved, total, cross_total, rates, text_kv, own_gate_up = attention_forward(
        count_b,
        count_s,
        size,
        lanes,
        scalars,
        (raw_q, raw_k, raw_v),
        gains,
        (cosine, sine),
        text_own,
        gate_up,
    )
    combined = combined.transpose(1, 0, 2).reshape(local, width)

    attended = dense(combined, full_output)
    (middle, ffn_full), post_pull = jax.vjp(
        post_attention, attended, tokens_in, modulated, norm_gains
    )
    normed_ffn = ffn_full.astype(narrow)

    lowered, plane, gate_values, hidden = ffn_forward(
        count_b, normed_ffn, own_gate_up, down_weight
    )
    mixed, finish_pull = jax.vjp(finish, lowered, middle, modulated, norm_gains)
    grad_lowered, grad_middle, grad_modulated_last, grad_norm_last = finish_pull(
        cotangent.astype(wide)
    )
    grad_lowered_low = grad_lowered.astype(narrow)
    grad_normed_ffn, grad_gate_up, grad_down = ffn_backward(
        count_b, grad_lowered_low, own_gate_up, down_weight, gate_values, plane, hidden
    )
    down_share = lax.psum_scatter(
        grad_down, "seq", scatter_dimension=0, tiled=True
    ).astype(wide)
    gate_share = lax.psum_scatter(
        grad_gate_up.reshape(count_b, gate_rows, 2 * own_hidden),
        "seq",
        scatter_dimension=1,
        tiled=True,
    )
    share_rows = gate_rows // count_s
    gate_share = lax.all_to_all(gate_share, "bucket", 0, 0, tiled=True)
    gate_share = (
        gate_share.reshape(count_b, share_rows, 2, own_hidden)
        .transpose(1, 2, 0, 3)
        .reshape(share_rows, 2 * count_b * own_hidden)
        .astype(wide)
    )

    grad_attended, grad_tokens_post, grad_modulated_post, grad_norm_post = post_pull(
        (grad_middle, grad_normed_ffn)
    )
    grad_attended_low = grad_attended.astype(narrow)
    grad_output = contract_rows(combined, grad_attended_low).astype(narrow)
    output_share = lax.psum_scatter(
        grad_output, ("bucket", "seq"), scatter_dimension=0, tiled=True
    ).astype(wide)
    own_place = jnp.arange(places, dtype=jnp.int32)[:, None] == my_clip
    grad_rows = (grad_modulated_post + grad_modulated_last)[:, width:].reshape(3, 1, width)
    grad_projected, gain_sums, grad_gates, grad_kv, early = attention_backward(
        count_b,
        count_s,
        size,
        lanes,
        scalars,
        grad_attended_low,
        full_output,
        saved,
        (raw_q, raw_k),
        rates,
        gains,
        (cosine, sine),
        text_kv,
        (total, cross_total),
        jnp.where(own_place[None], grad_rows, 0.0).reshape(3 * places, width),
    )
    early = early.reshape(count_b, 3, places, width)

    grad_kv = grad_kv.reshape(count_s, 2, cap_rows, own)
    grad_kv = grad_kv.transpose(1, 2, 0, 3).reshape(2, cap_rows, width).astype(wide)
    grad_pairs, grad_gain_text = text_pull((grad_kv[0], grad_kv[1]))
    grad_pairs_low = grad_pairs.astype(narrow)
    grad_normed, grad_words, text_share = end_exchange(
        count_b,
        count_s,
        grad_pairs_low,
        text_weight,
        words.transpose(0, 2, 1),
        grad_projected,
        own_projection,
    )
    grad_words = grad_words.transpose(1, 0, 2).reshape(places, cap_local, text_width)
    grad_captions = jnp.where(is_null, 0.0, grad_words.astype(wide))
    null_local = jnp.sum(jnp.where(is_null, grad_words.astype(wide), 0.0), axis=0).astype(narrow)
    null_share = lax.all_to_all(null_local, "bucket", 0, 0, tiled=True)
    null_share = jnp.sum(null_share.reshape(count_b, -1, text_width).astype(wide), axis=0)
    null_share = lax.ppermute(
        null_share,
        ("bucket", "seq"),
        [(i * count_s + j, j * count_b + i) for i in range(count_b) for j in range(count_s)],
    )

    grad_projection = contract_rows(flat(normed), flat(grad_projected)).astype(narrow)
    proj_share = lax.all_to_all(grad_projection, "bucket", 0, 0, tiled=True)
    proj_share = jnp.sum(
        proj_share.reshape(count_b, -1, 3 * own).astype(wide), axis=0
    ).astype(narrow)
    proj_share = lax.all_to_all(proj_share.reshape(count_s, -1, 3 * own), "seq", 0, 0, tiled=True)
    proj_share = (
        proj_share.reshape(count_s, -1, 3, own)
        .transpose(1, 2, 0, 3)
        .reshape(-1, 3 * width)
        .astype(wide)
    )
    grad_tokens_pre, grad_modulated_pre, grad_norm_pre = pre_pull(grad_normed)
    grad_tokens = grad_tokens_pre + grad_tokens_post

    share = width // (count_b * count_s)
    def place(values):
        return lax.dynamic_update_slice_in_dim(jnp.zeros((width,), wide), values, s * own, 0)

    gate_sums = lax.dynamic_update_slice_in_dim(
        jnp.zeros((heads,), wide),
        jnp.sum(grad_gates, axis=2).reshape(own_heads) * (1.0 - own_gates * own_gates),
        s * own_heads,
        0,
    )
    small = jnp.concatenate(
        [
            jnp.where(own_place, grad_modulated_pre[:, :width], 0.0),
            grad_norm_pre + grad_norm_post + grad_norm_last,
            jnp.stack(
                [
                    place(gain_sums[0]),
                    place(gain_sums[1]),
                    grad_gain_text,
                    jnp.pad(gate_sums, (0, width - heads)),
                ]
            ),
        ],
        axis=0,
    )
    small = gather_small(count_b, count_s, small, 7)
    grad_mod_rows = jnp.concatenate([small[:, None, :places], early], axis=1)
    cond_own = lax.dynamic_slice_in_dim(cond_columns, s * share, share, 2)
    mod_share = lax.dot_general(
        flat(cond_own),
        grad_mod_rows.transpose(0, 2, 1, 3).reshape(count_b * places, 4 * width),
        (((0,), (0,)), ((), ())),
        precision=HIGHEST,
    )
    sums = jnp.sum(small[:, places:], axis=0)
    own_sums = lax.dynamic_slice_in_dim(sums, (b * count_s + s) * share, share, 1)
    return (
        mixed.astype(narrow),
        grad_tokens,
        grad_captions,
        null_share,
        mod_share,
        proj_share,
        text_share,
        output_share,
        gate_share,
        down_share,
        own_sums[:4],
        own_sums[4:7],
        sums[7, :heads],
    )


def solution(mesh):
    whole = P(("bucket", "seq"), None)
    shard = P("bucket", None)
    return jax.shard_map(
        per_device,
        mesh=mesh,
        in_specs=(
            whole,
            shard,
            P("bucket", "seq", None),
            P("bucket"),
            P("bucket"),
            P("bucket"),
            P(),
            shard,
            shard,
            shard,
            shard,
            shard,
            shard,
            P(),
            P(),
            P(),
            whole,
        ),
        out_specs=(
            whole,
            whole,
            P("bucket", "seq", None),
            whole,
            whole,
            whole,
            whole,
            whole,
            whole,
            whole,
            P(None, ("bucket", "seq")),
            P(None, ("bucket", "seq")),
            P(),
        ),
        check_vma=False,
    )
```

```python
from functools import partial

import jax
import jax.numpy as jnp
from jax import lax
from jax.experimental import pallas as pl
from jax.experimental.pallas import tpu as pltpu
from jax.sharding import PartitionSpec as P

EPSILON = 1e-06
NEGATIVE = -1e30
HIGHEST = lax.Precision.HIGHEST
wide = jnp.float32
narrow = jnp.bfloat16
VMEM_LIMIT = 50 * 2**20


def rms_norm(values, norm_gain):
    return (
        values * lax.rsqrt(jnp.mean(values * values, axis=-1, keepdims=True) + EPSILON) * norm_gain
    )


def dense(leading, trailing):
    return jnp.dot(leading, trailing, preferred_element_type=wide)


def contract_rows(leading, trailing):
    return lax.dot_general(
        leading, trailing, (((0,), (0,)), ((), ())), preferred_element_type=wide
    )


def contract_cols(leading, trailing):
    return lax.dot_general(
        leading, trailing, (((1,), (1,)), ((), ())), preferred_element_type=wide
    )


def pre_attention(tokens_in, modulated, norm_gains):
    model_width = tokens_in.shape[1]
    return rms_norm(tokens_in, norm_gains[0]) * (1.0 + modulated[:, :model_width])


def text_heads(text_pairs, gain):
    model_width = text_pairs.shape[1] // 2
    return (rms_norm(text_pairs[:, :model_width], gain), text_pairs[:, model_width:])


def post_attention(attended, tokens_in, modulated, norm_gains):
    model_width = tokens_in.shape[1]
    middle = tokens_in + jnp.tanh(modulated[:, model_width : 2 * model_width]) * rms_norm(
        attended, norm_gains[1]
    )
    normed_ffn = rms_norm(middle, norm_gains[2]) * (
        1.0 + modulated[:, 2 * model_width : 3 * model_width]
    )
    return (middle, normed_ffn)


def swiglu(gate_values):
    hidden_width = gate_values.shape[1] // 2
    return jax.nn.silu(gate_values[:, :hidden_width]) * gate_values[:, hidden_width:]


def finish(lowered, middle, modulated, norm_gains):
    model_width = middle.shape[1]
    return middle + jnp.tanh(modulated[:, 3 * model_width :]) * rms_norm(lowered, norm_gains[3])


MESH = pl.DeviceIdType.MESH


class Transfers:
    def __init__(self, send, arrive):
        self.send, self.arrive, self.used = send, arrive, 0
        self.open = []

    def start(self, source, target, device):
        copy = pltpu.make_async_remote_copy(
            src_ref=source,
            dst_ref=target,
            send_sem=self.send.at[self.used],
            recv_sem=self.arrive.at[self.used],
            device_id=device,
            device_id_type=MESH,
        )
        self.used += 1
        copy.start()
        self.open.append(copy)
        return copy

    def finish(self):
        for copy in self.open:
            copy.wait_send()


def meet(devices):
    barrier = pltpu.get_barrier_semaphore()
    for device in devices:
        pl.semaphore_signal(barrier, inc=1, device_id=device, device_id_type=MESH)
    pl.semaphore_wait(barrier, len(devices))


def partner(bits):
    return {"bucket": jnp.bitwise_xor(lax.axis_index("bucket"), bits)}


def outer_bits(count):
    return [1 << i for i in range(1, count.bit_length() - 1)]


def block_index(k, count):
    return (k >> 1) + (k & 1) * (count // 2)


def last_bit(block, order):
    return [bit for bit in order if block & bit][-1]


class PlaneExchange:
    def __init__(
        self, count, links, gathered=None, partial=None, arrived_core=None, arrived_outer=None,
        natural=False,
    ):
        self.count, self.links, self.natural = count, links, natural
        self.index = lax.axis_index("bucket")
        self.gathered, self.partial = gathered, partial
        self.arrived_core, self.arrived_outer = arrived_core, arrived_outer
        bits = outer_bits(count)
        self.orders = (bits, bits[::-1])
        self.outer = [k for k in range(0, count, 2)]
        self.rows = (partial if gathered is None else gathered).shape[1] // 2
        self.coming, self.slots = {}, {}
        self.blocks = [0]

    def part(self, ref, block, half):
        return ref.at[block, pl.ds(half * self.rows, self.rows)]

    def place(self, block):
        return jnp.bitwise_xor(self.index, block) if self.natural else block_index(block, self.count)

    def onward(self, half, block, bit):
        source = self.place(block)
        target = source if self.natural else self.place(block | bit)
        self.coming[half, block | bit] = self.links.start(
            self.part(self.gathered, source, half),
            self.part(self.gathered, target, half),
            partner(bit),
        )

    def forward(self, half, block):
        order = self.orders[half]
        later = order if block == 0 else order[order.index(last_bit(block, order)) + 1 :]
        for bit in later:
            self.onward(half, block, bit)

    def forward_core(self, half, block):
        self.onward(half, block, 1)

    def arrive(self, block):
        for half in range(2):
            self.coming[half, block].wait_recv()

    def begin(self):
        for step in range(len(self.orders[0])):
            for half in range(2):
                self.onward(half, 0, self.orders[half][step])
        for half in range(2):
            self.forward_core(half, 0)

    def run_gather(self, compute, scatter=None):
        self.begin()
        compute([0])
        levels = len(self.orders[0])
        self.arrive(1)
        compute([block_index(1, self.count)])
        if scatter is not None:
            self.send_core(1)
        for level in range(1, levels + 1):
            here = [k for k in self.outer if bin(k).count("1") == level]
            self.forward_level(here)
            if level == 2 and scatter is not None:
                next(scatter)
            compute([block_index(k, self.count) for k in here])
            for k in here:
                self.arrive(k | 1)
            compute([block_index(k | 1, self.count) for k in here])
            for k in here:
                if scatter is not None:
                    self.send_core(k | 1)

    def gather(self):
        self.begin()
        yield
        for level in range(1, len(self.orders[0]) + 1):
            self.forward_level([k for k in self.outer if bin(k).count("1") == level])
            yield
        for block in self.outer:
            self.arrive(block | 1)

    def forward_level(self, here):
        steps = [(half, k) for k in here for half in range(2)]
        steps.sort(
            key=lambda s: [
                self.orders[s[0]].index(bit) for bit in self.orders[s[0]] if s[1] & bit
            ][::-1]
        )
        for half, k in steps:
            self.coming[half, k].wait_recv()
            self.forward(half, k)
            self.forward_core(half, k)

    def send_core(self, block):
        place = self.place(block)
        target = self.arrived_core.at[block >> 1]
        self.slots["core", block & ~1] = self.links.start(self.partial.at[place], target, partner(1))

    def total(self, half, block, slots):
        rows = pl.ds(half * self.rows, self.rows)
        value = self.partial[self.place(block), rows].astype(wide)
        value = value + self.arrived_core[block >> 1, rows].astype(wide)
        for slot in slots:
            value = value + self.arrived_outer[half, slot].astype(wide)
        return value

    def scatter(self, finish):
        slot_of = {}
        waiting = {(half, k): [] for half in range(2) for k in self.outer}
        core_seen = set()
        left = [list(self.outer), list(self.outer)]
        for step in range(len(self.orders[0])):
            jobs = []
            for half in range(2):
                bit = self.orders[half][::-1][step]
                jobs.append([(half, bit, k) for k in left[half] if k & bit])
                left[half] = [k for k in left[half] if not k & bit]
            for pair in zip(*jobs, strict=True):
                for half, bit, k in pair:
                    if k not in core_seen:
                        self.slots["core", k].wait_recv()
                        core_seen.add(k)
                    for copy, _ in waiting[half, k]:
                        copy.wait_recv()
                    rows = pl.ds(half * self.rows, self.rows)
                    total = self.total(half, k, [slot for _, slot in waiting[half, k]])
                    self.partial[self.place(k), rows] = total.astype(narrow)
                    slot = slot_of.setdefault((half, bit, k ^ bit), len([1 for h, *_ in slot_of if h == half]))
                    copy = self.links.start(
                        self.partial.at[self.place(k), rows],
                        self.arrived_outer.at[half, slot],
                        partner(bit),
                    )
                    waiting[half, k ^ bit].append((copy, slot))
                yield
        if 0 not in core_seen:
            self.slots["core", 0].wait_recv()
        for half in range(2):
            for copy, _ in waiting[half, 0]:
                copy.wait_recv()
            finish(half, self.total(half, 0, [slot for _, slot in waiting[half, 0]]))


def plane_partners(count):
    return [partner(bit) for bit in outer_bits(count) + [1]]


def plane_copies(count):
    outer = count // 2
    return 2 * (outer - 1) + 2 * outer, outer + 2 * (outer - 1)


def spans(blocks):
    runs = []
    for block in sorted(blocks):
        if runs and runs[-1][1] == block:
            runs[-1][1] = block + 1
        else:
            runs.append([block, block + 1])
    return runs


def each(blocks, body):
    for first, end in spans(blocks):
        if end - first == 1:
            body(first)
        else:
            lax.fori_loop(first, end, lambda i, _: (body(i), 0)[1], 0)


def ffn_kernel(
    count, x, gate_up, down, lowered, plane_out, values_out, hidden_out,
    plane, partial, core, outer, values, hidden, send, arrive, local,
):
    links = Transfers(send, arrive)
    meet(plane_partners(count))
    units = down.shape[0]
    wide_block = 256
    plane[0] = x[...]
    saved = pltpu.make_async_copy(plane, plane_out, local.at[0])

    def compute(blocks):
        def one(place):
            for start in range(0, units, wide_block):
                columns = slice(start, start + wide_block)
                after = slice(units + start, units + start + wide_block)
                gate = dense(plane[place], gate_up[:, columns])
                up = dense(plane[place], gate_up[:, after])
                values[place, :, columns] = gate
                values[place, :, after] = up
                hidden[place, :, columns] = (jax.nn.silu(gate) * up).astype(narrow)
            partial[place] = dense(hidden[place], down[...]).astype(narrow)

        each(blocks, one)

    exchange = PlaneExchange(count, links, plane, partial, core, outer)
    def finish(half, total):
        lowered[pl.ds(half * exchange.rows, exchange.rows)] = total

    sums = exchange.scatter(finish)
    exchange.run_gather(compute, sums)
    saved.start()
    kept = pltpu.make_async_copy(values, values_out, local.at[1])
    kept.start()
    held = pltpu.make_async_copy(hidden, hidden_out, local.at[2])
    held.start()

    for _ in sums:
        pass
    saved.wait()
    kept.wait()
    held.wait()
    links.finish()


def plane_scratch(count, rows, width):
    outer = count // 2
    return [
        pltpu.VMEM((count, rows, width), narrow),
        pltpu.VMEM((count, rows, width), narrow),
        pltpu.VMEM((outer, rows, width), narrow),
        pltpu.VMEM((2, outer - 1, rows // 2, width), narrow),
    ]


def ffn_forward(count, x, gate_up, down):
    rows, width = x.shape
    units = down.shape[0]
    copies = sum(plane_copies(count))
    vmem, anywhere = pl.BlockSpec(memory_space=pltpu.VMEM), pl.BlockSpec(memory_space=pl.ANY)
    return pl.pallas_call(
        partial(ffn_kernel, count),
        in_specs=[vmem] * 3,
        out_specs=[vmem] + [anywhere] * 3,
        out_shape=[
            jax.ShapeDtypeStruct((rows, width), wide),
            jax.ShapeDtypeStruct((count, rows, width), narrow),
            jax.ShapeDtypeStruct((count, rows, 2 * units), wide),
            jax.ShapeDtypeStruct((count, rows, units), narrow),
        ],
        scratch_shapes=plane_scratch(count, rows, width)
        + [
            pltpu.VMEM((count, rows, 2 * units), wide),
            pltpu.VMEM((count, rows, units), narrow),
            pltpu.SemaphoreType.DMA((copies,)),
            pltpu.SemaphoreType.DMA((copies,)),
            pltpu.SemaphoreType.DMA((3,)),
        ],
        compiler_params=pltpu.CompilerParams(
            collective_id=1, has_side_effects=True, vmem_limit_bytes=60 * 2**20
        ),
        name="ffn_forward",
    )(x, gate_up, down)

def ffn_back_kernel(
    count, g, gate_up, down, values_in, x_in, hidden_in, grad_normed, grad_gate_up, grad_down,
    plane, partial, core, outer, values, grads, taken, send, arrive, local,
):
    links = Transfers(send, arrive)
    fetch = pltpu.make_async_copy(values_in, values, local.at[2])
    fetch.start()
    meet(plane_partners(count))
    units, width = down.shape
    wide_block = 256
    plane[0] = g[...]
    fetched = []

    def compute(places):
        if not fetched:
            fetch.wait()
            fetched.append(True)

        def one(place):
            for start in range(0, units, wide_block):
                columns = slice(start, start + wide_block)
                after = slice(units + start, units + start + wide_block)
                back = contract_cols(plane[place], down[columns])
                gate, up = values[place, :, columns], values[place, :, after]
                sigma = jax.nn.sigmoid(gate)
                grads[place, :, columns] = (
                    back * up * (sigma * (1.0 + gate * (1.0 - sigma)))
                ).astype(narrow)
                grads[place, :, after] = (back * (gate * sigma)).astype(narrow)
            partial[place] = contract_cols(grads[place], gate_up[...]).astype(narrow)

        each(places, one)

    exchange = PlaneExchange(count, links, plane, partial, core, outer)

    def finish(half, total):
        grad_normed[pl.ds(half * exchange.rows, exchange.rows)] = total

    sums = exchange.scatter(finish)
    exchange.run_gather(compute, sums)

    jobs = [(x_in, grads, grad_gate_up, i) for i in range(width // wide_block)]
    jobs += [(hidden_in, plane, grad_down, i) for i in range(units // wide_block)]

    def take(number):
        source, _, _, i = jobs[number]
        columns = pl.ds(i * wide_block, wide_block)
        return pltpu.make_async_copy(
            source.at[:, :, columns], taken.at[number % 2], local.at[number % 2]
        )

    def work(number):
        if number + 1 < len(jobs):
            take(number + 1).start()
        take(number).wait()
        _, upstream, out, i = jobs[number]
        for start in range(0, upstream.shape[2], 512):
            columns = slice(start, start + 512)
            out[i * wide_block : (i + 1) * wide_block, columns] = contract_rows(
                flat(taken[number % 2]), flat(upstream[:, :, columns])
            ).astype(narrow)

    take(0).start()
    done = 0
    for _ in sums:
        for number in range(done, min(done + 3, len(jobs))):
            work(number)
            done += 1
    for number in range(done, len(jobs)):
        work(number)
    links.finish()


class GradientRing:
    def __init__(self, ring, own, held):
        self.ring, self.own, self.held = ring, own, held
        self.copies = []

    def piece(self, which, step):
        place = self.ring.source(step + 1)
        return self.own[0].at[:, place] if which == 0 else self.own[1].at[place]

    def first(self, landing):
        for which in range(2):
            self.copies.append(
                self.ring.links.start(self.piece(which, 0), landing[which], self.ring.right)
            )

    def arrived(self):
        for copy in self.copies:
            copy.wait_recv()
        self.copies = []

    def value(self, which, step):
        return self.piece(which, step)[...].astype(wide) + self.held[which][...].astype(wide)

    def onward(self, step, going, landing):
        self.arrived()
        for which in range(2):
            going[which][...] = self.value(which, step).astype(narrow)
            self.copies.append(
                self.ring.links.start(going[which], landing[which], self.ring.right)
            )
        self.held = landing


def ffn_backward(count, g, gate_up, down, values, x, hidden):
    rows, width = g.shape
    units = down.shape[0]
    copies = sum(plane_copies(count))
    vmem, anywhere = pl.BlockSpec(memory_space=pltpu.VMEM), pl.BlockSpec(memory_space=pl.ANY)
    return pl.pallas_call(
        partial(ffn_back_kernel, count),
        in_specs=[vmem] * 3 + [anywhere] * 3,
        out_specs=[vmem] * 3,
        out_shape=[
            jax.ShapeDtypeStruct((rows, width), wide),
            jax.ShapeDtypeStruct((width, 2 * units), narrow),
            jax.ShapeDtypeStruct((units, width), narrow),
        ],
        scratch_shapes=plane_scratch(count, rows, width)
        + [
            pltpu.VMEM((count, rows, 2 * units), wide),
            pltpu.VMEM((count, rows, 2 * units), narrow),
            pltpu.VMEM((2, count, rows, 256), narrow),
            pltpu.SemaphoreType.DMA((copies,)),
            pltpu.SemaphoreType.DMA((copies,)),
            pltpu.SemaphoreType.DMA((3,)),
        ],
        compiler_params=pltpu.CompilerParams(
            collective_id=2, has_side_effects=True, vmem_limit_bytes=62 * 2**20
        ),
        name="ffn_backward",
    )(g, gate_up, down, values, x, hidden)


def seq_device(index):
    return {"seq": index}


class Ring:
    def __init__(self, depth, links):
        self.depth, self.links = depth, links
        self.index = lax.axis_index("seq")
        self.right = seq_device(lax.rem(self.index + 1, depth))
        self.left = seq_device(lax.rem(self.index + depth - 1, depth))

    def source(self, step):
        return lax.rem(self.index - step + 2 * self.depth, self.depth)


def start_kernel(
    count, depth, clip, pieces, columns, shard, words, text, x, gain,
    got, mods, projection, spread, pairs, normed, q, k, v, rates,
    product, back, stat, stat_in, partial, core, outer, send, arrive,
):
    links = Transfers(send, arrive)
    ring = Ring(depth, links)
    b, s = lax.axis_index("bucket"), lax.axis_index("seq")
    others = [partner(k) for k in range(1, count)]
    along = [seq_device(lax.rem(s + step, depth)) for step in range(1, depth)]
    meet(others + along)
    first = [
        links.start(pieces.at[jnp.bitwise_xor(b, k)], got.at[k], others[k - 1])
        for k in range(1, count)
    ]
    got[0] = pieces[b]
    feature, width = text.shape

    def features(target):
        return words.at[:, pl.ds(pl.multiple_of(target * feature, 128), feature)]

    projection[b] = shard[...]
    spread[b] = words[:, pl.ds(pl.multiple_of(b * feature, 128), feature)]
    for copy in first:
        copy.wait_recv()
    for block in range(count):
        product[block] = dense(got[block].astype(narrow), columns[...])
    second = [
        links.start(product.at[block], back.at[block - 1], others[block - 1])
        for block in range(1, count)
    ]
    far = {}
    for block in sorted(range(1, count), key=lambda block: (bin(block >> 1).count("1"), block & 1)):
        far[block] = links.start(
            features(jnp.bitwise_xor(b, block)), spread.at[b], others[block - 1]
        )
    shards = PlaneExchange(count, links, projection, natural=True).gather()
    next(shards)

    total = product[0]
    for i, copy in enumerate(second):
        copy.wait_recv()
        total = total + back[i]
    mods[s] = total
    third = [links.start(mods.at[s], mods.at[s], device) for device in along]
    for copy in third:
        copy.wait_recv()
    places = mods.shape[1]
    parts = []
    for i in range(depth // 4):
        part = jnp.zeros((1, mods.shape[2]), wide)
        for place in range(places):
            part = part + jnp.where(clip[0] == place, mods[i, place : place + 1], 0.0)
        parts.append(part)
    scale = parts[0] if len(parts) == 1 else jnp.concatenate(parts, axis=1)
    value = x[...].astype(wide)
    rate = lax.rsqrt(jnp.mean(value * value, axis=1, keepdims=True) + EPSILON)
    normed[s] = (value * rate * gain[...] * (1.0 + scale)).astype(narrow)
    moving = [links.start(normed.at[s], normed.at[s], ring.right)]

    exchange = PlaneExchange(count, links, None, partial, core, outer)

    def pair(block):
        if block:
            far[block].wait_recv()
        source = spread[jnp.bitwise_xor(b, block)]
        place = block_index(block, count)
        for start in range(0, width, 512):
            span = slice(start, start + 512)
            partial[place, :, span] = dense(source, text[:, span]).astype(narrow)
        if block & 1:
            exchange.send_core(block)

    def finish(half, total):
        pairs[pl.ds(half * exchange.rows, exchange.rows)] = total

    sums = exchange.scatter(finish)
    order = sorted(exchange.outer, key=lambda block: (bin(block).count("1"), block))
    order = order[1:] + order[:1]
    levels = len(exchange.orders[0])
    for block in order[:levels]:
        pair(block | 1)
        pair(block)
    next(sums)
    for block in order[levels:]:
        pair(block | 1)
        pair(block)
    next(sums)
    own = q.shape[2]

    def project(step):
        place = ring.source(step)
        for i, out in enumerate((q, k, v)):
            span = slice(i * own, (i + 1) * own)
            weight = projection[:, :, span]
            out[place] = dense(normed[place], flat(weight))

    def onward(step):
        moving[-1].wait_recv()
        place = ring.source(step)
        if step < depth - 1:
            moving.append(links.start(normed.at[place], normed.at[place], ring.right))

    onward(1)
    for _ in shards:
        pass
    project(0)
    project(1)
    for step in range(2, depth):
        if step == depth - 1:
            next(sums)
        onward(step)
        project(step)
    for i, raw in enumerate((q, k)):
        for block in range(depth):
            place = i * depth + block
            stat[place : place + 1] = row_sums(raw[block] * raw[block])
    stats = [links.start(stat, stat_in.at[i], device) for i, device in enumerate(along)]
    for _ in sums:
        pass
    squares = stat[...]
    for i, copy in enumerate(stats):
        copy.wait_recv()
        squares = squares + stat_in[i]
    rates[...] = lax.rsqrt(squares / (own * depth) + EPSILON)
    links.finish()


def start_exchange(count, depth, clip, pieces, columns, shard, words, text, x, gain):
    vmem = pl.BlockSpec(memory_space=pltpu.VMEM)
    rows, width = x.shape
    own = shard.shape[1] // 3
    cap_rows, pair_width = words.shape[0], text.shape[1]
    places, mod_width = pieces.shape[1], columns.shape[1]
    copies = sum(plane_copies(count)) + 3 * (count - 1) + 3 * (depth - 1)
    raw = jax.ShapeDtypeStruct((depth, rows, own), wide)
    return pl.pallas_call(
        partial(start_kernel, count, depth),
        in_specs=[scalar_spec()] + [vmem] * 7,
        out_specs=[vmem] * 10,
        out_shape=[
            jax.ShapeDtypeStruct(pieces.shape, wide),
            jax.ShapeDtypeStruct((depth, places, mod_width), wide),
            jax.ShapeDtypeStruct((count,) + shard.shape, narrow),
            jax.ShapeDtypeStruct((count, cap_rows, words.shape[1] // count), narrow),
            jax.ShapeDtypeStruct((cap_rows, pair_width), wide),
            jax.ShapeDtypeStruct((depth, rows, width), narrow),
            raw,
            raw,
            raw,
            jax.ShapeDtypeStruct((2 * depth, rows), wide),
        ],
        scratch_shapes=[
            pltpu.VMEM((count, places, mod_width), wide),
            pltpu.VMEM((count - 1, places, mod_width), wide),
            pltpu.VMEM((2 * depth, rows), wide),
            pltpu.VMEM((depth - 1, 2 * depth, rows), wide),
        ]
        + plane_scratch(count, cap_rows, pair_width)[1:]
        + [pltpu.SemaphoreType.DMA((copies,)), pltpu.SemaphoreType.DMA((copies,))],
        compiler_params=pltpu.CompilerParams(
            collective_id=4, has_side_effects=True, vmem_limit_bytes=60 * 2**20
        ),
        name="start_exchange",
    )(clip, pieces, columns, shard, words, text, x, gain)


def end_kernel(
    count, depth, pairs, text, words, grads, projection, grad_gate, grad_down, gate_held, down_held,
    normed, grad_words, grad_weight, gate_next, down_next,
    plane, back, send_sum, ring_in, total, gate_go, down_go, send, arrive,
):
    links = Transfers(send, arrive)
    ring = Ring(depth, links)
    b = lax.axis_index("bucket")
    others = [partner(k) for k in range(1, count)]
    meet(others + [ring.left, ring.right])
    plane[0] = pairs[...]
    exchange = PlaneExchange(count, links, plane)
    feature, width = text.shape
    own_columns = pl.ds(pl.multiple_of(b * feature, 128), feature)
    moving = []

    def round_step(step):
        value = contract_cols(grads[ring.source(step + 1)], projection[...])
        if step > 0:
            moving[-1].wait_recv()
            value = value + ring_in[step - 1].astype(wide)
        if step < depth - 1:
            send_sum[step] = value.astype(narrow)
            moving.append(links.start(send_sum.at[step], ring_in.at[step], ring.right))
        else:
            normed[...] = value

    steps = [0]

    weights = GradientRing(ring, (grad_gate, grad_down), (gate_held, down_held))

    def advance():
        if steps[0] < depth - 1:
            round_step(steps[0])
            steps[0] += 1
            if steps[0] == depth - 1:
                weights.onward(1, (gate_go, down_go), (gate_next, down_next))

    arriving = []
    blocks = [None] * count
    for block in range(count):
        blocks[block_index(block, count)] = block

    def compute(places):
        for place in places:
            block = blocks[place]
            features = words[jnp.bitwise_xor(b, block)].astype(wide).T.astype(narrow)
            for first in range(0, width, 512):
                columns = slice(first, first + 512)
                part = dense(features, plane[place, :, columns])
                if place == 0:
                    total[:, columns] = part
                else:
                    total[:, columns] += part
            value = contract_cols(plane[place], text[...]).astype(narrow)
            if block == 0:
                grad_words[:, own_columns] = value
            else:
                back[place - 1] = value
                arriving.append(
                    links.start(
                        back.at[place - 1], grad_words.at[:, own_columns], others[block - 1]
                    )
                )
        advance()

    exchange.run_gather(compute)
    while steps[0] < depth - 1:
        advance()
    round_step(depth - 1)
    grad_weight[...] = total[...].astype(narrow)
    for copy in arriving + weights.copies:
        copy.wait_recv()
    links.finish()


def end_exchange(count, depth, pairs, text, words, grads, projection, ffn_grads, held):
    vmem = pl.BlockSpec(memory_space=pltpu.VMEM)
    cap_rows, pair_width = pairs.shape
    feature = text.shape[0]
    rows, width = grads.shape[1], projection.shape[0]
    copies = plane_copies(count)[0] + count - 1 + depth - 1 + 2
    return pl.pallas_call(
        partial(end_kernel, count, depth),
        in_specs=[vmem] * 9,
        out_specs=[vmem] * 5,
        out_shape=[
            jax.ShapeDtypeStruct((rows, width), wide),
            jax.ShapeDtypeStruct((cap_rows, count * feature), narrow),
            jax.ShapeDtypeStruct((feature, pair_width), narrow),
            jax.ShapeDtypeStruct(held[0].shape, narrow),
            jax.ShapeDtypeStruct(held[1].shape, narrow),
        ],
        scratch_shapes=[
            pltpu.VMEM((count, cap_rows, pair_width), narrow),
            pltpu.VMEM((count - 1, cap_rows, feature), narrow),
            pltpu.VMEM((depth - 1, rows, width), narrow),
            pltpu.VMEM((depth - 1, rows, width), narrow),
            pltpu.VMEM((feature, pair_width), wide),
            pltpu.VMEM(held[0].shape, narrow),
            pltpu.VMEM(held[1].shape, narrow),
            pltpu.SemaphoreType.DMA((copies,)),
            pltpu.SemaphoreType.DMA((copies,)),
        ],
        compiler_params=pltpu.CompilerParams(
            collective_id=5, has_side_effects=True, vmem_limit_bytes=63 * 2**20
        ),
        name="end_exchange",
    )(pairs, text, words, grads, projection, *ffn_grads, *held)


def sum_kernel(
    count, depth, flags, text, combined, upstream, normed, grads, grad_gate, grad_down, gate_held,
    down_held, words, row, small, down_share, text_share, output_share, proj_share, gate_share, null_share, rows_out, small_out,
    out_part, out_core, out_outer, proj_part, proj_core, proj_outer, send_low, low_in, out_go,
    out_come, proj_go, proj_come, gate, gate_come, null, null_come, small_come, small_go,
    small_land, gate_go, down_go, gate_land, down_land, send, arrive,
):
    links = Transfers(send, arrive)
    ring = Ring(depth, links)
    b, s = lax.axis_index("bucket"), lax.axis_index("seq")
    others = [partner(k) for k in range(1, count)]
    turns = [lax.rem(s + step, depth) for step in range(1, depth)]
    along = [seq_device(place) for place in turns]
    meet(others + along)

    rows_out[0, s] = row[...]
    tiny = []
    for i, (place, device) in enumerate(zip(turns, along, strict=True)):
        tiny.append(links.start(row, rows_out.at[0, s], device))
        tiny.append(links.start(small.at[place], small_come.at[i], device))

    low_rows = text.shape[0] // depth
    going = []

    def text_step(step):
        rows = pl.ds(pl.multiple_of(ring.source(step + 1) * low_rows, 16), low_rows)
        value = text[rows].astype(wide)
        if step > 0:
            going[-1].wait_recv()
            value = value + low_in[step - 1].astype(wide)
        if step < depth - 1:
            send_low[step] = value.astype(narrow)
            going.append(links.start(send_low.at[step], low_in.at[step], ring.right))
        else:
            text_share[...] = value

    weights = GradientRing(ring, (grad_gate, grad_down), (gate_held, down_held))

    def weights_step(step):
        slot = step - 2
        weights.onward(
            step,
            (gate_go.at[slot], down_go.at[slot]),
            (gate_land.at[slot], down_land.at[slot]),
        )

    text_step(0)
    weights_step(2)

    share = out_go.shape[1]
    pair = 2 * out_part.shape[1]

    def fill(part, leading, trailing):
        for first in range(0, count, 2):
            value = contract_rows(leading[:, first // 2 * pair : (first // 2 + 1) * pair], trailing)
            value = value.astype(narrow)
            part[first] = value[: pair // 2]
            part[first + 1] = value[pair // 2 :]

    def plane_sum(part, core, outer, go):
        exchange = PlaneExchange(count, links, None, part, core, outer, natural=True)
        for block in range(1, count, 2):
            exchange.send_core(block)

        def finish(half, total):
            low = total.astype(narrow)
            for i in range(depth // 2):
                go[half * (depth // 2) + i] = low[i * share : (i + 1) * share]

        return exchange.scatter(finish)

    fill(out_part, combined[...], upstream[...])
    out_sums = plane_sum(out_part, out_core, out_outer, out_go)
    fill(proj_part, flat(normed[...]), flat(grads[...]))
    proj_sums = plane_sum(proj_part, proj_core, proj_outer, proj_go)
    for _ in range(count // 4):
        next(out_sums)
    for _ in range(count // 4):
        next(proj_sums)
    text_step(1)

    places = flags.shape[0]
    cap_local = words.shape[0] // places
    null_rows = null.shape[1]
    for k in range(count):
        value = jnp.zeros((null_rows, words.shape[1]), wide)
        for place in range(places):
            first = place * cap_local + k * null_rows
            part = words[first : first + null_rows].astype(wide)
            value = value + jnp.where(flags[place] == 1, part, 0.0)
        null[k] = value
    next(out_sums)
    next(proj_sums)
    nulls = [
        links.start(null.at[jnp.bitwise_xor(b, k)], null_come.at[k - 1], others[k - 1])
        for k in range(1, count)
    ]

    def drain(sums):
        for _ in sums:
            pass

    def seq_sends(go, come):
        come[s] = go[s]
        return [
            links.start(go.at[place], come.at[s], device)
            for place, device in zip(turns, along, strict=True)
        ]

    for step in range(3, depth - 1):
        weights_step(step)
    weights.arrived()
    gate[...] = weights.value(0, depth - 1).astype(narrow)
    far = [
        links.start(gate.at[jnp.bitwise_xor(b, k)], gate_come.at[b], others[k - 1])
        for k in range(1, count)
    ]
    gate_come[b] = gate[b]
    down_share[...] = weights.value(1, depth - 1)
    own_small = small[s]
    for copy in tiny:
        copy.wait_recv()
    for i in range(depth - 1):
        own_small = own_small + small_come[i]
    small_go[...] = own_small
    spread = []
    for k in range(1, count):
        spread.append(links.start(rows_out.at[0], rows_out.at[k], others[k - 1]))
        spread.append(
            links.start(
                small_go.at[jnp.bitwise_xor(b, k)], small_land.at[k - 1], others[k - 1]
            )
        )
    drain(out_sums)
    out_far = seq_sends(out_go, out_come)
    drain(proj_sums)
    proj_far = seq_sends(proj_go, proj_come)
    for step in range(2, depth - 1):
        text_step(step)
    total = null[b]
    for i, copy in enumerate(nulls):
        copy.wait_recv()
        total = total + null_come[i]
    null_share[...] = total
    for copy in spread:
        copy.wait_recv()
    sums = small_go[b]
    for i in range(count - 1):
        sums = sums + small_land[i]
    small_out[...] = sums
    for copy in far:
        copy.wait_recv()
    units = gate.shape[2] // 2
    for block in range(count):
        for half in range(2):
            first = half * count * units + block * units
            gate_share[:, first : first + units] = gate_come[
                block, :, half * units : (half + 1) * units
            ].astype(wide)
    for copy in out_far + proj_far:
        copy.wait_recv()
    text_step(depth - 1)
    total = out_come[0].astype(wide)
    for i in range(1, depth):
        total = total + out_come[i].astype(wide)
    output_share[...] = total
    own = proj_come.shape[2] // 3
    for i in range(3):
        for source in range(depth):
            first = i * depth * own + source * own
            proj_share[:, first : first + own] = proj_come[
                source, :, i * own : (i + 1) * own
            ].astype(wide)
    links.finish()


def final_sums(
    count, depth, flags, text, combined, upstream, normed, grads, ffn_grads, held, words, row, small
):
    vmem = pl.BlockSpec(memory_space=pltpu.VMEM)
    feature, pair_width = text.shape
    width = combined.shape[1]
    own3 = grads.shape[2]
    share = width // (count * depth)
    null_rows = words.shape[0] // flags.shape[0] // count
    text_width = words.shape[1]
    outer = count // 2
    block_rows = width // count
    quarter = (depth - 1, feature // depth, pair_width)

    def plane_sums(columns):
        return [
            pltpu.VMEM((count, block_rows, columns), narrow),
            pltpu.VMEM((outer, block_rows, columns), narrow),
            pltpu.VMEM((2, outer - 1, block_rows // 2, columns), narrow),
        ]

    copies = 2 * (depth - 1) + depth - 1 + 2 * plane_copies(count)[1] + 4 * (count - 1)
    copies += 2 * (depth - 1) + 2 * (depth - 3)
    gate, down = held
    gates = pltpu.VMEM(gate.shape, narrow)
    return pl.pallas_call(
        partial(sum_kernel, count, depth),
        in_specs=[scalar_spec()] + [vmem] * 12,
        out_specs=[vmem] * 8,
        out_shape=[
            jax.ShapeDtypeStruct(down.shape, wide),
            jax.ShapeDtypeStruct((feature // depth, pair_width), wide),
            jax.ShapeDtypeStruct((share, width), wide),
            jax.ShapeDtypeStruct((share, depth * own3), wide),
            jax.ShapeDtypeStruct((share, count * gate.shape[2]), wide),
            jax.ShapeDtypeStruct((null_rows, text_width), wide),
            jax.ShapeDtypeStruct((count, depth) + row.shape, wide),
            jax.ShapeDtypeStruct(small.shape[2:], wide),
        ],
        scratch_shapes=plane_sums(width)
        + plane_sums(own3)
        + [
            pltpu.VMEM(quarter, narrow),
            pltpu.VMEM(quarter, narrow),
            pltpu.VMEM((depth, share, width), narrow),
            pltpu.VMEM((depth, share, width), narrow),
            pltpu.VMEM((depth, share, own3), narrow),
            pltpu.VMEM((depth, share, own3), narrow),
            gates,
            gates,
            pltpu.VMEM((count, null_rows, text_width), wide),
            pltpu.VMEM((count - 1, null_rows, text_width), wide),
            pltpu.VMEM((depth - 1,) + small.shape[1:], wide),
            pltpu.VMEM(small.shape[1:], wide),
            pltpu.VMEM((count - 1,) + small.shape[2:], wide),
            pltpu.VMEM((depth - 3,) + gate.shape, narrow),
            pltpu.VMEM((depth - 3,) + down.shape, narrow),
            pltpu.VMEM((depth - 3,) + gate.shape, narrow),
            pltpu.VMEM((depth - 3,) + down.shape, narrow),
            pltpu.SemaphoreType.DMA((copies,)),
            pltpu.SemaphoreType.DMA((copies,)),
        ],
        compiler_params=pltpu.CompilerParams(
            collective_id=10, has_side_effects=True, vmem_limit_bytes=60 * 2**20
        ),
        name="final_sums",
    )(flags, text, combined, upstream, normed, grads, *ffn_grads, *held, words, row, small)


def head_lanes(values, head, size):
    lane = lax.broadcasted_iota(jnp.int32, values.shape, 1)
    return jnp.where((lane >= head * size) & (lane < (head + 1) * size), values, 0)


def swap_halves(values, size):
    half = size // 2
    lanes = values.shape[1]
    if lanes % 128 == 0:
        lane = lax.broadcasted_iota(jnp.int32, values.shape, 1)
        ahead = pltpu.roll(values, lanes - half, 1)
        behind = pltpu.roll(values, half, 1)
        return jnp.where(lax.rem(lane, size) < half, ahead, behind)
    parts = []
    for start in range(0, lanes, size):
        parts.append(values[:, start + half : start + size])
        parts.append(values[:, start : start + half])
    return jnp.concatenate(parts, axis=1)


def turn(values, cosine, signed_sine, size):
    return values * cosine + swap_halves(values, size) * signed_sine


def flat(values):
    return values.reshape(-1, values.shape[-1])


def scalar_spec():
    return pl.BlockSpec(memory_space=pltpu.SMEM)


def row_sums(values):
    ones = jnp.ones((8, values.shape[1]), wide)
    return lax.dot_general(
        ones, values, (((1,), (1,)), ((), ())), precision=HIGHEST, preferred_element_type=wide
    )[:1]


def loop(count, body):
    if count == 1:
        body(0)
    else:
        lax.fori_loop(0, count, lambda i, _: (body(i), 0)[1], 0)


def lane_block(index, lanes):
    if isinstance(index, int):
        return pl.ds(index * lanes, lanes)
    return pl.ds(pl.multiple_of(index * lanes, 128), lanes)


def block_rows_of(index, rows):
    if isinstance(index, int):
        return pl.ds(index * rows, rows)
    return pl.ds(pl.multiple_of(index * rows, 128), rows)


def forward_kernel(
    count, depth, size, lanes, spans, lengths, gates, raw_q, raw_k, raw_v, rates, gain_q, gain_k,
    cosine, sine, text_own, gate_up, combined, q, k, v, qc, total, cross_total, text, gathered,
    self_out, staged, send, arrive, local,
):
    links = Transfers(send, arrive)
    b, s = lax.axis_index("bucket"), lax.axis_index("seq")
    others = [partner(k) for k in range(1, count)]
    turns = [lax.rem(s + step, depth) for step in range(1, depth)]
    along = [seq_device(place) for place in turns]
    meet(others + along)
    block_rows, own = raw_q.shape[1:]
    rows = depth * block_rows
    width = own * depth
    grid, heads = own // lanes, lanes // size
    scaling = size ** (-0.5)
    words = [
        links.start(text_own.at[place], text.at[s], device)
        for place, device in zip(turns, along, strict=True)
    ]
    text[s] = text_own[s]
    gate_rows, units = gate_up.shape[0], gathered.shape[1] // 2
    half_width = gate_up.shape[1] // 2
    here = pl.ds(pl.multiple_of(b * gate_rows, 16), gate_rows)
    weights, kept = [], []
    for block in range(count):
        target = jnp.bitwise_xor(b, block)
        for half in range(2):
            source = gate_up.at[
                :, pl.ds(pl.multiple_of(half * half_width + target * units, 128), units)
            ]
            landing = gathered.at[here, pl.ds(half * units, units)]
            if block:
                weights.append(links.start(source, landing, others[block - 1]))
            else:
                copy = pltpu.make_async_copy(source, landing, local.at[half])
                copy.start()
                kept.append(copy)
    for block in range(depth):
        v[block_rows_of(block, block_rows)] = raw_v[block].astype(narrow)
    columns = rates[...].T
    for block in range(depth):
        at = block_rows_of(block, block_rows)
        cos, sin = cosine[at], sine[at]
        for group in range(grid):
            span = lane_block(group, lanes)
            norm_q = raw_q[block, :, span] * columns[:, block : block + 1] * gain_q[:, span]
            norm_k = (
                raw_k[block, :, span]
                * columns[:, depth + block : depth + block + 1]
                * gain_k[:, span]
            )
            turned = turn(norm_q, cos, sin, size).astype(narrow).astype(wide)
            q[at, span] = (turned * scaling).astype(narrow)
            qc[at, span] = (norm_q.astype(narrow).astype(wide) * scaling).astype(narrow)
            k[at, span] = turn(norm_k, cos, sin, size).astype(narrow)
    key_index = lax.broadcasted_iota(jnp.int32, (rows, block_rows), 0)

    def attend_self(group):
        span = lane_block(group, lanes)
        value_t = v[:, span].astype(wide).T.astype(narrow)
        for block in range(depth):
            at = block_rows_of(block, block_rows)
            allowed = (key_index >= spans[0, block]) & (key_index < spans[1, block])
            outs = []
            for head in range(heads):
                scores = contract_cols(k[:, span], head_lanes(q[at, span], head, size))
                scores = jnp.where(allowed, scores, NEGATIVE)
                peak = jnp.max(scores, axis=0, keepdims=True)
                shares = jnp.exp(scores - peak)
                mass = jnp.sum(shares, axis=0, keepdims=True)
                part = slice(head * size, (head + 1) * size)
                outs.append(dense(value_t[part], shares.astype(narrow)) / mass)
                total[group, head : head + 1, at] = peak + jnp.log(mass)
            self_out[at, span] = jnp.concatenate(outs, axis=0).T

    loop(grid, attend_self)
    for copy in words:
        copy.wait_recv()
    cap = text.shape[0] * text.shape[3]
    cap_index = lax.broadcasted_iota(jnp.int32, (cap, block_rows), 0)
    results = []
    for step in range(depth):
        block = lax.rem(s + 1 + step, depth)
        at = block_rows_of(block, block_rows)
        clip = spans[2, block]
        live = cap_index < lengths[clip]

        def attend_cross(group):
            span = lane_block(group, lanes)
            text_key = flat(text[:, 0, clip, :, span])
            value_t = flat(text[:, 1, clip, :, span]).astype(wide).T.astype(narrow)
            outs = []
            for head in range(heads):
                scores = contract_cols(text_key, head_lanes(qc[at, span], head, size))
                scores = jnp.where(live, scores, NEGATIVE)
                peak = jnp.max(scores, axis=0, keepdims=True)
                shares = jnp.exp(scores - peak)
                mass = jnp.sum(shares, axis=0, keepdims=True)
                part = slice(head * size, (head + 1) * size)
                gate = gates[group * heads + head]
                outs.append(dense(value_t[part], shares.astype(narrow)) * (gate / mass))
                cross_total[group, head : head + 1, at] = peak + jnp.log(mass)
            staged[step, :, span] = (
                self_out[at, span] + jnp.concatenate(outs, axis=0).T
            ).astype(narrow)

        loop(grid, attend_cross)
        if step < depth - 1:
            results.append(links.start(staged.at[step], combined.at[s], along[step]))
        else:
            combined[s] = staged[step]
    for copy in results + weights:
        copy.wait_recv()
    for copy in kept:
        copy.wait()
    links.finish()


def attention_forward(
    count, depth, size, lanes, scalars, raws, rates, gains, angles, text_own, gate_up
):
    block_rows, own = raws[0].shape[1:]
    rows = depth * block_rows
    grid, heads = own // lanes, lanes // size
    vmem, anywhere = pl.BlockSpec(memory_space=pltpu.VMEM), pl.BlockSpec(memory_space=pl.ANY)
    units = gate_up.shape[1] // (2 * count)
    copies = 2 * (depth - 1) + 2 * (count - 1)
    row_block = jax.ShapeDtypeStruct((rows, own), narrow)
    totals = jax.ShapeDtypeStruct((grid, heads, rows), wide)
    return pl.pallas_call(
        partial(forward_kernel, count, depth, size, lanes),
        in_specs=[scalar_spec()] * 3 + [vmem] * 9 + [anywhere],
        out_specs=[vmem] * 9,
        out_shape=[
            jax.ShapeDtypeStruct((depth, block_rows, own), narrow),
            row_block,
            row_block,
            row_block,
            row_block,
            totals,
            totals,
            jax.ShapeDtypeStruct(text_own.shape, narrow),
            jax.ShapeDtypeStruct((count * gate_up.shape[0], 2 * units), narrow),
        ],
        scratch_shapes=[
            pltpu.VMEM((rows, own), wide),
            pltpu.VMEM((depth, block_rows, own), narrow),
            pltpu.SemaphoreType.DMA((copies,)),
            pltpu.SemaphoreType.DMA((copies,)),
            pltpu.SemaphoreType.DMA((2,)),
        ],
        compiler_params=pltpu.CompilerParams(
            collective_id=8, has_side_effects=True, vmem_limit_bytes=60 * 2**20
        ),
        name="attention_forward",
    )(*scalars, *raws, rates, *gains, *angles, text_own, gate_up)


def backward_kernel(
    count, depth, size, lanes, spans, lengths, gates, upstream, weight, q, k, v, qc, raw_q, raw_k,
    rates, gain_q, gain_k, cosine, sine, text, total, cross_total, small, grad_gate, grad_down,
    projected, gain_sums, dgate, grad_text, small_out, gate_held, down_held, go, send_go, dqc, back_q, back_k, parts, send_text, stat,
    stat_in, sum_k, sum_v, send, arrive,
):
    links = Transfers(send, arrive)
    s = lax.axis_index("seq")
    others = [partner(k) for k in range(1, count)]
    turns = [lax.rem(s + step, depth) for step in range(1, depth)]
    along = [seq_device(place) for place in turns]
    meet(others + along)
    block_rows, own = upstream.shape[0], q.shape[1]
    rows = depth * block_rows
    width = own * depth
    grid, heads = own // lanes, lanes // size
    scaling = size ** (-0.5)

    small_out[0, s] = small[...]
    smalls = [links.start(small, small_out.at[0, s], device) for device in along]

    def grad_out(place):
        at = pl.ds(pl.multiple_of(place * own, 64), own)
        return contract_cols(upstream[...], weight[at]).astype(narrow)

    arriving = []
    for i, (place, device) in enumerate(zip(turns, along, strict=True)):
        send_go[i] = grad_out(place)
        arriving.append(links.start(send_go.at[i], go.at[s], device))
    go[s] = grad_out(s)
    ring = Ring(depth, links)
    weights = GradientRing(ring, (grad_gate, grad_down), None)

    cap_local = text.shape[3]
    cap = text.shape[0] * cap_local
    places = text.shape[2]
    cap_index = lax.broadcasted_iota(jnp.int32, (cap, block_rows), 0)
    clips = []
    for step in range(depth):
        block = lax.rem(s - step + depth, depth)
        if step:
            arriving[step - 1].wait_recv()
        if step == depth - 1:
            weights.first((gate_held, down_held))
        at = block_rows_of(block, block_rows)
        clip = spans[2, block]
        clips.append(clip)
        live = cap_index < lengths[clip]

        def back_cross(group):
            span = lane_block(group, lanes)
            text_key = flat(text[:, 0, clip, :, span])
            text_value = flat(text[:, 1, clip, :, span])
            key_t = text_key.astype(wide).T.astype(narrow)
            grads = []
            for head in range(heads):
                gate = gates[group * heads + head]
                query = head_lanes(qc[at, span], head, size)
                grad = head_lanes(go[block, :, span], head, size)
                scores = contract_cols(text_key, query)
                scores = jnp.where(live, scores, NEGATIVE)
                shares = jnp.exp(scores - cross_total[group, head : head + 1, at])
                grad_shares = contract_cols(text_value, grad)
                row = jnp.sum(grad_shares * shares, axis=0, keepdims=True)
                grad_scores = (gate * (shares * (grad_shares - row))).astype(narrow)
                grad_key = dense(grad_scores, query)
                grad_value = gate * dense(shares.astype(narrow), grad)
                if head == 0:
                    parts[step, 0, :, span] = grad_key
                    parts[step, 1, :, span] = grad_value
                else:
                    parts[step, 0, :, span] += grad_key
                    parts[step, 1, :, span] += grad_value
                part = slice(head * size, (head + 1) * size)
                grads.append(dense(key_t[part], grad_scores) * scaling)
                if step == 0:
                    dgate[group, head : head + 1] = row
                else:
                    dgate[group, head : head + 1] += row
            dqc[at, span] = jnp.concatenate(grads, axis=0).T

        loop(grid, back_cross)
    for which in range(2):
        for place in range(places):
            for target in range(depth):
                at = pl.ds(target * cap_local, cap_local)
                value = jnp.zeros((cap_local, own), wide)
                for step in range(depth):
                    value = value + jnp.where(
                        clips[step] == place, parts[step, which, at], 0.0
                    )
                send_text[target, which, place] = value.astype(narrow)
    words = [
        links.start(send_text.at[place], grad_text.at[s], device)
        for place, device in zip(turns, along, strict=True)
    ]
    grad_text[s] = send_text[s]
    for copy in smalls:
        copy.wait_recv()
    spread = [links.start(small_out.at[0], small_out.at[k], others[k - 1]) for k in range(1, count)]

    key_index = lax.broadcasted_iota(jnp.int32, (rows, block_rows), 0)

    def back_self(group):
        span = lane_block(group, lanes)
        key_t = k[:, span].astype(wide).T.astype(narrow)
        for block in range(depth):
            at = block_rows_of(block, block_rows)
            allowed = (key_index >= spans[0, block]) & (key_index < spans[1, block])
            grads = []
            for head in range(heads):
                query = head_lanes(q[at, span], head, size)
                grad = head_lanes(go[block, :, span], head, size)
                scores = contract_cols(k[:, span], query)
                scores = jnp.where(allowed, scores, NEGATIVE)
                shares = jnp.exp(scores - total[group, head : head + 1, at])
                grad_shares = contract_cols(v[:, span], grad)
                row = jnp.sum(grad_shares * shares, axis=0, keepdims=True)
                grad_scores = (shares * (grad_shares - row)).astype(narrow)
                if block == 0 and head == 0:
                    sum_v[...] = dense(shares.astype(narrow), grad)
                    sum_k[...] = dense(grad_scores, query)
                else:
                    sum_v[...] += dense(shares.astype(narrow), grad)
                    sum_k[...] += dense(grad_scores, query)
                part = slice(head * size, (head + 1) * size)
                grads.append(dense(key_t[part], grad_scores) * scaling)
            back = jnp.concatenate(grads, axis=0).T
            back_q[at, span] = turn(back, cosine[at], -sine[at], size) + dqc[at, span]
        back_k[:, span] = turn(sum_k[...], cosine[...], -sine[...], size)
        for block in range(depth):
            at = block_rows_of(block, block_rows)
            if isinstance(group, int):
                to = pl.ds(2 * own + group * lanes, lanes)
            else:
                to = pl.ds(pl.multiple_of(2 * own + group * lanes, 128), lanes)
            projected[block, :, to] = sum_v[at].astype(narrow)

    loop(grid, back_self)
    columns = rates[...].T
    pairs = ((raw_q, back_q, gain_q), (raw_k, back_k, gain_k))
    for i, (raw, back, gain) in enumerate(pairs):
        gains = jnp.zeros((1, own), wide)
        for block in range(depth):
            place = i * depth + block
            at = block_rows_of(block, block_rows)
            hat = raw[block] * columns[:, place : place + 1]
            gains = gains + jnp.sum(back[at] * hat, axis=0, keepdims=True)
            stat[place : place + 1] = row_sums(back[at] * gain[...] * hat)
        gain_sums[i : i + 1] = gains
    stats = [links.start(stat, stat_in.at[i], device) for i, device in enumerate(along)]
    means = stat[...]
    for i, copy in enumerate(stats):
        copy.wait_recv()
        means = means + stat_in[i]
    means = (means / width).T
    for i, (raw, back, gain) in enumerate(pairs):
        for block in range(depth):
            place = slice(i * depth + block, i * depth + block + 1)
            at = block_rows_of(block, block_rows)
            rate = columns[:, place]
            hat = raw[block] * rate
            projected[block, :, i * own : (i + 1) * own] = (
                rate * (back[at] * gain[...] - hat * means[:, place])
            ).astype(narrow)
    for copy in words + spread + weights.copies:
        copy.wait_recv()
    links.finish()


def attention_backward(
    count, depth, size, lanes, scalars, upstream, weight, saved, raws, rates, gains, angles, text,
    totals, small, ffn_grads,
):
    block_rows, own = raws[0].shape[1:]
    rows = depth * block_rows
    grid, heads = own // lanes, lanes // size
    vmem = pl.BlockSpec(memory_space=pltpu.VMEM)
    copies = 4 * (depth - 1) + count - 1 + 2
    cap = text.shape[0] * text.shape[3]
    args = (*scalars, upstream, weight, *saved, *raws, rates, *gains, *angles, text, *totals, small)
    args = args + tuple(ffn_grads)
    return pl.pallas_call(
        partial(backward_kernel, count, depth, size, lanes),
        in_specs=[scalar_spec()] * 3 + [vmem] * (len(args) - 3),
        out_specs=[vmem] * 7,
        out_shape=[
            jax.ShapeDtypeStruct((depth, block_rows, 3 * own), narrow),
            jax.ShapeDtypeStruct((2, own), wide),
            jax.ShapeDtypeStruct((grid, heads, block_rows), wide),
            jax.ShapeDtypeStruct(text.shape, narrow),
            jax.ShapeDtypeStruct((count, depth) + small.shape, wide),
            jax.ShapeDtypeStruct(ffn_grads[0].shape[:1] + ffn_grads[0].shape[2:], narrow),
            jax.ShapeDtypeStruct(ffn_grads[1].shape[1:], narrow),
        ],
        scratch_shapes=[
            pltpu.VMEM((depth, block_rows, own), narrow),
            pltpu.VMEM((depth - 1, block_rows, own), narrow),
            pltpu.VMEM((rows, own), wide),
            pltpu.VMEM((rows, own), wide),
            pltpu.VMEM((rows, own), wide),
            pltpu.VMEM((depth, 2, cap, own), wide),
            pltpu.VMEM(text.shape, narrow),
            pltpu.VMEM((2 * depth, block_rows), wide),
            pltpu.VMEM((depth - 1, 2 * depth, block_rows), wide),
            pltpu.VMEM((rows, lanes), wide),
            pltpu.VMEM((rows, lanes), wide),
            pltpu.SemaphoreType.DMA((copies,)),
            pltpu.SemaphoreType.DMA((copies,)),
        ],
        compiler_params=pltpu.CompilerParams(
            collective_id=9, has_side_effects=True, vmem_limit_bytes=60 * 2**20
        ),
        name="attention_backward",
    )(*args)


def per_device(
    tokens,
    condition,
    captions,
    caption_lengths,
    null_flags,
    slot_buckets,
    null_caption,
    modulation,
    projection,
    text_weight,
    output_weight,
    gate_up,
    down_weight,
    norm_gains,
    head_gains,
    cross_gates,
    cotangent,
):
    count_s, count_b = lax.axis_size("seq"), lax.axis_size("bucket")
    s, b = lax.axis_index("seq"), lax.axis_index("bucket")
    assert count_s % 4 == 0
    local, width = tokens.shape
    heads = cross_gates.shape[0]
    size = width // heads
    own_heads = heads // count_s
    own = width // count_s
    rows = local * count_s
    places, cap_local, text_width = captions.shape
    cap_rows = places * cap_local
    bucket = slot_buckets[0]
    clip_length = jnp.where(
        bucket == 0, rows // 4, jnp.where(bucket == 1, rows // 2, rows)
    ).astype(jnp.int32)

    own_hidden = down_weight.shape[0]
    gate_rows = gate_up.shape[0]
    text_rows = text_weight.shape[0]
    null_rows = lax.dynamic_slice_in_dim(null_caption, s * cap_local, cap_local, 0)
    is_null = null_flags[:, None, None] == 1
    words_own = jnp.where(is_null, null_rows[None], captions).reshape(cap_rows, text_width)
    own_projection = jnp.concatenate(
        [
            lax.dynamic_slice_in_dim(projection, i * width + s * own, own, 1)
            for i in range(3)
        ],
        axis=1,
    )

    silu_cond = jax.nn.silu(condition).astype(narrow)
    mod_width = modulation.shape[1] // count_s
    pieces = silu_cond.astype(wide).reshape(places, count_b, -1).transpose(1, 0, 2)
    my_clip = (s * local) // clip_length
    (
        cond_columns,
        mods,
        own_projection,
        words,
        text_pairs,
        normed,
        raw_q,
        raw_k,
        raw_v,
        rates,
    ) = start_exchange(
        count_b,
        count_s,
        my_clip.astype(jnp.int32)[None],
        pieces,
        lax.dynamic_slice_in_dim(modulation, s * mod_width, mod_width, 1),
        own_projection,
        words_own,
        text_weight,
        tokens,
        norm_gains[:1],
    )
    own_projection = own_projection.reshape(width, 3 * own)
    modulated = lax.dynamic_index_in_dim(mods, my_clip, 1, keepdims=False).reshape(1, 4 * width)
    tokens_in = tokens.astype(wide)
    _, pre_pull = jax.vjp(pre_attention, tokens_in, modulated, norm_gains)

    text_outs, text_pull = jax.vjp(text_heads, text_pairs, head_gains[2])
    text_own = jnp.stack([o.astype(narrow).reshape(cap_rows, count_s, own) for o in text_outs])
    text_own = text_own.transpose(2, 0, 1, 3).reshape(count_s, 2, places, cap_local, own)

    gains = [lax.dynamic_slice_in_dim(head_gains[i : i + 1], s * own, own, 1) for i in range(2)]
    inside = lax.rem(jnp.arange(rows, dtype=jnp.int32), clip_length)
    half = size // 2
    frequency = 10000.0 ** (-jnp.arange(half, dtype=wide) / half)
    angles = inside.astype(wide)[:, None] * frequency[None, :]
    lanes = 128 if own % 128 == 0 else own
    block_heads = lanes // size
    cosine = jnp.tile(jnp.cos(angles), (1, 2 * block_heads))
    sine = jnp.tile(
        jnp.concatenate([-jnp.sin(angles), jnp.sin(angles)], axis=1), (1, block_heads)
    )
    tanh_gates = jnp.tanh(cross_gates)
    own_gates = lax.dynamic_slice_in_dim(tanh_gates, s * own_heads, own_heads, 0)
    clip_of = (jnp.arange(count_s, dtype=jnp.int32) * local) // clip_length
    spans = jnp.stack([clip_of * clip_length, (clip_of + 1) * clip_length, clip_of])
    scalars = (spans, caption_lengths, own_gates)
    full_output, text_own = lax.optimization_barrier((output_weight, text_own))
    full_output = lax.all_gather(full_output, "bucket", axis=0, tiled=True)
    combined, *saved, total, cross_total, text_kv, own_gate_up = attention_forward(
        count_b,
        count_s,
        size,
        lanes,
        scalars,
        (raw_q, raw_k, raw_v),
        rates,
        gains,
        (cosine, sine),
        text_own,
        gate_up,
    )
    combined = combined.transpose(1, 0, 2).reshape(local, width)

    attended = dense(combined, full_output)
    (middle, ffn_full), post_pull = jax.vjp(
        post_attention, attended, tokens_in, modulated, norm_gains
    )
    normed_ffn = ffn_full.astype(narrow)

    lowered, plane, gate_values, hidden = ffn_forward(
        count_b, normed_ffn, own_gate_up, down_weight
    )
    mixed, finish_pull = jax.vjp(finish, lowered, middle, modulated, norm_gains)
    grad_lowered, grad_middle, grad_modulated_last, grad_norm_last = finish_pull(
        cotangent.astype(wide)
    )
    grad_lowered_low = grad_lowered.astype(narrow)
    grad_normed_ffn, grad_gate_up, grad_down = ffn_backward(
        count_b, grad_lowered_low, own_gate_up, down_weight, gate_values, plane, hidden
    )
    share = width // (count_b * count_s)
    ffn_grads = (
        grad_gate_up.reshape(count_b, count_s, share, 2 * own_hidden),
        grad_down.reshape(count_s, own_hidden // count_s, width),
    )

    grad_attended, grad_tokens_post, grad_modulated_post, grad_norm_post = post_pull(
        (grad_middle, grad_normed_ffn)
    )
    grad_attended_low = grad_attended.astype(narrow)
    grad_projected, gain_sums, grad_gates, grad_kv, early, *held = attention_backward(
        count_b,
        count_s,
        size,
        lanes,
        scalars,
        grad_attended_low,
        full_output,
        saved,
        (raw_q, raw_k),
        rates,
        gains,
        (cosine, sine),
        text_kv,
        (total, cross_total),
        (grad_modulated_post + grad_modulated_last)[:, width:],
        ffn_grads,
    )

    grad_kv = grad_kv.reshape(count_s, 2, cap_rows, own)
    grad_kv = grad_kv.transpose(1, 2, 0, 3).reshape(2, cap_rows, width).astype(wide)
    grad_pairs, grad_gain_text = text_pull((grad_kv[0], grad_kv[1]))
    grad_pairs_low = grad_pairs.astype(narrow)
    grad_normed, grad_words, grad_text, *held = end_exchange(
        count_b,
        count_s,
        grad_pairs_low,
        text_weight,
        words,
        grad_projected,
        own_projection,
        ffn_grads,
        held,
    )
    grad_tokens_pre, grad_modulated_pre, grad_norm_pre = pre_pull(grad_normed)
    grad_tokens = grad_tokens_pre + grad_tokens_post

    def place(values):
        return lax.dynamic_update_slice_in_dim(jnp.zeros((width,), wide), values, s * own, 0)

    gate_sums = lax.dynamic_update_slice_in_dim(
        jnp.zeros((heads,), wide),
        jnp.sum(grad_gates, axis=2).reshape(own_heads) * (1.0 - own_gates * own_gates),
        s * own_heads,
        0,
    )
    small = jnp.concatenate(
        [
            grad_norm_pre + grad_norm_post + grad_norm_last,
            jnp.stack(
                [
                    place(gain_sums[0]),
                    place(gain_sums[1]),
                    grad_gain_text,
                    jnp.zeros((width,), wide),
                ]
            ),
        ],
        axis=0,
    )
    own_clip = (jnp.arange(places, dtype=jnp.int32) == my_clip).astype(wide)
    row = jnp.concatenate(
        [
            jnp.pad(gate_sums, (0, 128 - heads)),
            jnp.pad(own_clip, (0, width - 128 - places)),
        ]
    )
    row = jnp.stack([grad_modulated_pre[0, :width], row], axis=0)
    (
        down_share,
        text_share,
        output_share,
        proj_share,
        gate_share,
        null_share,
        grad_rows,
        own_sums,
    ) = final_sums(
        count_b,
        count_s,
        null_flags,
        grad_text,
        combined,
        grad_attended_low,
        normed,
        grad_projected,
        ffn_grads,
        held,
        grad_words,
        row,
        small.reshape(8, count_b, count_s, share).transpose(2, 1, 0, 3),
    )
    null_share = lax.ppermute(
        null_share,
        ("bucket", "seq"),
        [(i * count_s + j, j * count_b + i) for i in range(count_b) for j in range(count_s)],
    )
    grad_words = grad_words.reshape(places, cap_local, text_width).astype(wide)
    grad_captions = jnp.where(is_null, 0.0, grad_words)

    cond_own = lax.dynamic_slice_in_dim(cond_columns, s * share, share, 2)
    at_clip = grad_rows[:, :, 1, 128 : 128 + places]
    cond_rows = jnp.sum(at_clip[:, :, :, None] * cond_own[:, None], axis=2)
    mod_share = lax.dot_general(
        flat(cond_rows),
        jnp.concatenate([flat(grad_rows[:, :, 0]), flat(early)], axis=1),
        (((0,), (0,)), ((), ())),
        precision=HIGHEST,
    )
    return (
        mixed.astype(narrow),
        grad_tokens,
        grad_captions,
        null_share,
        mod_share,
        proj_share,
        text_share,
        output_share,
        gate_share,
        down_share,
        own_sums[:4],
        own_sums[4:7],
        jnp.sum(grad_rows[:, :, 1, :heads], axis=(0, 1)),
    )


def solution(mesh):
    whole = P(("bucket", "seq"), None)
    shard = P("bucket", None)
    return jax.shard_map(
        per_device,
        mesh=mesh,
        in_specs=(
            whole,
            shard,
            P("bucket", "seq", None),
            P("bucket"),
            P("bucket"),
            P("bucket"),
            P(),
            shard,
            shard,
            shard,
            shard,
            shard,
            shard,
            P(),
            P(),
            P(),
            whole,
        ),
        out_specs=(
            whole,
            whole,
            P("bucket", "seq", None),
            whole,
            whole,
            whole,
            whole,
            whole,
            whole,
            whole,
            P(None, ("bucket", "seq")),
            P(None, ("bucket", "seq")),
            P(),
        ),
        check_vma=False,
    )
```

```python
from functools import partial

import jax
import jax.numpy as jnp
from jax import lax
from jax.experimental import pallas as pl
from jax.experimental.pallas import tpu as pltpu
from jax.sharding import PartitionSpec as P

EPSILON = 1e-06
NEGATIVE = -1e30
HIGHEST = lax.Precision.HIGHEST
wide = jnp.float32
narrow = jnp.bfloat16
VMEM_LIMIT = 50 * 2**20


def rms_norm(values, norm_gain):
    return (
        values * lax.rsqrt(jnp.mean(values * values, axis=-1, keepdims=True) + EPSILON) * norm_gain
    )


def dense(leading, trailing):
    return jnp.dot(leading, trailing, preferred_element_type=wide)


def contract_rows(leading, trailing):
    return lax.dot_general(
        leading, trailing, (((0,), (0,)), ((), ())), preferred_element_type=wide
    )


def contract_cols(leading, trailing):
    return lax.dot_general(
        leading, trailing, (((1,), (1,)), ((), ())), preferred_element_type=wide
    )


def pre_attention(tokens_in, modulated, norm_gains):
    model_width = tokens_in.shape[1]
    return rms_norm(tokens_in, norm_gains[0]) * (1.0 + modulated[:, :model_width])


def text_heads(text_pairs, gain):
    model_width = text_pairs.shape[1] // 2
    return (rms_norm(text_pairs[:, :model_width], gain), text_pairs[:, model_width:])


def post_attention(attended, tokens_in, modulated, norm_gains):
    model_width = tokens_in.shape[1]
    middle = tokens_in + jnp.tanh(modulated[:, model_width : 2 * model_width]) * rms_norm(
        attended, norm_gains[1]
    )
    normed_ffn = rms_norm(middle, norm_gains[2]) * (
        1.0 + modulated[:, 2 * model_width : 3 * model_width]
    )
    return (middle, normed_ffn)


def swiglu(gate_values):
    hidden_width = gate_values.shape[1] // 2
    return jax.nn.silu(gate_values[:, :hidden_width]) * gate_values[:, hidden_width:]


def finish(lowered, middle, modulated, norm_gains):
    model_width = middle.shape[1]
    return middle + jnp.tanh(modulated[:, 3 * model_width :]) * rms_norm(lowered, norm_gains[3])


MESH = pl.DeviceIdType.MESH


class Transfers:
    def __init__(self, send, arrive):
        self.send, self.arrive, self.used = send, arrive, 0
        self.open = []

    def start(self, source, target, device):
        copy = pltpu.make_async_remote_copy(
            src_ref=source,
            dst_ref=target,
            send_sem=self.send.at[self.used],
            recv_sem=self.arrive.at[self.used],
            device_id=device,
            device_id_type=MESH,
        )
        self.used += 1
        copy.start()
        self.open.append(copy)
        return copy

    def finish(self):
        for copy in self.open:
            copy.wait_send()


def meet(devices):
    barrier = pltpu.get_barrier_semaphore()
    for device in devices:
        pl.semaphore_signal(barrier, inc=1, device_id=device, device_id_type=MESH)
    pl.semaphore_wait(barrier, len(devices))


def partner(bits):
    return {"bucket": jnp.bitwise_xor(lax.axis_index("bucket"), bits)}


def outer_bits(count):
    return [1 << i for i in range(1, count.bit_length() - 1)]


def block_index(k, count):
    return (k >> 1) + (k & 1) * (count // 2)


def last_bit(block, order):
    return [bit for bit in order if block & bit][-1]


class PlaneExchange:
    def __init__(
        self, count, links, gathered=None, partial=None, arrived_core=None, arrived_outer=None,
        natural=False,
    ):
        self.count, self.links, self.natural = count, links, natural
        self.index = lax.axis_index("bucket")
        self.gathered, self.partial = gathered, partial
        self.arrived_core, self.arrived_outer = arrived_core, arrived_outer
        bits = outer_bits(count)
        self.orders = (bits, bits[::-1])
        self.outer = [k for k in range(0, count, 2)]
        self.rows = (partial if gathered is None else gathered).shape[1] // 2
        self.coming, self.slots = {}, {}
        self.blocks = [0]

    def part(self, ref, block, half):
        return ref.at[block, pl.ds(half * self.rows, self.rows)]

    def place(self, block):
        return jnp.bitwise_xor(self.index, block) if self.natural else block_index(block, self.count)

    def onward(self, half, block, bit):
        source = self.place(block)
        target = source if self.natural else self.place(block | bit)
        self.coming[half, block | bit] = self.links.start(
            self.part(self.gathered, source, half),
            self.part(self.gathered, target, half),
            partner(bit),
        )

    def forward(self, half, block):
        order = self.orders[half]
        later = order if block == 0 else order[order.index(last_bit(block, order)) + 1 :]
        for bit in later:
            self.onward(half, block, bit)

    def forward_core(self, half, block):
        self.onward(half, block, 1)

    def arrive(self, block):
        for half in range(2):
            self.coming[half, block].wait_recv()

    def begin(self):
        for step in range(len(self.orders[0])):
            for half in range(2):
                self.onward(half, 0, self.orders[half][step])
        for half in range(2):
            self.forward_core(half, 0)

    def run_gather(self, compute, scatter=None):
        self.begin()
        compute([0])
        levels = len(self.orders[0])
        self.arrive(1)
        compute([block_index(1, self.count)])
        if scatter is not None:
            self.send_core(1)
        for level in range(1, levels + 1):
            here = [k for k in self.outer if bin(k).count("1") == level]
            self.forward_level(here)
            if level == 2 and scatter is not None:
                next(scatter)
            compute([block_index(k, self.count) for k in here])
            for k in here:
                self.arrive(k | 1)
            compute([block_index(k | 1, self.count) for k in here])
            for k in here:
                if scatter is not None:
                    self.send_core(k | 1)

    def gather(self):
        self.begin()
        yield
        for level in range(1, len(self.orders[0]) + 1):
            self.forward_level([k for k in self.outer if bin(k).count("1") == level])
            yield
        for block in self.outer:
            self.arrive(block | 1)

    def forward_level(self, here):
        steps = [(half, k) for k in here for half in range(2)]
        steps.sort(
            key=lambda s: [
                self.orders[s[0]].index(bit) for bit in self.orders[s[0]] if s[1] & bit
            ][::-1]
        )
        for half, k in steps:
            self.coming[half, k].wait_recv()
            self.forward(half, k)
            self.forward_core(half, k)

    def send_core(self, block):
        place = self.place(block)
        target = self.arrived_core.at[block >> 1]
        self.slots["core", block & ~1] = self.links.start(self.partial.at[place], target, partner(1))

    def total(self, half, block, slots):
        rows = pl.ds(half * self.rows, self.rows)
        value = self.partial[self.place(block), rows].astype(wide)
        value = value + self.arrived_core[block >> 1, rows].astype(wide)
        for slot in slots:
            value = value + self.arrived_outer[half, slot].astype(wide)
        return value

    def scatter(self, finish):
        slot_of = {}
        waiting = {(half, k): [] for half in range(2) for k in self.outer}
        core_seen = set()
        left = [list(self.outer), list(self.outer)]
        for step in range(len(self.orders[0])):
            jobs = []
            for half in range(2):
                bit = self.orders[half][::-1][step]
                jobs.append([(half, bit, k) for k in left[half] if k & bit])
                left[half] = [k for k in left[half] if not k & bit]
            for pair in zip(*jobs, strict=True):
                for half, bit, k in pair:
                    if k not in core_seen:
                        self.slots["core", k].wait_recv()
                        core_seen.add(k)
                    for copy, _ in waiting[half, k]:
                        copy.wait_recv()
                    rows = pl.ds(half * self.rows, self.rows)
                    total = self.total(half, k, [slot for _, slot in waiting[half, k]])
                    self.partial[self.place(k), rows] = total.astype(narrow)
                    slot = slot_of.setdefault((half, bit, k ^ bit), len([1 for h, *_ in slot_of if h == half]))
                    copy = self.links.start(
                        self.partial.at[self.place(k), rows],
                        self.arrived_outer.at[half, slot],
                        partner(bit),
                    )
                    waiting[half, k ^ bit].append((copy, slot))
                yield
        if 0 not in core_seen:
            self.slots["core", 0].wait_recv()
        for half in range(2):
            for copy, _ in waiting[half, 0]:
                copy.wait_recv()
            finish(half, self.total(half, 0, [slot for _, slot in waiting[half, 0]]))


def plane_partners(count):
    return [partner(bit) for bit in outer_bits(count) + [1]]


def plane_copies(count):
    outer = count // 2
    return 2 * (outer - 1) + 2 * outer, outer + 2 * (outer - 1)


def spans(blocks):
    runs = []
    for block in sorted(blocks):
        if runs and runs[-1][1] == block:
            runs[-1][1] = block + 1
        else:
            runs.append([block, block + 1])
    return runs


def each(blocks, body):
    for first, end in spans(blocks):
        if end - first == 1:
            body(first)
        else:
            lax.fori_loop(first, end, lambda i, _: (body(i), 0)[1], 0)


def ffn_kernel(
    count, x, gate_up, down, lowered, plane_out, values_out, hidden_out,
    plane, partial, core, outer, values, hidden, send, arrive, local,
):
    links = Transfers(send, arrive)
    meet(plane_partners(count))
    units = down.shape[0]
    wide_block = 256
    plane[0] = x[...]
    saved = pltpu.make_async_copy(plane, plane_out, local.at[0])

    def compute(blocks):
        def one(place):
            for start in range(0, units, wide_block):
                columns = slice(start, start + wide_block)
                after = slice(units + start, units + start + wide_block)
                gate = dense(plane[place], gate_up[:, columns])
                up = dense(plane[place], gate_up[:, after])
                values[place, :, columns] = gate
                values[place, :, after] = up
                hidden[place, :, columns] = (jax.nn.silu(gate) * up).astype(narrow)
            partial[place] = dense(hidden[place], down[...]).astype(narrow)

        each(blocks, one)

    exchange = PlaneExchange(count, links, plane, partial, core, outer)
    def finish(half, total):
        lowered[pl.ds(half * exchange.rows, exchange.rows)] = total

    sums = exchange.scatter(finish)
    exchange.run_gather(compute, sums)
    saved.start()
    kept = pltpu.make_async_copy(values, values_out, local.at[1])
    kept.start()
    held = pltpu.make_async_copy(hidden, hidden_out, local.at[2])
    held.start()

    for _ in sums:
        pass
    saved.wait()
    kept.wait()
    held.wait()
    links.finish()


def plane_scratch(count, rows, width):
    outer = count // 2
    return [
        pltpu.VMEM((count, rows, width), narrow),
        pltpu.VMEM((count, rows, width), narrow),
        pltpu.VMEM((outer, rows, width), narrow),
        pltpu.VMEM((2, outer - 1, rows // 2, width), narrow),
    ]


def ffn_forward(count, x, gate_up, down):
    rows, width = x.shape
    units = down.shape[0]
    copies = sum(plane_copies(count))
    vmem, anywhere = pl.BlockSpec(memory_space=pltpu.VMEM), pl.BlockSpec(memory_space=pl.ANY)
    return pl.pallas_call(
        partial(ffn_kernel, count),
        in_specs=[vmem] * 3,
        out_specs=[vmem] + [anywhere] * 3,
        out_shape=[
            jax.ShapeDtypeStruct((rows, width), wide),
            jax.ShapeDtypeStruct((count, rows, width), narrow),
            jax.ShapeDtypeStruct((count, rows, 2 * units), wide),
            jax.ShapeDtypeStruct((count, rows, units), narrow),
        ],
        scratch_shapes=plane_scratch(count, rows, width)
        + [
            pltpu.VMEM((count, rows, 2 * units), wide),
            pltpu.VMEM((count, rows, units), narrow),
            pltpu.SemaphoreType.DMA((copies,)),
            pltpu.SemaphoreType.DMA((copies,)),
            pltpu.SemaphoreType.DMA((3,)),
        ],
        compiler_params=pltpu.CompilerParams(
            collective_id=1, has_side_effects=True, vmem_limit_bytes=60 * 2**20
        ),
        name="ffn_forward",
    )(x, gate_up, down)

def ffn_back_kernel(
    count, g, gate_up, down, values_in, x_in, hidden_in, grad_normed, grad_gate_up, grad_down,
    plane, partial, core, outer, values, grads, taken, send, arrive, local,
):
    links = Transfers(send, arrive)
    fetch = pltpu.make_async_copy(values_in, values, local.at[2])
    fetch.start()
    meet(plane_partners(count))
    units, width = down.shape
    wide_block = 256
    plane[0] = g[...]
    fetched = []

    def compute(places):
        if not fetched:
            fetch.wait()
            fetched.append(True)

        def one(place):
            for start in range(0, units, wide_block):
                columns = slice(start, start + wide_block)
                after = slice(units + start, units + start + wide_block)
                back = contract_cols(plane[place], down[columns])
                gate, up = values[place, :, columns], values[place, :, after]
                sigma = jax.nn.sigmoid(gate)
                grads[place, :, columns] = (
                    back * up * (sigma * (1.0 + gate * (1.0 - sigma)))
                ).astype(narrow)
                grads[place, :, after] = (back * (gate * sigma)).astype(narrow)
            partial[place] = contract_cols(grads[place], gate_up[...]).astype(narrow)

        each(places, one)

    exchange = PlaneExchange(count, links, plane, partial, core, outer)

    def finish(half, total):
        grad_normed[pl.ds(half * exchange.rows, exchange.rows)] = total

    sums = exchange.scatter(finish)
    exchange.run_gather(compute, sums)

    jobs = [(x_in, grads, grad_gate_up, i) for i in range(width // wide_block)]
    jobs += [(hidden_in, plane, grad_down, i) for i in range(units // wide_block)]

    def take(number):
        source, _, _, i = jobs[number]
        columns = pl.ds(i * wide_block, wide_block)
        return pltpu.make_async_copy(
            source.at[:, :, columns], taken.at[number % 2], local.at[number % 2]
        )

    def work(number):
        if number + 1 < len(jobs):
            take(number + 1).start()
        take(number).wait()
        _, upstream, out, i = jobs[number]
        for start in range(0, upstream.shape[2], 512):
            columns = slice(start, start + 512)
            out[i * wide_block : (i + 1) * wide_block, columns] = contract_rows(
                flat(taken[number % 2]), flat(upstream[:, :, columns])
            ).astype(narrow)

    take(0).start()
    done = 0
    for _ in sums:
        for number in range(done, min(done + 3, len(jobs))):
            work(number)
            done += 1
    for number in range(done, len(jobs)):
        work(number)
    links.finish()


class Late:
    def __init__(self, source, target, semaphore):
        self.copy = pltpu.make_async_copy(source, target, semaphore)
        self.target, self.there = target, False
        self.copy.start()

    def get(self):
        if not self.there:
            self.copy.wait()
            self.there = True
        return self.target


class GradientRing:
    def __init__(self, ring, own, held):
        self.ring, self.own, self.held = ring, own, held
        self.copies, self.pieces = [], {}

    def piece(self, which, step):
        place = self.ring.source(step + 1)
        return self.own[0].at[:, place] if which == 0 else self.own[1].at[place]

    def fetch(self, first, targets, semaphores):
        for slot in range(targets[0].shape[0]):
            for which in range(2):
                self.pieces[which, first + slot] = Late(
                    self.piece(which, first + slot),
                    targets[which].at[slot],
                    semaphores.at[2 * slot + which],
                )

    def first(self, landing):
        for which in range(2):
            self.copies.append(
                self.ring.links.start(self.piece(which, 0), landing[which], self.ring.right)
            )

    def arrived(self):
        for copy in self.copies:
            copy.wait_recv()
        self.copies = []

    def value(self, which, step):
        piece = self.pieces[which, step].get()
        return piece[...].astype(wide) + self.held[which][...].astype(wide)

    def onward(self, step, going, landing):
        self.arrived()
        for which in range(2):
            going[which][...] = self.value(which, step).astype(narrow)
            self.copies.append(
                self.ring.links.start(going[which], landing[which], self.ring.right)
            )
        self.held = landing


def ffn_backward(count, g, gate_up, down, values, x, hidden):
    rows, width = g.shape
    units = down.shape[0]
    copies = sum(plane_copies(count))
    vmem, anywhere = pl.BlockSpec(memory_space=pltpu.VMEM), pl.BlockSpec(memory_space=pl.ANY)
    return pl.pallas_call(
        partial(ffn_back_kernel, count),
        in_specs=[vmem] * 3 + [anywhere] * 3,
        out_specs=[vmem] * 3,
        out_shape=[
            jax.ShapeDtypeStruct((rows, width), wide),
            jax.ShapeDtypeStruct((width, 2 * units), narrow),
            jax.ShapeDtypeStruct((units, width), narrow),
        ],
        scratch_shapes=plane_scratch(count, rows, width)
        + [
            pltpu.VMEM((count, rows, 2 * units), wide),
            pltpu.VMEM((count, rows, 2 * units), narrow),
            pltpu.VMEM((2, count, rows, 256), narrow),
            pltpu.SemaphoreType.DMA((copies,)),
            pltpu.SemaphoreType.DMA((copies,)),
            pltpu.SemaphoreType.DMA((3,)),
        ],
        compiler_params=pltpu.CompilerParams(
            collective_id=2, has_side_effects=True, vmem_limit_bytes=62 * 2**20
        ),
        name="ffn_backward",
    )(g, gate_up, down, values, x, hidden)


def seq_device(index):
    return {"seq": index}


class Ring:
    def __init__(self, depth, links):
        self.depth, self.links = depth, links
        self.index = lax.axis_index("seq")
        self.right = seq_device(lax.rem(self.index + 1, depth))
        self.left = seq_device(lax.rem(self.index + depth - 1, depth))

    def source(self, step):
        return lax.rem(self.index - step + 2 * self.depth, self.depth)


def start_kernel(
    count, depth, clip, pieces, columns, shard, words, text, x, gain, text_gain,
    got, mods, projection, spread, pairs, text_own, normed, q, k, v, rates,
    product, back, stat, stat_in, partial, core, outer, send, arrive,
):
    links = Transfers(send, arrive)
    ring = Ring(depth, links)
    b, s = lax.axis_index("bucket"), lax.axis_index("seq")
    others = [partner(k) for k in range(1, count)]
    along = [seq_device(lax.rem(s + step, depth)) for step in range(1, depth)]
    meet(others + along)
    first = [
        links.start(pieces.at[jnp.bitwise_xor(b, k)], got.at[k], others[k - 1])
        for k in range(1, count)
    ]
    got[0] = pieces[b]
    feature, width = text.shape

    def features(target):
        return words.at[:, pl.ds(pl.multiple_of(target * feature, 128), feature)]

    projection[b] = shard[...]
    spread[b] = words[:, pl.ds(pl.multiple_of(b * feature, 128), feature)]
    for copy in first:
        copy.wait_recv()
    for block in range(count):
        product[block] = dense(got[block].astype(narrow), columns[...])
    second = [
        links.start(product.at[block], back.at[block - 1], others[block - 1])
        for block in range(1, count)
    ]
    far = {}
    for block in sorted(range(1, count), key=lambda block: (bin(block >> 1).count("1"), block & 1)):
        far[block] = links.start(
            features(jnp.bitwise_xor(b, block)), spread.at[b], others[block - 1]
        )
    shards = PlaneExchange(count, links, projection, natural=True).gather()
    next(shards)

    total = product[0]
    for i, copy in enumerate(second):
        copy.wait_recv()
        total = total + back[i]
    mods[s] = total
    third = [links.start(mods.at[s], mods.at[s], device) for device in along]
    for copy in third:
        copy.wait_recv()
    places = mods.shape[1]
    parts = []
    for i in range(depth // 4):
        part = jnp.zeros((1, mods.shape[2]), wide)
        for place in range(places):
            part = part + jnp.where(clip[0] == place, mods[i, place : place + 1], 0.0)
        parts.append(part)
    scale = parts[0] if len(parts) == 1 else jnp.concatenate(parts, axis=1)
    value = x[...].astype(wide)
    rate = lax.rsqrt(jnp.mean(value * value, axis=1, keepdims=True) + EPSILON)
    normed[s] = (value * rate * gain[...] * (1.0 + scale)).astype(narrow)
    moving = [links.start(normed.at[s], normed.at[s], ring.right)]

    exchange = PlaneExchange(count, links, None, partial, core, outer)

    def pair(block):
        if block:
            far[block].wait_recv()
        source = spread[jnp.bitwise_xor(b, block)]
        place = block_index(block, count)
        for start in range(0, width, 512):
            span = slice(start, start + 512)
            partial[place, :, span] = dense(source, text[:, span]).astype(narrow)
        if block & 1:
            exchange.send_core(block)

    def finish(half, total):
        pairs[pl.ds(half * exchange.rows, exchange.rows)] = total
        keys = total[:, : width // 2]
        rate = lax.rsqrt(jnp.mean(keys * keys, axis=1, keepdims=True) + EPSILON)
        kinds = (keys * rate * text_gain[...]).astype(narrow), total[:, width // 2 :].astype(narrow)
        cap_local, part = text_own.shape[3:]
        for kind, value in enumerate(kinds):
            for i in range(exchange.rows // cap_local):
                place = half * (exchange.rows // cap_local) + i
                rows = slice(i * cap_local, (i + 1) * cap_local)
                for target in range(depth):
                    text_own[target, kind, place] = value[
                        rows, target * part : (target + 1) * part
                    ]

    sums = exchange.scatter(finish)
    order = sorted(exchange.outer, key=lambda block: (bin(block).count("1"), block))
    order = order[1:] + order[:1]
    levels = len(exchange.orders[0])
    for block in order[:levels]:
        pair(block | 1)
        pair(block)
    next(sums)
    for block in order[levels:]:
        pair(block | 1)
        pair(block)
    next(sums)
    own = q.shape[2]

    def project(step):
        place = ring.source(step)
        for i, out in enumerate((q, k, v)):
            span = slice(i * own, (i + 1) * own)
            weight = projection[:, :, span]
            out[place] = dense(normed[place], flat(weight))

    def onward(step):
        moving[-1].wait_recv()
        place = ring.source(step)
        if step < depth - 1:
            moving.append(links.start(normed.at[place], normed.at[place], ring.right))

    onward(1)
    for _ in shards:
        pass
    project(0)
    project(1)
    for step in range(2, depth):
        if step == depth - 1:
            next(sums)
        onward(step)
        project(step)
    for i, raw in enumerate((q, k)):
        for block in range(depth):
            place = i * depth + block
            stat[place : place + 1] = row_sums(raw[block] * raw[block])
    stats = [links.start(stat, stat_in.at[i], device) for i, device in enumerate(along)]
    for _ in sums:
        pass
    squares = stat[...]
    for i, copy in enumerate(stats):
        copy.wait_recv()
        squares = squares + stat_in[i]
    rates[...] = lax.rsqrt(squares / (own * depth) + EPSILON)
    links.finish()


def start_exchange(
    count, depth, clip, pieces, columns, shard, words, text, x, gain, text_gain
):
    vmem = pl.BlockSpec(memory_space=pltpu.VMEM)
    rows, width = x.shape
    own = shard.shape[1] // 3
    cap_rows, pair_width = words.shape[0], text.shape[1]
    places, mod_width = pieces.shape[1], columns.shape[1]
    copies = sum(plane_copies(count)) + 3 * (count - 1) + 3 * (depth - 1)
    raw = jax.ShapeDtypeStruct((depth, rows, own), wide)
    return pl.pallas_call(
        partial(start_kernel, count, depth),
        in_specs=[scalar_spec()] + [vmem] * 8,
        out_specs=[vmem] * 11,
        out_shape=[
            jax.ShapeDtypeStruct(pieces.shape, wide),
            jax.ShapeDtypeStruct((depth, places, mod_width), wide),
            jax.ShapeDtypeStruct((count,) + shard.shape, narrow),
            jax.ShapeDtypeStruct((count, cap_rows, words.shape[1] // count), narrow),
            jax.ShapeDtypeStruct((cap_rows, pair_width), wide),
            jax.ShapeDtypeStruct((depth, 2, places, cap_rows // places, own), narrow),
            jax.ShapeDtypeStruct((depth, rows, width), narrow),
            raw,
            raw,
            raw,
            jax.ShapeDtypeStruct((2 * depth, rows), wide),
        ],
        scratch_shapes=[
            pltpu.VMEM((count, places, mod_width), wide),
            pltpu.VMEM((count - 1, places, mod_width), wide),
            pltpu.VMEM((2 * depth, rows), wide),
            pltpu.VMEM((depth - 1, 2 * depth, rows), wide),
        ]
        + plane_scratch(count, cap_rows, pair_width)[1:]
        + [pltpu.SemaphoreType.DMA((copies,)), pltpu.SemaphoreType.DMA((copies,))],
        compiler_params=pltpu.CompilerParams(
            collective_id=4, has_side_effects=True, vmem_limit_bytes=60 * 2**20
        ),
        name="start_exchange",
    )(clip, pieces, columns, shard, words, text, x, gain, text_gain)


def end_kernel(
    count, depth, pairs, text_hbm, words_hbm, grads_hbm, projection_hbm, grad_gate, grad_down,
    gate_held, down_held, normed, grad_words, grad_weight, gate_next, down_next,
    text, words, grads, projection, gate_piece, down_piece, local,
    plane, back, send_sum, ring_in, total, gate_go, down_go, send, arrive,
):
    links = Transfers(send, arrive)
    ring = Ring(depth, links)
    late = [
        Late(source, target, local.at[2 + i])
        for i, (source, target) in enumerate(
            zip(
                (text_hbm, words_hbm, grads_hbm, projection_hbm),
                (text, words, grads, projection),
                strict=True,
            )
        )
    ]
    weights = GradientRing(ring, (grad_gate, grad_down), (gate_held, down_held))
    weights.fetch(1, (gate_piece, down_piece), local)
    b = lax.axis_index("bucket")
    others = [partner(k) for k in range(1, count)]
    meet(others + [ring.left, ring.right])
    plane[0] = pairs[...]
    exchange = PlaneExchange(count, links, plane)
    feature, width = text.shape
    own_columns = pl.ds(pl.multiple_of(b * feature, 128), feature)
    moving = []

    def round_step(step):
        value = contract_cols(grads[ring.source(step + 1)], projection[...])
        if step > 0:
            moving[-1].wait_recv()
            value = value + ring_in[step - 1].astype(wide)
        if step < depth - 1:
            send_sum[step] = value.astype(narrow)
            moving.append(links.start(send_sum.at[step], ring_in.at[step], ring.right))
        else:
            normed[...] = value

    steps = [0]

    def advance():
        if steps[0] < depth - 1:
            round_step(steps[0])
            steps[0] += 1
            if steps[0] == depth - 1:
                weights.onward(1, (gate_go, down_go), (gate_next, down_next))

    arriving = []
    blocks = [None] * count
    for block in range(count):
        blocks[block_index(block, count)] = block

    def compute(places):
        for copy in late:
            copy.get()
        for place in places:
            block = blocks[place]
            features = words[jnp.bitwise_xor(b, block)].astype(wide).T.astype(narrow)
            for first in range(0, width, 512):
                columns = slice(first, first + 512)
                part = dense(features, plane[place, :, columns])
                if place == 0:
                    total[:, columns] = part
                else:
                    total[:, columns] += part
            value = contract_cols(plane[place], text[...]).astype(narrow)
            if block == 0:
                grad_words[:, own_columns] = value
            else:
                back[place - 1] = value
                arriving.append(
                    links.start(
                        back.at[place - 1], grad_words.at[:, own_columns], others[block - 1]
                    )
                )
        advance()

    exchange.run_gather(compute)
    while steps[0] < depth - 1:
        advance()
    round_step(depth - 1)
    grad_weight[...] = total[...].astype(narrow)
    for copy in arriving + weights.copies:
        copy.wait_recv()
    links.finish()


def end_exchange(count, depth, pairs, text, words, grads, projection, ffn_grads, held):
    vmem = pl.BlockSpec(memory_space=pltpu.VMEM)
    cap_rows, pair_width = pairs.shape
    feature = text.shape[0]
    rows, width = grads.shape[1], projection.shape[0]
    copies = plane_copies(count)[0] + count - 1 + depth - 1 + 2
    return pl.pallas_call(
        partial(end_kernel, count, depth),
        in_specs=[vmem] + [pl.BlockSpec(memory_space=pl.ANY)] * 6 + [vmem] * 2,
        out_specs=[vmem] * 5,
        out_shape=[
            jax.ShapeDtypeStruct((rows, width), wide),
            jax.ShapeDtypeStruct((cap_rows, count * feature), narrow),
            jax.ShapeDtypeStruct((feature, pair_width), narrow),
            jax.ShapeDtypeStruct(held[0].shape, narrow),
            jax.ShapeDtypeStruct(held[1].shape, narrow),
        ],
        scratch_shapes=[
            pltpu.VMEM(text.shape, narrow),
            pltpu.VMEM(words.shape, narrow),
            pltpu.VMEM(grads.shape, narrow),
            pltpu.VMEM(projection.shape, narrow),
            pltpu.VMEM((1,) + held[0].shape, narrow),
            pltpu.VMEM((1,) + held[1].shape, narrow),
            pltpu.SemaphoreType.DMA((6,)),
            pltpu.VMEM((count, cap_rows, pair_width), narrow),
            pltpu.VMEM((count - 1, cap_rows, feature), narrow),
            pltpu.VMEM((depth - 1, rows, width), narrow),
            pltpu.VMEM((depth - 1, rows, width), narrow),
            pltpu.VMEM((feature, pair_width), wide),
            pltpu.VMEM(held[0].shape, narrow),
            pltpu.VMEM(held[1].shape, narrow),
            pltpu.SemaphoreType.DMA((copies,)),
            pltpu.SemaphoreType.DMA((copies,)),
        ],
        compiler_params=pltpu.CompilerParams(
            collective_id=5, has_side_effects=True, vmem_limit_bytes=63 * 2**20
        ),
        name="end_exchange",
    )(pairs, text, words, grads, projection, *ffn_grads, *held)


def sum_kernel(
    count, depth, flags, text, combined, upstream, normed_hbm, grads_hbm, grad_gate, grad_down,
    gate_held, down_held, words_hbm, row, small, down_share, text_share, output_share, proj_share, gate_share, null_share, rows_out, small_out,
    normed, grads, words, gate_piece, down_piece, local, out_part, out_core, out_outer, proj_part, proj_core, proj_outer, send_low, low_in, out_go,
    out_come, proj_go, proj_come, gate, gate_come, null, null_come, small_come, small_go,
    small_land, gate_go, down_go, gate_land, down_land, send, arrive,
):
    links = Transfers(send, arrive)
    ring = Ring(depth, links)
    late = [
        Late(source, target, local.at[i])
        for i, (source, target) in enumerate(
            zip((normed_hbm, grads_hbm, words_hbm), (normed, grads, words), strict=True)
        )
    ]
    weights = GradientRing(ring, (grad_gate, grad_down), (gate_held, down_held))
    weights.fetch(2, (gate_piece, down_piece), local.at[pl.ds(3, 2 * (depth - 2))])
    b, s = lax.axis_index("bucket"), lax.axis_index("seq")
    others = [partner(k) for k in range(1, count)]
    turns = [lax.rem(s + step, depth) for step in range(1, depth)]
    along = [seq_device(place) for place in turns]
    meet(others + along)

    rows_out[0, s] = row[...]
    tiny = []
    for i, (place, device) in enumerate(zip(turns, along, strict=True)):
        tiny.append(links.start(row, rows_out.at[0, s], device))
        tiny.append(links.start(small.at[place], small_come.at[i], device))

    low_rows = text.shape[0] // depth
    going = []

    def text_step(step):
        rows = pl.ds(pl.multiple_of(ring.source(step + 1) * low_rows, 16), low_rows)
        value = text[rows].astype(wide)
        if step > 0:
            going[-1].wait_recv()
            value = value + low_in[step - 1].astype(wide)
        if step < depth - 1:
            send_low[step] = value.astype(narrow)
            going.append(links.start(send_low.at[step], low_in.at[step], ring.right))
        else:
            text_share[...] = value

    def weights_step(step):
        slot = step - 2
        weights.onward(
            step,
            (gate_go.at[slot], down_go.at[slot]),
            (gate_land.at[slot], down_land.at[slot]),
        )

    text_step(0)
    weights_step(2)

    share = out_go.shape[1]
    pair = 2 * out_part.shape[1]

    def fill(part, leading, trailing):
        for first in range(0, count, 2):
            value = contract_rows(leading[:, first // 2 * pair : (first // 2 + 1) * pair], trailing)
            value = value.astype(narrow)
            part[first] = value[: pair // 2]
            part[first + 1] = value[pair // 2 :]

    def plane_sum(part, core, outer, go):
        exchange = PlaneExchange(count, links, None, part, core, outer, natural=True)
        for block in range(1, count, 2):
            exchange.send_core(block)

        def finish(half, total):
            low = total.astype(narrow)
            for i in range(depth // 2):
                go[half * (depth // 2) + i] = low[i * share : (i + 1) * share]

        return exchange.scatter(finish)

    fill(out_part, combined[...], upstream[...])
    out_sums = plane_sum(out_part, out_core, out_outer, out_go)
    for copy in late:
        copy.get()
    fill(proj_part, flat(normed[...]), flat(grads[...]))
    proj_sums = plane_sum(proj_part, proj_core, proj_outer, proj_go)
    for _ in range(count // 4):
        next(out_sums)
    for _ in range(count // 4):
        next(proj_sums)
    text_step(1)

    places = flags.shape[0]
    cap_local = words.shape[0] // places
    null_rows = null.shape[1]
    for k in range(count):
        value = jnp.zeros((null_rows, words.shape[1]), wide)
        for place in range(places):
            first = place * cap_local + k * null_rows
            part = words[first : first + null_rows].astype(wide)
            value = value + jnp.where(flags[place] == 1, part, 0.0)
        null[k] = value
    next(out_sums)
    next(proj_sums)
    nulls = [
        links.start(null.at[jnp.bitwise_xor(b, k)], null_come.at[k - 1], others[k - 1])
        for k in range(1, count)
    ]

    def drain(sums):
        for _ in sums:
            pass

    def seq_sends(go, come):
        come[s] = go[s]
        return [
            links.start(go.at[place], come.at[s], device)
            for place, device in zip(turns, along, strict=True)
        ]

    for step in range(3, depth - 1):
        weights_step(step)
    weights.arrived()
    gate[...] = weights.value(0, depth - 1).astype(narrow)
    far = [
        links.start(gate.at[jnp.bitwise_xor(b, k)], gate_come.at[b], others[k - 1])
        for k in range(1, count)
    ]
    gate_come[b] = gate[b]
    down_share[...] = weights.value(1, depth - 1)
    own_small = small[s]
    for copy in tiny:
        copy.wait_recv()
    for i in range(depth - 1):
        own_small = own_small + small_come[i]
    small_go[...] = own_small
    spread = []
    for k in range(1, count):
        spread.append(links.start(rows_out.at[0], rows_out.at[k], others[k - 1]))
        spread.append(
            links.start(
                small_go.at[jnp.bitwise_xor(b, k)], small_land.at[k - 1], others[k - 1]
            )
        )
    drain(out_sums)
    out_far = seq_sends(out_go, out_come)
    drain(proj_sums)
    proj_far = seq_sends(proj_go, proj_come)
    for step in range(2, depth - 1):
        text_step(step)
    total = null[b]
    for i, copy in enumerate(nulls):
        copy.wait_recv()
        total = total + null_come[i]
    null_share[...] = total
    for copy in spread:
        copy.wait_recv()
    sums = small_go[b]
    for i in range(count - 1):
        sums = sums + small_land[i]
    small_out[...] = sums
    for copy in far:
        copy.wait_recv()
    units = gate.shape[2] // 2
    for block in range(count):
        for half in range(2):
            first = half * count * units + block * units
            gate_share[:, first : first + units] = gate_come[
                block, :, half * units : (half + 1) * units
            ].astype(wide)
    for copy in out_far + proj_far:
        copy.wait_recv()
    text_step(depth - 1)
    total = out_come[0].astype(wide)
    for i in range(1, depth):
        total = total + out_come[i].astype(wide)
    output_share[...] = total
    own = proj_come.shape[2] // 3
    for i in range(3):
        for source in range(depth):
            first = i * depth * own + source * own
            proj_share[:, first : first + own] = proj_come[
                source, :, i * own : (i + 1) * own
            ].astype(wide)
    links.finish()


def final_sums(
    count, depth, flags, text, combined, upstream, normed, grads, ffn_grads, held, words, row, small
):
    vmem = pl.BlockSpec(memory_space=pltpu.VMEM)
    feature, pair_width = text.shape
    width = combined.shape[1]
    own3 = grads.shape[2]
    share = width // (count * depth)
    null_rows = words.shape[0] // flags.shape[0] // count
    text_width = words.shape[1]
    outer = count // 2
    block_rows = width // count
    quarter = (depth - 1, feature // depth, pair_width)

    def plane_sums(columns):
        return [
            pltpu.VMEM((count, block_rows, columns), narrow),
            pltpu.VMEM((outer, block_rows, columns), narrow),
            pltpu.VMEM((2, outer - 1, block_rows // 2, columns), narrow),
        ]

    copies = 2 * (depth - 1) + depth - 1 + 2 * plane_copies(count)[1] + 4 * (count - 1)
    copies += 2 * (depth - 1) + 2 * (depth - 3)
    gate, down = held
    gates = pltpu.VMEM(gate.shape, narrow)
    anywhere = pl.BlockSpec(memory_space=pl.ANY)
    return pl.pallas_call(
        partial(sum_kernel, count, depth),
        in_specs=[scalar_spec()]
        + [vmem] * 3
        + [anywhere] * 4
        + [vmem] * 2
        + [anywhere]
        + [vmem] * 2,
        out_specs=[vmem] * 8,
        out_shape=[
            jax.ShapeDtypeStruct(down.shape, wide),
            jax.ShapeDtypeStruct((feature // depth, pair_width), wide),
            jax.ShapeDtypeStruct((share, width), wide),
            jax.ShapeDtypeStruct((share, depth * own3), wide),
            jax.ShapeDtypeStruct((share, count * gate.shape[2]), wide),
            jax.ShapeDtypeStruct((null_rows, text_width), wide),
            jax.ShapeDtypeStruct((count, depth) + row.shape, wide),
            jax.ShapeDtypeStruct(small.shape[2:], wide),
        ],
        scratch_shapes=[
            pltpu.VMEM(normed.shape, narrow),
            pltpu.VMEM(grads.shape, narrow),
            pltpu.VMEM(words.shape, narrow),
            pltpu.VMEM((depth - 2,) + gate.shape, narrow),
            pltpu.VMEM((depth - 2,) + down.shape, narrow),
            pltpu.SemaphoreType.DMA((3 + 2 * (depth - 2),)),
        ]
        + plane_sums(width)
        + plane_sums(own3)
        + [
            pltpu.VMEM(quarter, narrow),
            pltpu.VMEM(quarter, narrow),
            pltpu.VMEM((depth, share, width), narrow),
            pltpu.VMEM((depth, share, width), narrow),
            pltpu.VMEM((depth, share, own3), narrow),
            pltpu.VMEM((depth, share, own3), narrow),
            gates,
            gates,
            pltpu.VMEM((count, null_rows, text_width), wide),
            pltpu.VMEM((count - 1, null_rows, text_width), wide),
            pltpu.VMEM((depth - 1,) + small.shape[1:], wide),
            pltpu.VMEM(small.shape[1:], wide),
            pltpu.VMEM((count - 1,) + small.shape[2:], wide),
            pltpu.VMEM((depth - 3,) + gate.shape, narrow),
            pltpu.VMEM((depth - 3,) + down.shape, narrow),
            pltpu.VMEM((depth - 3,) + gate.shape, narrow),
            pltpu.VMEM((depth - 3,) + down.shape, narrow),
            pltpu.SemaphoreType.DMA((copies,)),
            pltpu.SemaphoreType.DMA((copies,)),
        ],
        compiler_params=pltpu.CompilerParams(
            collective_id=10, has_side_effects=True, vmem_limit_bytes=60 * 2**20
        ),
        name="final_sums",
    )(flags, text, combined, upstream, normed, grads, *ffn_grads, *held, words, row, small)


def head_lanes(values, head, size):
    lane = lax.broadcasted_iota(jnp.int32, values.shape, 1)
    return jnp.where((lane >= head * size) & (lane < (head + 1) * size), values, 0)


def swap_halves(values, size):
    half = size // 2
    lanes = values.shape[1]
    if lanes % 128 == 0:
        lane = lax.broadcasted_iota(jnp.int32, values.shape, 1)
        ahead = pltpu.roll(values, lanes - half, 1)
        behind = pltpu.roll(values, half, 1)
        return jnp.where(lax.rem(lane, size) < half, ahead, behind)
    parts = []
    for start in range(0, lanes, size):
        parts.append(values[:, start + half : start + size])
        parts.append(values[:, start : start + half])
    return jnp.concatenate(parts, axis=1)


def turn(values, cosine, signed_sine, size):
    return values * cosine + swap_halves(values, size) * signed_sine


def flat(values):
    return values.reshape(-1, values.shape[-1])


def scalar_spec():
    return pl.BlockSpec(memory_space=pltpu.SMEM)


def row_sums(values):
    ones = jnp.ones((8, values.shape[1]), wide)
    return lax.dot_general(
        ones, values, (((1,), (1,)), ((), ())), precision=HIGHEST, preferred_element_type=wide
    )[:1]


def loop(count, body):
    if count == 1:
        body(0)
    else:
        lax.fori_loop(0, count, lambda i, _: (body(i), 0)[1], 0)


def lane_block(index, lanes):
    if isinstance(index, int):
        return pl.ds(index * lanes, lanes)
    return pl.ds(pl.multiple_of(index * lanes, 128), lanes)


def block_rows_of(index, rows):
    if isinstance(index, int):
        return pl.ds(index * rows, rows)
    return pl.ds(pl.multiple_of(index * rows, 128), rows)


def forward_kernel(
    count, depth, size, lanes, spans, lengths, gates, raw_q, raw_k, raw_v, rates, gain_q, gain_k,
    cosine, sine, text_own, gate_up, combined, q, k, v, qc, total, cross_total, text, gathered,
    self_out, staged, send, arrive, local,
):
    links = Transfers(send, arrive)
    b, s = lax.axis_index("bucket"), lax.axis_index("seq")
    others = [partner(k) for k in range(1, count)]
    turns = [lax.rem(s + step, depth) for step in range(1, depth)]
    along = [seq_device(place) for place in turns]
    meet(others + along)
    block_rows, own = raw_q.shape[1:]
    rows = depth * block_rows
    width = own * depth
    grid, heads = own // lanes, lanes // size
    scaling = size ** (-0.5)
    words = [
        links.start(text_own.at[place], text.at[s], device)
        for place, device in zip(turns, along, strict=True)
    ]
    text[s] = text_own[s]
    gate_rows, units = gate_up.shape[0], gathered.shape[1] // 2
    half_width = gate_up.shape[1] // 2
    here = pl.ds(pl.multiple_of(b * gate_rows, 16), gate_rows)
    weights, kept = [], []
    for block in range(count):
        target = jnp.bitwise_xor(b, block)
        for half in range(2):
            source = gate_up.at[
                :, pl.ds(pl.multiple_of(half * half_width + target * units, 128), units)
            ]
            landing = gathered.at[here, pl.ds(half * units, units)]
            if block:
                weights.append(links.start(source, landing, others[block - 1]))
            else:
                copy = pltpu.make_async_copy(source, landing, local.at[half])
                copy.start()
                kept.append(copy)
    for block in range(depth):
        v[block_rows_of(block, block_rows)] = raw_v[block].astype(narrow)
    columns = rates[...].T
    for block in range(depth):
        at = block_rows_of(block, block_rows)
        cos, sin = cosine[at], sine[at]
        for group in range(grid):
            span = lane_block(group, lanes)
            norm_q = raw_q[block, :, span] * columns[:, block : block + 1] * gain_q[:, span]
            norm_k = (
                raw_k[block, :, span]
                * columns[:, depth + block : depth + block + 1]
                * gain_k[:, span]
            )
            turned = turn(norm_q, cos, sin, size).astype(narrow).astype(wide)
            q[at, span] = (turned * scaling).astype(narrow)
            qc[at, span] = (norm_q.astype(narrow).astype(wide) * scaling).astype(narrow)
            k[at, span] = turn(norm_k, cos, sin, size).astype(narrow)
    key_index = lax.broadcasted_iota(jnp.int32, (rows, block_rows), 0)

    def attend_self(group):
        span = lane_block(group, lanes)
        value_t = v[:, span].astype(wide).T.astype(narrow)
        for block in range(depth):
            at = block_rows_of(block, block_rows)
            allowed = (key_index >= spans[0, block]) & (key_index < spans[1, block])
            outs = []
            for head in range(heads):
                scores = contract_cols(k[:, span], head_lanes(q[at, span], head, size))
                scores = jnp.where(allowed, scores, NEGATIVE)
                peak = jnp.max(scores, axis=0, keepdims=True)
                shares = jnp.exp(scores - peak)
                mass = jnp.sum(shares, axis=0, keepdims=True)
                part = slice(head * size, (head + 1) * size)
                outs.append(dense(value_t[part], shares.astype(narrow)) / mass)
                total[group, head : head + 1, at] = peak + jnp.log(mass)
            self_out[at, span] = jnp.concatenate(outs, axis=0).T

    loop(grid, attend_self)
    for copy in words:
        copy.wait_recv()
    cap = text.shape[0] * text.shape[3]
    cap_index = lax.broadcasted_iota(jnp.int32, (cap, block_rows), 0)
    results = []
    for step in range(depth):
        block = lax.rem(s + 1 + step, depth)
        at = block_rows_of(block, block_rows)
        clip = spans[2, block]
        live = cap_index < lengths[clip]

        def attend_cross(group):
            span = lane_block(group, lanes)
            text_key = flat(text[:, 0, clip, :, span])
            value_t = flat(text[:, 1, clip, :, span]).astype(wide).T.astype(narrow)
            outs = []
            for head in range(heads):
                scores = contract_cols(text_key, head_lanes(qc[at, span], head, size))
                scores = jnp.where(live, scores, NEGATIVE)
                peak = jnp.max(scores, axis=0, keepdims=True)
                shares = jnp.exp(scores - peak)
                mass = jnp.sum(shares, axis=0, keepdims=True)
                part = slice(head * size, (head + 1) * size)
                gate = gates[group * heads + head]
                outs.append(dense(value_t[part], shares.astype(narrow)) * (gate / mass))
                cross_total[group, head : head + 1, at] = peak + jnp.log(mass)
            staged[step, :, span] = (
                self_out[at, span] + jnp.concatenate(outs, axis=0).T
            ).astype(narrow)

        loop(grid, attend_cross)
        if step < depth - 1:
            results.append(links.start(staged.at[step], combined.at[s], along[step]))
        else:
            combined[s] = staged[step]
    for copy in results + weights:
        copy.wait_recv()
    for copy in kept:
        copy.wait()
    links.finish()


def attention_forward(
    count, depth, size, lanes, scalars, raws, rates, gains, angles, text_own, gate_up
):
    block_rows, own = raws[0].shape[1:]
    rows = depth * block_rows
    grid, heads = own // lanes, lanes // size
    vmem, anywhere = pl.BlockSpec(memory_space=pltpu.VMEM), pl.BlockSpec(memory_space=pl.ANY)
    units = gate_up.shape[1] // (2 * count)
    copies = 2 * (depth - 1) + 2 * (count - 1)
    row_block = jax.ShapeDtypeStruct((rows, own), narrow)
    totals = jax.ShapeDtypeStruct((grid, heads, rows), wide)
    return pl.pallas_call(
        partial(forward_kernel, count, depth, size, lanes),
        in_specs=[scalar_spec()] * 3 + [vmem] * 9 + [anywhere],
        out_specs=[vmem] * 9,
        out_shape=[
            jax.ShapeDtypeStruct((depth, block_rows, own), narrow),
            row_block,
            row_block,
            row_block,
            row_block,
            totals,
            totals,
            jax.ShapeDtypeStruct(text_own.shape, narrow),
            jax.ShapeDtypeStruct((count * gate_up.shape[0], 2 * units), narrow),
        ],
        scratch_shapes=[
            pltpu.VMEM((rows, own), wide),
            pltpu.VMEM((depth, block_rows, own), narrow),
            pltpu.SemaphoreType.DMA((copies,)),
            pltpu.SemaphoreType.DMA((copies,)),
            pltpu.SemaphoreType.DMA((2,)),
        ],
        compiler_params=pltpu.CompilerParams(
            collective_id=8, has_side_effects=True, vmem_limit_bytes=60 * 2**20
        ),
        name="attention_forward",
    )(*scalars, *raws, rates, *gains, *angles, text_own, gate_up)


def backward_kernel(
    count, depth, size, lanes, spans, lengths, gates, upstream, weight, q, k_hbm, v_hbm, qc, raw_q_hbm,
    raw_k_hbm, rates, gain_q, gain_k, cosine, sine, text, total, cross_total, small, text_gain, text_pairs,
    grad_gate, grad_down,
    projected, gain_sums, dgate, grad_pairs, text_gain_sum, small_out, gate_held, down_held,
    k, v, raw_q, raw_k, cosine_in, sine_in, pairs_in, local, grad_text, go, send_go, dqc, back_q, back_k, parts, send_text, stat,
    stat_in, sum_k, sum_v, send, arrive,
):
    links = Transfers(send, arrive)
    s = lax.axis_index("seq")
    others = [partner(k) for k in range(1, count)]
    turns = [lax.rem(s + step, depth) for step in range(1, depth)]
    along = [seq_device(place) for place in turns]
    late = [
        Late(source, target, local.at[i])
        for i, (source, target) in enumerate(
            zip(
                (k_hbm, v_hbm, raw_q_hbm, raw_k_hbm, cosine, sine, text_pairs),
                (k, v, raw_q, raw_k, cosine_in, sine_in, pairs_in),
                strict=True,
            )
        )
    ]
    cosine, sine = cosine_in, sine_in
    meet(others + along)
    block_rows, own = upstream.shape[0], q.shape[1]
    rows = depth * block_rows
    width = own * depth
    grid, heads = own // lanes, lanes // size
    scaling = size ** (-0.5)

    small_out[0, s] = small[...]
    smalls = [links.start(small, small_out.at[0, s], device) for device in along]

    def grad_out(place):
        at = pl.ds(pl.multiple_of(place * own, 64), own)
        return contract_cols(upstream[...], weight[at]).astype(narrow)

    arriving = []
    for i, (place, device) in enumerate(zip(turns, along, strict=True)):
        send_go[i] = grad_out(place)
        arriving.append(links.start(send_go.at[i], go.at[s], device))
    go[s] = grad_out(s)
    ring = Ring(depth, links)
    weights = GradientRing(ring, (grad_gate, grad_down), None)

    cap_local = text.shape[3]
    cap = text.shape[0] * cap_local
    places = text.shape[2]
    cap_index = lax.broadcasted_iota(jnp.int32, (cap, block_rows), 0)
    clips = []
    for step in range(depth):
        block = lax.rem(s - step + depth, depth)
        if step:
            arriving[step - 1].wait_recv()
        if step == depth - 1:
            weights.first((gate_held, down_held))
        at = block_rows_of(block, block_rows)
        clip = spans[2, block]
        clips.append(clip)
        live = cap_index < lengths[clip]

        def back_cross(group):
            span = lane_block(group, lanes)
            text_key = flat(text[:, 0, clip, :, span])
            text_value = flat(text[:, 1, clip, :, span])
            key_t = text_key.astype(wide).T.astype(narrow)
            grads = []
            for head in range(heads):
                gate = gates[group * heads + head]
                query = head_lanes(qc[at, span], head, size)
                grad = head_lanes(go[block, :, span], head, size)
                scores = contract_cols(text_key, query)
                scores = jnp.where(live, scores, NEGATIVE)
                shares = jnp.exp(scores - cross_total[group, head : head + 1, at])
                grad_shares = contract_cols(text_value, grad)
                row = jnp.sum(grad_shares * shares, axis=0, keepdims=True)
                grad_scores = (gate * (shares * (grad_shares - row))).astype(narrow)
                grad_key = dense(grad_scores, query)
                grad_value = gate * dense(shares.astype(narrow), grad)
                if head == 0:
                    parts[step, 0, :, span] = grad_key
                    parts[step, 1, :, span] = grad_value
                else:
                    parts[step, 0, :, span] += grad_key
                    parts[step, 1, :, span] += grad_value
                part = slice(head * size, (head + 1) * size)
                grads.append(dense(key_t[part], grad_scores) * scaling)
                if step == 0:
                    dgate[group, head : head + 1] = row
                else:
                    dgate[group, head : head + 1] += row
            dqc[at, span] = jnp.concatenate(grads, axis=0).T

        loop(grid, back_cross)
    for which in range(2):
        for place in range(places):
            for target in range(depth):
                at = pl.ds(target * cap_local, cap_local)
                value = jnp.zeros((cap_local, own), wide)
                for step in range(depth):
                    value = value + jnp.where(
                        clips[step] == place, parts[step, which, at], 0.0
                    )
                send_text[target, which, place] = value.astype(narrow)
    words = [
        links.start(send_text.at[place], grad_text.at[s], device)
        for place, device in zip(turns, along, strict=True)
    ]
    grad_text[s] = send_text[s]
    for copy in smalls:
        copy.wait_recv()
    spread = [links.start(small_out.at[0], small_out.at[k], others[k - 1]) for k in range(1, count)]

    for copy in late:
        copy.get()
    key_index = lax.broadcasted_iota(jnp.int32, (rows, block_rows), 0)

    def back_self(group):
        span = lane_block(group, lanes)
        key_t = k[:, span].astype(wide).T.astype(narrow)
        for block in range(depth):
            at = block_rows_of(block, block_rows)
            allowed = (key_index >= spans[0, block]) & (key_index < spans[1, block])
            grads = []
            for head in range(heads):
                query = head_lanes(q[at, span], head, size)
                grad = head_lanes(go[block, :, span], head, size)
                scores = contract_cols(k[:, span], query)
                scores = jnp.where(allowed, scores, NEGATIVE)
                shares = jnp.exp(scores - total[group, head : head + 1, at])
                grad_shares = contract_cols(v[:, span], grad)
                row = jnp.sum(grad_shares * shares, axis=0, keepdims=True)
                grad_scores = (shares * (grad_shares - row)).astype(narrow)
                if block == 0 and head == 0:
                    sum_v[...] = dense(shares.astype(narrow), grad)
                    sum_k[...] = dense(grad_scores, query)
                else:
                    sum_v[...] += dense(shares.astype(narrow), grad)
                    sum_k[...] += dense(grad_scores, query)
                part = slice(head * size, (head + 1) * size)
                grads.append(dense(key_t[part], grad_scores) * scaling)
            back = jnp.concatenate(grads, axis=0).T
            back_q[at, span] = turn(back, cosine[at], -sine[at], size) + dqc[at, span]
        back_k[:, span] = turn(sum_k[...], cosine[...], -sine[...], size)
        for block in range(depth):
            at = block_rows_of(block, block_rows)
            if isinstance(group, int):
                to = pl.ds(2 * own + group * lanes, lanes)
            else:
                to = pl.ds(pl.multiple_of(2 * own + group * lanes, 128), lanes)
            projected[block, :, to] = sum_v[at].astype(narrow)

    loop(grid, back_self)
    columns = rates[...].T
    pairs = ((raw_q, back_q, gain_q), (raw_k, back_k, gain_k))
    for i, (raw, back, gain) in enumerate(pairs):
        gains = jnp.zeros((1, own), wide)
        for block in range(depth):
            place = i * depth + block
            at = block_rows_of(block, block_rows)
            hat = raw[block] * columns[:, place : place + 1]
            gains = gains + jnp.sum(back[at] * hat, axis=0, keepdims=True)
            stat[place : place + 1] = row_sums(back[at] * gain[...] * hat)
        gain_sums[i : i + 1] = gains
    stats = [links.start(stat, stat_in.at[i], device) for i, device in enumerate(along)]
    means = stat[...]
    for i, copy in enumerate(stats):
        copy.wait_recv()
        means = means + stat_in[i]
    means = (means / width).T
    for i, (raw, back, gain) in enumerate(pairs):
        for block in range(depth):
            place = slice(i * depth + block, i * depth + block + 1)
            at = block_rows_of(block, block_rows)
            rate = columns[:, place]
            hat = raw[block] * rate
            projected[block, :, i * own : (i + 1) * own] = (
                rate * (back[at] * gain[...] - hat * means[:, place])
            ).astype(narrow)
    for copy in words:
        copy.wait_recv()

    for target in range(depth):
        text_gain_sum[:, target * own : (target + 1) * own] = jnp.zeros((1, own), wide)
    for place in range(places):
        at = slice(place * cap_local, (place + 1) * cap_local)
        keys = pairs_in[at, :width]
        rate = lax.rsqrt(jnp.mean(keys * keys, axis=1, keepdims=True) + EPSILON)
        mean = jnp.zeros((cap_local, 1), wide)
        for target in range(depth):
            span = slice(target * own, (target + 1) * own)
            hat = pairs_in[at, span] * rate
            grad = grad_text[target, 0, place].astype(wide)
            mean = mean + jnp.sum(grad * text_gain[:, span] * hat, axis=1, keepdims=True)
            text_gain_sum[:, span] += jnp.sum(grad * hat, axis=0, keepdims=True)
        mean = mean / width
        for target in range(depth):
            span = slice(target * own, (target + 1) * own)
            hat = pairs_in[at, span] * rate
            grad = grad_text[target, 0, place].astype(wide)
            grad_pairs[at, span] = (rate * (grad * text_gain[:, span] - hat * mean)).astype(narrow)
            after = slice(width + target * own, width + (target + 1) * own)
            grad_pairs[at, after] = grad_text[target, 1, place]
    for copy in spread + weights.copies:
        copy.wait_recv()
    links.finish()


def attention_backward(
    count, depth, size, lanes, scalars, upstream, weight, saved, raws, rates, gains, angles, text,
    totals, small, text_gain, text_pairs, ffn_grads,
):
    block_rows, own = raws[0].shape[1:]
    rows = depth * block_rows
    grid, heads = own // lanes, lanes // size
    vmem = pl.BlockSpec(memory_space=pltpu.VMEM)
    copies = 4 * (depth - 1) + count - 1 + 2
    cap = text.shape[0] * text.shape[3]
    args = (*scalars, upstream, weight, *saved, *raws, rates, *gains, *angles, text, *totals, small)
    args = args + (text_gain, text_pairs) + tuple(ffn_grads)
    anywhere = pl.BlockSpec(memory_space=pl.ANY)
    specs = [scalar_spec()] * 3 + [vmem] * (len(args) - 3)
    for i in (6, 7, 9, 10, 14, 15, len(args) - 3, len(args) - 2, len(args) - 1):
        specs[i] = anywhere
    return pl.pallas_call(
        partial(backward_kernel, count, depth, size, lanes),
        in_specs=specs,
        out_specs=[vmem] * 8,
        out_shape=[
            jax.ShapeDtypeStruct((depth, block_rows, 3 * own), narrow),
            jax.ShapeDtypeStruct((2, own), wide),
            jax.ShapeDtypeStruct((grid, heads, block_rows), wide),
            jax.ShapeDtypeStruct(text_pairs.shape, narrow),
            jax.ShapeDtypeStruct((1, own * depth), wide),
            jax.ShapeDtypeStruct((count, depth) + small.shape, wide),
            jax.ShapeDtypeStruct(ffn_grads[0].shape[:1] + ffn_grads[0].shape[2:], narrow),
            jax.ShapeDtypeStruct(ffn_grads[1].shape[1:], narrow),
        ],
        scratch_shapes=[
            pltpu.VMEM((rows, own), narrow),
            pltpu.VMEM((rows, own), narrow),
            pltpu.VMEM(raws[0].shape, wide),
            pltpu.VMEM(raws[1].shape, wide),
            pltpu.VMEM(angles[0].shape, wide),
            pltpu.VMEM(angles[1].shape, wide),
            pltpu.VMEM(text_pairs.shape, wide),
            pltpu.SemaphoreType.DMA((7,)),
            pltpu.VMEM(text.shape, narrow),
            pltpu.VMEM((depth, block_rows, own), narrow),
            pltpu.VMEM((depth - 1, block_rows, own), narrow),
            pltpu.VMEM((rows, own), wide),
            pltpu.VMEM((rows, own), wide),
            pltpu.VMEM((rows, own), wide),
            pltpu.VMEM((depth, 2, cap, own), wide),
            pltpu.VMEM(text.shape, narrow),
            pltpu.VMEM((2 * depth, block_rows), wide),
            pltpu.VMEM((depth - 1, 2 * depth, block_rows), wide),
            pltpu.VMEM((rows, lanes), wide),
            pltpu.VMEM((rows, lanes), wide),
            pltpu.SemaphoreType.DMA((copies,)),
            pltpu.SemaphoreType.DMA((copies,)),
        ],
        compiler_params=pltpu.CompilerParams(
            collective_id=9, has_side_effects=True, vmem_limit_bytes=60 * 2**20
        ),
        name="attention_backward",
    )(*args)


def per_device(
    tokens,
    condition,
    captions,
    caption_lengths,
    null_flags,
    slot_buckets,
    null_caption,
    modulation,
    projection,
    text_weight,
    output_weight,
    gate_up,
    down_weight,
    norm_gains,
    head_gains,
    cross_gates,
    cotangent,
):
    count_s, count_b = lax.axis_size("seq"), lax.axis_size("bucket")
    s, b = lax.axis_index("seq"), lax.axis_index("bucket")
    assert count_s % 4 == 0
    local, width = tokens.shape
    heads = cross_gates.shape[0]
    size = width // heads
    own_heads = heads // count_s
    own = width // count_s
    rows = local * count_s
    places, cap_local, text_width = captions.shape
    cap_rows = places * cap_local
    bucket = slot_buckets[0]
    clip_length = jnp.where(
        bucket == 0, rows // 4, jnp.where(bucket == 1, rows // 2, rows)
    ).astype(jnp.int32)

    own_hidden = down_weight.shape[0]
    gate_rows = gate_up.shape[0]
    text_rows = text_weight.shape[0]
    null_rows = lax.dynamic_slice_in_dim(null_caption, s * cap_local, cap_local, 0)
    is_null = null_flags[:, None, None] == 1
    words_own = jnp.where(is_null, null_rows[None], captions).reshape(cap_rows, text_width)
    own_projection = jnp.concatenate(
        [
            lax.dynamic_slice_in_dim(projection, i * width + s * own, own, 1)
            for i in range(3)
        ],
        axis=1,
    )

    silu_cond = jax.nn.silu(condition).astype(narrow)
    mod_width = modulation.shape[1] // count_s
    pieces = silu_cond.astype(wide).reshape(places, count_b, -1).transpose(1, 0, 2)
    my_clip = (s * local) // clip_length
    (
        cond_columns,
        mods,
        own_projection,
        words,
        text_pairs,
        text_own,
        normed,
        raw_q,
        raw_k,
        raw_v,
        rates,
    ) = start_exchange(
        count_b,
        count_s,
        my_clip.astype(jnp.int32)[None],
        pieces,
        lax.dynamic_slice_in_dim(modulation, s * mod_width, mod_width, 1),
        own_projection,
        words_own,
        text_weight,
        tokens,
        norm_gains[:1],
        head_gains[2:],
    )
    own_projection = own_projection.reshape(width, 3 * own)
    modulated = lax.dynamic_index_in_dim(mods, my_clip, 1, keepdims=False).reshape(1, 4 * width)
    tokens_in = tokens.astype(wide)
    _, pre_pull = jax.vjp(pre_attention, tokens_in, modulated, norm_gains)

    gains = [lax.dynamic_slice_in_dim(head_gains[i : i + 1], s * own, own, 1) for i in range(2)]
    inside = lax.rem(jnp.arange(rows, dtype=jnp.int32), clip_length)
    half = size // 2
    frequency = 10000.0 ** (-jnp.arange(half, dtype=wide) / half)
    angles = inside.astype(wide)[:, None] * frequency[None, :]
    lanes = 128 if own % 128 == 0 else own
    block_heads = lanes // size
    cosine = jnp.tile(jnp.cos(angles), (1, 2 * block_heads))
    sine = jnp.tile(
        jnp.concatenate([-jnp.sin(angles), jnp.sin(angles)], axis=1), (1, block_heads)
    )
    tanh_gates = jnp.tanh(cross_gates)
    own_gates = lax.dynamic_slice_in_dim(tanh_gates, s * own_heads, own_heads, 0)
    clip_of = (jnp.arange(count_s, dtype=jnp.int32) * local) // clip_length
    spans = jnp.stack([clip_of * clip_length, (clip_of + 1) * clip_length, clip_of])
    scalars = (spans, caption_lengths, own_gates)
    full_output, text_own = lax.optimization_barrier((output_weight, text_own))
    full_output = lax.all_gather(full_output, "bucket", axis=0, tiled=True)
    combined, *saved, total, cross_total, text_kv, own_gate_up = attention_forward(
        count_b,
        count_s,
        size,
        lanes,
        scalars,
        (raw_q, raw_k, raw_v),
        rates,
        gains,
        (cosine, sine),
        text_own,
        gate_up,
    )
    combined = combined.transpose(1, 0, 2).reshape(local, width)

    attended = dense(combined, full_output)
    (middle, ffn_full), post_pull = jax.vjp(
        post_attention, attended, tokens_in, modulated, norm_gains
    )
    normed_ffn = ffn_full.astype(narrow)

    lowered, plane, gate_values, hidden = ffn_forward(
        count_b, normed_ffn, own_gate_up, down_weight
    )
    mixed, finish_pull = jax.vjp(finish, lowered, middle, modulated, norm_gains)
    grad_lowered, grad_middle, grad_modulated_last, grad_norm_last = finish_pull(
        cotangent.astype(wide)
    )
    grad_lowered_low = grad_lowered.astype(narrow)
    grad_normed_ffn, grad_gate_up, grad_down = ffn_backward(
        count_b, grad_lowered_low, own_gate_up, down_weight, gate_values, plane, hidden
    )
    share = width // (count_b * count_s)
    ffn_grads = (
        grad_gate_up.reshape(count_b, count_s, share, 2 * own_hidden),
        grad_down.reshape(count_s, own_hidden // count_s, width),
    )

    grad_attended, grad_tokens_post, grad_modulated_post, grad_norm_post = post_pull(
        (grad_middle, grad_normed_ffn)
    )
    grad_attended_low = grad_attended.astype(narrow)
    grad_projected, gain_sums, grad_gates, grad_pairs_low, text_gain_sum, early, *held = (
        attention_backward(
            count_b,
            count_s,
            size,
            lanes,
            scalars,
            grad_attended_low,
            full_output,
            saved,
            (raw_q, raw_k),
            rates,
            gains,
            (cosine, sine),
            text_kv,
            (total, cross_total),
            (grad_modulated_post + grad_modulated_last)[:, width:],
            head_gains[2:],
            text_pairs,
            ffn_grads,
        )
    )

    grad_normed, grad_words, grad_text, *held = end_exchange(
        count_b,
        count_s,
        grad_pairs_low,
        text_weight,
        words,
        grad_projected,
        own_projection,
        ffn_grads,
        held,
    )
    grad_tokens_pre, grad_modulated_pre, grad_norm_pre = pre_pull(grad_normed)
    grad_tokens = grad_tokens_pre + grad_tokens_post

    def place(values):
        return lax.dynamic_update_slice_in_dim(jnp.zeros((width,), wide), values, s * own, 0)

    gate_sums = lax.dynamic_update_slice_in_dim(
        jnp.zeros((heads,), wide),
        jnp.sum(grad_gates, axis=2).reshape(own_heads) * (1.0 - own_gates * own_gates),
        s * own_heads,
        0,
    )
    small = jnp.concatenate(
        [
            grad_norm_pre + grad_norm_post + grad_norm_last,
            jnp.stack(
                [
                    place(gain_sums[0]),
                    place(gain_sums[1]),
                    text_gain_sum[0],
                    jnp.zeros((width,), wide),
                ]
            ),
        ],
        axis=0,
    )
    own_clip = (jnp.arange(places, dtype=jnp.int32) == my_clip).astype(wide)
    row = jnp.concatenate(
        [
            jnp.pad(gate_sums, (0, 128 - heads)),
            jnp.pad(own_clip, (0, width - 128 - places)),
        ]
    )
    row = jnp.stack([grad_modulated_pre[0, :width], row], axis=0)
    (
        down_share,
        text_share,
        output_share,
        proj_share,
        gate_share,
        null_share,
        grad_rows,
        own_sums,
    ) = final_sums(
        count_b,
        count_s,
        null_flags,
        grad_text,
        combined,
        grad_attended_low,
        normed,
        grad_projected,
        ffn_grads,
        held,
        grad_words,
        row,
        small.reshape(8, count_b, count_s, share).transpose(2, 1, 0, 3),
    )
    null_share = lax.ppermute(
        null_share,
        ("bucket", "seq"),
        [(i * count_s + j, j * count_b + i) for i in range(count_b) for j in range(count_s)],
    )
    grad_words = grad_words.reshape(places, cap_local, text_width).astype(wide)
    grad_captions = jnp.where(is_null, 0.0, grad_words)

    cond_own = lax.dynamic_slice_in_dim(cond_columns, s * share, share, 2)
    at_clip = grad_rows[:, :, 1, 128 : 128 + places]
    cond_rows = jnp.sum(at_clip[:, :, :, None] * cond_own[:, None], axis=2)
    mod_share = lax.dot_general(
        flat(cond_rows),
        jnp.concatenate([flat(grad_rows[:, :, 0]), flat(early)], axis=1),
        (((0,), (0,)), ((), ())),
        precision=HIGHEST,
    )
    return (
        mixed.astype(narrow),
        grad_tokens,
        grad_captions,
        null_share,
        mod_share,
        proj_share,
        text_share,
        output_share,
        gate_share,
        down_share,
        own_sums[:4],
        own_sums[4:7],
        jnp.sum(grad_rows[:, :, 1, :heads], axis=(0, 1)),
    )


def solution(mesh):
    whole = P(("bucket", "seq"), None)
    shard = P("bucket", None)
    return jax.shard_map(
        per_device,
        mesh=mesh,
        in_specs=(
            whole,
            shard,
            P("bucket", "seq", None),
            P("bucket"),
            P("bucket"),
            P("bucket"),
            P(),
            shard,
            shard,
            shard,
            shard,
            shard,
            shard,
            P(),
            P(),
            P(),
            whole,
        ),
        out_specs=(
            whole,
            whole,
            P("bucket", "seq", None),
            whole,
            whole,
            whole,
            whole,
            whole,
            whole,
            whole,
            P(None, ("bucket", "seq")),
            P(None, ("bucket", "seq")),
            P(),
        ),
        check_vma=False,
    )
```

```python
from functools import partial

import jax
import jax.numpy as jnp
from jax import lax
from jax.experimental import pallas as pl
from jax.experimental.pallas import tpu as pltpu
from jax.sharding import PartitionSpec as P

EPSILON = 1e-06
NEGATIVE = -1e30
HIGHEST = lax.Precision.HIGHEST
wide = jnp.float32
narrow = jnp.bfloat16
VMEM_LIMIT = 50 * 2**20


def rms_norm(values, norm_gain):
    return (
        values * lax.rsqrt(jnp.mean(values * values, axis=-1, keepdims=True) + EPSILON) * norm_gain
    )


def dense(leading, trailing):
    return jnp.dot(leading, trailing, preferred_element_type=wide)


def contract_rows(leading, trailing):
    return lax.dot_general(
        leading, trailing, (((0,), (0,)), ((), ())), preferred_element_type=wide
    )


def contract_cols(leading, trailing):
    return lax.dot_general(
        leading, trailing, (((1,), (1,)), ((), ())), preferred_element_type=wide
    )


def pre_attention(tokens_in, modulated, norm_gains):
    model_width = tokens_in.shape[1]
    return rms_norm(tokens_in, norm_gains[0]) * (1.0 + modulated[:, :model_width])


def text_heads(text_pairs, gain):
    model_width = text_pairs.shape[1] // 2
    return (rms_norm(text_pairs[:, :model_width], gain), text_pairs[:, model_width:])


def post_attention(attended, tokens_in, modulated, norm_gains):
    model_width = tokens_in.shape[1]
    middle = tokens_in + jnp.tanh(modulated[:, model_width : 2 * model_width]) * rms_norm(
        attended, norm_gains[1]
    )
    normed_ffn = rms_norm(middle, norm_gains[2]) * (
        1.0 + modulated[:, 2 * model_width : 3 * model_width]
    )
    return (middle, normed_ffn)


def swiglu(gate_values):
    hidden_width = gate_values.shape[1] // 2
    return jax.nn.silu(gate_values[:, :hidden_width]) * gate_values[:, hidden_width:]


def finish(lowered, middle, modulated, norm_gains):
    model_width = middle.shape[1]
    return middle + jnp.tanh(modulated[:, 3 * model_width :]) * rms_norm(lowered, norm_gains[3])


MESH = pl.DeviceIdType.MESH


class Transfers:
    def __init__(self, send, arrive):
        self.send, self.arrive, self.used = send, arrive, 0
        self.open = []

    def start(self, source, target, device):
        copy = pltpu.make_async_remote_copy(
            src_ref=source,
            dst_ref=target,
            send_sem=self.send.at[self.used],
            recv_sem=self.arrive.at[self.used],
            device_id=device,
            device_id_type=MESH,
        )
        self.used += 1
        copy.start()
        self.open.append(copy)
        return copy

    def finish(self):
        for copy in self.open:
            copy.wait_send()


def meet(devices):
    barrier = pltpu.get_barrier_semaphore()
    for device in devices:
        pl.semaphore_signal(barrier, inc=1, device_id=device, device_id_type=MESH)
    pl.semaphore_wait(barrier, len(devices))


def partner(bits):
    return {"bucket": jnp.bitwise_xor(lax.axis_index("bucket"), bits)}


def outer_bits(count):
    return [1 << i for i in range(1, count.bit_length() - 1)]


def block_index(k, count):
    return (k >> 1) + (k & 1) * (count // 2)


def last_bit(block, order):
    return [bit for bit in order if block & bit][-1]


class PlaneExchange:
    def __init__(
        self, count, links, gathered=None, partial=None, arrived_core=None, arrived_outer=None,
        natural=False,
    ):
        self.count, self.links, self.natural = count, links, natural
        self.index = lax.axis_index("bucket")
        self.gathered, self.partial = gathered, partial
        self.arrived_core, self.arrived_outer = arrived_core, arrived_outer
        bits = outer_bits(count)
        self.orders = (bits, bits[::-1])
        self.outer = [k for k in range(0, count, 2)]
        self.rows = (partial if gathered is None else gathered).shape[1] // 2
        self.coming, self.slots = {}, {}
        self.blocks = [0]

    def part(self, ref, block, half):
        return ref.at[block, pl.ds(half * self.rows, self.rows)]

    def place(self, block):
        return jnp.bitwise_xor(self.index, block) if self.natural else block_index(block, self.count)

    def onward(self, half, block, bit):
        source = self.place(block)
        target = source if self.natural else self.place(block | bit)
        self.coming[half, block | bit] = self.links.start(
            self.part(self.gathered, source, half),
            self.part(self.gathered, target, half),
            partner(bit),
        )

    def forward(self, half, block):
        order = self.orders[half]
        later = order if block == 0 else order[order.index(last_bit(block, order)) + 1 :]
        for bit in later:
            self.onward(half, block, bit)

    def forward_core(self, half, block):
        self.onward(half, block, 1)

    def arrive(self, block):
        for half in range(2):
            self.coming[half, block].wait_recv()

    def begin(self):
        for step in range(len(self.orders[0])):
            for half in range(2):
                self.onward(half, 0, self.orders[half][step])
        for half in range(2):
            self.forward_core(half, 0)

    def run_gather(self, compute, scatter=None):
        self.begin()
        compute([0])
        levels = len(self.orders[0])
        self.arrive(1)
        compute([block_index(1, self.count)])
        if scatter is not None:
            self.send_core(1)
        for level in range(1, levels + 1):
            here = [k for k in self.outer if bin(k).count("1") == level]
            self.forward_level(here)
            if level == 2 and scatter is not None:
                next(scatter)
            compute([block_index(k, self.count) for k in here])
            for k in here:
                self.arrive(k | 1)
            compute([block_index(k | 1, self.count) for k in here])
            for k in here:
                if scatter is not None:
                    self.send_core(k | 1)

    def gather(self):
        self.begin()
        yield
        for level in range(1, len(self.orders[0]) + 1):
            self.forward_level([k for k in self.outer if bin(k).count("1") == level])
            yield
        for block in self.outer:
            self.arrive(block | 1)

    def forward_level(self, here):
        steps = [(half, k) for k in here for half in range(2)]
        steps.sort(
            key=lambda s: [
                self.orders[s[0]].index(bit) for bit in self.orders[s[0]] if s[1] & bit
            ][::-1]
        )
        for half, k in steps:
            self.coming[half, k].wait_recv()
            self.forward(half, k)
            self.forward_core(half, k)

    def send_core(self, block):
        place = self.place(block)
        target = self.arrived_core.at[block >> 1]
        self.slots["core", block & ~1] = self.links.start(self.partial.at[place], target, partner(1))

    def total(self, half, block, slots):
        rows = pl.ds(half * self.rows, self.rows)
        value = self.partial[self.place(block), rows].astype(wide)
        value = value + self.arrived_core[block >> 1, rows].astype(wide)
        for slot in slots:
            value = value + self.arrived_outer[half, slot].astype(wide)
        return value

    def scatter(self, finish):
        slot_of = {}
        waiting = {(half, k): [] for half in range(2) for k in self.outer}
        core_seen = set()
        left = [list(self.outer), list(self.outer)]
        for step in range(len(self.orders[0])):
            jobs = []
            for half in range(2):
                bit = self.orders[half][::-1][step]
                jobs.append([(half, bit, k) for k in left[half] if k & bit])
                left[half] = [k for k in left[half] if not k & bit]
            for pair in zip(*jobs, strict=True):
                for half, bit, k in pair:
                    if k not in core_seen:
                        self.slots["core", k].wait_recv()
                        core_seen.add(k)
                    for copy, _ in waiting[half, k]:
                        copy.wait_recv()
                    rows = pl.ds(half * self.rows, self.rows)
                    total = self.total(half, k, [slot for _, slot in waiting[half, k]])
                    self.partial[self.place(k), rows] = total.astype(narrow)
                    slot = slot_of.setdefault((half, bit, k ^ bit), len([1 for h, *_ in slot_of if h == half]))
                    copy = self.links.start(
                        self.partial.at[self.place(k), rows],
                        self.arrived_outer.at[half, slot],
                        partner(bit),
                    )
                    waiting[half, k ^ bit].append((copy, slot))
                yield
        if 0 not in core_seen:
            self.slots["core", 0].wait_recv()
        for half in range(2):
            for copy, _ in waiting[half, 0]:
                copy.wait_recv()
            finish(half, self.total(half, 0, [slot for _, slot in waiting[half, 0]]))


def plane_partners(count):
    return [partner(bit) for bit in outer_bits(count) + [1]]


def plane_copies(count):
    outer = count // 2
    return 2 * (outer - 1) + 2 * outer, outer + 2 * (outer - 1)


def spans(blocks):
    runs = []
    for block in sorted(blocks):
        if runs and runs[-1][1] == block:
            runs[-1][1] = block + 1
        else:
            runs.append([block, block + 1])
    return runs


def each(blocks, body):
    for first, end in spans(blocks):
        if end - first == 1:
            body(first)
        else:
            lax.fori_loop(first, end, lambda i, _: (body(i), 0)[1], 0)


class Late:
    def __init__(self, source, target, semaphore):
        self.copy = pltpu.make_async_copy(source, target, semaphore)
        self.target, self.there = target, False
        self.copy.start()

    def get(self):
        if not self.there:
            self.copy.wait()
            self.there = True
        return self.target


def ffn_kernel(
    count, x, gate_up_hbm, down_hbm, lowered, plane_out, values_out, hidden_out,
    gate_up, down, plane, partial, core, outer, values, hidden, send, arrive, local,
):
    links = Transfers(send, arrive)
    late = Late(gate_up_hbm, gate_up, local.at[3]), Late(down_hbm, down, local.at[4])
    meet(plane_partners(count))
    units = down.shape[0]
    wide_block = 256
    plane[0] = x[...]
    saved = pltpu.make_async_copy(plane, plane_out, local.at[0])

    def compute(blocks):
        for copy in late:
            copy.get()

        def one(place):
            for start in range(0, units, wide_block):
                columns = slice(start, start + wide_block)
                after = slice(units + start, units + start + wide_block)
                gate = dense(plane[place], gate_up[:, columns])
                up = dense(plane[place], gate_up[:, after])
                values[place, :, columns] = gate
                values[place, :, after] = up
                hidden[place, :, columns] = (jax.nn.silu(gate) * up).astype(narrow)
            partial[place] = dense(hidden[place], down[...]).astype(narrow)

        each(blocks, one)

    exchange = PlaneExchange(count, links, plane, partial, core, outer)
    def finish(half, total):
        lowered[pl.ds(half * exchange.rows, exchange.rows)] = total

    sums = exchange.scatter(finish)
    exchange.run_gather(compute, sums)
    saved.start()
    kept = pltpu.make_async_copy(values, values_out, local.at[1])
    kept.start()
    held = pltpu.make_async_copy(hidden, hidden_out, local.at[2])
    held.start()

    for _ in sums:
        pass
    saved.wait()
    kept.wait()
    held.wait()
    links.finish()


def plane_scratch(count, rows, width):
    outer = count // 2
    return [
        pltpu.VMEM((count, rows, width), narrow),
        pltpu.VMEM((count, rows, width), narrow),
        pltpu.VMEM((outer, rows, width), narrow),
        pltpu.VMEM((2, outer - 1, rows // 2, width), narrow),
    ]


def ffn_forward(count, x, gate_up, down):
    rows, width = x.shape
    units = down.shape[0]
    copies = sum(plane_copies(count))
    vmem, anywhere = pl.BlockSpec(memory_space=pltpu.VMEM), pl.BlockSpec(memory_space=pl.ANY)
    return pl.pallas_call(
        partial(ffn_kernel, count),
        in_specs=[vmem] + [anywhere] * 2,
        out_specs=[vmem] + [anywhere] * 3,
        out_shape=[
            jax.ShapeDtypeStruct((rows, width), wide),
            jax.ShapeDtypeStruct((count, rows, width), narrow),
            jax.ShapeDtypeStruct((count, rows, 2 * units), wide),
            jax.ShapeDtypeStruct((count, rows, units), narrow),
        ],
        scratch_shapes=[pltpu.VMEM(gate_up.shape, narrow), pltpu.VMEM(down.shape, narrow)]
        + plane_scratch(count, rows, width)
        + [
            pltpu.VMEM((count, rows, 2 * units), wide),
            pltpu.VMEM((count, rows, units), narrow),
            pltpu.SemaphoreType.DMA((copies,)),
            pltpu.SemaphoreType.DMA((copies,)),
            pltpu.SemaphoreType.DMA((5,)),
        ],
        compiler_params=pltpu.CompilerParams(
            collective_id=1, has_side_effects=True, vmem_limit_bytes=60 * 2**20
        ),
        name="ffn_forward",
    )(x, gate_up, down)

def ffn_back_kernel(
    count, g, gate_up_hbm, down_hbm, values_in, x_in, hidden_in, grad_normed, grad_gate_up,
    grad_down, gate_up, down, plane, partial, core, outer, values, grads, taken, send, arrive,
    local,
):
    links = Transfers(send, arrive)
    late = Late(down_hbm, down, local.at[4]), Late(gate_up_hbm, gate_up, local.at[3])
    fetch = pltpu.make_async_copy(values_in, values, local.at[2])
    fetch.start()
    meet(plane_partners(count))
    units, width = down.shape
    wide_block = 256
    plane[0] = g[...]
    fetched = []

    def compute(places):
        if not fetched:
            fetch.wait()
            fetched.append(True)
            for copy in late:
                copy.get()

        def one(place):
            for start in range(0, units, wide_block):
                columns = slice(start, start + wide_block)
                after = slice(units + start, units + start + wide_block)
                back = contract_cols(plane[place], down[columns])
                gate, up = values[place, :, columns], values[place, :, after]
                sigma = jax.nn.sigmoid(gate)
                grads[place, :, columns] = (
                    back * up * (sigma * (1.0 + gate * (1.0 - sigma)))
                ).astype(narrow)
                grads[place, :, after] = (back * (gate * sigma)).astype(narrow)
            partial[place] = contract_cols(grads[place], gate_up[...]).astype(narrow)

        each(places, one)

    exchange = PlaneExchange(count, links, plane, partial, core, outer)

    def finish(half, total):
        grad_normed[pl.ds(half * exchange.rows, exchange.rows)] = total

    sums = exchange.scatter(finish)
    exchange.run_gather(compute, sums)

    jobs = [(x_in, grads, grad_gate_up, i) for i in range(width // wide_block)]
    jobs += [(hidden_in, plane, grad_down, i) for i in range(units // wide_block)]

    def take(number):
        source, _, _, i = jobs[number]
        columns = pl.ds(i * wide_block, wide_block)
        return pltpu.make_async_copy(
            source.at[:, :, columns], taken.at[number % 2], local.at[number % 2]
        )

    def work(number):
        if number + 1 < len(jobs):
            take(number + 1).start()
        take(number).wait()
        _, upstream, out, i = jobs[number]
        for start in range(0, upstream.shape[2], 512):
            columns = slice(start, start + 512)
            out[i * wide_block : (i + 1) * wide_block, columns] = contract_rows(
                flat(taken[number % 2]), flat(upstream[:, :, columns])
            ).astype(narrow)

    take(0).start()
    done = 0
    for _ in sums:
        for number in range(done, min(done + 3, len(jobs))):
            work(number)
            done += 1
    for number in range(done, len(jobs)):
        work(number)
    links.finish()


class GradientRing:
    def __init__(self, ring, own, held):
        self.ring, self.own, self.held = ring, own, held
        self.copies, self.pieces = [], {}

    def piece(self, which, step):
        place = self.ring.source(step + 1)
        return self.own[0].at[:, place] if which == 0 else self.own[1].at[place]

    def fetch(self, first, targets, semaphores):
        for slot in range(targets[0].shape[0]):
            for which in range(2):
                self.pieces[which, first + slot] = Late(
                    self.piece(which, first + slot),
                    targets[which].at[slot],
                    semaphores.at[2 * slot + which],
                )

    def first(self, landing):
        for which in range(2):
            self.copies.append(
                self.ring.links.start(self.piece(which, 0), landing[which], self.ring.right)
            )

    def arrived(self):
        for copy in self.copies:
            copy.wait_recv()
        self.copies = []

    def value(self, which, step):
        piece = self.pieces[which, step].get()
        return piece[...].astype(wide) + self.held[which][...].astype(wide)

    def onward(self, step, going, landing):
        self.arrived()
        for which in range(2):
            going[which][...] = self.value(which, step).astype(narrow)
            self.copies.append(
                self.ring.links.start(going[which], landing[which], self.ring.right)
            )
        self.held = landing


def ffn_backward(count, g, gate_up, down, values, x, hidden):
    rows, width = g.shape
    units = down.shape[0]
    copies = sum(plane_copies(count))
    vmem, anywhere = pl.BlockSpec(memory_space=pltpu.VMEM), pl.BlockSpec(memory_space=pl.ANY)
    return pl.pallas_call(
        partial(ffn_back_kernel, count),
        in_specs=[vmem] + [anywhere] * 5,
        out_specs=[vmem] * 3,
        out_shape=[
            jax.ShapeDtypeStruct((rows, width), wide),
            jax.ShapeDtypeStruct((width, 2 * units), narrow),
            jax.ShapeDtypeStruct((units, width), narrow),
        ],
        scratch_shapes=[pltpu.VMEM(gate_up.shape, narrow), pltpu.VMEM(down.shape, narrow)]
        + plane_scratch(count, rows, width)
        + [
            pltpu.VMEM((count, rows, 2 * units), wide),
            pltpu.VMEM((count, rows, 2 * units), narrow),
            pltpu.VMEM((2, count, rows, 256), narrow),
            pltpu.SemaphoreType.DMA((copies,)),
            pltpu.SemaphoreType.DMA((copies,)),
            pltpu.SemaphoreType.DMA((5,)),
        ],
        compiler_params=pltpu.CompilerParams(
            collective_id=2, has_side_effects=True, vmem_limit_bytes=62 * 2**20
        ),
        name="ffn_backward",
    )(g, gate_up, down, values, x, hidden)


def seq_device(index):
    return {"seq": index}


class Ring:
    def __init__(self, depth, links):
        self.depth, self.links = depth, links
        self.index = lax.axis_index("seq")
        self.right = seq_device(lax.rem(self.index + 1, depth))
        self.left = seq_device(lax.rem(self.index + depth - 1, depth))

    def source(self, step):
        return lax.rem(self.index - step + 2 * self.depth, self.depth)


def start_kernel(
    count, depth, clip, pieces, columns, shard, words, text_hbm, x, gain, text_gain,
    got, mods, projection, spread, pairs, text_own, normed, q, k, v, rates,
    text, local, product, back, stat, stat_in, partial, core, outer, send, arrive,
):
    links = Transfers(send, arrive)
    late = Late(text_hbm, text, local.at[0])
    ring = Ring(depth, links)
    b, s = lax.axis_index("bucket"), lax.axis_index("seq")
    others = [partner(k) for k in range(1, count)]
    along = [seq_device(lax.rem(s + step, depth)) for step in range(1, depth)]
    meet(others + along)
    first = [
        links.start(pieces.at[jnp.bitwise_xor(b, k)], got.at[k], others[k - 1])
        for k in range(1, count)
    ]
    got[0] = pieces[b]
    feature, width = text.shape

    def features(target):
        return words.at[:, pl.ds(pl.multiple_of(target * feature, 128), feature)]

    projection[b] = shard[...]
    spread[b] = words[:, pl.ds(pl.multiple_of(b * feature, 128), feature)]
    for copy in first:
        copy.wait_recv()
    for block in range(count):
        product[block] = dense(got[block].astype(narrow), columns[...])
    second = [
        links.start(product.at[block], back.at[block - 1], others[block - 1])
        for block in range(1, count)
    ]
    shards = PlaneExchange(count, links, projection, natural=True).gather()
    next(shards)
    far = {}
    for block in sorted(range(1, count), key=lambda block: (bin(block >> 1).count("1"), block & 1)):
        far[block] = links.start(
            features(jnp.bitwise_xor(b, block)), spread.at[b], others[block - 1]
        )

    total = product[0]
    for i, copy in enumerate(second):
        copy.wait_recv()
        total = total + back[i]
    mods[s] = total
    third = [links.start(mods.at[s], mods.at[s], device) for device in along]
    for copy in third:
        copy.wait_recv()
    places = mods.shape[1]
    parts = []
    for i in range(depth // 4):
        part = jnp.zeros((1, mods.shape[2]), wide)
        for place in range(places):
            part = part + jnp.where(clip[0] == place, mods[i, place : place + 1], 0.0)
        parts.append(part)
    scale = parts[0] if len(parts) == 1 else jnp.concatenate(parts, axis=1)
    value = x[...].astype(wide)
    rate = lax.rsqrt(jnp.mean(value * value, axis=1, keepdims=True) + EPSILON)
    normed[s] = (value * rate * gain[...] * (1.0 + scale)).astype(narrow)
    moving = [links.start(normed.at[s], normed.at[s], ring.right)]
    next(shards)

    exchange = PlaneExchange(count, links, None, partial, core, outer)

    def pair(block):
        if block:
            far[block].wait_recv()
        source = spread[jnp.bitwise_xor(b, block)]
        place = block_index(block, count)
        for start in range(0, width, 512):
            span = slice(start, start + 512)
            partial[place, :, span] = dense(source, text[:, span]).astype(narrow)
        if block & 1:
            exchange.send_core(block)

    def finish(half, total):
        pairs[pl.ds(half * exchange.rows, exchange.rows)] = total
        keys = total[:, : width // 2]
        rate = lax.rsqrt(jnp.mean(keys * keys, axis=1, keepdims=True) + EPSILON)
        kinds = (keys * rate * text_gain[...]).astype(narrow), total[:, width // 2 :].astype(narrow)
        cap_local, part = text_own.shape[3:]
        for kind, value in enumerate(kinds):
            for i in range(exchange.rows // cap_local):
                place = half * (exchange.rows // cap_local) + i
                rows = slice(i * cap_local, (i + 1) * cap_local)
                for target in range(depth):
                    text_own[target, kind, place] = value[
                        rows, target * part : (target + 1) * part
                    ]

    late.get()
    sums = exchange.scatter(finish)
    order = sorted(exchange.outer, key=lambda block: (bin(block).count("1"), block))
    order = order[1:] + order[:1]
    levels = len(exchange.orders[0])
    for block in order[:levels]:
        pair(block | 1)
        pair(block)
    own = q.shape[2]

    def project(step):
        place = ring.source(step)
        for i, out in enumerate((q, k, v)):
            span = slice(i * own, (i + 1) * own)
            weight = projection[:, :, span]
            out[place] = dense(normed[place], flat(weight))

    def onward(step):
        moving[-1].wait_recv()
        place = ring.source(step)
        if step < depth - 1:
            moving.append(links.start(normed.at[place], normed.at[place], ring.right))

    next(sums)
    onward(1)
    for block in order[levels:]:
        pair(block | 1)
        pair(block)
    next(sums)
    for _ in shards:
        pass
    project(0)
    project(1)
    for step in range(2, depth - 1):
        onward(step)
        project(step)
    next(sums)
    onward(depth - 1)
    project(depth - 1)
    for i, raw in enumerate((q, k)):
        for block in range(depth):
            place = i * depth + block
            stat[place : place + 1] = row_sums(raw[block] * raw[block])
    stats = [links.start(stat, stat_in.at[i], device) for i, device in enumerate(along)]
    for _ in sums:
        pass
    squares = stat[...]
    for i, copy in enumerate(stats):
        copy.wait_recv()
        squares = squares + stat_in[i]
    rates[...] = lax.rsqrt(squares / (own * depth) + EPSILON)
    links.finish()


def start_exchange(
    count, depth, clip, pieces, columns, shard, words, text, x, gain, text_gain
):
    vmem = pl.BlockSpec(memory_space=pltpu.VMEM)
    rows, width = x.shape
    own = shard.shape[1] // 3
    cap_rows, pair_width = words.shape[0], text.shape[1]
    places, mod_width = pieces.shape[1], columns.shape[1]
    copies = sum(plane_copies(count)) + 3 * (count - 1) + 3 * (depth - 1)
    raw = jax.ShapeDtypeStruct((depth, rows, own), wide)
    return pl.pallas_call(
        partial(start_kernel, count, depth),
        in_specs=[scalar_spec()] + [vmem] * 4 + [pl.BlockSpec(memory_space=pl.ANY)] + [vmem] * 3,
        out_specs=[vmem] * 11,
        out_shape=[
            jax.ShapeDtypeStruct(pieces.shape, wide),
            jax.ShapeDtypeStruct((depth, places, mod_width), wide),
            jax.ShapeDtypeStruct((count,) + shard.shape, narrow),
            jax.ShapeDtypeStruct((count, cap_rows, words.shape[1] // count), narrow),
            jax.ShapeDtypeStruct((cap_rows, pair_width), wide),
            jax.ShapeDtypeStruct((depth, 2, places, cap_rows // places, own), narrow),
            jax.ShapeDtypeStruct((depth, rows, width), narrow),
            raw,
            raw,
            raw,
            jax.ShapeDtypeStruct((2 * depth, rows), wide),
        ],
        scratch_shapes=[
            pltpu.VMEM(text.shape, narrow),
            pltpu.SemaphoreType.DMA((1,)),
            pltpu.VMEM((count, places, mod_width), wide),
            pltpu.VMEM((count - 1, places, mod_width), wide),
            pltpu.VMEM((2 * depth, rows), wide),
            pltpu.VMEM((depth - 1, 2 * depth, rows), wide),
        ]
        + plane_scratch(count, cap_rows, pair_width)[1:]
        + [pltpu.SemaphoreType.DMA((copies,)), pltpu.SemaphoreType.DMA((copies,))],
        compiler_params=pltpu.CompilerParams(
            collective_id=4, has_side_effects=True, vmem_limit_bytes=60 * 2**20
        ),
        name="start_exchange",
    )(clip, pieces, columns, shard, words, text, x, gain, text_gain)


def end_kernel(
    count, depth, pairs, text_hbm, words_hbm, grads_hbm, projection_hbm, grad_gate, grad_down,
    gate_held, down_held, normed, grad_words, grad_weight, gate_next, down_next,
    text, words, grads, projection, gate_piece, down_piece, local,
    plane, back, send_sum, ring_in, total, gate_go, down_go, send, arrive,
):
    links = Transfers(send, arrive)
    ring = Ring(depth, links)
    late = [
        Late(source, target, local.at[2 + i])
        for i, (source, target) in enumerate(
            zip(
                (text_hbm, words_hbm, grads_hbm, projection_hbm),
                (text, words, grads, projection),
                strict=True,
            )
        )
    ]
    weights = GradientRing(ring, (grad_gate, grad_down), (gate_held, down_held))
    weights.fetch(1, (gate_piece, down_piece), local)
    b = lax.axis_index("bucket")
    others = [partner(k) for k in range(1, count)]
    meet(others + [ring.left, ring.right])
    plane[0] = pairs[...]
    exchange = PlaneExchange(count, links, plane)
    feature, width = text.shape
    own_columns = pl.ds(pl.multiple_of(b * feature, 128), feature)
    moving = []

    def round_step(step):
        value = contract_cols(grads[ring.source(step + 1)], projection[...])
        if step > 0:
            moving[-1].wait_recv()
            value = value + ring_in[step - 1].astype(wide)
        if step < depth - 1:
            send_sum[step] = value.astype(narrow)
            moving.append(links.start(send_sum.at[step], ring_in.at[step], ring.right))
        else:
            normed[...] = value

    steps = [0]

    def advance():
        if steps[0] < depth - 1:
            round_step(steps[0])
            steps[0] += 1
            if steps[0] == depth - 1:
                weights.onward(1, (gate_go, down_go), (gate_next, down_next))

    arriving = []
    blocks = [None] * count
    for block in range(count):
        blocks[block_index(block, count)] = block

    def compute(places):
        for copy in late:
            copy.get()
        for place in places:
            block = blocks[place]
            features = words[jnp.bitwise_xor(b, block)].astype(wide).T.astype(narrow)
            for first in range(0, width, 512):
                columns = slice(first, first + 512)
                part = dense(features, plane[place, :, columns])
                if place == 0:
                    total[:, columns] = part
                else:
                    total[:, columns] += part
            value = contract_cols(plane[place], text[...]).astype(narrow)
            if block == 0:
                grad_words[:, own_columns] = value
            else:
                back[place - 1] = value
                arriving.append(
                    links.start(
                        back.at[place - 1], grad_words.at[:, own_columns], others[block - 1]
                    )
                )
        advance()

    exchange.run_gather(compute)
    while steps[0] < depth - 1:
        advance()
    round_step(depth - 1)
    grad_weight[...] = total[...].astype(narrow)
    for copy in arriving + weights.copies:
        copy.wait_recv()
    links.finish()


def end_exchange(count, depth, pairs, text, words, grads, projection, ffn_grads, held):
    vmem = pl.BlockSpec(memory_space=pltpu.VMEM)
    cap_rows, pair_width = pairs.shape
    feature = text.shape[0]
    rows, width = grads.shape[1], projection.shape[0]
    copies = plane_copies(count)[0] + count - 1 + depth - 1 + 2
    return pl.pallas_call(
        partial(end_kernel, count, depth),
        in_specs=[vmem] + [pl.BlockSpec(memory_space=pl.ANY)] * 6 + [vmem] * 2,
        out_specs=[vmem] * 5,
        out_shape=[
            jax.ShapeDtypeStruct((rows, width), wide),
            jax.ShapeDtypeStruct((cap_rows, count * feature), narrow),
            jax.ShapeDtypeStruct((feature, pair_width), narrow),
            jax.ShapeDtypeStruct(held[0].shape, narrow),
            jax.ShapeDtypeStruct(held[1].shape, narrow),
        ],
        scratch_shapes=[
            pltpu.VMEM(text.shape, narrow),
            pltpu.VMEM(words.shape, narrow),
            pltpu.VMEM(grads.shape, narrow),
            pltpu.VMEM(projection.shape, narrow),
            pltpu.VMEM((1,) + held[0].shape, narrow),
            pltpu.VMEM((1,) + held[1].shape, narrow),
            pltpu.SemaphoreType.DMA((6,)),
            pltpu.VMEM((count, cap_rows, pair_width), narrow),
            pltpu.VMEM((count - 1, cap_rows, feature), narrow),
            pltpu.VMEM((depth - 1, rows, width), narrow),
            pltpu.VMEM((depth - 1, rows, width), narrow),
            pltpu.VMEM((feature, pair_width), wide),
            pltpu.VMEM(held[0].shape, narrow),
            pltpu.VMEM(held[1].shape, narrow),
            pltpu.SemaphoreType.DMA((copies,)),
            pltpu.SemaphoreType.DMA((copies,)),
        ],
        compiler_params=pltpu.CompilerParams(
            collective_id=5, has_side_effects=True, vmem_limit_bytes=63 * 2**20
        ),
        name="end_exchange",
    )(pairs, text, words, grads, projection, *ffn_grads, *held)


def sum_kernel(
    count, depth, flags, text, combined, upstream, normed_hbm, grads_hbm, grad_gate, grad_down,
    gate_held, down_held, words_hbm, row, small, early, conditions, mod_share, down_share, text_share, output_share, proj_share, gate_share, null_share, rows_out, small_out,
    normed, grads, words, gate_piece, down_piece, local, out_part, out_core, out_outer, proj_part, proj_core, proj_outer, send_low, low_in, out_go,
    out_come, proj_go, proj_come, gate, gate_come, null, null_come, small_come, small_go,
    small_land, gate_go, down_go, gate_land, down_land, cond_rows, all_rows, send, arrive,
):
    links = Transfers(send, arrive)
    ring = Ring(depth, links)
    late = [
        Late(source, target, local.at[i])
        for i, (source, target) in enumerate(
            zip((normed_hbm, grads_hbm, words_hbm), (normed, grads, words), strict=True)
        )
    ]
    weights = GradientRing(ring, (grad_gate, grad_down), (gate_held, down_held))
    weights.fetch(2, (gate_piece, down_piece), local.at[pl.ds(3, 2 * (depth - 2))])
    b, s = lax.axis_index("bucket"), lax.axis_index("seq")
    others = [partner(k) for k in range(1, count)]
    turns = [lax.rem(s + step, depth) for step in range(1, depth)]
    along = [seq_device(place) for place in turns]
    meet(others + along)

    rows_out[0, s] = row[...]
    tiny = []
    for i, (place, device) in enumerate(zip(turns, along, strict=True)):
        tiny.append(links.start(row, rows_out.at[0, s], device))
        tiny.append(links.start(small.at[place], small_come.at[i], device))

    low_rows = text.shape[0] // depth
    going = []

    def text_step(step):
        rows = pl.ds(pl.multiple_of(ring.source(step + 1) * low_rows, 16), low_rows)
        value = text[rows].astype(wide)
        if step > 0:
            going[-1].wait_recv()
            value = value + low_in[step - 1].astype(wide)
        if step < depth - 1:
            send_low[step] = value.astype(narrow)
            going.append(links.start(send_low.at[step], low_in.at[step], ring.right))
        else:
            text_share[...] = value

    def weights_step(step):
        slot = step - 2
        weights.onward(
            step,
            (gate_go.at[slot], down_go.at[slot]),
            (gate_land.at[slot], down_land.at[slot]),
        )

    text_step(0)
    weights_step(2)

    share = out_go.shape[1]
    pair = 2 * out_part.shape[1]

    def fill(part, leading, trailing):
        for first in range(0, count, 2):
            value = contract_rows(leading[:, first // 2 * pair : (first // 2 + 1) * pair], trailing)
            value = value.astype(narrow)
            part[first] = value[: pair // 2]
            part[first + 1] = value[pair // 2 :]

    def plane_sum(part, core, outer, go):
        exchange = PlaneExchange(count, links, None, part, core, outer, natural=True)
        for block in range(1, count, 2):
            exchange.send_core(block)

        def finish(half, total):
            low = total.astype(narrow)
            for i in range(depth // 2):
                go[half * (depth // 2) + i] = low[i * share : (i + 1) * share]

        return exchange.scatter(finish)

    fill(out_part, combined[...], upstream[...])
    out_sums = plane_sum(out_part, out_core, out_outer, out_go)
    for copy in late:
        copy.get()
    fill(proj_part, flat(normed[...]), flat(grads[...]))
    proj_sums = plane_sum(proj_part, proj_core, proj_outer, proj_go)
    for _ in range(count // 4):
        next(out_sums)
    for _ in range(count // 4):
        next(proj_sums)
    text_step(1)

    places = flags.shape[0]
    cap_local = words.shape[0] // places
    null_rows = null.shape[1]
    for k in range(count):
        value = jnp.zeros((null_rows, words.shape[1]), wide)
        for place in range(places):
            first = place * cap_local + k * null_rows
            part = words[first : first + null_rows].astype(wide)
            value = value + jnp.where(flags[place] == 1, part, 0.0)
        null[k] = value
    next(out_sums)
    next(proj_sums)
    nulls = [
        links.start(null.at[jnp.bitwise_xor(b, k)], null_come.at[k - 1], others[k - 1])
        for k in range(1, count)
    ]

    def drain(sums):
        for _ in sums:
            pass

    def seq_sends(go, come):
        come[s] = go[s]
        return [
            links.start(go.at[place], come.at[s], device)
            for place, device in zip(turns, along, strict=True)
        ]

    for step in range(3, depth - 1):
        weights_step(step)
    weights.arrived()
    gate[...] = weights.value(0, depth - 1).astype(narrow)
    far = [
        links.start(gate.at[jnp.bitwise_xor(b, k)], gate_come.at[b], others[k - 1])
        for k in range(1, count)
    ]
    gate_come[b] = gate[b]
    down_share[...] = weights.value(1, depth - 1)
    own_small = small[s]
    for copy in tiny:
        copy.wait_recv()
    for i in range(depth - 1):
        own_small = own_small + small_come[i]
    small_go[...] = own_small
    spread = []
    for k in range(1, count):
        spread.append(links.start(rows_out.at[0], rows_out.at[k], others[k - 1]))
        spread.append(
            links.start(
                small_go.at[jnp.bitwise_xor(b, k)], small_land.at[k - 1], others[k - 1]
            )
        )
    drain(out_sums)
    out_far = seq_sends(out_go, out_come)
    drain(proj_sums)
    proj_far = seq_sends(proj_go, proj_come)
    for step in range(2, depth - 1):
        text_step(step)
    total = null[b]
    for i, copy in enumerate(nulls):
        copy.wait_recv()
        total = total + null_come[i]
    null_share[...] = total
    for copy in spread:
        copy.wait_recv()
    sums = small_go[b]
    for i in range(count - 1):
        sums = sums + small_land[i]
    small_out[...] = sums

    width = row.shape[1]
    for block in range(count):
        for source in range(depth):
            at = slice(block * depth + source, block * depth + source + 1)
            value = jnp.zeros((1, share), wide)
            for place in range(places):
                mark = rows_out[block, source, 1:2, 128 + place : 129 + place]
                value = value + mark * conditions[block, place : place + 1]
            cond_rows[at] = value
            all_rows[at, :width] = rows_out[block, source, 0:1]
            all_rows[at, width:] = early[block, source]
    for first in range(0, 4 * width, 1536):
        columns = slice(first, first + 1536)
        mod_share[:, columns] = lax.dot_general(
            cond_rows[...],
            all_rows[:, columns],
            (((0,), (0,)), ((), ())),
            precision=HIGHEST,
            preferred_element_type=wide,
        )
    for copy in far:
        copy.wait_recv()
    units = gate.shape[2] // 2
    for block in range(count):
        for half in range(2):
            first = half * count * units + block * units
            gate_share[:, first : first + units] = gate_come[
                block, :, half * units : (half + 1) * units
            ].astype(wide)
    for copy in out_far + proj_far:
        copy.wait_recv()
    text_step(depth - 1)
    total = out_come[0].astype(wide)
    for i in range(1, depth):
        total = total + out_come[i].astype(wide)
    output_share[...] = total
    own = proj_come.shape[2] // 3
    for i in range(3):
        for source in range(depth):
            first = i * depth * own + source * own
            proj_share[:, first : first + own] = proj_come[
                source, :, i * own : (i + 1) * own
            ].astype(wide)
    links.finish()


def final_sums(
    count, depth, flags, text, combined, upstream, normed, grads, ffn_grads, held, words, row, small,
    early, conditions,
):
    vmem = pl.BlockSpec(memory_space=pltpu.VMEM)
    feature, pair_width = text.shape
    width = combined.shape[1]
    own3 = grads.shape[2]
    share = width // (count * depth)
    null_rows = words.shape[0] // flags.shape[0] // count
    text_width = words.shape[1]
    outer = count // 2
    block_rows = width // count
    quarter = (depth - 1, feature // depth, pair_width)

    def plane_sums(columns):
        return [
            pltpu.VMEM((count, block_rows, columns), narrow),
            pltpu.VMEM((outer, block_rows, columns), narrow),
            pltpu.VMEM((2, outer - 1, block_rows // 2, columns), narrow),
        ]

    copies = 2 * (depth - 1) + depth - 1 + 2 * plane_copies(count)[1] + 4 * (count - 1)
    copies += 2 * (depth - 1) + 2 * (depth - 3)
    gate, down = held
    gates = pltpu.VMEM(gate.shape, narrow)
    anywhere = pl.BlockSpec(memory_space=pl.ANY)
    return pl.pallas_call(
        partial(sum_kernel, count, depth),
        in_specs=[scalar_spec()]
        + [vmem] * 3
        + [anywhere] * 4
        + [vmem] * 2
        + [anywhere]
        + [vmem] * 4,
        out_specs=[vmem] * 9,
        out_shape=[
            jax.ShapeDtypeStruct((share, 4 * width), wide),
            jax.ShapeDtypeStruct(down.shape, wide),
            jax.ShapeDtypeStruct((feature // depth, pair_width), wide),
            jax.ShapeDtypeStruct((share, width), wide),
            jax.ShapeDtypeStruct((share, depth * own3), wide),
            jax.ShapeDtypeStruct((share, count * gate.shape[2]), wide),
            jax.ShapeDtypeStruct((null_rows, text_width), wide),
            jax.ShapeDtypeStruct((count, depth) + row.shape, wide),
            jax.ShapeDtypeStruct(small.shape[2:], wide),
        ],
        scratch_shapes=[
            pltpu.VMEM(normed.shape, narrow),
            pltpu.VMEM(grads.shape, narrow),
            pltpu.VMEM(words.shape, narrow),
            pltpu.VMEM((depth - 2,) + gate.shape, narrow),
            pltpu.VMEM((depth - 2,) + down.shape, narrow),
            pltpu.SemaphoreType.DMA((3 + 2 * (depth - 2),)),
        ]
        + plane_sums(width)
        + plane_sums(own3)
        + [
            pltpu.VMEM(quarter, narrow),
            pltpu.VMEM(quarter, narrow),
            pltpu.VMEM((depth, share, width), narrow),
            pltpu.VMEM((depth, share, width), narrow),
            pltpu.VMEM((depth, share, own3), narrow),
            pltpu.VMEM((depth, share, own3), narrow),
            gates,
            gates,
            pltpu.VMEM((count, null_rows, text_width), wide),
            pltpu.VMEM((count - 1, null_rows, text_width), wide),
            pltpu.VMEM((depth - 1,) + small.shape[1:], wide),
            pltpu.VMEM(small.shape[1:], wide),
            pltpu.VMEM((count - 1,) + small.shape[2:], wide),
            pltpu.VMEM((depth - 3,) + gate.shape, narrow),
            pltpu.VMEM((depth - 3,) + down.shape, narrow),
            pltpu.VMEM((depth - 3,) + gate.shape, narrow),
            pltpu.VMEM((depth - 3,) + down.shape, narrow),
            pltpu.VMEM((count * depth, share), wide),
            pltpu.VMEM((count * depth, 4 * width), wide),
            pltpu.SemaphoreType.DMA((copies,)),
            pltpu.SemaphoreType.DMA((copies,)),
        ],
        compiler_params=pltpu.CompilerParams(
            collective_id=10, has_side_effects=True, vmem_limit_bytes=60 * 2**20
        ),
        name="final_sums",
    )(flags, text, combined, upstream, normed, grads, *ffn_grads, *held, words, row, small, early, conditions)


def head_lanes(values, head, size):
    lane = lax.broadcasted_iota(jnp.int32, values.shape, 1)
    return jnp.where((lane >= head * size) & (lane < (head + 1) * size), values, 0)


def swap_halves(values, size):
    half = size // 2
    lanes = values.shape[1]
    if lanes % 128 == 0:
        lane = lax.broadcasted_iota(jnp.int32, values.shape, 1)
        ahead = pltpu.roll(values, lanes - half, 1)
        behind = pltpu.roll(values, half, 1)
        return jnp.where(lax.rem(lane, size) < half, ahead, behind)
    parts = []
    for start in range(0, lanes, size):
        parts.append(values[:, start + half : start + size])
        parts.append(values[:, start : start + half])
    return jnp.concatenate(parts, axis=1)


def turn(values, cosine, signed_sine, size):
    return values * cosine + swap_halves(values, size) * signed_sine


def flat(values):
    return values.reshape(-1, values.shape[-1])


def scalar_spec():
    return pl.BlockSpec(memory_space=pltpu.SMEM)


def row_sums(values):
    ones = jnp.ones((8, values.shape[1]), wide)
    return lax.dot_general(
        ones, values, (((1,), (1,)), ((), ())), precision=HIGHEST, preferred_element_type=wide
    )[:1]


def loop(count, body):
    if count == 1:
        body(0)
    else:
        lax.fori_loop(0, count, lambda i, _: (body(i), 0)[1], 0)


def lane_block(index, lanes):
    if isinstance(index, int):
        return pl.ds(index * lanes, lanes)
    return pl.ds(pl.multiple_of(index * lanes, 128), lanes)


def block_rows_of(index, rows):
    if isinstance(index, int):
        return pl.ds(index * rows, rows)
    return pl.ds(pl.multiple_of(index * rows, 128), rows)


def forward_kernel(
    count, depth, size, lanes, spans, lengths, gates, raw_q_hbm, raw_k_hbm, raw_v_hbm, rates, gain_q,
    gain_k, cosine_hbm, sine_hbm, text_own, gate_up, combined, q, k, v, qc, total, cross_total, text, gathered,
    raw_q, raw_k, raw_v, cosine, sine, self_out, staged, send, arrive, local,
):
    links = Transfers(send, arrive)
    late = [
        Late(source, target, local.at[2 + i])
        for i, (source, target) in enumerate(
            zip(
                (raw_v_hbm, raw_q_hbm, raw_k_hbm, cosine_hbm, sine_hbm),
                (raw_v, raw_q, raw_k, cosine, sine),
                strict=True,
            )
        )
    ]
    b, s = lax.axis_index("bucket"), lax.axis_index("seq")
    others = [partner(k) for k in range(1, count)]
    turns = [lax.rem(s + step, depth) for step in range(1, depth)]
    along = [seq_device(place) for place in turns]
    meet(others + along)
    block_rows, own = raw_q.shape[1:]
    rows = depth * block_rows
    width = own * depth
    grid, heads = own // lanes, lanes // size
    scaling = size ** (-0.5)
    words = [
        links.start(text_own.at[place], text.at[s], device)
        for place, device in zip(turns, along, strict=True)
    ]
    text[s] = text_own[s]
    gate_rows, units = gate_up.shape[0], gathered.shape[1] // 2
    half_width = gate_up.shape[1] // 2
    here = pl.ds(pl.multiple_of(b * gate_rows, 16), gate_rows)
    weights, kept = [], []
    for block in range(count):
        target = jnp.bitwise_xor(b, block)
        for half in range(2):
            source = gate_up.at[
                :, pl.ds(pl.multiple_of(half * half_width + target * units, 128), units)
            ]
            landing = gathered.at[here, pl.ds(half * units, units)]
            if block:
                weights.append(links.start(source, landing, others[block - 1]))
            else:
                copy = pltpu.make_async_copy(source, landing, local.at[half])
                copy.start()
                kept.append(copy)
    for copy in late:
        copy.get()
    for block in range(depth):
        v[block_rows_of(block, block_rows)] = raw_v[block].astype(narrow)
    columns = rates[...].T
    for block in range(depth):
        at = block_rows_of(block, block_rows)
        cos, sin = cosine[at], sine[at]
        for group in range(grid):
            span = lane_block(group, lanes)
            norm_q = raw_q[block, :, span] * columns[:, block : block + 1] * gain_q[:, span]
            norm_k = (
                raw_k[block, :, span]
                * columns[:, depth + block : depth + block + 1]
                * gain_k[:, span]
            )
            turned = turn(norm_q, cos, sin, size).astype(narrow).astype(wide)
            q[at, span] = (turned * scaling).astype(narrow)
            qc[at, span] = (norm_q.astype(narrow).astype(wide) * scaling).astype(narrow)
            k[at, span] = turn(norm_k, cos, sin, size).astype(narrow)
    key_index = lax.broadcasted_iota(jnp.int32, (rows, block_rows), 0)

    def attend_self(group):
        span = lane_block(group, lanes)
        value_t = v[:, span].astype(wide).T.astype(narrow)
        for block in range(depth):
            at = block_rows_of(block, block_rows)
            allowed = (key_index >= spans[0, block]) & (key_index < spans[1, block])
            outs = []
            for head in range(heads):
                scores = contract_cols(k[:, span], head_lanes(q[at, span], head, size))
                scores = jnp.where(allowed, scores, NEGATIVE)
                peak = jnp.max(scores, axis=0, keepdims=True)
                shares = jnp.exp(scores - peak)
                mass = jnp.sum(shares, axis=0, keepdims=True)
                part = slice(head * size, (head + 1) * size)
                outs.append(dense(value_t[part], shares.astype(narrow)) / mass)
                total[group, head : head + 1, at] = peak + jnp.log(mass)
            self_out[at, span] = jnp.concatenate(outs, axis=0).T

    loop(grid, attend_self)
    for copy in words:
        copy.wait_recv()
    cap = text.shape[0] * text.shape[3]
    cap_index = lax.broadcasted_iota(jnp.int32, (cap, block_rows), 0)
    results = []
    for step in range(depth):
        block = lax.rem(s + 1 + step, depth)
        at = block_rows_of(block, block_rows)
        clip = spans[2, block]
        live = cap_index < lengths[clip]

        def attend_cross(group):
            span = lane_block(group, lanes)
            text_key = flat(text[:, 0, clip, :, span])
            value_t = flat(text[:, 1, clip, :, span]).astype(wide).T.astype(narrow)
            outs = []
            for head in range(heads):
                scores = contract_cols(text_key, head_lanes(qc[at, span], head, size))
                scores = jnp.where(live, scores, NEGATIVE)
                peak = jnp.max(scores, axis=0, keepdims=True)
                shares = jnp.exp(scores - peak)
                mass = jnp.sum(shares, axis=0, keepdims=True)
                part = slice(head * size, (head + 1) * size)
                gate = gates[group * heads + head]
                outs.append(dense(value_t[part], shares.astype(narrow)) * (gate / mass))
                cross_total[group, head : head + 1, at] = peak + jnp.log(mass)
            staged[step, :, span] = (
                self_out[at, span] + jnp.concatenate(outs, axis=0).T
            ).astype(narrow)

        loop(grid, attend_cross)
        if step < depth - 1:
            results.append(links.start(staged.at[step], combined.at[s], along[step]))
        else:
            combined[s] = staged[step]
    for copy in results + weights:
        copy.wait_recv()
    for copy in kept:
        copy.wait()
    links.finish()


def attention_forward(
    count, depth, size, lanes, scalars, raws, rates, gains, angles, text_own, gate_up
):
    block_rows, own = raws[0].shape[1:]
    rows = depth * block_rows
    grid, heads = own // lanes, lanes // size
    vmem, anywhere = pl.BlockSpec(memory_space=pltpu.VMEM), pl.BlockSpec(memory_space=pl.ANY)
    units = gate_up.shape[1] // (2 * count)
    copies = 2 * (depth - 1) + 2 * (count - 1)
    row_block = jax.ShapeDtypeStruct((rows, own), narrow)
    totals = jax.ShapeDtypeStruct((grid, heads, rows), wide)
    return pl.pallas_call(
        partial(forward_kernel, count, depth, size, lanes),
        in_specs=[scalar_spec()] * 3
        + [anywhere] * 3
        + [vmem] * 3
        + [anywhere] * 2
        + [vmem, anywhere],
        out_specs=[vmem] * 9,
        out_shape=[
            jax.ShapeDtypeStruct((depth, block_rows, own), narrow),
            row_block,
            row_block,
            row_block,
            row_block,
            totals,
            totals,
            jax.ShapeDtypeStruct(text_own.shape, narrow),
            jax.ShapeDtypeStruct((count * gate_up.shape[0], 2 * units), narrow),
        ],
        scratch_shapes=[
            pltpu.VMEM(raws[0].shape, wide),
            pltpu.VMEM(raws[0].shape, wide),
            pltpu.VMEM(raws[0].shape, wide),
            pltpu.VMEM(angles[0].shape, wide),
            pltpu.VMEM(angles[0].shape, wide),
            pltpu.VMEM((rows, own), wide),
            pltpu.VMEM((depth, block_rows, own), narrow),
            pltpu.SemaphoreType.DMA((copies,)),
            pltpu.SemaphoreType.DMA((copies,)),
            pltpu.SemaphoreType.DMA((7,)),
        ],
        compiler_params=pltpu.CompilerParams(
            collective_id=8, has_side_effects=True, vmem_limit_bytes=60 * 2**20
        ),
        name="attention_forward",
    )(*scalars, *raws, rates, *gains, *angles, text_own, gate_up)


def backward_kernel(
    count, depth, size, lanes, spans, lengths, gates, upstream, weight, q, k_hbm, v_hbm, qc, raw_q_hbm,
    raw_k_hbm, rates, gain_q, gain_k, cosine, sine, text, total, cross_total, small, text_gain, text_pairs,
    grad_gate, grad_down,
    projected, gain_sums, dgate, grad_pairs, text_gain_sum, small_out, gate_held, down_held,
    k, v, raw_q, raw_k, cosine_in, sine_in, pairs_in, local, grad_text, go, send_go, dqc, back_q, back_k, parts, send_text, stat,
    stat_in, sum_k, sum_v, send, arrive,
):
    links = Transfers(send, arrive)
    s = lax.axis_index("seq")
    others = [partner(k) for k in range(1, count)]
    turns = [lax.rem(s + step, depth) for step in range(1, depth)]
    along = [seq_device(place) for place in turns]
    late = [
        Late(source, target, local.at[i])
        for i, (source, target) in enumerate(
            zip(
                (k_hbm, v_hbm, raw_q_hbm, raw_k_hbm, cosine, sine, text_pairs),
                (k, v, raw_q, raw_k, cosine_in, sine_in, pairs_in),
                strict=True,
            )
        )
    ]
    cosine, sine = cosine_in, sine_in
    meet(others + along)
    block_rows, own = upstream.shape[0], q.shape[1]
    rows = depth * block_rows
    width = own * depth
    grid, heads = own // lanes, lanes // size
    scaling = size ** (-0.5)

    small_out[0, s] = small[...]
    smalls = [links.start(small, small_out.at[0, s], device) for device in along]

    def grad_out(place):
        at = pl.ds(pl.multiple_of(place * own, 64), own)
        return contract_cols(upstream[...], weight[at]).astype(narrow)

    arriving = []
    for i, (place, device) in enumerate(zip(turns, along, strict=True)):
        send_go[i] = grad_out(place)
        arriving.append(links.start(send_go.at[i], go.at[s], device))
    go[s] = grad_out(s)
    ring = Ring(depth, links)
    weights = GradientRing(ring, (grad_gate, grad_down), None)

    cap_local = text.shape[3]
    cap = text.shape[0] * cap_local
    places = text.shape[2]
    cap_index = lax.broadcasted_iota(jnp.int32, (cap, block_rows), 0)
    clips = []
    for step in range(depth):
        block = lax.rem(s - step + depth, depth)
        if step:
            arriving[step - 1].wait_recv()
        if step == depth - 1:
            weights.first((gate_held, down_held))
        at = block_rows_of(block, block_rows)
        clip = spans[2, block]
        clips.append(clip)
        live = cap_index < lengths[clip]

        def back_cross(group):
            span = lane_block(group, lanes)
            text_key = flat(text[:, 0, clip, :, span])
            text_value = flat(text[:, 1, clip, :, span])
            key_t = text_key.astype(wide).T.astype(narrow)
            grads = []
            for head in range(heads):
                gate = gates[group * heads + head]
                query = head_lanes(qc[at, span], head, size)
                grad = head_lanes(go[block, :, span], head, size)
                scores = contract_cols(text_key, query)
                scores = jnp.where(live, scores, NEGATIVE)
                shares = jnp.exp(scores - cross_total[group, head : head + 1, at])
                grad_shares = contract_cols(text_value, grad)
                row = jnp.sum(grad_shares * shares, axis=0, keepdims=True)
                grad_scores = (gate * (shares * (grad_shares - row))).astype(narrow)
                grad_key = dense(grad_scores, query)
                grad_value = gate * dense(shares.astype(narrow), grad)
                if head == 0:
                    parts[step, 0, :, span] = grad_key
                    parts[step, 1, :, span] = grad_value
                else:
                    parts[step, 0, :, span] += grad_key
                    parts[step, 1, :, span] += grad_value
                part = slice(head * size, (head + 1) * size)
                grads.append(dense(key_t[part], grad_scores) * scaling)
                if step == 0:
                    dgate[group, head : head + 1] = row
                else:
                    dgate[group, head : head + 1] += row
            dqc[at, span] = jnp.concatenate(grads, axis=0).T

        loop(grid, back_cross)
    for which in range(2):
        for place in range(places):
            for target in range(depth):
                at = pl.ds(target * cap_local, cap_local)
                value = jnp.zeros((cap_local, own), wide)
                for step in range(depth):
                    value = value + jnp.where(
                        clips[step] == place, parts[step, which, at], 0.0
                    )
                send_text[target, which, place] = value.astype(narrow)
    words = [
        links.start(send_text.at[place], grad_text.at[s], device)
        for place, device in zip(turns, along, strict=True)
    ]
    grad_text[s] = send_text[s]
    for copy in smalls:
        copy.wait_recv()
    spread = [links.start(small_out.at[0], small_out.at[k], others[k - 1]) for k in range(1, count)]

    for copy in late:
        copy.get()
    key_index = lax.broadcasted_iota(jnp.int32, (rows, block_rows), 0)

    def back_self(group):
        span = lane_block(group, lanes)
        key_t = k[:, span].astype(wide).T.astype(narrow)
        for block in range(depth):
            at = block_rows_of(block, block_rows)
            allowed = (key_index >= spans[0, block]) & (key_index < spans[1, block])
            grads = []
            for head in range(heads):
                query = head_lanes(q[at, span], head, size)
                grad = head_lanes(go[block, :, span], head, size)
                scores = contract_cols(k[:, span], query)
                scores = jnp.where(allowed, scores, NEGATIVE)
                shares = jnp.exp(scores - total[group, head : head + 1, at])
                grad_shares = contract_cols(v[:, span], grad)
                row = jnp.sum(grad_shares * shares, axis=0, keepdims=True)
                grad_scores = (shares * (grad_shares - row)).astype(narrow)
                if block == 0 and head == 0:
                    sum_v[...] = dense(shares.astype(narrow), grad)
                    sum_k[...] = dense(grad_scores, query)
                else:
                    sum_v[...] += dense(shares.astype(narrow), grad)
                    sum_k[...] += dense(grad_scores, query)
                part = slice(head * size, (head + 1) * size)
                grads.append(dense(key_t[part], grad_scores) * scaling)
            back = jnp.concatenate(grads, axis=0).T
            back_q[at, span] = turn(back, cosine[at], -sine[at], size) + dqc[at, span]
        back_k[:, span] = turn(sum_k[...], cosine[...], -sine[...], size)
        for block in range(depth):
            at = block_rows_of(block, block_rows)
            if isinstance(group, int):
                to = pl.ds(2 * own + group * lanes, lanes)
            else:
                to = pl.ds(pl.multiple_of(2 * own + group * lanes, 128), lanes)
            projected[block, :, to] = sum_v[at].astype(narrow)

    loop(grid, back_self)
    columns = rates[...].T
    pairs = ((raw_q, back_q, gain_q), (raw_k, back_k, gain_k))
    for i, (raw, back, gain) in enumerate(pairs):
        gains = jnp.zeros((1, own), wide)
        for block in range(depth):
            place = i * depth + block
            at = block_rows_of(block, block_rows)
            hat = raw[block] * columns[:, place : place + 1]
            gains = gains + jnp.sum(back[at] * hat, axis=0, keepdims=True)
            stat[place : place + 1] = row_sums(back[at] * gain[...] * hat)
        gain_sums[i : i + 1] = gains
    stats = [links.start(stat, stat_in.at[i], device) for i, device in enumerate(along)]
    means = stat[...]
    for i, copy in enumerate(stats):
        copy.wait_recv()
        means = means + stat_in[i]
    means = (means / width).T
    for i, (raw, back, gain) in enumerate(pairs):
        for block in range(depth):
            place = slice(i * depth + block, i * depth + block + 1)
            at = block_rows_of(block, block_rows)
            rate = columns[:, place]
            hat = raw[block] * rate
            projected[block, :, i * own : (i + 1) * own] = (
                rate * (back[at] * gain[...] - hat * means[:, place])
            ).astype(narrow)
    for copy in words:
        copy.wait_recv()

    for target in range(depth):
        text_gain_sum[:, target * own : (target + 1) * own] = jnp.zeros((1, own), wide)
    for place in range(places):
        at = slice(place * cap_local, (place + 1) * cap_local)
        keys = pairs_in[at, :width]
        rate = lax.rsqrt(jnp.mean(keys * keys, axis=1, keepdims=True) + EPSILON)
        mean = jnp.zeros((cap_local, 1), wide)
        for target in range(depth):
            span = slice(target * own, (target + 1) * own)
            hat = pairs_in[at, span] * rate
            grad = grad_text[target, 0, place].astype(wide)
            mean = mean + jnp.sum(grad * text_gain[:, span] * hat, axis=1, keepdims=True)
            text_gain_sum[:, span] += jnp.sum(grad * hat, axis=0, keepdims=True)
        mean = mean / width
        for target in range(depth):
            span = slice(target * own, (target + 1) * own)
            hat = pairs_in[at, span] * rate
            grad = grad_text[target, 0, place].astype(wide)
            grad_pairs[at, span] = (rate * (grad * text_gain[:, span] - hat * mean)).astype(narrow)
            after = slice(width + target * own, width + (target + 1) * own)
            grad_pairs[at, after] = grad_text[target, 1, place]
    for copy in spread + weights.copies:
        copy.wait_recv()
    links.finish()


def attention_backward(
    count, depth, size, lanes, scalars, upstream, weight, saved, raws, rates, gains, angles, text,
    totals, small, text_gain, text_pairs, ffn_grads,
):
    block_rows, own = raws[0].shape[1:]
    rows = depth * block_rows
    grid, heads = own // lanes, lanes // size
    vmem = pl.BlockSpec(memory_space=pltpu.VMEM)
    copies = 4 * (depth - 1) + count - 1 + 2
    cap = text.shape[0] * text.shape[3]
    args = (*scalars, upstream, weight, *saved, *raws, rates, *gains, *angles, text, *totals, small)
    args = args + (text_gain, text_pairs) + tuple(ffn_grads)
    anywhere = pl.BlockSpec(memory_space=pl.ANY)
    specs = [scalar_spec()] * 3 + [vmem] * (len(args) - 3)
    for i in (6, 7, 9, 10, 14, 15, len(args) - 3, len(args) - 2, len(args) - 1):
        specs[i] = anywhere
    return pl.pallas_call(
        partial(backward_kernel, count, depth, size, lanes),
        in_specs=specs,
        out_specs=[vmem] * 8,
        out_shape=[
            jax.ShapeDtypeStruct((depth, block_rows, 3 * own), narrow),
            jax.ShapeDtypeStruct((2, own), wide),
            jax.ShapeDtypeStruct((grid, heads, block_rows), wide),
            jax.ShapeDtypeStruct(text_pairs.shape, narrow),
            jax.ShapeDtypeStruct((1, own * depth), wide),
            jax.ShapeDtypeStruct((count, depth) + small.shape, wide),
            jax.ShapeDtypeStruct(ffn_grads[0].shape[:1] + ffn_grads[0].shape[2:], narrow),
            jax.ShapeDtypeStruct(ffn_grads[1].shape[1:], narrow),
        ],
        scratch_shapes=[
            pltpu.VMEM((rows, own), narrow),
            pltpu.VMEM((rows, own), narrow),
            pltpu.VMEM(raws[0].shape, wide),
            pltpu.VMEM(raws[1].shape, wide),
            pltpu.VMEM(angles[0].shape, wide),
            pltpu.VMEM(angles[1].shape, wide),
            pltpu.VMEM(text_pairs.shape, wide),
            pltpu.SemaphoreType.DMA((7,)),
            pltpu.VMEM(text.shape, narrow),
            pltpu.VMEM((depth, block_rows, own), narrow),
            pltpu.VMEM((depth - 1, block_rows, own), narrow),
            pltpu.VMEM((rows, own), wide),
            pltpu.VMEM((rows, own), wide),
            pltpu.VMEM((rows, own), wide),
            pltpu.VMEM((depth, 2, cap, own), wide),
            pltpu.VMEM(text.shape, narrow),
            pltpu.VMEM((2 * depth, block_rows), wide),
            pltpu.VMEM((depth - 1, 2 * depth, block_rows), wide),
            pltpu.VMEM((rows, lanes), wide),
            pltpu.VMEM((rows, lanes), wide),
            pltpu.SemaphoreType.DMA((copies,)),
            pltpu.SemaphoreType.DMA((copies,)),
        ],
        compiler_params=pltpu.CompilerParams(
            collective_id=9, has_side_effects=True, vmem_limit_bytes=60 * 2**20
        ),
        name="attention_backward",
    )(*args)


def per_device(
    tokens,
    condition,
    captions,
    caption_lengths,
    null_flags,
    slot_buckets,
    null_caption,
    modulation,
    projection,
    text_weight,
    output_weight,
    gate_up,
    down_weight,
    norm_gains,
    head_gains,
    cross_gates,
    cotangent,
):
    count_s, count_b = lax.axis_size("seq"), lax.axis_size("bucket")
    s, b = lax.axis_index("seq"), lax.axis_index("bucket")
    assert count_s % 4 == 0
    local, width = tokens.shape
    heads = cross_gates.shape[0]
    size = width // heads
    own_heads = heads // count_s
    own = width // count_s
    rows = local * count_s
    places, cap_local, text_width = captions.shape
    cap_rows = places * cap_local
    bucket = slot_buckets[0]
    clip_length = jnp.where(
        bucket == 0, rows // 4, jnp.where(bucket == 1, rows // 2, rows)
    ).astype(jnp.int32)

    own_hidden = down_weight.shape[0]
    gate_rows = gate_up.shape[0]
    text_rows = text_weight.shape[0]
    null_rows = lax.dynamic_slice_in_dim(null_caption, s * cap_local, cap_local, 0)
    is_null = null_flags[:, None, None] == 1
    words_own = jnp.where(is_null, null_rows[None], captions).reshape(cap_rows, text_width)
    own_projection = jnp.concatenate(
        [
            lax.dynamic_slice_in_dim(projection, i * width + s * own, own, 1)
            for i in range(3)
        ],
        axis=1,
    )

    silu_cond = jax.nn.silu(condition).astype(narrow)
    mod_width = modulation.shape[1] // count_s
    pieces = silu_cond.astype(wide).reshape(places, count_b, -1).transpose(1, 0, 2)
    my_clip = (s * local) // clip_length
    (
        cond_columns,
        mods,
        own_projection,
        words,
        text_pairs,
        text_own,
        normed,
        raw_q,
        raw_k,
        raw_v,
        rates,
    ) = start_exchange(
        count_b,
        count_s,
        my_clip.astype(jnp.int32)[None],
        pieces,
        lax.dynamic_slice_in_dim(modulation, s * mod_width, mod_width, 1),
        own_projection,
        words_own,
        text_weight,
        tokens,
        norm_gains[:1],
        head_gains[2:],
    )
    own_projection = own_projection.reshape(width, 3 * own)
    modulated = lax.dynamic_index_in_dim(mods, my_clip, 1, keepdims=False).reshape(1, 4 * width)
    tokens_in = tokens.astype(wide)
    _, pre_pull = jax.vjp(pre_attention, tokens_in, modulated, norm_gains)

    gains = [lax.dynamic_slice_in_dim(head_gains[i : i + 1], s * own, own, 1) for i in range(2)]
    inside = lax.rem(jnp.arange(rows, dtype=jnp.int32), clip_length)
    half = size // 2
    frequency = 10000.0 ** (-jnp.arange(half, dtype=wide) / half)
    angles = inside.astype(wide)[:, None] * frequency[None, :]
    lanes = 128 if own % 128 == 0 else own
    block_heads = lanes // size
    cosine = jnp.tile(jnp.cos(angles), (1, 2 * block_heads))
    sine = jnp.tile(
        jnp.concatenate([-jnp.sin(angles), jnp.sin(angles)], axis=1), (1, block_heads)
    )
    tanh_gates = jnp.tanh(cross_gates)
    own_gates = lax.dynamic_slice_in_dim(tanh_gates, s * own_heads, own_heads, 0)
    clip_of = (jnp.arange(count_s, dtype=jnp.int32) * local) // clip_length
    spans = jnp.stack([clip_of * clip_length, (clip_of + 1) * clip_length, clip_of])
    scalars = (spans, caption_lengths, own_gates)
    full_output, text_own = lax.optimization_barrier((output_weight, text_own))
    full_output = lax.all_gather(full_output, "bucket", axis=0, tiled=True)
    combined, *saved, total, cross_total, text_kv, own_gate_up = attention_forward(
        count_b,
        count_s,
        size,
        lanes,
        scalars,
        (raw_q, raw_k, raw_v),
        rates,
        gains,
        (cosine, sine),
        text_own,
        gate_up,
    )
    combined = combined.transpose(1, 0, 2).reshape(local, width)

    attended = dense(combined, full_output)
    (middle, ffn_full), post_pull = jax.vjp(
        post_attention, attended, tokens_in, modulated, norm_gains
    )
    normed_ffn = ffn_full.astype(narrow)

    lowered, plane, gate_values, hidden = ffn_forward(
        count_b, normed_ffn, own_gate_up, down_weight
    )
    mixed, finish_pull = jax.vjp(finish, lowered, middle, modulated, norm_gains)
    grad_lowered, grad_middle, grad_modulated_last, grad_norm_last = finish_pull(
        cotangent.astype(wide)
    )
    grad_lowered_low = grad_lowered.astype(narrow)
    grad_normed_ffn, grad_gate_up, grad_down = ffn_backward(
        count_b, grad_lowered_low, own_gate_up, down_weight, gate_values, plane, hidden
    )
    share = width // (count_b * count_s)
    ffn_grads = (
        grad_gate_up.reshape(count_b, count_s, share, 2 * own_hidden),
        grad_down.reshape(count_s, own_hidden // count_s, width),
    )

    grad_attended, grad_tokens_post, grad_modulated_post, grad_norm_post = post_pull(
        (grad_middle, grad_normed_ffn)
    )
    grad_attended_low = grad_attended.astype(narrow)
    grad_projected, gain_sums, grad_gates, grad_pairs_low, text_gain_sum, early, *held = (
        attention_backward(
            count_b,
            count_s,
            size,
            lanes,
            scalars,
            grad_attended_low,
            full_output,
            saved,
            (raw_q, raw_k),
            rates,
            gains,
            (cosine, sine),
            text_kv,
            (total, cross_total),
            (grad_modulated_post + grad_modulated_last)[:, width:],
            head_gains[2:],
            text_pairs,
            ffn_grads,
        )
    )

    grad_normed, grad_words, grad_text, *held = end_exchange(
        count_b,
        count_s,
        grad_pairs_low,
        text_weight,
        words,
        grad_projected,
        own_projection,
        ffn_grads,
        held,
    )
    grad_tokens_pre, grad_modulated_pre, grad_norm_pre = pre_pull(grad_normed)
    grad_tokens = grad_tokens_pre + grad_tokens_post

    def place(values):
        return lax.dynamic_update_slice_in_dim(jnp.zeros((width,), wide), values, s * own, 0)

    gate_sums = lax.dynamic_update_slice_in_dim(
        jnp.zeros((heads,), wide),
        jnp.sum(grad_gates, axis=2).reshape(own_heads) * (1.0 - own_gates * own_gates),
        s * own_heads,
        0,
    )
    small = jnp.concatenate(
        [
            grad_norm_pre + grad_norm_post + grad_norm_last,
            jnp.stack(
                [
                    place(gain_sums[0]),
                    place(gain_sums[1]),
                    text_gain_sum[0],
                    jnp.zeros((width,), wide),
                ]
            ),
        ],
        axis=0,
    )
    own_clip = (jnp.arange(places, dtype=jnp.int32) == my_clip).astype(wide)
    row = jnp.concatenate(
        [
            jnp.pad(gate_sums, (0, 128 - heads)),
            jnp.pad(own_clip, (0, width - 128 - places)),
        ]
    )
    row = jnp.stack([grad_modulated_pre[0, :width], row], axis=0)
    (
        mod_share,
        down_share,
        text_share,
        output_share,
        proj_share,
        gate_share,
        null_share,
        grad_rows,
        own_sums,
    ) = final_sums(
        count_b,
        count_s,
        null_flags,
        grad_text,
        combined,
        grad_attended_low,
        normed,
        grad_projected,
        ffn_grads,
        held,
        grad_words,
        row,
        small.reshape(8, count_b, count_s, share).transpose(2, 1, 0, 3),
        early,
        lax.dynamic_slice_in_dim(cond_columns, s * share, share, 2),
    )
    null_share = lax.ppermute(
        null_share,
        ("bucket", "seq"),
        [(i * count_s + j, j * count_b + i) for i in range(count_b) for j in range(count_s)],
    )
    grad_words = grad_words.reshape(places, cap_local, text_width).astype(wide)
    grad_captions = jnp.where(is_null, 0.0, grad_words)

    return (
        mixed.astype(narrow),
        grad_tokens,
        grad_captions,
        null_share,
        mod_share,
        proj_share,
        text_share,
        output_share,
        gate_share,
        down_share,
        own_sums[:4],
        own_sums[4:7],
        jnp.sum(grad_rows[:, :, 1, :heads], axis=(0, 1)),
    )


def solution(mesh):
    whole = P(("bucket", "seq"), None)
    shard = P("bucket", None)
    return jax.shard_map(
        per_device,
        mesh=mesh,
        in_specs=(
            whole,
            shard,
            P("bucket", "seq", None),
            P("bucket"),
            P("bucket"),
            P("bucket"),
            P(),
            shard,
            shard,
            shard,
            shard,
            shard,
            shard,
            P(),
            P(),
            P(),
            whole,
        ),
        out_specs=(
            whole,
            whole,
            P("bucket", "seq", None),
            whole,
            whole,
            whole,
            whole,
            whole,
            whole,
            whole,
            P(None, ("bucket", "seq")),
            P(None, ("bucket", "seq")),
            P(),
        ),
        check_vma=False,
    )
```

```python
from functools import partial

import jax
import jax.numpy as jnp
from jax import lax
from jax.experimental import pallas as pl
from jax.experimental.pallas import tpu as pltpu
from jax.sharding import PartitionSpec as P

EPSILON = 1e-06
NEGATIVE = -1e30
HIGHEST = lax.Precision.HIGHEST
wide = jnp.float32
narrow = jnp.bfloat16
VMEM_LIMIT = 50 * 2**20


def rms_norm(values, norm_gain):
    return (
        values * lax.rsqrt(jnp.mean(values * values, axis=-1, keepdims=True) + EPSILON) * norm_gain
    )


def dense(leading, trailing):
    return jnp.dot(leading, trailing, preferred_element_type=wide)


def contract_rows(leading, trailing):
    return lax.dot_general(
        leading, trailing, (((0,), (0,)), ((), ())), preferred_element_type=wide
    )


def contract_cols(leading, trailing):
    return lax.dot_general(
        leading, trailing, (((1,), (1,)), ((), ())), preferred_element_type=wide
    )


def pre_attention(tokens_in, modulated, norm_gains):
    model_width = tokens_in.shape[1]
    return rms_norm(tokens_in, norm_gains[0]) * (1.0 + modulated[:, :model_width])


def text_heads(text_pairs, gain):
    model_width = text_pairs.shape[1] // 2
    return (rms_norm(text_pairs[:, :model_width], gain), text_pairs[:, model_width:])


def post_attention(attended, tokens_in, modulated, norm_gains):
    model_width = tokens_in.shape[1]
    middle = tokens_in + jnp.tanh(modulated[:, model_width : 2 * model_width]) * rms_norm(
        attended, norm_gains[1]
    )
    normed_ffn = rms_norm(middle, norm_gains[2]) * (
        1.0 + modulated[:, 2 * model_width : 3 * model_width]
    )
    return (middle, normed_ffn)


def swiglu(gate_values):
    hidden_width = gate_values.shape[1] // 2
    return jax.nn.silu(gate_values[:, :hidden_width]) * gate_values[:, hidden_width:]


def finish(lowered, middle, modulated, norm_gains):
    model_width = middle.shape[1]
    return middle + jnp.tanh(modulated[:, 3 * model_width :]) * rms_norm(lowered, norm_gains[3])


MESH = pl.DeviceIdType.MESH


class Transfers:
    def __init__(self, send, arrive):
        self.send, self.arrive, self.used = send, arrive, 0
        self.open = []

    def start(self, source, target, device):
        copy = pltpu.make_async_remote_copy(
            src_ref=source,
            dst_ref=target,
            send_sem=self.send.at[self.used],
            recv_sem=self.arrive.at[self.used],
            device_id=device,
            device_id_type=MESH,
        )
        self.used += 1
        copy.start()
        self.open.append(copy)
        return copy

    def finish(self):
        for copy in self.open:
            copy.wait_send()


def meet(devices):
    barrier = pltpu.get_barrier_semaphore()
    for device in devices:
        pl.semaphore_signal(barrier, inc=1, device_id=device, device_id_type=MESH)
    pl.semaphore_wait(barrier, len(devices))


def partner(bits):
    return {"bucket": jnp.bitwise_xor(lax.axis_index("bucket"), bits)}


def outer_bits(count):
    return [1 << i for i in range(1, count.bit_length() - 1)]


def block_index(k, count):
    return (k >> 1) + (k & 1) * (count // 2)


def last_bit(block, order):
    return [bit for bit in order if block & bit][-1]


class PlaneExchange:
    def __init__(
        self, count, links, gathered=None, partial=None, arrived_core=None, arrived_outer=None,
        natural=False,
    ):
        self.count, self.links, self.natural = count, links, natural
        self.index = lax.axis_index("bucket")
        self.gathered, self.partial = gathered, partial
        self.arrived_core, self.arrived_outer = arrived_core, arrived_outer
        bits = outer_bits(count)
        self.orders = (bits, bits[::-1])
        self.outer = [k for k in range(0, count, 2)]
        self.rows = (partial if gathered is None else gathered).shape[1] // 2
        self.coming, self.slots = {}, {}
        self.blocks = [0]

    def part(self, ref, block, half):
        return ref.at[block, pl.ds(half * self.rows, self.rows)]

    def place(self, block):
        return jnp.bitwise_xor(self.index, block) if self.natural else block_index(block, self.count)

    def onward(self, half, block, bit):
        source = self.place(block)
        target = source if self.natural else self.place(block | bit)
        self.coming[half, block | bit] = self.links.start(
            self.part(self.gathered, source, half),
            self.part(self.gathered, target, half),
            partner(bit),
        )

    def forward(self, half, block):
        order = self.orders[half]
        later = order if block == 0 else order[order.index(last_bit(block, order)) + 1 :]
        for bit in later:
            self.onward(half, block, bit)

    def forward_core(self, half, block):
        self.onward(half, block, 1)

    def arrive(self, block):
        for half in range(2):
            self.coming[half, block].wait_recv()

    def begin(self):
        for step in range(len(self.orders[0])):
            for half in range(2):
                self.onward(half, 0, self.orders[half][step])
        for half in range(2):
            self.forward_core(half, 0)

    def run_gather(self, compute, scatter=None):
        self.begin()
        compute([0])
        levels = len(self.orders[0])
        self.arrive(1)
        compute([block_index(1, self.count)])
        if scatter is not None:
            self.send_core(1)
        for level in range(1, levels + 1):
            here = [k for k in self.outer if bin(k).count("1") == level]
            self.forward_level(here)
            if level == 2 and scatter is not None:
                next(scatter)
            compute([block_index(k, self.count) for k in here])
            for k in here:
                self.arrive(k | 1)
            compute([block_index(k | 1, self.count) for k in here])
            for k in here:
                if scatter is not None:
                    self.send_core(k | 1)

    def gather(self):
        self.begin()
        yield
        for level in range(1, len(self.orders[0]) + 1):
            self.forward_level([k for k in self.outer if bin(k).count("1") == level])
            yield
        for block in self.outer:
            self.arrive(block | 1)

    def forward_level(self, here):
        steps = [(half, k) for k in here for half in range(2)]
        steps.sort(
            key=lambda s: [
                self.orders[s[0]].index(bit) for bit in self.orders[s[0]] if s[1] & bit
            ][::-1]
        )
        for half, k in steps:
            self.coming[half, k].wait_recv()
            self.forward(half, k)
            self.forward_core(half, k)

    def send_core(self, block):
        place = self.place(block)
        target = self.arrived_core.at[block >> 1]
        self.slots["core", block & ~1] = self.links.start(self.partial.at[place], target, partner(1))

    def total(self, half, block, slots):
        rows = pl.ds(half * self.rows, self.rows)
        value = self.partial[self.place(block), rows].astype(wide)
        value = value + self.arrived_core[block >> 1, rows].astype(wide)
        for slot in slots:
            value = value + self.arrived_outer[half, slot].astype(wide)
        return value

    def scatter(self, finish):
        slot_of = {}
        waiting = {(half, k): [] for half in range(2) for k in self.outer}
        core_seen = set()
        left = [list(self.outer), list(self.outer)]
        for step in range(len(self.orders[0])):
            jobs = []
            for half in range(2):
                bit = self.orders[half][::-1][step]
                jobs.append([(half, bit, k) for k in left[half] if k & bit])
                left[half] = [k for k in left[half] if not k & bit]
            for pair in zip(*jobs, strict=True):
                for half, bit, k in pair:
                    if k not in core_seen:
                        self.slots["core", k].wait_recv()
                        core_seen.add(k)
                    for copy, _ in waiting[half, k]:
                        copy.wait_recv()
                    rows = pl.ds(half * self.rows, self.rows)
                    total = self.total(half, k, [slot for _, slot in waiting[half, k]])
                    self.partial[self.place(k), rows] = total.astype(narrow)
                    slot = slot_of.setdefault((half, bit, k ^ bit), len([1 for h, *_ in slot_of if h == half]))
                    copy = self.links.start(
                        self.partial.at[self.place(k), rows],
                        self.arrived_outer.at[half, slot],
                        partner(bit),
                    )
                    waiting[half, k ^ bit].append((copy, slot))
                yield
        if 0 not in core_seen:
            self.slots["core", 0].wait_recv()
        for half in range(2):
            for copy, _ in waiting[half, 0]:
                copy.wait_recv()
            finish(half, self.total(half, 0, [slot for _, slot in waiting[half, 0]]))


def plane_partners(count):
    return [partner(bit) for bit in outer_bits(count) + [1]]


def plane_copies(count):
    outer = count // 2
    return 2 * (outer - 1) + 2 * outer, outer + 2 * (outer - 1)


def spans(blocks):
    runs = []
    for block in sorted(blocks):
        if runs and runs[-1][1] == block:
            runs[-1][1] = block + 1
        else:
            runs.append([block, block + 1])
    return runs


def each(blocks, body):
    for first, end in spans(blocks):
        if end - first == 1:
            body(first)
        else:
            lax.fori_loop(first, end, lambda i, _: (body(i), 0)[1], 0)


class Late:
    def __init__(self, source, target, semaphore):
        self.copy = pltpu.make_async_copy(source, target, semaphore)
        self.target, self.there = target, False
        self.copy.start()

    def get(self):
        if not self.there:
            self.copy.wait()
            self.there = True
        return self.target


def ffn_kernel(
    count, x, gate_up_hbm, down_hbm, lowered, plane_out, values_out, hidden_out,
    gate_up, down, plane, partial, core, outer, values, hidden, send, arrive, local,
):
    links = Transfers(send, arrive)
    late = Late(gate_up_hbm, gate_up, local.at[3]), Late(down_hbm, down, local.at[4])
    meet(plane_partners(count))
    units = down.shape[0]
    wide_block = 256
    plane[0] = x[...]
    saved = pltpu.make_async_copy(plane, plane_out, local.at[0])

    def compute(blocks):
        for copy in late:
            copy.get()

        def one(place):
            for start in range(0, units, wide_block):
                columns = slice(start, start + wide_block)
                after = slice(units + start, units + start + wide_block)
                gate = dense(plane[place], gate_up[:, columns])
                up = dense(plane[place], gate_up[:, after])
                values[place, :, columns] = gate
                values[place, :, after] = up
                hidden[place, :, columns] = (jax.nn.silu(gate) * up).astype(narrow)
            partial[place] = dense(hidden[place], down[...]).astype(narrow)

        each(blocks, one)

    exchange = PlaneExchange(count, links, plane, partial, core, outer)
    def finish(half, total):
        lowered[pl.ds(half * exchange.rows, exchange.rows)] = total

    sums = exchange.scatter(finish)
    exchange.run_gather(compute, sums)
    saved.start()
    kept = pltpu.make_async_copy(values, values_out, local.at[1])
    kept.start()
    held = pltpu.make_async_copy(hidden, hidden_out, local.at[2])
    held.start()

    for _ in sums:
        pass
    saved.wait()
    kept.wait()
    held.wait()
    links.finish()


def plane_scratch(count, rows, width):
    outer = count // 2
    return [
        pltpu.VMEM((count, rows, width), narrow),
        pltpu.VMEM((count, rows, width), narrow),
        pltpu.VMEM((outer, rows, width), narrow),
        pltpu.VMEM((2, outer - 1, rows // 2, width), narrow),
    ]


def ffn_forward(count, x, gate_up, down):
    rows, width = x.shape
    units = down.shape[0]
    copies = sum(plane_copies(count))
    vmem, anywhere = pl.BlockSpec(memory_space=pltpu.VMEM), pl.BlockSpec(memory_space=pl.ANY)
    return pl.pallas_call(
        partial(ffn_kernel, count),
        in_specs=[vmem] + [anywhere] * 2,
        out_specs=[vmem] + [anywhere] * 3,
        out_shape=[
            jax.ShapeDtypeStruct((rows, width), wide),
            jax.ShapeDtypeStruct((count, rows, width), narrow),
            jax.ShapeDtypeStruct((count, rows, 2 * units), wide),
            jax.ShapeDtypeStruct((count, rows, units), narrow),
        ],
        scratch_shapes=[pltpu.VMEM(gate_up.shape, narrow), pltpu.VMEM(down.shape, narrow)]
        + plane_scratch(count, rows, width)
        + [
            pltpu.VMEM((count, rows, 2 * units), wide),
            pltpu.VMEM((count, rows, units), narrow),
            pltpu.SemaphoreType.DMA((copies,)),
            pltpu.SemaphoreType.DMA((copies,)),
            pltpu.SemaphoreType.DMA((5,)),
        ],
        compiler_params=pltpu.CompilerParams(
            collective_id=1, has_side_effects=True, vmem_limit_bytes=60 * 2**20
        ),
        name="ffn_forward",
    )(x, gate_up, down)

def ffn_back_kernel(
    count, g, gate_up_hbm, down_hbm, values_in, x_in, hidden_in, grad_normed, grad_gate_up,
    grad_down, gate_up, down, plane, partial, core, outer, values, grads, taken, send, arrive,
    local,
):
    links = Transfers(send, arrive)
    late = Late(down_hbm, down, local.at[4]), Late(gate_up_hbm, gate_up, local.at[3])
    fetch = pltpu.make_async_copy(values_in, values, local.at[2])
    fetch.start()
    meet(plane_partners(count))
    units, width = down.shape
    wide_block = 256
    plane[0] = g[...]
    fetched = []

    def compute(places):
        if not fetched:
            fetch.wait()
            fetched.append(True)
            for copy in late:
                copy.get()

        def one(place):
            for start in range(0, units, wide_block):
                columns = slice(start, start + wide_block)
                after = slice(units + start, units + start + wide_block)
                back = contract_cols(plane[place], down[columns])
                gate, up = values[place, :, columns], values[place, :, after]
                sigma = jax.nn.sigmoid(gate)
                grads[place, :, columns] = (
                    back * up * (sigma * (1.0 + gate * (1.0 - sigma)))
                ).astype(narrow)
                grads[place, :, after] = (back * (gate * sigma)).astype(narrow)
            partial[place] = contract_cols(grads[place], gate_up[...]).astype(narrow)

        each(places, one)

    exchange = PlaneExchange(count, links, plane, partial, core, outer)

    def finish(half, total):
        grad_normed[pl.ds(half * exchange.rows, exchange.rows)] = total

    sums = exchange.scatter(finish)
    exchange.run_gather(compute, sums)

    jobs = [(x_in, grads, grad_gate_up, i) for i in range(width // wide_block)]
    jobs += [(hidden_in, plane, grad_down, i) for i in range(units // wide_block)]

    def take(number):
        source, _, _, i = jobs[number]
        columns = pl.ds(i * wide_block, wide_block)
        return pltpu.make_async_copy(
            source.at[:, :, columns], taken.at[number % 2], local.at[number % 2]
        )

    def work(number):
        if number + 1 < len(jobs):
            take(number + 1).start()
        take(number).wait()
        _, upstream, out, i = jobs[number]
        for start in range(0, upstream.shape[2], 512):
            columns = slice(start, start + 512)
            out[i * wide_block : (i + 1) * wide_block, columns] = contract_rows(
                flat(taken[number % 2]), flat(upstream[:, :, columns])
            ).astype(narrow)

    take(0).start()
    done = 0
    for _ in sums:
        for number in range(done, min(done + 3, len(jobs))):
            work(number)
            done += 1
    for number in range(done, len(jobs)):
        work(number)
    links.finish()


class GradientRing:
    def __init__(self, ring, own, held):
        self.ring, self.own, self.held = ring, own, held
        self.copies, self.pieces = [], {}

    def piece(self, which, step):
        place = self.ring.source(step + 1)
        return self.own[0].at[:, place] if which == 0 else self.own[1].at[place]

    def fetch(self, first, targets, semaphores):
        for slot in range(targets[0].shape[0]):
            for which in range(2):
                self.pieces[which, first + slot] = Late(
                    self.piece(which, first + slot),
                    targets[which].at[slot],
                    semaphores.at[2 * slot + which],
                )

    def first(self, landing):
        for which in range(2):
            self.copies.append(
                self.ring.links.start(self.piece(which, 0), landing[which], self.ring.right)
            )

    def arrived(self):
        for copy in self.copies:
            copy.wait_recv()
        self.copies = []

    def value(self, which, step):
        piece = self.pieces[which, step].get()
        return piece[...].astype(wide) + self.held[which][...].astype(wide)

    def onward(self, step, going, landing):
        self.arrived()
        for which in range(2):
            going[which][...] = self.value(which, step).astype(narrow)
            self.copies.append(
                self.ring.links.start(going[which], landing[which], self.ring.right)
            )
        self.held = landing


def ffn_backward(count, g, gate_up, down, values, x, hidden):
    rows, width = g.shape
    units = down.shape[0]
    copies = sum(plane_copies(count))
    vmem, anywhere = pl.BlockSpec(memory_space=pltpu.VMEM), pl.BlockSpec(memory_space=pl.ANY)
    return pl.pallas_call(
        partial(ffn_back_kernel, count),
        in_specs=[vmem] + [anywhere] * 5,
        out_specs=[vmem] * 3,
        out_shape=[
            jax.ShapeDtypeStruct((rows, width), wide),
            jax.ShapeDtypeStruct((width, 2 * units), narrow),
            jax.ShapeDtypeStruct((units, width), narrow),
        ],
        scratch_shapes=[pltpu.VMEM(gate_up.shape, narrow), pltpu.VMEM(down.shape, narrow)]
        + plane_scratch(count, rows, width)
        + [
            pltpu.VMEM((count, rows, 2 * units), wide),
            pltpu.VMEM((count, rows, 2 * units), narrow),
            pltpu.VMEM((2, count, rows, 256), narrow),
            pltpu.SemaphoreType.DMA((copies,)),
            pltpu.SemaphoreType.DMA((copies,)),
            pltpu.SemaphoreType.DMA((5,)),
        ],
        compiler_params=pltpu.CompilerParams(
            collective_id=2, has_side_effects=True, vmem_limit_bytes=62 * 2**20
        ),
        name="ffn_backward",
    )(g, gate_up, down, values, x, hidden)


def seq_device(index):
    return {"seq": index}


class Ring:
    def __init__(self, depth, links):
        self.depth, self.links = depth, links
        self.index = lax.axis_index("seq")
        self.right = seq_device(lax.rem(self.index + 1, depth))
        self.left = seq_device(lax.rem(self.index + depth - 1, depth))

    def source(self, step):
        return lax.rem(self.index - step + 2 * self.depth, self.depth)


def start_kernel(
    count, depth, clip, pieces, modulation, shard, words, text_hbm, x, gain, text_gain,
    got, mods, projection, spread, pairs, text_own, normed, q, k, v, rates,
    text, columns, local, product, back, stat, stat_in, partial, core, outer, send, arrive,
):
    links = Transfers(send, arrive)
    late = Late(text_hbm, text, local.at[0])
    mod_width = columns.shape[1]
    at = pl.multiple_of(lax.axis_index("seq") * mod_width, 128)
    own_columns = Late(modulation.at[:, pl.ds(at, mod_width)], columns, local.at[1])
    ring = Ring(depth, links)
    b, s = lax.axis_index("bucket"), lax.axis_index("seq")
    others = [partner(k) for k in range(1, count)]
    along = [seq_device(lax.rem(s + step, depth)) for step in range(1, depth)]
    meet(others + along)
    first = [
        links.start(pieces.at[jnp.bitwise_xor(b, k)], got.at[k], others[k - 1])
        for k in range(1, count)
    ]
    got[0] = pieces[b]
    feature, width = text.shape

    def features(target):
        return words.at[:, pl.ds(pl.multiple_of(target * feature, 128), feature)]

    projection[b] = shard[...]
    spread[b] = words[:, pl.ds(pl.multiple_of(b * feature, 128), feature)]
    for copy in first:
        copy.wait_recv()
    own_columns.get()
    for block in range(count):
        product[block] = dense(got[block].astype(narrow), columns[...])
    second = [
        links.start(product.at[block], back.at[block - 1], others[block - 1])
        for block in range(1, count)
    ]
    shards = PlaneExchange(count, links, projection, natural=True).gather()
    next(shards)
    far = {}
    for block in sorted(range(1, count), key=lambda block: (bin(block >> 1).count("1"), block & 1)):
        far[block] = links.start(
            features(jnp.bitwise_xor(b, block)), spread.at[b], others[block - 1]
        )

    total = product[0]
    for i, copy in enumerate(second):
        copy.wait_recv()
        total = total + back[i]
    mods[s] = total
    third = [links.start(mods.at[s], mods.at[s], device) for device in along]
    for copy in third:
        copy.wait_recv()
    places = mods.shape[1]
    parts = []
    for i in range(depth // 4):
        part = jnp.zeros((1, mods.shape[2]), wide)
        for place in range(places):
            part = part + jnp.where(clip[0] == place, mods[i, place : place + 1], 0.0)
        parts.append(part)
    scale = parts[0] if len(parts) == 1 else jnp.concatenate(parts, axis=1)
    value = x[...].astype(wide)
    rate = lax.rsqrt(jnp.mean(value * value, axis=1, keepdims=True) + EPSILON)
    normed[s] = (value * rate * gain[0:1] * (1.0 + scale)).astype(narrow)
    moving = [links.start(normed.at[s], normed.at[s], ring.right)]
    next(shards)

    exchange = PlaneExchange(count, links, None, partial, core, outer)

    def pair(block):
        if block:
            far[block].wait_recv()
        source = spread[jnp.bitwise_xor(b, block)]
        place = block_index(block, count)
        for start in range(0, width, 512):
            span = slice(start, start + 512)
            partial[place, :, span] = dense(source, text[:, span]).astype(narrow)
        if block & 1:
            exchange.send_core(block)

    def finish(half, total):
        pairs[pl.ds(half * exchange.rows, exchange.rows)] = total
        keys = total[:, : width // 2]
        rate = lax.rsqrt(jnp.mean(keys * keys, axis=1, keepdims=True) + EPSILON)
        kinds = (keys * rate * text_gain[2:3]).astype(narrow), total[:, width // 2 :].astype(narrow)
        cap_local, part = text_own.shape[3:]
        for kind, value in enumerate(kinds):
            for i in range(exchange.rows // cap_local):
                place = half * (exchange.rows // cap_local) + i
                rows = slice(i * cap_local, (i + 1) * cap_local)
                for target in range(depth):
                    text_own[target, kind, place] = value[
                        rows, target * part : (target + 1) * part
                    ]

    late.get()
    sums = exchange.scatter(finish)
    order = sorted(exchange.outer, key=lambda block: (bin(block).count("1"), block))
    order = order[1:] + order[:1]
    levels = len(exchange.orders[0])
    for block in order[:levels]:
        pair(block | 1)
        pair(block)
    own = q.shape[2]

    def project(step):
        place = ring.source(step)
        for i, out in enumerate((q, k, v)):
            span = slice(i * own, (i + 1) * own)
            weight = projection[:, :, span]
            out[place] = dense(normed[place], flat(weight))

    def onward(step):
        moving[-1].wait_recv()
        place = ring.source(step)
        if step < depth - 1:
            moving.append(links.start(normed.at[place], normed.at[place], ring.right))

    next(sums)
    onward(1)
    for block in order[levels:]:
        pair(block | 1)
        pair(block)
    next(sums)
    for _ in shards:
        pass
    project(0)
    project(1)
    for step in range(2, depth - 1):
        onward(step)
        project(step)
    next(sums)
    onward(depth - 1)
    project(depth - 1)
    for i, raw in enumerate((q, k)):
        for block in range(depth):
            place = i * depth + block
            stat[place : place + 1] = row_sums(raw[block] * raw[block])
    stats = [links.start(stat, stat_in.at[i], device) for i, device in enumerate(along)]
    for _ in sums:
        pass
    squares = stat[...]
    for i, copy in enumerate(stats):
        copy.wait_recv()
        squares = squares + stat_in[i]
    rates[...] = lax.rsqrt(squares / (own * depth) + EPSILON)
    links.finish()


def start_exchange(
    count, depth, clip, pieces, modulation, shard, words, text, x, gain, text_gain
):
    vmem, anywhere = pl.BlockSpec(memory_space=pltpu.VMEM), pl.BlockSpec(memory_space=pl.ANY)
    rows, width = x.shape
    own = shard.shape[1] // 3
    cap_rows, pair_width = words.shape[0], text.shape[1]
    places, mod_width = pieces.shape[1], modulation.shape[1] // depth
    copies = sum(plane_copies(count)) + 3 * (count - 1) + 3 * (depth - 1)
    raw = jax.ShapeDtypeStruct((depth, rows, own), wide)
    return pl.pallas_call(
        partial(start_kernel, count, depth),
        in_specs=[scalar_spec(), vmem, anywhere, vmem, vmem, anywhere] + [vmem] * 3,
        out_specs=[vmem] * 11,
        out_shape=[
            jax.ShapeDtypeStruct(pieces.shape, wide),
            jax.ShapeDtypeStruct((depth, places, mod_width), wide),
            jax.ShapeDtypeStruct((count,) + shard.shape, narrow),
            jax.ShapeDtypeStruct((count, cap_rows, words.shape[1] // count), narrow),
            jax.ShapeDtypeStruct((cap_rows, pair_width), wide),
            jax.ShapeDtypeStruct((depth, 2, places, cap_rows // places, own), narrow),
            jax.ShapeDtypeStruct((depth, rows, width), narrow),
            raw,
            raw,
            raw,
            jax.ShapeDtypeStruct((2 * depth, rows), wide),
        ],
        scratch_shapes=[
            pltpu.VMEM(text.shape, narrow),
            pltpu.VMEM((modulation.shape[0], mod_width), narrow),
            pltpu.SemaphoreType.DMA((2,)),
            pltpu.VMEM((count, places, mod_width), wide),
            pltpu.VMEM((count - 1, places, mod_width), wide),
            pltpu.VMEM((2 * depth, rows), wide),
            pltpu.VMEM((depth - 1, 2 * depth, rows), wide),
        ]
        + plane_scratch(count, cap_rows, pair_width)[1:]
        + [pltpu.SemaphoreType.DMA((copies,)), pltpu.SemaphoreType.DMA((copies,))],
        compiler_params=pltpu.CompilerParams(
            collective_id=4, has_side_effects=True, vmem_limit_bytes=60 * 2**20
        ),
        name="start_exchange",
    )(clip, pieces, modulation, shard, words, text, x, gain, text_gain)


def end_kernel(
    count, depth, pairs, text_hbm, words_hbm, grads_hbm, projection_hbm, grad_gate, grad_down,
    gate_held, down_held, normed, grad_words, grad_weight, gate_next, down_next,
    text, words, grads, projection, gate_piece, down_piece, local,
    plane, back, send_sum, ring_in, total, gate_go, down_go, send, arrive,
):
    links = Transfers(send, arrive)
    ring = Ring(depth, links)
    late = [
        Late(source, target, local.at[2 + i])
        for i, (source, target) in enumerate(
            zip(
                (text_hbm, words_hbm, grads_hbm, projection_hbm),
                (text, words, grads, projection),
                strict=True,
            )
        )
    ]
    weights = GradientRing(ring, (grad_gate, grad_down), (gate_held, down_held))
    weights.fetch(1, (gate_piece, down_piece), local)
    b = lax.axis_index("bucket")
    others = [partner(k) for k in range(1, count)]
    meet(others + [ring.left, ring.right])
    plane[0] = pairs[...]
    exchange = PlaneExchange(count, links, plane)
    feature, width = text.shape
    own_columns = pl.ds(pl.multiple_of(b * feature, 128), feature)
    moving = []

    def round_step(step):
        value = contract_cols(grads[ring.source(step + 1)], projection[...])
        if step > 0:
            moving[-1].wait_recv()
            value = value + ring_in[step - 1].astype(wide)
        if step < depth - 1:
            send_sum[step] = value.astype(narrow)
            moving.append(links.start(send_sum.at[step], ring_in.at[step], ring.right))
        else:
            normed[...] = value

    steps = [0]

    def advance():
        if steps[0] < depth - 1:
            round_step(steps[0])
            steps[0] += 1
            if steps[0] == depth - 1:
                weights.onward(1, (gate_go, down_go), (gate_next, down_next))

    arriving = []
    blocks = [None] * count
    for block in range(count):
        blocks[block_index(block, count)] = block

    def compute(places):
        for copy in late:
            copy.get()
        for place in places:
            block = blocks[place]
            features = words[jnp.bitwise_xor(b, block)].astype(wide).T.astype(narrow)
            for first in range(0, width, 512):
                columns = slice(first, first + 512)
                part = dense(features, plane[place, :, columns])
                if place == 0:
                    total[:, columns] = part
                else:
                    total[:, columns] += part
            value = contract_cols(plane[place], text[...]).astype(narrow)
            if block == 0:
                grad_words[:, own_columns] = value
            else:
                back[place - 1] = value
                arriving.append(
                    links.start(
                        back.at[place - 1], grad_words.at[:, own_columns], others[block - 1]
                    )
                )
        advance()

    exchange.run_gather(compute)
    while steps[0] < depth - 1:
        advance()
    round_step(depth - 1)
    grad_weight[...] = total[...].astype(narrow)
    for copy in arriving + weights.copies:
        copy.wait_recv()
    links.finish()


def end_exchange(count, depth, pairs, text, words, grads, projection, ffn_grads, held):
    vmem = pl.BlockSpec(memory_space=pltpu.VMEM)
    cap_rows, pair_width = pairs.shape
    feature = text.shape[0]
    rows, width = grads.shape[1], projection.shape[0]
    copies = plane_copies(count)[0] + count - 1 + depth - 1 + 2
    return pl.pallas_call(
        partial(end_kernel, count, depth),
        in_specs=[vmem] + [pl.BlockSpec(memory_space=pl.ANY)] * 6 + [vmem] * 2,
        out_specs=[vmem] * 5,
        out_shape=[
            jax.ShapeDtypeStruct((rows, width), wide),
            jax.ShapeDtypeStruct((cap_rows, count * feature), narrow),
            jax.ShapeDtypeStruct((feature, pair_width), narrow),
            jax.ShapeDtypeStruct(held[0].shape, narrow),
            jax.ShapeDtypeStruct(held[1].shape, narrow),
        ],
        scratch_shapes=[
            pltpu.VMEM(text.shape, narrow),
            pltpu.VMEM(words.shape, narrow),
            pltpu.VMEM(grads.shape, narrow),
            pltpu.VMEM(projection.shape, narrow),
            pltpu.VMEM((1,) + held[0].shape, narrow),
            pltpu.VMEM((1,) + held[1].shape, narrow),
            pltpu.SemaphoreType.DMA((6,)),
            pltpu.VMEM((count, cap_rows, pair_width), narrow),
            pltpu.VMEM((count - 1, cap_rows, feature), narrow),
            pltpu.VMEM((depth - 1, rows, width), narrow),
            pltpu.VMEM((depth - 1, rows, width), narrow),
            pltpu.VMEM((feature, pair_width), wide),
            pltpu.VMEM(held[0].shape, narrow),
            pltpu.VMEM(held[1].shape, narrow),
            pltpu.SemaphoreType.DMA((copies,)),
            pltpu.SemaphoreType.DMA((copies,)),
        ],
        compiler_params=pltpu.CompilerParams(
            collective_id=5, has_side_effects=True, vmem_limit_bytes=63 * 2**20
        ),
        name="end_exchange",
    )(pairs, text, words, grads, projection, *ffn_grads, *held)


def sum_kernel(
    count, depth, flags, text, combined, upstream, normed_hbm, grads_hbm, grad_gate, grad_down,
    gate_held, down_held, words_hbm, row, small, early, conditions, mod_share, down_share, text_share, output_share, proj_share, gate_share, null_share, rows_out, small_out,
    normed, grads, words, gate_piece, down_piece, local, out_part, out_core, out_outer, proj_part, proj_core, proj_outer, send_low, low_in, out_go,
    out_come, proj_go, proj_come, gate, gate_come, null, null_come, small_come, small_go,
    small_land, gate_go, down_go, gate_land, down_land, cond_rows, all_rows, send, arrive,
):
    links = Transfers(send, arrive)
    ring = Ring(depth, links)
    late = [
        Late(source, target, local.at[i])
        for i, (source, target) in enumerate(
            zip((normed_hbm, grads_hbm, words_hbm), (normed, grads, words), strict=True)
        )
    ]
    weights = GradientRing(ring, (grad_gate, grad_down), (gate_held, down_held))
    weights.fetch(2, (gate_piece, down_piece), local.at[pl.ds(3, 2 * (depth - 2))])
    b, s = lax.axis_index("bucket"), lax.axis_index("seq")
    others = [partner(k) for k in range(1, count)]
    turns = [lax.rem(s + step, depth) for step in range(1, depth)]
    along = [seq_device(place) for place in turns]
    meet(others + along)

    rows_out[0, s] = row[...]
    tiny = []
    for i, (place, device) in enumerate(zip(turns, along, strict=True)):
        tiny.append(links.start(row, rows_out.at[0, s], device))
        tiny.append(links.start(small.at[place], small_come.at[i], device))

    low_rows = text.shape[0] // depth
    going = []

    def text_step(step):
        rows = pl.ds(pl.multiple_of(ring.source(step + 1) * low_rows, 16), low_rows)
        value = text[rows].astype(wide)
        if step > 0:
            going[-1].wait_recv()
            value = value + low_in[step - 1].astype(wide)
        if step < depth - 1:
            send_low[step] = value.astype(narrow)
            going.append(links.start(send_low.at[step], low_in.at[step], ring.right))
        else:
            text_share[...] = value

    def weights_step(step):
        slot = step - 2
        weights.onward(
            step,
            (gate_go.at[slot], down_go.at[slot]),
            (gate_land.at[slot], down_land.at[slot]),
        )

    text_step(0)
    weights_step(2)

    share = out_go.shape[1]
    pair = 2 * out_part.shape[1]

    def fill(part, leading, trailing):
        for first in range(0, count, 2):
            value = contract_rows(leading[:, first // 2 * pair : (first // 2 + 1) * pair], trailing)
            value = value.astype(narrow)
            part[first] = value[: pair // 2]
            part[first + 1] = value[pair // 2 :]

    def plane_sum(part, core, outer, go):
        exchange = PlaneExchange(count, links, None, part, core, outer, natural=True)
        for block in range(1, count, 2):
            exchange.send_core(block)

        def finish(half, total):
            low = total.astype(narrow)
            for i in range(depth // 2):
                go[half * (depth // 2) + i] = low[i * share : (i + 1) * share]

        return exchange.scatter(finish)

    fill(out_part, combined[...], upstream[...])
    out_sums = plane_sum(out_part, out_core, out_outer, out_go)
    for copy in late:
        copy.get()
    fill(proj_part, flat(normed[...]), flat(grads[...]))
    proj_sums = plane_sum(proj_part, proj_core, proj_outer, proj_go)
    for _ in range(count // 4):
        next(out_sums)
    for _ in range(count // 4):
        next(proj_sums)
    text_step(1)

    places = flags.shape[0]
    cap_local = words.shape[0] // places
    null_rows = null.shape[1]
    for first in range(0, words.shape[1], 512):
        columns = slice(first, first + 512)
        value = jnp.zeros((cap_local, 512), wide)
        for place in range(places):
            part = words[place * cap_local : (place + 1) * cap_local, columns].astype(wide)
            value = value + jnp.where(flags[place] == 1, part, 0.0)
        for k in range(count):
            null[k, :, columns] = value[k * null_rows : (k + 1) * null_rows]
    next(out_sums)
    next(proj_sums)
    nulls = [
        links.start(null.at[jnp.bitwise_xor(b, k)], null_come.at[k - 1], others[k - 1])
        for k in range(1, count)
    ]

    def drain(sums):
        for _ in sums:
            pass

    def seq_sends(go, come):
        come[s] = go[s]
        return [
            links.start(go.at[place], come.at[s], device)
            for place, device in zip(turns, along, strict=True)
        ]

    for step in range(3, depth - 1):
        weights_step(step)
    weights.arrived()
    gate[...] = weights.value(0, depth - 1).astype(narrow)
    far = [
        links.start(gate.at[jnp.bitwise_xor(b, k)], gate_come.at[b], others[k - 1])
        for k in range(1, count)
    ]
    gate_come[b] = gate[b]
    down_share[...] = weights.value(1, depth - 1)
    own_small = small[s]
    for copy in tiny:
        copy.wait_recv()
    for i in range(depth - 1):
        own_small = own_small + small_come[i]
    small_go[...] = own_small
    spread = []
    for k in range(1, count):
        spread.append(links.start(rows_out.at[0], rows_out.at[k], others[k - 1]))
        spread.append(
            links.start(
                small_go.at[jnp.bitwise_xor(b, k)], small_land.at[k - 1], others[k - 1]
            )
        )
    drain(out_sums)
    out_far = seq_sends(out_go, out_come)
    drain(proj_sums)
    proj_far = seq_sends(proj_go, proj_come)
    for step in range(2, depth - 1):
        text_step(step)
    total = null[b]
    for i, copy in enumerate(nulls):
        copy.wait_recv()
        total = total + null_come[i]
    null_share[...] = total
    for copy in spread:
        copy.wait_recv()
    sums = small_go[b]
    for i in range(count - 1):
        sums = sums + small_land[i]
    small_out[...] = sums

    width = row.shape[1]
    for block in range(count):
        for source in range(depth):
            at = slice(block * depth + source, block * depth + source + 1)
            value = jnp.zeros((1, share), wide)
            for place in range(places):
                mark = rows_out[block, source, 1:2, 128 + place : 129 + place]
                value = value + mark * conditions[block, place : place + 1]
            cond_rows[at] = value
            all_rows[at, :width] = rows_out[block, source, 0:1]
            all_rows[at, width:] = early[block, source]
    for first in range(0, 4 * width, 1536):
        columns = slice(first, first + 1536)
        mod_share[:, columns] = lax.dot_general(
            cond_rows[...],
            all_rows[:, columns],
            (((0,), (0,)), ((), ())),
            precision=HIGHEST,
            preferred_element_type=wide,
        )
    for copy in far:
        copy.wait_recv()
    units = gate.shape[2] // 2
    for block in range(count):
        for half in range(2):
            first = half * count * units + block * units
            gate_share[:, first : first + units] = gate_come[
                block, :, half * units : (half + 1) * units
            ].astype(wide)
    for copy in out_far + proj_far:
        copy.wait_recv()
    text_step(depth - 1)
    total = out_come[0].astype(wide)
    for i in range(1, depth):
        total = total + out_come[i].astype(wide)
    output_share[...] = total
    own = proj_come.shape[2] // 3
    for i in range(3):
        for source in range(depth):
            first = i * depth * own + source * own
            proj_share[:, first : first + own] = proj_come[
                source, :, i * own : (i + 1) * own
            ].astype(wide)
    links.finish()


def final_sums(
    count, depth, flags, text, combined, upstream, normed, grads, ffn_grads, held, words, row, small,
    early, conditions,
):
    vmem = pl.BlockSpec(memory_space=pltpu.VMEM)
    feature, pair_width = text.shape
    width = combined.shape[1]
    own3 = grads.shape[2]
    share = width // (count * depth)
    null_rows = words.shape[0] // flags.shape[0] // count
    text_width = words.shape[1]
    outer = count // 2
    block_rows = width // count
    quarter = (depth - 1, feature // depth, pair_width)

    def plane_sums(columns):
        return [
            pltpu.VMEM((count, block_rows, columns), narrow),
            pltpu.VMEM((outer, block_rows, columns), narrow),
            pltpu.VMEM((2, outer - 1, block_rows // 2, columns), narrow),
        ]

    copies = 2 * (depth - 1) + depth - 1 + 2 * plane_copies(count)[1] + 4 * (count - 1)
    copies += 2 * (depth - 1) + 2 * (depth - 3)
    gate, down = held
    gates = pltpu.VMEM(gate.shape, narrow)
    anywhere = pl.BlockSpec(memory_space=pl.ANY)
    return pl.pallas_call(
        partial(sum_kernel, count, depth),
        in_specs=[scalar_spec()]
        + [vmem] * 3
        + [anywhere] * 4
        + [vmem] * 2
        + [anywhere]
        + [vmem] * 4,
        out_specs=[vmem] * 9,
        out_shape=[
            jax.ShapeDtypeStruct((share, 4 * width), wide),
            jax.ShapeDtypeStruct(down.shape, wide),
            jax.ShapeDtypeStruct((feature // depth, pair_width), wide),
            jax.ShapeDtypeStruct((share, width), wide),
            jax.ShapeDtypeStruct((share, depth * own3), wide),
            jax.ShapeDtypeStruct((share, count * gate.shape[2]), wide),
            jax.ShapeDtypeStruct((null_rows, text_width), wide),
            jax.ShapeDtypeStruct((count, depth) + row.shape, wide),
            jax.ShapeDtypeStruct(small.shape[2:], wide),
        ],
        scratch_shapes=[
            pltpu.VMEM(normed.shape, narrow),
            pltpu.VMEM(grads.shape, narrow),
            pltpu.VMEM(words.shape, narrow),
            pltpu.VMEM((depth - 2,) + gate.shape, narrow),
            pltpu.VMEM((depth - 2,) + down.shape, narrow),
            pltpu.SemaphoreType.DMA((3 + 2 * (depth - 2),)),
        ]
        + plane_sums(width)
        + plane_sums(own3)
        + [
            pltpu.VMEM(quarter, narrow),
            pltpu.VMEM(quarter, narrow),
            pltpu.VMEM((depth, share, width), narrow),
            pltpu.VMEM((depth, share, width), narrow),
            pltpu.VMEM((depth, share, own3), narrow),
            pltpu.VMEM((depth, share, own3), narrow),
            gates,
            gates,
            pltpu.VMEM((count, null_rows, text_width), wide),
            pltpu.VMEM((count - 1, null_rows, text_width), wide),
            pltpu.VMEM((depth - 1,) + small.shape[1:], wide),
            pltpu.VMEM(small.shape[1:], wide),
            pltpu.VMEM((count - 1,) + small.shape[2:], wide),
            pltpu.VMEM((depth - 3,) + gate.shape, narrow),
            pltpu.VMEM((depth - 3,) + down.shape, narrow),
            pltpu.VMEM((depth - 3,) + gate.shape, narrow),
            pltpu.VMEM((depth - 3,) + down.shape, narrow),
            pltpu.VMEM((count * depth, share), wide),
            pltpu.VMEM((count * depth, 4 * width), wide),
            pltpu.SemaphoreType.DMA((copies,)),
            pltpu.SemaphoreType.DMA((copies,)),
        ],
        compiler_params=pltpu.CompilerParams(
            collective_id=10, has_side_effects=True, vmem_limit_bytes=60 * 2**20
        ),
        name="final_sums",
    )(flags, text, combined, upstream, normed, grads, *ffn_grads, *held, words, row, small, early, conditions)


def head_lanes(values, head, size):
    lane = lax.broadcasted_iota(jnp.int32, values.shape, 1)
    return jnp.where((lane >= head * size) & (lane < (head + 1) * size), values, 0)


def swap_halves(values, size):
    half = size // 2
    lanes = values.shape[1]
    if lanes % 128 == 0:
        lane = lax.broadcasted_iota(jnp.int32, values.shape, 1)
        ahead = pltpu.roll(values, lanes - half, 1)
        behind = pltpu.roll(values, half, 1)
        return jnp.where(lax.rem(lane, size) < half, ahead, behind)
    parts = []
    for start in range(0, lanes, size):
        parts.append(values[:, start + half : start + size])
        parts.append(values[:, start : start + half])
    return jnp.concatenate(parts, axis=1)


def turn(values, cosine, signed_sine, size):
    return values * cosine + swap_halves(values, size) * signed_sine


def flat(values):
    return values.reshape(-1, values.shape[-1])


def scalar_spec():
    return pl.BlockSpec(memory_space=pltpu.SMEM)


def row_sums(values):
    ones = jnp.ones((8, values.shape[1]), wide)
    return lax.dot_general(
        ones, values, (((1,), (1,)), ((), ())), precision=HIGHEST, preferred_element_type=wide
    )[:1]


def loop(count, body):
    if count == 1:
        body(0)
    else:
        lax.fori_loop(0, count, lambda i, _: (body(i), 0)[1], 0)


def lane_block(index, lanes):
    if isinstance(index, int):
        return pl.ds(index * lanes, lanes)
    return pl.ds(pl.multiple_of(index * lanes, 128), lanes)


def block_rows_of(index, rows):
    if isinstance(index, int):
        return pl.ds(index * rows, rows)
    return pl.ds(pl.multiple_of(index * rows, 128), rows)


def forward_kernel(
    count, depth, size, lanes, spans, lengths, gates, raw_q_hbm, raw_k_hbm, raw_v_hbm, rates, gain_q,
    gain_k, cosine_hbm, sine_hbm, text_own, gate_up, combined, q, k, v, qc, total, cross_total, text, gathered,
    raw_q, raw_k, raw_v, cosine, sine, self_out, staged, send, arrive, local,
):
    links = Transfers(send, arrive)
    late = [
        Late(source, target, local.at[2 + i])
        for i, (source, target) in enumerate(
            zip(
                (raw_v_hbm, raw_q_hbm, raw_k_hbm, cosine_hbm, sine_hbm),
                (raw_v, raw_q, raw_k, cosine, sine),
                strict=True,
            )
        )
    ]
    b, s = lax.axis_index("bucket"), lax.axis_index("seq")
    others = [partner(k) for k in range(1, count)]
    turns = [lax.rem(s + step, depth) for step in range(1, depth)]
    along = [seq_device(place) for place in turns]
    meet(others + along)
    block_rows, own = raw_q.shape[1:]
    rows = depth * block_rows
    width = own * depth
    grid, heads = own // lanes, lanes // size
    scaling = size ** (-0.5)
    words = [
        links.start(text_own.at[place], text.at[s], device)
        for place, device in zip(turns, along, strict=True)
    ]
    text[s] = text_own[s]
    gate_rows, units = gate_up.shape[0], gathered.shape[1] // 2
    half_width = gate_up.shape[1] // 2
    here = pl.ds(pl.multiple_of(b * gate_rows, 16), gate_rows)
    weights, kept = [], []
    for block in range(count):
        target = jnp.bitwise_xor(b, block)
        for half in range(2):
            source = gate_up.at[
                :, pl.ds(pl.multiple_of(half * half_width + target * units, 128), units)
            ]
            landing = gathered.at[here, pl.ds(half * units, units)]
            if block:
                weights.append(links.start(source, landing, others[block - 1]))
            else:
                copy = pltpu.make_async_copy(source, landing, local.at[half])
                copy.start()
                kept.append(copy)
    for copy in late:
        copy.get()
    for block in range(depth):
        v[block_rows_of(block, block_rows)] = raw_v[block].astype(narrow)
    columns = rates[...].T
    for block in range(depth):
        at = block_rows_of(block, block_rows)
        cos, sin = cosine[at], sine[at]
        for group in range(grid):
            span = lane_block(group, lanes)
            norm_q = raw_q[block, :, span] * columns[:, block : block + 1] * gain_q[:, span]
            norm_k = (
                raw_k[block, :, span]
                * columns[:, depth + block : depth + block + 1]
                * gain_k[:, span]
            )
            turned = turn(norm_q, cos, sin, size).astype(narrow).astype(wide)
            q[at, span] = (turned * scaling).astype(narrow)
            qc[at, span] = (norm_q.astype(narrow).astype(wide) * scaling).astype(narrow)
            k[at, span] = turn(norm_k, cos, sin, size).astype(narrow)
    key_index = lax.broadcasted_iota(jnp.int32, (rows, block_rows), 0)

    def attend_self(group):
        span = lane_block(group, lanes)
        value_t = v[:, span].astype(wide).T.astype(narrow)
        for block in range(depth):
            at = block_rows_of(block, block_rows)
            allowed = (key_index >= spans[0, block]) & (key_index < spans[1, block])
            outs = []
            for head in range(heads):
                scores = contract_cols(k[:, span], head_lanes(q[at, span], head, size))
                scores = jnp.where(allowed, scores, NEGATIVE)
                peak = jnp.max(scores, axis=0, keepdims=True)
                shares = jnp.exp(scores - peak)
                mass = jnp.sum(shares, axis=0, keepdims=True)
                part = slice(head * size, (head + 1) * size)
                outs.append(dense(value_t[part], shares.astype(narrow)) / mass)
                total[group, head : head + 1, at] = peak + jnp.log(mass)
            self_out[at, span] = jnp.concatenate(outs, axis=0).T

    loop(grid, attend_self)
    for copy in words:
        copy.wait_recv()
    cap = text.shape[0] * text.shape[3]
    cap_index = lax.broadcasted_iota(jnp.int32, (cap, block_rows), 0)
    results = []
    for step in range(depth):
        block = lax.rem(s + 1 + step, depth)
        at = block_rows_of(block, block_rows)
        clip = spans[2, block]
        live = cap_index < lengths[clip]

        def attend_cross(group):
            span = lane_block(group, lanes)
            text_key = flat(text[:, 0, clip, :, span])
            value_t = flat(text[:, 1, clip, :, span]).astype(wide).T.astype(narrow)
            outs = []
            for head in range(heads):
                scores = contract_cols(text_key, head_lanes(qc[at, span], head, size))
                scores = jnp.where(live, scores, NEGATIVE)
                peak = jnp.max(scores, axis=0, keepdims=True)
                shares = jnp.exp(scores - peak)
                mass = jnp.sum(shares, axis=0, keepdims=True)
                part = slice(head * size, (head + 1) * size)
                gate = gates[group * heads + head]
                outs.append(dense(value_t[part], shares.astype(narrow)) * (gate / mass))
                cross_total[group, head : head + 1, at] = peak + jnp.log(mass)
            staged[step, :, span] = (
                self_out[at, span] + jnp.concatenate(outs, axis=0).T
            ).astype(narrow)

        loop(grid, attend_cross)
        if step < depth - 1:
            results.append(links.start(staged.at[step], combined.at[s], along[step]))
        else:
            combined[s] = staged[step]
    for copy in results + weights:
        copy.wait_recv()
    for copy in kept:
        copy.wait()
    links.finish()


def attention_forward(
    count, depth, size, lanes, scalars, raws, rates, gains, angles, text_own, gate_up
):
    block_rows, own = raws[0].shape[1:]
    rows = depth * block_rows
    grid, heads = own // lanes, lanes // size
    vmem, anywhere = pl.BlockSpec(memory_space=pltpu.VMEM), pl.BlockSpec(memory_space=pl.ANY)
    units = gate_up.shape[1] // (2 * count)
    copies = 2 * (depth - 1) + 2 * (count - 1)
    row_block = jax.ShapeDtypeStruct((rows, own), narrow)
    totals = jax.ShapeDtypeStruct((grid, heads, rows), wide)
    return pl.pallas_call(
        partial(forward_kernel, count, depth, size, lanes),
        in_specs=[scalar_spec()] * 3
        + [anywhere] * 3
        + [vmem] * 3
        + [anywhere] * 2
        + [vmem, anywhere],
        out_specs=[vmem] * 9,
        out_shape=[
            jax.ShapeDtypeStruct((depth, block_rows, own), narrow),
            row_block,
            row_block,
            row_block,
            row_block,
            totals,
            totals,
            jax.ShapeDtypeStruct(text_own.shape, narrow),
            jax.ShapeDtypeStruct((count * gate_up.shape[0], 2 * units), narrow),
        ],
        scratch_shapes=[
            pltpu.VMEM(raws[0].shape, wide),
            pltpu.VMEM(raws[0].shape, wide),
            pltpu.VMEM(raws[0].shape, wide),
            pltpu.VMEM(angles[0].shape, wide),
            pltpu.VMEM(angles[0].shape, wide),
            pltpu.VMEM((rows, own), wide),
            pltpu.VMEM((depth, block_rows, own), narrow),
            pltpu.SemaphoreType.DMA((copies,)),
            pltpu.SemaphoreType.DMA((copies,)),
            pltpu.SemaphoreType.DMA((7,)),
        ],
        compiler_params=pltpu.CompilerParams(
            collective_id=8, has_side_effects=True, vmem_limit_bytes=60 * 2**20
        ),
        name="attention_forward",
    )(*scalars, *raws, rates, *gains, *angles, text_own, gate_up)


def backward_kernel(
    count, depth, size, lanes, spans, lengths, gates, upstream, weight, q, k_hbm, v_hbm, qc, raw_q_hbm,
    raw_k_hbm, rates, gain_q, gain_k, cosine, sine, text, total, cross_total, small, text_gain, text_pairs,
    grad_gate, grad_down,
    projected, gain_sums, dgate, grad_pairs, text_gain_sum, small_out, gate_held, down_held,
    k, v, raw_q, raw_k, cosine_in, sine_in, pairs_in, local, grad_text, go, send_go, dqc, back_q, back_k, parts, send_text, stat,
    stat_in, sum_k, sum_v, send, arrive,
):
    links = Transfers(send, arrive)
    s = lax.axis_index("seq")
    others = [partner(k) for k in range(1, count)]
    turns = [lax.rem(s + step, depth) for step in range(1, depth)]
    along = [seq_device(place) for place in turns]
    late = [
        Late(source, target, local.at[i])
        for i, (source, target) in enumerate(
            zip(
                (k_hbm, v_hbm, raw_q_hbm, raw_k_hbm, cosine, sine, text_pairs),
                (k, v, raw_q, raw_k, cosine_in, sine_in, pairs_in),
                strict=True,
            )
        )
    ]
    cosine, sine = cosine_in, sine_in
    meet(others + along)
    block_rows, own = upstream.shape[0], q.shape[1]
    rows = depth * block_rows
    width = own * depth
    grid, heads = own // lanes, lanes // size
    scaling = size ** (-0.5)

    small_out[0, s] = small[...]
    smalls = [links.start(small, small_out.at[0, s], device) for device in along]

    def grad_out(place):
        at = pl.ds(pl.multiple_of(place * own, 64), own)
        return contract_cols(upstream[...], weight[at]).astype(narrow)

    arriving = []
    for i, (place, device) in enumerate(zip(turns, along, strict=True)):
        send_go[i] = grad_out(place)
        arriving.append(links.start(send_go.at[i], go.at[s], device))
    go[s] = grad_out(s)
    ring = Ring(depth, links)
    weights = GradientRing(ring, (grad_gate, grad_down), None)

    cap_local = text.shape[3]
    cap = text.shape[0] * cap_local
    places = text.shape[2]
    cap_index = lax.broadcasted_iota(jnp.int32, (cap, block_rows), 0)
    clips = []
    for step in range(depth):
        block = lax.rem(s - step + depth, depth)
        if step:
            arriving[step - 1].wait_recv()
        if step == depth - 1:
            weights.first((gate_held, down_held))
        at = block_rows_of(block, block_rows)
        clip = spans[2, block]
        clips.append(clip)
        live = cap_index < lengths[clip]

        def back_cross(group):
            span = lane_block(group, lanes)
            text_key = flat(text[:, 0, clip, :, span])
            text_value = flat(text[:, 1, clip, :, span])
            key_t = text_key.astype(wide).T.astype(narrow)
            grads = []
            for head in range(heads):
                gate = gates[group * heads + head]
                query = head_lanes(qc[at, span], head, size)
                grad = head_lanes(go[block, :, span], head, size)
                scores = contract_cols(text_key, query)
                scores = jnp.where(live, scores, NEGATIVE)
                shares = jnp.exp(scores - cross_total[group, head : head + 1, at])
                grad_shares = contract_cols(text_value, grad)
                row = jnp.sum(grad_shares * shares, axis=0, keepdims=True)
                grad_scores = (gate * (shares * (grad_shares - row))).astype(narrow)
                grad_key = dense(grad_scores, query)
                grad_value = gate * dense(shares.astype(narrow), grad)
                if head == 0:
                    parts[step, 0, :, span] = grad_key
                    parts[step, 1, :, span] = grad_value
                else:
                    parts[step, 0, :, span] += grad_key
                    parts[step, 1, :, span] += grad_value
                part = slice(head * size, (head + 1) * size)
                grads.append(dense(key_t[part], grad_scores) * scaling)
                if step == 0:
                    dgate[group, head : head + 1] = row
                else:
                    dgate[group, head : head + 1] += row
            dqc[at, span] = jnp.concatenate(grads, axis=0).T

        loop(grid, back_cross)
    for which in range(2):
        for place in range(places):
            for target in range(depth):
                at = pl.ds(target * cap_local, cap_local)
                value = jnp.zeros((cap_local, own), wide)
                for step in range(depth):
                    value = value + jnp.where(
                        clips[step] == place, parts[step, which, at], 0.0
                    )
                send_text[target, which, place] = value.astype(narrow)
    words = [
        links.start(send_text.at[place], grad_text.at[s], device)
        for place, device in zip(turns, along, strict=True)
    ]
    grad_text[s] = send_text[s]
    for copy in smalls:
        copy.wait_recv()
    spread = [links.start(small_out.at[0], small_out.at[k], others[k - 1]) for k in range(1, count)]

    for copy in late:
        copy.get()
    key_index = lax.broadcasted_iota(jnp.int32, (rows, block_rows), 0)

    def back_self(group):
        span = lane_block(group, lanes)
        key_t = k[:, span].astype(wide).T.astype(narrow)
        for block in range(depth):
            at = block_rows_of(block, block_rows)
            allowed = (key_index >= spans[0, block]) & (key_index < spans[1, block])
            grads = []
            for head in range(heads):
                query = head_lanes(q[at, span], head, size)
                grad = head_lanes(go[block, :, span], head, size)
                scores = contract_cols(k[:, span], query)
                scores = jnp.where(allowed, scores, NEGATIVE)
                shares = jnp.exp(scores - total[group, head : head + 1, at])
                grad_shares = contract_cols(v[:, span], grad)
                row = jnp.sum(grad_shares * shares, axis=0, keepdims=True)
                grad_scores = (shares * (grad_shares - row)).astype(narrow)
                if block == 0 and head == 0:
                    sum_v[...] = dense(shares.astype(narrow), grad)
                    sum_k[...] = dense(grad_scores, query)
                else:
                    sum_v[...] += dense(shares.astype(narrow), grad)
                    sum_k[...] += dense(grad_scores, query)
                part = slice(head * size, (head + 1) * size)
                grads.append(dense(key_t[part], grad_scores) * scaling)
            back = jnp.concatenate(grads, axis=0).T
            back_q[at, span] = turn(back, cosine[at], -sine[at], size) + dqc[at, span]
        back_k[:, span] = turn(sum_k[...], cosine[...], -sine[...], size)
        for block in range(depth):
            at = block_rows_of(block, block_rows)
            if isinstance(group, int):
                to = pl.ds(2 * own + group * lanes, lanes)
            else:
                to = pl.ds(pl.multiple_of(2 * own + group * lanes, 128), lanes)
            projected[block, :, to] = sum_v[at].astype(narrow)

    loop(grid, back_self)
    columns = rates[...].T
    pairs = ((raw_q, back_q, gain_q), (raw_k, back_k, gain_k))
    for i, (raw, back, gain) in enumerate(pairs):
        gains = jnp.zeros((1, own), wide)
        for block in range(depth):
            place = i * depth + block
            at = block_rows_of(block, block_rows)
            hat = raw[block] * columns[:, place : place + 1]
            gains = gains + jnp.sum(back[at] * hat, axis=0, keepdims=True)
            stat[place : place + 1] = row_sums(back[at] * gain[...] * hat)
        gain_sums[i : i + 1] = gains
    stats = [links.start(stat, stat_in.at[i], device) for i, device in enumerate(along)]
    means = stat[...]
    for i, copy in enumerate(stats):
        copy.wait_recv()
        means = means + stat_in[i]
    means = (means / width).T
    for i, (raw, back, gain) in enumerate(pairs):
        for block in range(depth):
            place = slice(i * depth + block, i * depth + block + 1)
            at = block_rows_of(block, block_rows)
            rate = columns[:, place]
            hat = raw[block] * rate
            projected[block, :, i * own : (i + 1) * own] = (
                rate * (back[at] * gain[...] - hat * means[:, place])
            ).astype(narrow)
    for copy in words:
        copy.wait_recv()

    for target in range(depth):
        text_gain_sum[:, target * own : (target + 1) * own] = jnp.zeros((1, own), wide)
    for place in range(places):
        at = slice(place * cap_local, (place + 1) * cap_local)
        keys = pairs_in[at, :width]
        rate = lax.rsqrt(jnp.mean(keys * keys, axis=1, keepdims=True) + EPSILON)
        mean = jnp.zeros((cap_local, 1), wide)
        for target in range(depth):
            span = slice(target * own, (target + 1) * own)
            hat = pairs_in[at, span] * rate
            grad = grad_text[target, 0, place].astype(wide)
            mean = mean + jnp.sum(grad * text_gain[:, span] * hat, axis=1, keepdims=True)
            text_gain_sum[:, span] += jnp.sum(grad * hat, axis=0, keepdims=True)
        mean = mean / width
        for target in range(depth):
            span = slice(target * own, (target + 1) * own)
            hat = pairs_in[at, span] * rate
            grad = grad_text[target, 0, place].astype(wide)
            grad_pairs[at, span] = (rate * (grad * text_gain[:, span] - hat * mean)).astype(narrow)
            after = slice(width + target * own, width + (target + 1) * own)
            grad_pairs[at, after] = grad_text[target, 1, place]
    for copy in spread + weights.copies:
        copy.wait_recv()
    links.finish()


def attention_backward(
    count, depth, size, lanes, scalars, upstream, weight, saved, raws, rates, gains, angles, text,
    totals, small, text_gain, text_pairs, ffn_grads,
):
    block_rows, own = raws[0].shape[1:]
    rows = depth * block_rows
    grid, heads = own // lanes, lanes // size
    vmem = pl.BlockSpec(memory_space=pltpu.VMEM)
    copies = 4 * (depth - 1) + count - 1 + 2
    cap = text.shape[0] * text.shape[3]
    args = (*scalars, upstream, weight, *saved, *raws, rates, *gains, *angles, text, *totals, small)
    args = args + (text_gain, text_pairs) + tuple(ffn_grads)
    anywhere = pl.BlockSpec(memory_space=pl.ANY)
    specs = [scalar_spec()] * 3 + [vmem] * (len(args) - 3)
    for i in (6, 7, 9, 10, 14, 15, len(args) - 3, len(args) - 2, len(args) - 1):
        specs[i] = anywhere
    return pl.pallas_call(
        partial(backward_kernel, count, depth, size, lanes),
        in_specs=specs,
        out_specs=[vmem] * 8,
        out_shape=[
            jax.ShapeDtypeStruct((depth, block_rows, 3 * own), narrow),
            jax.ShapeDtypeStruct((2, own), wide),
            jax.ShapeDtypeStruct((grid, heads, block_rows), wide),
            jax.ShapeDtypeStruct(text_pairs.shape, narrow),
            jax.ShapeDtypeStruct((1, own * depth), wide),
            jax.ShapeDtypeStruct((count, depth) + small.shape, wide),
            jax.ShapeDtypeStruct(ffn_grads[0].shape[:1] + ffn_grads[0].shape[2:], narrow),
            jax.ShapeDtypeStruct(ffn_grads[1].shape[1:], narrow),
        ],
        scratch_shapes=[
            pltpu.VMEM((rows, own), narrow),
            pltpu.VMEM((rows, own), narrow),
            pltpu.VMEM(raws[0].shape, wide),
            pltpu.VMEM(raws[1].shape, wide),
            pltpu.VMEM(angles[0].shape, wide),
            pltpu.VMEM(angles[1].shape, wide),
            pltpu.VMEM(text_pairs.shape, wide),
            pltpu.SemaphoreType.DMA((7,)),
            pltpu.VMEM(text.shape, narrow),
            pltpu.VMEM((depth, block_rows, own), narrow),
            pltpu.VMEM((depth - 1, block_rows, own), narrow),
            pltpu.VMEM((rows, own), wide),
            pltpu.VMEM((rows, own), wide),
            pltpu.VMEM((rows, own), wide),
            pltpu.VMEM((depth, 2, cap, own), wide),
            pltpu.VMEM(text.shape, narrow),
            pltpu.VMEM((2 * depth, block_rows), wide),
            pltpu.VMEM((depth - 1, 2 * depth, block_rows), wide),
            pltpu.VMEM((rows, lanes), wide),
            pltpu.VMEM((rows, lanes), wide),
            pltpu.SemaphoreType.DMA((copies,)),
            pltpu.SemaphoreType.DMA((copies,)),
        ],
        compiler_params=pltpu.CompilerParams(
            collective_id=9, has_side_effects=True, vmem_limit_bytes=60 * 2**20
        ),
        name="attention_backward",
    )(*args)


def per_device(
    tokens,
    condition,
    captions,
    caption_lengths,
    null_flags,
    slot_buckets,
    null_caption,
    modulation,
    projection,
    text_weight,
    output_weight,
    gate_up,
    down_weight,
    norm_gains,
    head_gains,
    cross_gates,
    cotangent,
):
    count_s, count_b = lax.axis_size("seq"), lax.axis_size("bucket")
    s, b = lax.axis_index("seq"), lax.axis_index("bucket")
    assert count_s % 4 == 0
    local, width = tokens.shape
    heads = cross_gates.shape[0]
    size = width // heads
    own_heads = heads // count_s
    own = width // count_s
    rows = local * count_s
    places, cap_local, text_width = captions.shape
    cap_rows = places * cap_local
    bucket = slot_buckets[0]
    clip_length = jnp.where(
        bucket == 0, rows // 4, jnp.where(bucket == 1, rows // 2, rows)
    ).astype(jnp.int32)

    own_hidden = down_weight.shape[0]
    gate_rows = gate_up.shape[0]
    text_rows = text_weight.shape[0]
    null_rows = lax.dynamic_slice_in_dim(null_caption, s * cap_local, cap_local, 0)
    is_null = null_flags[:, None, None] == 1
    words_own = jnp.where(is_null, null_rows[None], captions).reshape(cap_rows, text_width)
    own_projection = jnp.concatenate(
        [
            lax.dynamic_slice_in_dim(projection, i * width + s * own, own, 1)
            for i in range(3)
        ],
        axis=1,
    )

    silu_cond = jax.nn.silu(condition).astype(narrow)
    pieces = silu_cond.astype(wide).reshape(places, count_b, -1).transpose(1, 0, 2)
    my_clip = (s * local) // clip_length
    (
        cond_columns,
        mods,
        own_projection,
        words,
        text_pairs,
        text_own,
        normed,
        raw_q,
        raw_k,
        raw_v,
        rates,
    ) = start_exchange(
        count_b,
        count_s,
        my_clip.astype(jnp.int32)[None],
        pieces,
        modulation,
        own_projection,
        words_own,
        text_weight,
        tokens,
        norm_gains,
        head_gains,
    )
    own_projection = own_projection.reshape(width, 3 * own)
    modulated = lax.dynamic_index_in_dim(mods, my_clip, 1, keepdims=False).reshape(1, 4 * width)
    tokens_in = tokens.astype(wide)
    _, pre_pull = jax.vjp(pre_attention, tokens_in, modulated, norm_gains)

    gains = [lax.dynamic_slice_in_dim(head_gains[i : i + 1], s * own, own, 1) for i in range(2)]
    inside = lax.rem(jnp.arange(rows, dtype=jnp.int32), clip_length)
    half = size // 2
    frequency = 10000.0 ** (-jnp.arange(half, dtype=wide) / half)
    angles = inside.astype(wide)[:, None] * frequency[None, :]
    lanes = 128 if own % 128 == 0 else own
    block_heads = lanes // size
    cosine = jnp.tile(jnp.cos(angles), (1, 2 * block_heads))
    sine = jnp.tile(
        jnp.concatenate([-jnp.sin(angles), jnp.sin(angles)], axis=1), (1, block_heads)
    )
    tanh_gates = jnp.tanh(cross_gates)
    own_gates = lax.dynamic_slice_in_dim(tanh_gates, s * own_heads, own_heads, 0)
    clip_of = (jnp.arange(count_s, dtype=jnp.int32) * local) // clip_length
    spans = jnp.stack([clip_of * clip_length, (clip_of + 1) * clip_length, clip_of])
    scalars = (spans, caption_lengths, own_gates)
    full_output, text_own = lax.optimization_barrier((output_weight, text_own))
    full_output = lax.all_gather(full_output, "bucket", axis=0, tiled=True)
    combined, *saved, total, cross_total, text_kv, own_gate_up = attention_forward(
        count_b,
        count_s,
        size,
        lanes,
        scalars,
        (raw_q, raw_k, raw_v),
        rates,
        gains,
        (cosine, sine),
        text_own,
        gate_up,
    )
    combined = combined.transpose(1, 0, 2).reshape(local, width)

    attended = dense(combined, full_output)
    (middle, ffn_full), post_pull = jax.vjp(
        post_attention, attended, tokens_in, modulated, norm_gains
    )
    normed_ffn = ffn_full.astype(narrow)

    lowered, plane, gate_values, hidden = ffn_forward(
        count_b, normed_ffn, own_gate_up, down_weight
    )
    mixed, finish_pull = jax.vjp(finish, lowered, middle, modulated, norm_gains)
    grad_lowered, grad_middle, grad_modulated_last, grad_norm_last = finish_pull(
        cotangent.astype(wide)
    )
    grad_lowered_low = grad_lowered.astype(narrow)
    grad_normed_ffn, grad_gate_up, grad_down = ffn_backward(
        count_b, grad_lowered_low, own_gate_up, down_weight, gate_values, plane, hidden
    )
    share = width // (count_b * count_s)
    ffn_grads = (
        grad_gate_up.reshape(count_b, count_s, share, 2 * own_hidden),
        grad_down.reshape(count_s, own_hidden // count_s, width),
    )

    grad_attended, grad_tokens_post, grad_modulated_post, grad_norm_post = post_pull(
        (grad_middle, grad_normed_ffn)
    )
    grad_attended_low = grad_attended.astype(narrow)
    grad_projected, gain_sums, grad_gates, grad_pairs_low, text_gain_sum, early, *held = (
        attention_backward(
            count_b,
            count_s,
            size,
            lanes,
            scalars,
            grad_attended_low,
            full_output,
            saved,
            (raw_q, raw_k),
            rates,
            gains,
            (cosine, sine),
            text_kv,
            (total, cross_total),
            (grad_modulated_post + grad_modulated_last)[:, width:],
            head_gains[2:],
            text_pairs,
            ffn_grads,
        )
    )

    grad_normed, grad_words, grad_text, *held = end_exchange(
        count_b,
        count_s,
        grad_pairs_low,
        text_weight,
        words,
        grad_projected,
        own_projection,
        ffn_grads,
        held,
    )
    grad_tokens_pre, grad_modulated_pre, grad_norm_pre = pre_pull(grad_normed)
    grad_tokens = grad_tokens_pre + grad_tokens_post

    def place(values):
        return lax.dynamic_update_slice_in_dim(jnp.zeros((width,), wide), values, s * own, 0)

    gate_sums = lax.dynamic_update_slice_in_dim(
        jnp.zeros((heads,), wide),
        jnp.sum(grad_gates, axis=2).reshape(own_heads) * (1.0 - own_gates * own_gates),
        s * own_heads,
        0,
    )
    small = jnp.concatenate(
        [
            grad_norm_pre + grad_norm_post + grad_norm_last,
            jnp.stack(
                [
                    place(gain_sums[0]),
                    place(gain_sums[1]),
                    text_gain_sum[0],
                    jnp.zeros((width,), wide),
                ]
            ),
        ],
        axis=0,
    )
    own_clip = (jnp.arange(places, dtype=jnp.int32) == my_clip).astype(wide)
    row = jnp.concatenate(
        [
            jnp.pad(gate_sums, (0, 128 - heads)),
            jnp.pad(own_clip, (0, width - 128 - places)),
        ]
    )
    row = jnp.stack([grad_modulated_pre[0, :width], row], axis=0)
    (
        mod_share,
        down_share,
        text_share,
        output_share,
        proj_share,
        gate_share,
        null_share,
        grad_rows,
        own_sums,
    ) = final_sums(
        count_b,
        count_s,
        null_flags,
        grad_text,
        combined,
        grad_attended_low,
        normed,
        grad_projected,
        ffn_grads,
        held,
        grad_words,
        row,
        small.reshape(8, count_b, count_s, share).transpose(2, 1, 0, 3),
        early,
        lax.dynamic_slice_in_dim(cond_columns, s * share, share, 2),
    )
    null_share = lax.ppermute(
        null_share,
        ("bucket", "seq"),
        [(i * count_s + j, j * count_b + i) for i in range(count_b) for j in range(count_s)],
    )
    grad_words = grad_words.reshape(places, cap_local, text_width).astype(wide)
    grad_captions = jnp.where(is_null, 0.0, grad_words)

    return (
        mixed.astype(narrow),
        grad_tokens,
        grad_captions,
        null_share,
        mod_share,
        proj_share,
        text_share,
        output_share,
        gate_share,
        down_share,
        own_sums[:4],
        own_sums[4:7],
        jnp.sum(grad_rows[:, :, 1, :heads], axis=(0, 1)),
    )


def solution(mesh):
    whole = P(("bucket", "seq"), None)
    shard = P("bucket", None)
    return jax.shard_map(
        per_device,
        mesh=mesh,
        in_specs=(
            whole,
            shard,
            P("bucket", "seq", None),
            P("bucket"),
            P("bucket"),
            P("bucket"),
            P(),
            shard,
            shard,
            shard,
            shard,
            shard,
            shard,
            P(),
            P(),
            P(),
            whole,
        ),
        out_specs=(
            whole,
            whole,
            P("bucket", "seq", None),
            whole,
            whole,
            whole,
            whole,
            whole,
            whole,
            whole,
            P(None, ("bucket", "seq")),
            P(None, ("bucket", "seq")),
            P(),
        ),
        check_vma=False,
    )
```

```python
from functools import partial

import jax
import jax.numpy as jnp
from jax import lax
from jax.experimental import pallas as pl
from jax.experimental.pallas import tpu as pltpu
from jax.sharding import PartitionSpec as P

EPSILON = 1e-06
NEGATIVE = -1e30
HIGHEST = lax.Precision.HIGHEST
wide = jnp.float32
narrow = jnp.bfloat16
VMEM_LIMIT = 50 * 2**20


def rms_norm(values, norm_gain):
    return (
        values * lax.rsqrt(jnp.mean(values * values, axis=-1, keepdims=True) + EPSILON) * norm_gain
    )


def dense(leading, trailing):
    return jnp.dot(leading, trailing, preferred_element_type=wide)


def contract_rows(leading, trailing):
    return lax.dot_general(
        leading, trailing, (((0,), (0,)), ((), ())), preferred_element_type=wide
    )


def contract_cols(leading, trailing):
    return lax.dot_general(
        leading, trailing, (((1,), (1,)), ((), ())), preferred_element_type=wide
    )


def pre_attention(tokens_in, modulated, norm_gains):
    model_width = tokens_in.shape[1]
    return rms_norm(tokens_in, norm_gains[0]) * (1.0 + modulated[:, :model_width])


def text_heads(text_pairs, gain):
    model_width = text_pairs.shape[1] // 2
    return (rms_norm(text_pairs[:, :model_width], gain), text_pairs[:, model_width:])


def post_attention(attended, tokens_in, modulated, norm_gains):
    model_width = tokens_in.shape[1]
    middle = tokens_in + jnp.tanh(modulated[:, model_width : 2 * model_width]) * rms_norm(
        attended, norm_gains[1]
    )
    normed_ffn = rms_norm(middle, norm_gains[2]) * (
        1.0 + modulated[:, 2 * model_width : 3 * model_width]
    )
    return (middle, normed_ffn)


def swiglu(gate_values):
    hidden_width = gate_values.shape[1] // 2
    return jax.nn.silu(gate_values[:, :hidden_width]) * gate_values[:, hidden_width:]


def finish(lowered, middle, modulated, norm_gains):
    model_width = middle.shape[1]
    return middle + jnp.tanh(modulated[:, 3 * model_width :]) * rms_norm(lowered, norm_gains[3])


MESH = pl.DeviceIdType.MESH


class Transfers:
    def __init__(self, send, arrive):
        self.send, self.arrive, self.used = send, arrive, 0
        self.open = []

    def start(self, source, target, device):
        copy = pltpu.make_async_remote_copy(
            src_ref=source,
            dst_ref=target,
            send_sem=self.send.at[self.used],
            recv_sem=self.arrive.at[self.used],
            device_id=device,
            device_id_type=MESH,
        )
        self.used += 1
        copy.start()
        self.open.append(copy)
        return copy

    def finish(self):
        for copy in self.open:
            copy.wait_send()


def meet(devices):
    barrier = pltpu.get_barrier_semaphore()
    for device in devices:
        pl.semaphore_signal(barrier, inc=1, device_id=device, device_id_type=MESH)
    pl.semaphore_wait(barrier, len(devices))


def partner(bits):
    return {"bucket": jnp.bitwise_xor(lax.axis_index("bucket"), bits)}


def outer_bits(count):
    return [1 << i for i in range(1, count.bit_length() - 1)]


def block_index(k, count):
    return (k >> 1) + (k & 1) * (count // 2)


def last_bit(block, order):
    return [bit for bit in order if block & bit][-1]


class PlaneExchange:
    def __init__(
        self, count, links, gathered=None, partial=None, arrived_core=None, arrived_outer=None,
        natural=False,
    ):
        self.count, self.links, self.natural = count, links, natural
        self.index = lax.axis_index("bucket")
        self.gathered, self.partial = gathered, partial
        self.arrived_core, self.arrived_outer = arrived_core, arrived_outer
        bits = outer_bits(count)
        self.orders = (bits, bits[::-1])
        self.outer = [k for k in range(0, count, 2)]
        self.rows = (partial if gathered is None else gathered).shape[1] // 2
        self.coming, self.slots = {}, {}
        self.blocks = [0]

    def part(self, ref, block, half):
        return ref.at[block, pl.ds(half * self.rows, self.rows)]

    def place(self, block):
        return jnp.bitwise_xor(self.index, block) if self.natural else block_index(block, self.count)

    def onward(self, half, block, bit):
        source = self.place(block)
        target = source if self.natural else self.place(block | bit)
        self.coming[half, block | bit] = self.links.start(
            self.part(self.gathered, source, half),
            self.part(self.gathered, target, half),
            partner(bit),
        )

    def forward(self, half, block):
        order = self.orders[half]
        later = order if block == 0 else order[order.index(last_bit(block, order)) + 1 :]
        for bit in later:
            self.onward(half, block, bit)

    def forward_core(self, half, block):
        self.onward(half, block, 1)

    def arrive(self, block):
        for half in range(2):
            self.coming[half, block].wait_recv()

    def begin(self):
        for step in range(len(self.orders[0])):
            for half in range(2):
                self.onward(half, 0, self.orders[half][step])
        for half in range(2):
            self.forward_core(half, 0)

    def run_gather(self, compute, scatter=None):
        self.begin()
        compute([0])
        levels = len(self.orders[0])
        self.arrive(1)
        compute([block_index(1, self.count)])
        if scatter is not None:
            self.send_core(1)
        for level in range(1, levels + 1):
            here = [k for k in self.outer if bin(k).count("1") == level]
            self.forward_level(here)
            if level == 2 and scatter is not None:
                next(scatter)
            compute([block_index(k, self.count) for k in here])
            for k in here:
                self.arrive(k | 1)
            compute([block_index(k | 1, self.count) for k in here])
            for k in here:
                if scatter is not None:
                    self.send_core(k | 1)

    def gather(self):
        self.begin()
        yield
        for level in range(1, len(self.orders[0]) + 1):
            self.forward_level([k for k in self.outer if bin(k).count("1") == level])
            yield
        for block in self.outer:
            self.arrive(block | 1)

    def forward_level(self, here):
        steps = [(half, k) for k in here for half in range(2)]
        steps.sort(
            key=lambda s: [
                self.orders[s[0]].index(bit) for bit in self.orders[s[0]] if s[1] & bit
            ][::-1]
        )
        for half, k in steps:
            self.coming[half, k].wait_recv()
            self.forward(half, k)
            self.forward_core(half, k)

    def send_core(self, block):
        place = self.place(block)
        target = self.arrived_core.at[block >> 1]
        self.slots["core", block & ~1] = self.links.start(self.partial.at[place], target, partner(1))

    def total(self, half, block, slots):
        rows = pl.ds(half * self.rows, self.rows)
        value = self.partial[self.place(block), rows].astype(wide)
        value = value + self.arrived_core[block >> 1, rows].astype(wide)
        for slot in slots:
            value = value + self.arrived_outer[half, slot].astype(wide)
        return value

    def scatter(self, finish):
        slot_of = {}
        waiting = {(half, k): [] for half in range(2) for k in self.outer}
        core_seen = set()
        left = [list(self.outer), list(self.outer)]
        for step in range(len(self.orders[0])):
            jobs = []
            for half in range(2):
                bit = self.orders[half][::-1][step]
                jobs.append([(half, bit, k) for k in left[half] if k & bit])
                left[half] = [k for k in left[half] if not k & bit]
            for pair in zip(*jobs, strict=True):
                for half, bit, k in pair:
                    if k not in core_seen:
                        self.slots["core", k].wait_recv()
                        core_seen.add(k)
                    for copy, _ in waiting[half, k]:
                        copy.wait_recv()
                    rows = pl.ds(half * self.rows, self.rows)
                    total = self.total(half, k, [slot for _, slot in waiting[half, k]])
                    self.partial[self.place(k), rows] = total.astype(narrow)
                    slot = slot_of.setdefault((half, bit, k ^ bit), len([1 for h, *_ in slot_of if h == half]))
                    copy = self.links.start(
                        self.partial.at[self.place(k), rows],
                        self.arrived_outer.at[half, slot],
                        partner(bit),
                    )
                    waiting[half, k ^ bit].append((copy, slot))
                yield
        if 0 not in core_seen:
            self.slots["core", 0].wait_recv()
        for half in range(2):
            for copy, _ in waiting[half, 0]:
                copy.wait_recv()
            finish(half, self.total(half, 0, [slot for _, slot in waiting[half, 0]]))


def plane_partners(count):
    return [partner(bit) for bit in outer_bits(count) + [1]]


def plane_copies(count):
    outer = count // 2
    return 2 * (outer - 1) + 2 * outer, outer + 2 * (outer - 1)


def spans(blocks):
    runs = []
    for block in sorted(blocks):
        if runs and runs[-1][1] == block:
            runs[-1][1] = block + 1
        else:
            runs.append([block, block + 1])
    return runs


def each(blocks, body):
    for first, end in spans(blocks):
        if end - first == 1:
            body(first)
        else:
            lax.fori_loop(first, end, lambda i, _: (body(i), 0)[1], 0)


class Late:
    def __init__(self, source, target, semaphore):
        self.copy = pltpu.make_async_copy(source, target, semaphore)
        self.target, self.there = target, False
        self.copy.start()

    def get(self):
        if not self.there:
            self.copy.wait()
            self.there = True
        return self.target


def ffn_kernel(
    count, x, gate_up_hbm, down_hbm, lowered, plane_out, values_out, hidden_out,
    gate_up, down, plane, partial, core, outer, values, hidden, send, arrive, local,
):
    links = Transfers(send, arrive)
    late = Late(gate_up_hbm, gate_up, local.at[3]), Late(down_hbm, down, local.at[4])
    meet(plane_partners(count))
    units = down.shape[0]
    wide_block = 256
    plane[0] = x[...]
    saved = pltpu.make_async_copy(plane, plane_out, local.at[0])

    def compute(blocks):
        for copy in late:
            copy.get()

        def one(place):
            for start in range(0, units, wide_block):
                columns = slice(start, start + wide_block)
                after = slice(units + start, units + start + wide_block)
                gate = dense(plane[place], gate_up[:, columns])
                up = dense(plane[place], gate_up[:, after])
                values[place, :, columns] = gate
                values[place, :, after] = up
                hidden[place, :, columns] = (jax.nn.silu(gate) * up).astype(narrow)
            partial[place] = dense(hidden[place], down[...]).astype(narrow)

        each(blocks, one)

    exchange = PlaneExchange(count, links, plane, partial, core, outer)
    def finish(half, total):
        lowered[pl.ds(half * exchange.rows, exchange.rows)] = total

    sums = exchange.scatter(finish)
    exchange.run_gather(compute, sums)
    saved.start()
    kept = pltpu.make_async_copy(values, values_out, local.at[1])
    kept.start()
    held = pltpu.make_async_copy(hidden, hidden_out, local.at[2])
    held.start()

    for _ in sums:
        pass
    saved.wait()
    kept.wait()
    held.wait()
    links.finish()


def plane_scratch(count, rows, width):
    outer = count // 2
    return [
        pltpu.VMEM((count, rows, width), narrow),
        pltpu.VMEM((count, rows, width), narrow),
        pltpu.VMEM((outer, rows, width), narrow),
        pltpu.VMEM((2, outer - 1, rows // 2, width), narrow),
    ]


def ffn_forward(count, x, gate_up, down):
    rows, width = x.shape
    units = down.shape[0]
    copies = sum(plane_copies(count))
    vmem, anywhere = pl.BlockSpec(memory_space=pltpu.VMEM), pl.BlockSpec(memory_space=pl.ANY)
    return pl.pallas_call(
        partial(ffn_kernel, count),
        in_specs=[vmem] + [anywhere] * 2,
        out_specs=[vmem] + [anywhere] * 3,
        out_shape=[
            jax.ShapeDtypeStruct((rows, width), wide),
            jax.ShapeDtypeStruct((count, rows, width), narrow),
            jax.ShapeDtypeStruct((count, rows, 2 * units), wide),
            jax.ShapeDtypeStruct((count, rows, units), narrow),
        ],
        scratch_shapes=[pltpu.VMEM(gate_up.shape, narrow), pltpu.VMEM(down.shape, narrow)]
        + plane_scratch(count, rows, width)
        + [
            pltpu.VMEM((count, rows, 2 * units), wide),
            pltpu.VMEM((count, rows, units), narrow),
            pltpu.SemaphoreType.DMA((copies,)),
            pltpu.SemaphoreType.DMA((copies,)),
            pltpu.SemaphoreType.DMA((5,)),
        ],
        compiler_params=pltpu.CompilerParams(
            collective_id=1, has_side_effects=True, vmem_limit_bytes=60 * 2**20
        ),
        name="ffn_forward",
    )(x, gate_up, down)

def ffn_back_kernel(
    count, g, gate_up_hbm, down_hbm, values_in, x_in, hidden_in, grad_normed, grad_gate_up,
    grad_down, gate_up, down, plane, partial, core, outer, values, grads, taken, send, arrive,
    local,
):
    links = Transfers(send, arrive)
    late = Late(down_hbm, down, local.at[4]), Late(gate_up_hbm, gate_up, local.at[3])
    fetch = pltpu.make_async_copy(values_in, values, local.at[2])
    fetch.start()
    meet(plane_partners(count))
    units, width = down.shape
    wide_block = 256
    plane[0] = g[...]
    fetched = []

    def compute(places):
        if not fetched:
            fetch.wait()
            fetched.append(True)
            for copy in late:
                copy.get()

        def one(place):
            for start in range(0, units, wide_block):
                columns = slice(start, start + wide_block)
                after = slice(units + start, units + start + wide_block)
                back = contract_cols(plane[place], down[columns])
                gate, up = values[place, :, columns], values[place, :, after]
                sigma = jax.nn.sigmoid(gate)
                grads[place, :, columns] = (
                    back * up * (sigma * (1.0 + gate * (1.0 - sigma)))
                ).astype(narrow)
                grads[place, :, after] = (back * (gate * sigma)).astype(narrow)
            partial[place] = contract_cols(grads[place], gate_up[...]).astype(narrow)

        each(places, one)

    exchange = PlaneExchange(count, links, plane, partial, core, outer)

    def finish(half, total):
        grad_normed[pl.ds(half * exchange.rows, exchange.rows)] = total

    sums = exchange.scatter(finish)
    exchange.run_gather(compute, sums)

    jobs = [(x_in, grads, grad_gate_up, i) for i in range(width // wide_block)]
    jobs += [(hidden_in, plane, grad_down, i) for i in range(units // wide_block)]

    def take(number):
        source, _, _, i = jobs[number]
        columns = pl.ds(i * wide_block, wide_block)
        return pltpu.make_async_copy(
            source.at[:, :, columns], taken.at[number % 2], local.at[number % 2]
        )

    def work(number):
        if number + 1 < len(jobs):
            take(number + 1).start()
        take(number).wait()
        _, upstream, out, i = jobs[number]
        for start in range(0, upstream.shape[2], 512):
            columns = slice(start, start + 512)
            out[i * wide_block : (i + 1) * wide_block, columns] = contract_rows(
                flat(taken[number % 2]), flat(upstream[:, :, columns])
            ).astype(narrow)

    take(0).start()
    done = 0
    for _ in sums:
        for number in range(done, 3 if done == 0 else len(jobs)):
            work(number)
            done += 1
    for number in range(done, len(jobs)):
        work(number)
    links.finish()


class GradientRing:
    def __init__(self, ring, own, held):
        self.ring, self.own, self.held = ring, own, held
        self.copies, self.pieces = [], {}

    def piece(self, which, step):
        place = self.ring.source(step + 1)
        return self.own[0].at[:, place] if which == 0 else self.own[1].at[place]

    def fetch(self, first, targets, semaphores):
        for slot in range(targets[0].shape[0]):
            for which in range(2):
                self.pieces[which, first + slot] = Late(
                    self.piece(which, first + slot),
                    targets[which].at[slot],
                    semaphores.at[2 * slot + which],
                )

    def first(self, landing):
        for which in range(2):
            self.copies.append(
                self.ring.links.start(self.piece(which, 0), landing[which], self.ring.right)
            )

    def arrived(self):
        for copy in self.copies:
            copy.wait_recv()
        self.copies = []

    def value(self, which, step):
        piece = self.pieces[which, step].get()
        return piece[...].astype(wide) + self.held[which][...].astype(wide)

    def onward(self, step, going, landing):
        self.arrived()
        for which in range(2):
            going[which][...] = self.value(which, step).astype(narrow)
            self.copies.append(
                self.ring.links.start(going[which], landing[which], self.ring.right)
            )
        self.held = landing


def ffn_backward(count, g, gate_up, down, values, x, hidden):
    rows, width = g.shape
    units = down.shape[0]
    copies = sum(plane_copies(count))
    vmem, anywhere = pl.BlockSpec(memory_space=pltpu.VMEM), pl.BlockSpec(memory_space=pl.ANY)
    return pl.pallas_call(
        partial(ffn_back_kernel, count),
        in_specs=[vmem] + [anywhere] * 5,
        out_specs=[vmem] * 3,
        out_shape=[
            jax.ShapeDtypeStruct((rows, width), wide),
            jax.ShapeDtypeStruct((width, 2 * units), narrow),
            jax.ShapeDtypeStruct((units, width), narrow),
        ],
        scratch_shapes=[pltpu.VMEM(gate_up.shape, narrow), pltpu.VMEM(down.shape, narrow)]
        + plane_scratch(count, rows, width)
        + [
            pltpu.VMEM((count, rows, 2 * units), wide),
            pltpu.VMEM((count, rows, 2 * units), narrow),
            pltpu.VMEM((2, count, rows, 256), narrow),
            pltpu.SemaphoreType.DMA((copies,)),
            pltpu.SemaphoreType.DMA((copies,)),
            pltpu.SemaphoreType.DMA((5,)),
        ],
        compiler_params=pltpu.CompilerParams(
            collective_id=2, has_side_effects=True, vmem_limit_bytes=62 * 2**20
        ),
        name="ffn_backward",
    )(g, gate_up, down, values, x, hidden)


def seq_device(index):
    return {"seq": index}


class Ring:
    def __init__(self, depth, links):
        self.depth, self.links = depth, links
        self.index = lax.axis_index("seq")
        self.right = seq_device(lax.rem(self.index + 1, depth))
        self.left = seq_device(lax.rem(self.index + depth - 1, depth))

    def source(self, step):
        return lax.rem(self.index - step + 2 * self.depth, self.depth)


def start_kernel(
    count, depth, clip, pieces, modulation, shard, words, text_hbm, x, gain, text_gain,
    got, mods, projection, spread, pairs, text_own, normed, q, k, v, rates,
    text, columns, local, product, back, stat, stat_in, partial, core, outer, send, arrive,
):
    links = Transfers(send, arrive)
    late = Late(text_hbm, text, local.at[0])
    mod_width = columns.shape[1]
    at = pl.multiple_of(lax.axis_index("seq") * mod_width, 128)
    own_columns = Late(modulation.at[:, pl.ds(at, mod_width)], columns, local.at[1])
    ring = Ring(depth, links)
    b, s = lax.axis_index("bucket"), lax.axis_index("seq")
    others = [partner(k) for k in range(1, count)]
    along = [seq_device(lax.rem(s + step, depth)) for step in range(1, depth)]
    meet(others + along)
    first = [
        links.start(pieces.at[jnp.bitwise_xor(b, k)], got.at[k], others[k - 1])
        for k in range(1, count)
    ]
    got[0] = pieces[b]
    feature, width = text.shape

    def features(target):
        return words.at[:, pl.ds(pl.multiple_of(target * feature, 128), feature)]

    projection[b] = shard[...]
    spread[b] = words[:, pl.ds(pl.multiple_of(b * feature, 128), feature)]
    for copy in first:
        copy.wait_recv()
    own_columns.get()
    for block in range(count):
        product[block] = dense(got[block].astype(narrow), columns[...])
    second = [
        links.start(product.at[block], back.at[block - 1], others[block - 1])
        for block in range(1, count)
    ]
    shards = PlaneExchange(count, links, projection, natural=True).gather()
    next(shards)
    far = {}
    for block in sorted(range(1, count), key=lambda block: (bin(block >> 1).count("1"), block & 1)):
        far[block] = links.start(
            features(jnp.bitwise_xor(b, block)), spread.at[b], others[block - 1]
        )

    total = product[0]
    for i, copy in enumerate(second):
        copy.wait_recv()
        total = total + back[i]
    mods[s] = total
    third = [links.start(mods.at[s], mods.at[s], device) for device in along]
    for copy in third:
        copy.wait_recv()
    places = mods.shape[1]
    parts = []
    for i in range(depth // 4):
        part = jnp.zeros((1, mods.shape[2]), wide)
        for place in range(places):
            part = part + jnp.where(clip[0] == place, mods[i, place : place + 1], 0.0)
        parts.append(part)
    scale = parts[0] if len(parts) == 1 else jnp.concatenate(parts, axis=1)
    value = x[...].astype(wide)
    rate = lax.rsqrt(jnp.mean(value * value, axis=1, keepdims=True) + EPSILON)
    normed[s] = (value * rate * gain[0:1] * (1.0 + scale)).astype(narrow)
    moving = [links.start(normed.at[s], normed.at[s], ring.right)]
    next(shards)

    exchange = PlaneExchange(count, links, None, partial, core, outer)

    def pair(block):
        if block:
            far[block].wait_recv()
        source = spread[jnp.bitwise_xor(b, block)]
        place = block_index(block, count)
        for start in range(0, width, 512):
            span = slice(start, start + 512)
            partial[place, :, span] = dense(source, text[:, span]).astype(narrow)
        if block & 1:
            exchange.send_core(block)

    def finish(half, total):
        pairs[pl.ds(half * exchange.rows, exchange.rows)] = total
        keys = total[:, : width // 2]
        rate = lax.rsqrt(jnp.mean(keys * keys, axis=1, keepdims=True) + EPSILON)
        kinds = (keys * rate * text_gain[2:3]).astype(narrow), total[:, width // 2 :].astype(narrow)
        cap_local, part = text_own.shape[3:]
        for kind, value in enumerate(kinds):
            for i in range(exchange.rows // cap_local):
                place = half * (exchange.rows // cap_local) + i
                rows = slice(i * cap_local, (i + 1) * cap_local)
                for target in range(depth):
                    text_own[target, kind, place] = value[
                        rows, target * part : (target + 1) * part
                    ]

    late.get()
    sums = exchange.scatter(finish)
    order = sorted(exchange.outer, key=lambda block: (bin(block).count("1"), block))
    order = order[1:] + order[:1]
    levels = len(exchange.orders[0])
    for block in order[:levels]:
        pair(block | 1)
        pair(block)
    own = q.shape[2]

    def project(step):
        place = ring.source(step)
        for i, out in enumerate((q, k, v)):
            span = slice(i * own, (i + 1) * own)
            weight = projection[:, :, span]
            out[place] = dense(normed[place], flat(weight))

    def onward(step):
        moving[-1].wait_recv()
        place = ring.source(step)
        if step < depth - 1:
            moving.append(links.start(normed.at[place], normed.at[place], ring.right))

    next(sums)
    onward(1)
    for block in order[levels:]:
        pair(block | 1)
        pair(block)
    next(sums)
    for _ in shards:
        pass
    project(0)
    project(1)
    for step in range(2, depth - 1):
        onward(step)
        project(step)
    next(sums)
    onward(depth - 1)
    project(depth - 1)
    for i, raw in enumerate((q, k)):
        for block in range(depth):
            place = i * depth + block
            stat[place : place + 1] = row_sums(raw[block] * raw[block])
    stats = [links.start(stat, stat_in.at[i], device) for i, device in enumerate(along)]
    for _ in sums:
        pass
    squares = stat[...]
    for i, copy in enumerate(stats):
        copy.wait_recv()
        squares = squares + stat_in[i]
    rates[...] = lax.rsqrt(squares / (own * depth) + EPSILON)
    links.finish()


def start_exchange(
    count, depth, clip, pieces, modulation, shard, words, text, x, gain, text_gain
):
    vmem, anywhere = pl.BlockSpec(memory_space=pltpu.VMEM), pl.BlockSpec(memory_space=pl.ANY)
    rows, width = x.shape
    own = shard.shape[1] // 3
    cap_rows, pair_width = words.shape[0], text.shape[1]
    places, mod_width = pieces.shape[1], modulation.shape[1] // depth
    copies = sum(plane_copies(count)) + 3 * (count - 1) + 3 * (depth - 1)
    raw = jax.ShapeDtypeStruct((depth, rows, own), wide)
    return pl.pallas_call(
        partial(start_kernel, count, depth),
        in_specs=[scalar_spec(), vmem, anywhere, vmem, vmem, anywhere] + [vmem] * 3,
        out_specs=[vmem] * 11,
        out_shape=[
            jax.ShapeDtypeStruct(pieces.shape, wide),
            jax.ShapeDtypeStruct((depth, places, mod_width), wide),
            jax.ShapeDtypeStruct((count,) + shard.shape, narrow),
            jax.ShapeDtypeStruct((count, cap_rows, words.shape[1] // count), narrow),
            jax.ShapeDtypeStruct((cap_rows, pair_width), wide),
            jax.ShapeDtypeStruct((depth, 2, places, cap_rows // places, own), narrow),
            jax.ShapeDtypeStruct((depth, rows, width), narrow),
            raw,
            raw,
            raw,
            jax.ShapeDtypeStruct((2 * depth, rows), wide),
        ],
        scratch_shapes=[
            pltpu.VMEM(text.shape, narrow),
            pltpu.VMEM((modulation.shape[0], mod_width), narrow),
            pltpu.SemaphoreType.DMA((2,)),
            pltpu.VMEM((count, places, mod_width), wide),
            pltpu.VMEM((count - 1, places, mod_width), wide),
            pltpu.VMEM((2 * depth, rows), wide),
            pltpu.VMEM((depth - 1, 2 * depth, rows), wide),
        ]
        + plane_scratch(count, cap_rows, pair_width)[1:]
        + [pltpu.SemaphoreType.DMA((copies,)), pltpu.SemaphoreType.DMA((copies,))],
        compiler_params=pltpu.CompilerParams(
            collective_id=4, has_side_effects=True, vmem_limit_bytes=60 * 2**20
        ),
        name="start_exchange",
    )(clip, pieces, modulation, shard, words, text, x, gain, text_gain)


def end_kernel(
    count, depth, pairs, text_hbm, words_hbm, grads_hbm, projection_hbm, grad_gate, grad_down,
    gate_held, down_held, normed, grad_words, grad_weight, gate_next, down_next,
    text, words, grads, projection, gate_piece, down_piece, local,
    plane, back, send_sum, ring_in, total, gate_go, down_go, send, arrive,
):
    links = Transfers(send, arrive)
    ring = Ring(depth, links)
    late = [
        Late(source, target, local.at[2 + i])
        for i, (source, target) in enumerate(
            zip(
                (text_hbm, words_hbm, grads_hbm, projection_hbm),
                (text, words, grads, projection),
                strict=True,
            )
        )
    ]
    weights = GradientRing(ring, (grad_gate, grad_down), (gate_held, down_held))
    weights.fetch(1, (gate_piece, down_piece), local)
    b = lax.axis_index("bucket")
    others = [partner(k) for k in range(1, count)]
    meet(others + [ring.left, ring.right])
    plane[0] = pairs[...]
    exchange = PlaneExchange(count, links, plane)
    feature, width = text.shape
    own_columns = pl.ds(pl.multiple_of(b * feature, 128), feature)
    moving = []

    def round_step(step):
        value = contract_cols(grads[ring.source(step + 1)], projection[...])
        if step > 0:
            moving[-1].wait_recv()
            value = value + ring_in[step - 1].astype(wide)
        if step < depth - 1:
            send_sum[step] = value.astype(narrow)
            moving.append(links.start(send_sum.at[step], ring_in.at[step], ring.right))
        else:
            normed[...] = value

    steps = [0]

    def advance():
        if steps[0] < depth - 1:
            round_step(steps[0])
            steps[0] += 1
            if steps[0] == depth - 1:
                weights.onward(1, (gate_go, down_go), (gate_next, down_next))

    arriving = []
    blocks = [None] * count
    for block in range(count):
        blocks[block_index(block, count)] = block

    def compute(places):
        for copy in late:
            copy.get()
        for place in places:
            block = blocks[place]
            features = words[jnp.bitwise_xor(b, block)].astype(wide).T.astype(narrow)
            for first in range(0, width, 512):
                columns = slice(first, first + 512)
                part = dense(features, plane[place, :, columns])
                if place == 0:
                    total[:, columns] = part
                else:
                    total[:, columns] += part
            value = contract_cols(plane[place], text[...]).astype(narrow)
            if block == 0:
                grad_words[:, own_columns] = value
            else:
                back[place - 1] = value
                arriving.append(
                    links.start(
                        back.at[place - 1], grad_words.at[:, own_columns], others[block - 1]
                    )
                )
        advance()

    exchange.run_gather(compute)
    while steps[0] < depth - 1:
        advance()
    round_step(depth - 1)
    grad_weight[...] = total[...].astype(narrow)
    for copy in arriving + weights.copies:
        copy.wait_recv()
    links.finish()


def end_exchange(count, depth, pairs, text, words, grads, projection, ffn_grads, held):
    vmem = pl.BlockSpec(memory_space=pltpu.VMEM)
    cap_rows, pair_width = pairs.shape
    feature = text.shape[0]
    rows, width = grads.shape[1], projection.shape[0]
    copies = plane_copies(count)[0] + count - 1 + depth - 1 + 2
    return pl.pallas_call(
        partial(end_kernel, count, depth),
        in_specs=[vmem] + [pl.BlockSpec(memory_space=pl.ANY)] * 6 + [vmem] * 2,
        out_specs=[vmem] * 5,
        out_shape=[
            jax.ShapeDtypeStruct((rows, width), wide),
            jax.ShapeDtypeStruct((cap_rows, count * feature), narrow),
            jax.ShapeDtypeStruct((feature, pair_width), narrow),
            jax.ShapeDtypeStruct(held[0].shape, narrow),
            jax.ShapeDtypeStruct(held[1].shape, narrow),
        ],
        scratch_shapes=[
            pltpu.VMEM(text.shape, narrow),
            pltpu.VMEM(words.shape, narrow),
            pltpu.VMEM(grads.shape, narrow),
            pltpu.VMEM(projection.shape, narrow),
            pltpu.VMEM((1,) + held[0].shape, narrow),
            pltpu.VMEM((1,) + held[1].shape, narrow),
            pltpu.SemaphoreType.DMA((6,)),
            pltpu.VMEM((count, cap_rows, pair_width), narrow),
            pltpu.VMEM((count - 1, cap_rows, feature), narrow),
            pltpu.VMEM((depth - 1, rows, width), narrow),
            pltpu.VMEM((depth - 1, rows, width), narrow),
            pltpu.VMEM((feature, pair_width), wide),
            pltpu.VMEM(held[0].shape, narrow),
            pltpu.VMEM(held[1].shape, narrow),
            pltpu.SemaphoreType.DMA((copies,)),
            pltpu.SemaphoreType.DMA((copies,)),
        ],
        compiler_params=pltpu.CompilerParams(
            collective_id=5, has_side_effects=True, vmem_limit_bytes=63 * 2**20
        ),
        name="end_exchange",
    )(pairs, text, words, grads, projection, *ffn_grads, *held)


def sum_kernel(
    count, depth, flags, text, combined, upstream, normed_hbm, grads_hbm, grad_gate, grad_down,
    gate_held, down_held, words_hbm, row, small, early, conditions, mod_share, down_share, text_share, output_share, proj_share, gate_share, null_share, rows_out, small_out,
    normed, grads, words, gate_piece, down_piece, local, out_part, out_core, out_outer, proj_part, proj_core, proj_outer, send_low, low_in, out_go,
    out_come, proj_go, proj_come, gate, gate_come, null, null_come, small_come, small_go,
    small_land, gate_go, down_go, gate_land, down_land, cond_rows, all_rows, send, arrive,
):
    links = Transfers(send, arrive)
    ring = Ring(depth, links)
    late = [
        Late(source, target, local.at[i])
        for i, (source, target) in enumerate(
            zip((normed_hbm, grads_hbm, words_hbm), (normed, grads, words), strict=True)
        )
    ]
    weights = GradientRing(ring, (grad_gate, grad_down), (gate_held, down_held))
    weights.fetch(2, (gate_piece, down_piece), local.at[pl.ds(3, 2 * (depth - 2))])
    b, s = lax.axis_index("bucket"), lax.axis_index("seq")
    others = [partner(k) for k in range(1, count)]
    turns = [lax.rem(s + step, depth) for step in range(1, depth)]
    along = [seq_device(place) for place in turns]
    meet(others + along)

    rows_out[0, s] = row[...]
    tiny = []
    for i, (place, device) in enumerate(zip(turns, along, strict=True)):
        tiny.append(links.start(row, rows_out.at[0, s], device))
        tiny.append(links.start(small.at[place], small_come.at[i], device))

    low_rows = text.shape[0] // depth
    going = []

    def text_step(step):
        rows = pl.ds(pl.multiple_of(ring.source(step + 1) * low_rows, 16), low_rows)
        value = text[rows].astype(wide)
        if step > 0:
            going[-1].wait_recv()
            value = value + low_in[step - 1].astype(wide)
        if step < depth - 1:
            send_low[step] = value.astype(narrow)
            going.append(links.start(send_low.at[step], low_in.at[step], ring.right))
        else:
            text_share[...] = value

    def weights_step(step):
        slot = step - 2
        weights.onward(
            step,
            (gate_go.at[slot], down_go.at[slot]),
            (gate_land.at[slot], down_land.at[slot]),
        )

    text_step(0)
    weights_step(2)

    share = out_go.shape[1]
    pair = 2 * out_part.shape[1]

    def fill(part, leading, trailing):
        for first in range(0, count, 2):
            value = contract_rows(leading[:, first // 2 * pair : (first // 2 + 1) * pair], trailing)
            value = value.astype(narrow)
            part[first] = value[: pair // 2]
            part[first + 1] = value[pair // 2 :]

    def plane_sum(part, core, outer, go):
        exchange = PlaneExchange(count, links, None, part, core, outer, natural=True)
        for block in range(1, count, 2):
            exchange.send_core(block)

        def finish(half, total):
            low = total.astype(narrow)
            for i in range(depth // 2):
                go[half * (depth // 2) + i] = low[i * share : (i + 1) * share]

        return exchange.scatter(finish)

    fill(out_part, combined[...], upstream[...])
    out_sums = plane_sum(out_part, out_core, out_outer, out_go)
    for copy in late:
        copy.get()
    fill(proj_part, flat(normed[...]), flat(grads[...]))
    proj_sums = plane_sum(proj_part, proj_core, proj_outer, proj_go)
    for _ in range(count // 4):
        next(out_sums)
    for _ in range(count // 4):
        next(proj_sums)
    text_step(1)

    places = flags.shape[0]
    cap_local = words.shape[0] // places
    null_rows = null.shape[1]
    for first in range(0, words.shape[1], 512):
        columns = slice(first, first + 512)
        value = jnp.zeros((cap_local, 512), wide)
        for place in range(places):
            part = words[place * cap_local : (place + 1) * cap_local, columns].astype(wide)
            value = value + jnp.where(flags[place] == 1, part, 0.0)
        for k in range(count):
            null[k, :, columns] = value[k * null_rows : (k + 1) * null_rows]
    next(out_sums)
    next(proj_sums)
    nulls = [
        links.start(null.at[jnp.bitwise_xor(b, k)], null_come.at[k - 1], others[k - 1])
        for k in range(1, count)
    ]

    def drain(sums):
        for _ in sums:
            pass

    def seq_sends(go, come):
        come[s] = go[s]
        return [
            links.start(go.at[place], come.at[s], device)
            for place, device in zip(turns, along, strict=True)
        ]

    for step in range(3, depth - 1):
        weights_step(step)
    weights.arrived()
    gate[...] = weights.value(0, depth - 1).astype(narrow)
    far = [
        links.start(gate.at[jnp.bitwise_xor(b, k)], gate_come.at[b], others[k - 1])
        for k in range(1, count)
    ]
    gate_come[b] = gate[b]
    down_share[...] = weights.value(1, depth - 1)
    own_small = small[s]
    for copy in tiny:
        copy.wait_recv()
    for i in range(depth - 1):
        own_small = own_small + small_come[i]
    small_go[...] = own_small
    spread = []
    for k in range(1, count):
        spread.append(links.start(rows_out.at[0], rows_out.at[k], others[k - 1]))
        spread.append(
            links.start(
                small_go.at[jnp.bitwise_xor(b, k)], small_land.at[k - 1], others[k - 1]
            )
        )
    drain(out_sums)
    out_far = seq_sends(out_go, out_come)
    drain(proj_sums)
    proj_far = seq_sends(proj_go, proj_come)
    for step in range(2, depth - 1):
        text_step(step)
    total = null[b]
    for i, copy in enumerate(nulls):
        copy.wait_recv()
        total = total + null_come[i]
    null_share[...] = total
    for copy in spread:
        copy.wait_recv()
    sums = small_go[b]
    for i in range(count - 1):
        sums = sums + small_land[i]
    small_out[...] = sums

    width = row.shape[1]
    for block in range(count):
        for source in range(depth):
            at = slice(block * depth + source, block * depth + source + 1)
            value = jnp.zeros((1, share), wide)
            for place in range(places):
                mark = rows_out[block, source, 1:2, 128 + place : 129 + place]
                value = value + mark * conditions[block, place : place + 1]
            cond_rows[at] = value
            all_rows[at, :width] = rows_out[block, source, 0:1]
            all_rows[at, width:] = early[block, source]
    for first in range(0, 4 * width, 1536):
        columns = slice(first, first + 1536)
        mod_share[:, columns] = lax.dot_general(
            cond_rows[...],
            all_rows[:, columns],
            (((0,), (0,)), ((), ())),
            precision=HIGHEST,
            preferred_element_type=wide,
        )
    for copy in far:
        copy.wait_recv()
    units = gate.shape[2] // 2
    for block in range(count):
        for half in range(2):
            first = half * count * units + block * units
            gate_share[:, first : first + units] = gate_come[
                block, :, half * units : (half + 1) * units
            ].astype(wide)
    for copy in out_far + proj_far:
        copy.wait_recv()
    total = out_come[0].astype(wide)
    for i in range(1, depth):
        total = total + out_come[i].astype(wide)
    output_share[...] = total
    own = proj_come.shape[2] // 3
    for i in range(3):
        for source in range(depth):
            first = i * depth * own + source * own
            proj_share[:, first : first + own] = proj_come[
                source, :, i * own : (i + 1) * own
            ].astype(wide)
    text_step(depth - 1)
    links.finish()


def final_sums(
    count, depth, flags, text, combined, upstream, normed, grads, ffn_grads, held, words, row, small,
    early, conditions,
):
    vmem = pl.BlockSpec(memory_space=pltpu.VMEM)
    feature, pair_width = text.shape
    width = combined.shape[1]
    own3 = grads.shape[2]
    share = width // (count * depth)
    null_rows = words.shape[0] // flags.shape[0] // count
    text_width = words.shape[1]
    outer = count // 2
    block_rows = width // count
    quarter = (depth - 1, feature // depth, pair_width)

    def plane_sums(columns):
        return [
            pltpu.VMEM((count, block_rows, columns), narrow),
            pltpu.VMEM((outer, block_rows, columns), narrow),
            pltpu.VMEM((2, outer - 1, block_rows // 2, columns), narrow),
        ]

    copies = 2 * (depth - 1) + depth - 1 + 2 * plane_copies(count)[1] + 4 * (count - 1)
    copies += 2 * (depth - 1) + 2 * (depth - 3)
    gate, down = held
    gates = pltpu.VMEM(gate.shape, narrow)
    anywhere = pl.BlockSpec(memory_space=pl.ANY)
    return pl.pallas_call(
        partial(sum_kernel, count, depth),
        in_specs=[scalar_spec()]
        + [vmem] * 3
        + [anywhere] * 4
        + [vmem] * 2
        + [anywhere]
        + [vmem] * 4,
        out_specs=[vmem] * 9,
        out_shape=[
            jax.ShapeDtypeStruct((share, 4 * width), wide),
            jax.ShapeDtypeStruct(down.shape, wide),
            jax.ShapeDtypeStruct((feature // depth, pair_width), wide),
            jax.ShapeDtypeStruct((share, width), wide),
            jax.ShapeDtypeStruct((share, depth * own3), wide),
            jax.ShapeDtypeStruct((share, count * gate.shape[2]), wide),
            jax.ShapeDtypeStruct((null_rows, text_width), wide),
            jax.ShapeDtypeStruct((count, depth) + row.shape, wide),
            jax.ShapeDtypeStruct(small.shape[2:], wide),
        ],
        scratch_shapes=[
            pltpu.VMEM(normed.shape, narrow),
            pltpu.VMEM(grads.shape, narrow),
            pltpu.VMEM(words.shape, narrow),
            pltpu.VMEM((depth - 2,) + gate.shape, narrow),
            pltpu.VMEM((depth - 2,) + down.shape, narrow),
            pltpu.SemaphoreType.DMA((3 + 2 * (depth - 2),)),
        ]
        + plane_sums(width)
        + plane_sums(own3)
        + [
            pltpu.VMEM(quarter, narrow),
            pltpu.VMEM(quarter, narrow),
            pltpu.VMEM((depth, share, width), narrow),
            pltpu.VMEM((depth, share, width), narrow),
            pltpu.VMEM((depth, share, own3), narrow),
            pltpu.VMEM((depth, share, own3), narrow),
            gates,
            gates,
            pltpu.VMEM((count, null_rows, text_width), wide),
            pltpu.VMEM((count - 1, null_rows, text_width), wide),
            pltpu.VMEM((depth - 1,) + small.shape[1:], wide),
            pltpu.VMEM(small.shape[1:], wide),
            pltpu.VMEM((count - 1,) + small.shape[2:], wide),
            pltpu.VMEM((depth - 3,) + gate.shape, narrow),
            pltpu.VMEM((depth - 3,) + down.shape, narrow),
            pltpu.VMEM((depth - 3,) + gate.shape, narrow),
            pltpu.VMEM((depth - 3,) + down.shape, narrow),
            pltpu.VMEM((count * depth, share), wide),
            pltpu.VMEM((count * depth, 4 * width), wide),
            pltpu.SemaphoreType.DMA((copies,)),
            pltpu.SemaphoreType.DMA((copies,)),
        ],
        compiler_params=pltpu.CompilerParams(
            collective_id=10, has_side_effects=True, vmem_limit_bytes=60 * 2**20
        ),
        name="final_sums",
    )(flags, text, combined, upstream, normed, grads, *ffn_grads, *held, words, row, small, early, conditions)


def head_lanes(values, head, size):
    lane = lax.broadcasted_iota(jnp.int32, values.shape, 1)
    return jnp.where((lane >= head * size) & (lane < (head + 1) * size), values, 0)


def swap_halves(values, size):
    half = size // 2
    lanes = values.shape[1]
    if lanes % 128 == 0:
        lane = lax.broadcasted_iota(jnp.int32, values.shape, 1)
        ahead = pltpu.roll(values, lanes - half, 1)
        behind = pltpu.roll(values, half, 1)
        return jnp.where(lax.rem(lane, size) < half, ahead, behind)
    parts = []
    for start in range(0, lanes, size):
        parts.append(values[:, start + half : start + size])
        parts.append(values[:, start : start + half])
    return jnp.concatenate(parts, axis=1)


def turn(values, cosine, signed_sine, size):
    return values * cosine + swap_halves(values, size) * signed_sine


def flat(values):
    return values.reshape(-1, values.shape[-1])


def scalar_spec():
    return pl.BlockSpec(memory_space=pltpu.SMEM)


def row_sums(values):
    ones = jnp.ones((8, values.shape[1]), wide)
    return lax.dot_general(
        ones, values, (((1,), (1,)), ((), ())), precision=HIGHEST, preferred_element_type=wide
    )[:1]


def loop(count, body):
    if count == 1:
        body(0)
    else:
        lax.fori_loop(0, count, lambda i, _: (body(i), 0)[1], 0)


def lane_block(index, lanes):
    if isinstance(index, int):
        return pl.ds(index * lanes, lanes)
    return pl.ds(pl.multiple_of(index * lanes, 128), lanes)


def block_rows_of(index, rows):
    if isinstance(index, int):
        return pl.ds(index * rows, rows)
    return pl.ds(pl.multiple_of(index * rows, 128), rows)


def forward_kernel(
    count, depth, size, lanes, spans, lengths, gates, raw_q_hbm, raw_k_hbm, raw_v_hbm, rates, gain_q,
    gain_k, cosine_hbm, sine_hbm, text_own, gate_up, combined, q, k, v, qc, total, cross_total, text, gathered,
    raw_q, raw_k, raw_v, cosine, sine, self_out, staged, send, arrive, local,
):
    links = Transfers(send, arrive)
    late = [
        Late(source, target, local.at[2 + i])
        for i, (source, target) in enumerate(
            zip(
                (raw_v_hbm, raw_q_hbm, raw_k_hbm, cosine_hbm, sine_hbm),
                (raw_v, raw_q, raw_k, cosine, sine),
                strict=True,
            )
        )
    ]
    b, s = lax.axis_index("bucket"), lax.axis_index("seq")
    others = [partner(k) for k in range(1, count)]
    turns = [lax.rem(s + step, depth) for step in range(1, depth)]
    along = [seq_device(place) for place in turns]
    meet(others + along)
    block_rows, own = raw_q.shape[1:]
    rows = depth * block_rows
    width = own * depth
    grid, heads = own // lanes, lanes // size
    scaling = size ** (-0.5)
    words = [
        links.start(text_own.at[place], text.at[s], device)
        for place, device in zip(turns, along, strict=True)
    ]
    text[s] = text_own[s]
    gate_rows, units = gate_up.shape[0], gathered.shape[1] // 2
    half_width = gate_up.shape[1] // 2
    here = pl.ds(pl.multiple_of(b * gate_rows, 16), gate_rows)
    weights, kept = [], []
    for block in range(count):
        target = jnp.bitwise_xor(b, block)
        for half in range(2):
            source = gate_up.at[
                :, pl.ds(pl.multiple_of(half * half_width + target * units, 128), units)
            ]
            landing = gathered.at[here, pl.ds(half * units, units)]
            if block:
                weights.append(links.start(source, landing, others[block - 1]))
            else:
                copy = pltpu.make_async_copy(source, landing, local.at[half])
                copy.start()
                kept.append(copy)
    for copy in late:
        copy.get()
    for block in range(depth):
        v[block_rows_of(block, block_rows)] = raw_v[block].astype(narrow)
    columns = rates[...].T
    for block in range(depth):
        at = block_rows_of(block, block_rows)
        cos, sin = cosine[at], sine[at]
        for group in range(grid):
            span = lane_block(group, lanes)
            norm_q = raw_q[block, :, span] * columns[:, block : block + 1] * gain_q[:, span]
            norm_k = (
                raw_k[block, :, span]
                * columns[:, depth + block : depth + block + 1]
                * gain_k[:, span]
            )
            turned = turn(norm_q, cos, sin, size).astype(narrow).astype(wide)
            q[at, span] = (turned * scaling).astype(narrow)
            qc[at, span] = (norm_q.astype(narrow).astype(wide) * scaling).astype(narrow)
            k[at, span] = turn(norm_k, cos, sin, size).astype(narrow)
    key_index = lax.broadcasted_iota(jnp.int32, (rows, block_rows), 0)

    def attend_self(group):
        span = lane_block(group, lanes)
        value_t = v[:, span].astype(wide).T.astype(narrow)
        for block in range(depth):
            at = block_rows_of(block, block_rows)
            allowed = (key_index >= spans[0, block]) & (key_index < spans[1, block])
            outs = []
            for head in range(heads):
                scores = contract_cols(k[:, span], head_lanes(q[at, span], head, size))
                scores = jnp.where(allowed, scores, NEGATIVE)
                peak = jnp.max(scores, axis=0, keepdims=True)
                shares = jnp.exp(scores - peak)
                mass = jnp.sum(shares, axis=0, keepdims=True)
                part = slice(head * size, (head + 1) * size)
                outs.append(dense(value_t[part], shares.astype(narrow)) / mass)
                total[group, head : head + 1, at] = peak + jnp.log(mass)
            self_out[at, span] = jnp.concatenate(outs, axis=0).T

    loop(grid, attend_self)
    for copy in words:
        copy.wait_recv()
    cap = text.shape[0] * text.shape[3]
    cap_index = lax.broadcasted_iota(jnp.int32, (cap, block_rows), 0)
    results = []
    for step in range(depth):
        block = lax.rem(s + 1 + step, depth)
        at = block_rows_of(block, block_rows)
        clip = spans[2, block]
        live = cap_index < lengths[clip]

        def attend_cross(group):
            span = lane_block(group, lanes)
            text_key = flat(text[:, 0, clip, :, span])
            value_t = flat(text[:, 1, clip, :, span]).astype(wide).T.astype(narrow)
            outs = []
            for head in range(heads):
                scores = contract_cols(text_key, head_lanes(qc[at, span], head, size))
                scores = jnp.where(live, scores, NEGATIVE)
                peak = jnp.max(scores, axis=0, keepdims=True)
                shares = jnp.exp(scores - peak)
                mass = jnp.sum(shares, axis=0, keepdims=True)
                part = slice(head * size, (head + 1) * size)
                gate = gates[group * heads + head]
                outs.append(dense(value_t[part], shares.astype(narrow)) * (gate / mass))
                cross_total[group, head : head + 1, at] = peak + jnp.log(mass)
            staged[step, :, span] = (
                self_out[at, span] + jnp.concatenate(outs, axis=0).T
            ).astype(narrow)

        loop(grid, attend_cross)
        if step < depth - 1:
            results.append(links.start(staged.at[step], combined.at[s], along[step]))
        else:
            combined[s] = staged[step]
    for copy in results + weights:
        copy.wait_recv()
    for copy in kept:
        copy.wait()
    links.finish()


def attention_forward(
    count, depth, size, lanes, scalars, raws, rates, gains, angles, text_own, gate_up
):
    block_rows, own = raws[0].shape[1:]
    rows = depth * block_rows
    grid, heads = own // lanes, lanes // size
    vmem, anywhere = pl.BlockSpec(memory_space=pltpu.VMEM), pl.BlockSpec(memory_space=pl.ANY)
    units = gate_up.shape[1] // (2 * count)
    copies = 2 * (depth - 1) + 2 * (count - 1)
    row_block = jax.ShapeDtypeStruct((rows, own), narrow)
    totals = jax.ShapeDtypeStruct((grid, heads, rows), wide)
    return pl.pallas_call(
        partial(forward_kernel, count, depth, size, lanes),
        in_specs=[scalar_spec()] * 3
        + [anywhere] * 3
        + [vmem] * 3
        + [anywhere] * 2
        + [vmem, anywhere],
        out_specs=[vmem] * 9,
        out_shape=[
            jax.ShapeDtypeStruct((depth, block_rows, own), narrow),
            row_block,
            row_block,
            row_block,
            row_block,
            totals,
            totals,
            jax.ShapeDtypeStruct(text_own.shape, narrow),
            jax.ShapeDtypeStruct((count * gate_up.shape[0], 2 * units), narrow),
        ],
        scratch_shapes=[
            pltpu.VMEM(raws[0].shape, wide),
            pltpu.VMEM(raws[0].shape, wide),
            pltpu.VMEM(raws[0].shape, wide),
            pltpu.VMEM(angles[0].shape, wide),
            pltpu.VMEM(angles[0].shape, wide),
            pltpu.VMEM((rows, own), wide),
            pltpu.VMEM((depth, block_rows, own), narrow),
            pltpu.SemaphoreType.DMA((copies,)),
            pltpu.SemaphoreType.DMA((copies,)),
            pltpu.SemaphoreType.DMA((7,)),
        ],
        compiler_params=pltpu.CompilerParams(
            collective_id=8, has_side_effects=True, vmem_limit_bytes=60 * 2**20
        ),
        name="attention_forward",
    )(*scalars, *raws, rates, *gains, *angles, text_own, gate_up)


def backward_kernel(
    count, depth, size, lanes, spans, lengths, gates, upstream, weight, q, k_hbm, v_hbm, qc, raw_q_hbm,
    raw_k_hbm, rates, gain_q, gain_k, cosine, sine, text, total, cross_total, small, text_gain, text_pairs,
    grad_gate, grad_down,
    projected, gain_sums, dgate, grad_pairs, text_gain_sum, small_out, gate_held, down_held,
    k, v, raw_q, raw_k, cosine_in, sine_in, pairs_in, local, grad_text, go, send_go, dqc, back_q, back_k, parts, send_text, stat,
    stat_in, sum_k, sum_v, send, arrive,
):
    links = Transfers(send, arrive)
    s = lax.axis_index("seq")
    others = [partner(k) for k in range(1, count)]
    turns = [lax.rem(s + step, depth) for step in range(1, depth)]
    along = [seq_device(place) for place in turns]
    late = [
        Late(source, target, local.at[i])
        for i, (source, target) in enumerate(
            zip(
                (k_hbm, v_hbm, raw_q_hbm, raw_k_hbm, cosine, sine, text_pairs),
                (k, v, raw_q, raw_k, cosine_in, sine_in, pairs_in),
                strict=True,
            )
        )
    ]
    cosine, sine = cosine_in, sine_in
    meet(others + along)
    block_rows, own = upstream.shape[0], q.shape[1]
    rows = depth * block_rows
    width = own * depth
    grid, heads = own // lanes, lanes // size
    scaling = size ** (-0.5)

    small_out[0, s] = small[...]
    smalls = [links.start(small, small_out.at[0, s], device) for device in along]

    def grad_out(place):
        at = pl.ds(pl.multiple_of(place * own, 64), own)
        return contract_cols(upstream[...], weight[at]).astype(narrow)

    arriving = []
    for i, (place, device) in enumerate(zip(turns, along, strict=True)):
        send_go[i] = grad_out(place)
        arriving.append(links.start(send_go.at[i], go.at[s], device))
    go[s] = grad_out(s)
    ring = Ring(depth, links)
    weights = GradientRing(ring, (grad_gate, grad_down), None)

    cap_local = text.shape[3]
    cap = text.shape[0] * cap_local
    places = text.shape[2]
    cap_index = lax.broadcasted_iota(jnp.int32, (cap, block_rows), 0)
    clips = []
    for step in range(depth):
        block = lax.rem(s - step + depth, depth)
        if step:
            arriving[step - 1].wait_recv()
        if step == depth - 1:
            weights.first((gate_held, down_held))
        at = block_rows_of(block, block_rows)
        clip = spans[2, block]
        clips.append(clip)
        live = cap_index < lengths[clip]

        def back_cross(group):
            span = lane_block(group, lanes)
            text_key = flat(text[:, 0, clip, :, span])
            text_value = flat(text[:, 1, clip, :, span])
            key_t = text_key.astype(wide).T.astype(narrow)
            grads = []
            for head in range(heads):
                gate = gates[group * heads + head]
                query = head_lanes(qc[at, span], head, size)
                grad = head_lanes(go[block, :, span], head, size)
                scores = contract_cols(text_key, query)
                scores = jnp.where(live, scores, NEGATIVE)
                shares = jnp.exp(scores - cross_total[group, head : head + 1, at])
                grad_shares = contract_cols(text_value, grad)
                row = jnp.sum(grad_shares * shares, axis=0, keepdims=True)
                grad_scores = (gate * (shares * (grad_shares - row))).astype(narrow)
                grad_key = dense(grad_scores, query)
                grad_value = gate * dense(shares.astype(narrow), grad)
                if head == 0:
                    parts[step, 0, :, span] = grad_key
                    parts[step, 1, :, span] = grad_value
                else:
                    parts[step, 0, :, span] += grad_key
                    parts[step, 1, :, span] += grad_value
                part = slice(head * size, (head + 1) * size)
                grads.append(dense(key_t[part], grad_scores) * scaling)
                if step == 0:
                    dgate[group, head : head + 1] = row
                else:
                    dgate[group, head : head + 1] += row
            dqc[at, span] = jnp.concatenate(grads, axis=0).T

        loop(grid, back_cross)
    for which in range(2):
        for place in range(places):
            for target in range(depth):
                at = pl.ds(target * cap_local, cap_local)
                value = jnp.zeros((cap_local, own), wide)
                for step in range(depth):
                    value = value + jnp.where(
                        clips[step] == place, parts[step, which, at], 0.0
                    )
                send_text[target, which, place] = value.astype(narrow)
    words = [
        links.start(send_text.at[place], grad_text.at[s], device)
        for place, device in zip(turns, along, strict=True)
    ]
    grad_text[s] = send_text[s]
    for copy in smalls:
        copy.wait_recv()
    spread = [links.start(small_out.at[0], small_out.at[k], others[k - 1]) for k in range(1, count)]

    for copy in late:
        copy.get()
    key_index = lax.broadcasted_iota(jnp.int32, (rows, block_rows), 0)

    def back_self(group):
        span = lane_block(group, lanes)
        key_t = k[:, span].astype(wide).T.astype(narrow)
        for block in range(depth):
            at = block_rows_of(block, block_rows)
            allowed = (key_index >= spans[0, block]) & (key_index < spans[1, block])
            grads = []
            for head in range(heads):
                query = head_lanes(q[at, span], head, size)
                grad = head_lanes(go[block, :, span], head, size)
                scores = contract_cols(k[:, span], query)
                scores = jnp.where(allowed, scores, NEGATIVE)
                shares = jnp.exp(scores - total[group, head : head + 1, at])
                grad_shares = contract_cols(v[:, span], grad)
                row = jnp.sum(grad_shares * shares, axis=0, keepdims=True)
                grad_scores = (shares * (grad_shares - row)).astype(narrow)
                if block == 0 and head == 0:
                    sum_v[...] = dense(shares.astype(narrow), grad)
                    sum_k[...] = dense(grad_scores, query)
                else:
                    sum_v[...] += dense(shares.astype(narrow), grad)
                    sum_k[...] += dense(grad_scores, query)
                part = slice(head * size, (head + 1) * size)
                grads.append(dense(key_t[part], grad_scores) * scaling)
            back = jnp.concatenate(grads, axis=0).T
            back_q[at, span] = turn(back, cosine[at], -sine[at], size) + dqc[at, span]
        back_k[:, span] = turn(sum_k[...], cosine[...], -sine[...], size)
        for block in range(depth):
            at = block_rows_of(block, block_rows)
            if isinstance(group, int):
                to = pl.ds(2 * own + group * lanes, lanes)
            else:
                to = pl.ds(pl.multiple_of(2 * own + group * lanes, 128), lanes)
            projected[block, :, to] = sum_v[at].astype(narrow)

    loop(grid, back_self)
    columns = rates[...].T
    pairs = ((raw_q, back_q, gain_q), (raw_k, back_k, gain_k))
    for i, (raw, back, gain) in enumerate(pairs):
        gains = jnp.zeros((1, own), wide)
        for block in range(depth):
            place = i * depth + block
            at = block_rows_of(block, block_rows)
            hat = raw[block] * columns[:, place : place + 1]
            gains = gains + jnp.sum(back[at] * hat, axis=0, keepdims=True)
            stat[place : place + 1] = row_sums(back[at] * gain[...] * hat)
        gain_sums[i : i + 1] = gains
    stats = [links.start(stat, stat_in.at[i], device) for i, device in enumerate(along)]
    means = stat[...]
    for i, copy in enumerate(stats):
        copy.wait_recv()
        means = means + stat_in[i]
    means = (means / width).T
    for i, (raw, back, gain) in enumerate(pairs):
        for block in range(depth):
            place = slice(i * depth + block, i * depth + block + 1)
            at = block_rows_of(block, block_rows)
            rate = columns[:, place]
            hat = raw[block] * rate
            projected[block, :, i * own : (i + 1) * own] = (
                rate * (back[at] * gain[...] - hat * means[:, place])
            ).astype(narrow)
    for copy in words:
        copy.wait_recv()

    for target in range(depth):
        text_gain_sum[:, target * own : (target + 1) * own] = jnp.zeros((1, own), wide)
    for place in range(places):
        at = slice(place * cap_local, (place + 1) * cap_local)
        keys = pairs_in[at, :width]
        rate = lax.rsqrt(jnp.mean(keys * keys, axis=1, keepdims=True) + EPSILON)
        mean = jnp.zeros((cap_local, 1), wide)
        for target in range(depth):
            span = slice(target * own, (target + 1) * own)
            hat = pairs_in[at, span] * rate
            grad = grad_text[target, 0, place].astype(wide)
            mean = mean + jnp.sum(grad * text_gain[:, span] * hat, axis=1, keepdims=True)
            text_gain_sum[:, span] += jnp.sum(grad * hat, axis=0, keepdims=True)
        mean = mean / width
        for target in range(depth):
            span = slice(target * own, (target + 1) * own)
            hat = pairs_in[at, span] * rate
            grad = grad_text[target, 0, place].astype(wide)
            grad_pairs[at, span] = (rate * (grad * text_gain[:, span] - hat * mean)).astype(narrow)
            after = slice(width + target * own, width + (target + 1) * own)
            grad_pairs[at, after] = grad_text[target, 1, place]
    for copy in spread + weights.copies:
        copy.wait_recv()
    links.finish()


def attention_backward(
    count, depth, size, lanes, scalars, upstream, weight, saved, raws, rates, gains, angles, text,
    totals, small, text_gain, text_pairs, ffn_grads,
):
    block_rows, own = raws[0].shape[1:]
    rows = depth * block_rows
    grid, heads = own // lanes, lanes // size
    vmem = pl.BlockSpec(memory_space=pltpu.VMEM)
    copies = 4 * (depth - 1) + count - 1 + 2
    cap = text.shape[0] * text.shape[3]
    args = (*scalars, upstream, weight, *saved, *raws, rates, *gains, *angles, text, *totals, small)
    args = args + (text_gain, text_pairs) + tuple(ffn_grads)
    anywhere = pl.BlockSpec(memory_space=pl.ANY)
    specs = [scalar_spec()] * 3 + [vmem] * (len(args) - 3)
    for i in (6, 7, 9, 10, 14, 15, len(args) - 3, len(args) - 2, len(args) - 1):
        specs[i] = anywhere
    return pl.pallas_call(
        partial(backward_kernel, count, depth, size, lanes),
        in_specs=specs,
        out_specs=[vmem] * 8,
        out_shape=[
            jax.ShapeDtypeStruct((depth, block_rows, 3 * own), narrow),
            jax.ShapeDtypeStruct((2, own), wide),
            jax.ShapeDtypeStruct((grid, heads, block_rows), wide),
            jax.ShapeDtypeStruct(text_pairs.shape, narrow),
            jax.ShapeDtypeStruct((1, own * depth), wide),
            jax.ShapeDtypeStruct((count, depth) + small.shape, wide),
            jax.ShapeDtypeStruct(ffn_grads[0].shape[:1] + ffn_grads[0].shape[2:], narrow),
            jax.ShapeDtypeStruct(ffn_grads[1].shape[1:], narrow),
        ],
        scratch_shapes=[
            pltpu.VMEM((rows, own), narrow),
            pltpu.VMEM((rows, own), narrow),
            pltpu.VMEM(raws[0].shape, wide),
            pltpu.VMEM(raws[1].shape, wide),
            pltpu.VMEM(angles[0].shape, wide),
            pltpu.VMEM(angles[1].shape, wide),
            pltpu.VMEM(text_pairs.shape, wide),
            pltpu.SemaphoreType.DMA((7,)),
            pltpu.VMEM(text.shape, narrow),
            pltpu.VMEM((depth, block_rows, own), narrow),
            pltpu.VMEM((depth - 1, block_rows, own), narrow),
            pltpu.VMEM((rows, own), wide),
            pltpu.VMEM((rows, own), wide),
            pltpu.VMEM((rows, own), wide),
            pltpu.VMEM((depth, 2, cap, own), wide),
            pltpu.VMEM(text.shape, narrow),
            pltpu.VMEM((2 * depth, block_rows), wide),
            pltpu.VMEM((depth - 1, 2 * depth, block_rows), wide),
            pltpu.VMEM((rows, lanes), wide),
            pltpu.VMEM((rows, lanes), wide),
            pltpu.SemaphoreType.DMA((copies,)),
            pltpu.SemaphoreType.DMA((copies,)),
        ],
        compiler_params=pltpu.CompilerParams(
            collective_id=9, has_side_effects=True, vmem_limit_bytes=60 * 2**20
        ),
        name="attention_backward",
    )(*args)


def per_device(
    tokens,
    condition,
    captions,
    caption_lengths,
    null_flags,
    slot_buckets,
    null_caption,
    modulation,
    projection,
    text_weight,
    output_weight,
    gate_up,
    down_weight,
    norm_gains,
    head_gains,
    cross_gates,
    cotangent,
):
    count_s, count_b = lax.axis_size("seq"), lax.axis_size("bucket")
    s, b = lax.axis_index("seq"), lax.axis_index("bucket")
    assert count_s % 4 == 0
    local, width = tokens.shape
    heads = cross_gates.shape[0]
    size = width // heads
    own_heads = heads // count_s
    own = width // count_s
    rows = local * count_s
    places, cap_local, text_width = captions.shape
    cap_rows = places * cap_local
    bucket = slot_buckets[0]
    clip_length = jnp.where(
        bucket == 0, rows // 4, jnp.where(bucket == 1, rows // 2, rows)
    ).astype(jnp.int32)

    own_hidden = down_weight.shape[0]
    gate_rows = gate_up.shape[0]
    text_rows = text_weight.shape[0]
    null_rows = lax.dynamic_slice_in_dim(null_caption, s * cap_local, cap_local, 0)
    is_null = null_flags[:, None, None] == 1
    words_own = jnp.where(is_null, null_rows[None], captions).reshape(cap_rows, text_width)
    own_projection = jnp.concatenate(
        [
            lax.dynamic_slice_in_dim(projection, i * width + s * own, own, 1)
            for i in range(3)
        ],
        axis=1,
    )

    silu_cond = jax.nn.silu(condition).astype(narrow)
    pieces = silu_cond.astype(wide).reshape(places, count_b, -1).transpose(1, 0, 2)
    my_clip = (s * local) // clip_length
    (
        cond_columns,
        mods,
        own_projection,
        words,
        text_pairs,
        text_own,
        normed,
        raw_q,
        raw_k,
        raw_v,
        rates,
    ) = start_exchange(
        count_b,
        count_s,
        my_clip.astype(jnp.int32)[None],
        pieces,
        modulation,
        own_projection,
        words_own,
        text_weight,
        tokens,
        norm_gains,
        head_gains,
    )
    own_projection = own_projection.reshape(width, 3 * own)
    modulated = lax.dynamic_index_in_dim(mods, my_clip, 1, keepdims=False).reshape(1, 4 * width)
    tokens_in = tokens.astype(wide)
    _, pre_pull = jax.vjp(pre_attention, tokens_in, modulated, norm_gains)

    gains = [lax.dynamic_slice_in_dim(head_gains[i : i + 1], s * own, own, 1) for i in range(2)]
    inside = lax.rem(jnp.arange(rows, dtype=jnp.int32), clip_length)
    half = size // 2
    frequency = 10000.0 ** (-jnp.arange(half, dtype=wide) / half)
    angles = inside.astype(wide)[:, None] * frequency[None, :]
    lanes = 128 if own % 128 == 0 else own
    block_heads = lanes // size
    cosine = jnp.tile(jnp.cos(angles), (1, 2 * block_heads))
    sine = jnp.tile(
        jnp.concatenate([-jnp.sin(angles), jnp.sin(angles)], axis=1), (1, block_heads)
    )
    tanh_gates = jnp.tanh(cross_gates)
    own_gates = lax.dynamic_slice_in_dim(tanh_gates, s * own_heads, own_heads, 0)
    clip_of = (jnp.arange(count_s, dtype=jnp.int32) * local) // clip_length
    spans = jnp.stack([clip_of * clip_length, (clip_of + 1) * clip_length, clip_of])
    scalars = (spans, caption_lengths, own_gates)
    full_output, text_own = lax.optimization_barrier((output_weight, text_own))
    full_output = lax.all_gather(full_output, "bucket", axis=0, tiled=True)
    combined, *saved, total, cross_total, text_kv, own_gate_up = attention_forward(
        count_b,
        count_s,
        size,
        lanes,
        scalars,
        (raw_q, raw_k, raw_v),
        rates,
        gains,
        (cosine, sine),
        text_own,
        gate_up,
    )
    combined = combined.transpose(1, 0, 2).reshape(local, width)

    attended = dense(combined, full_output)
    (middle, ffn_full), post_pull = jax.vjp(
        post_attention, attended, tokens_in, modulated, norm_gains
    )
    normed_ffn = ffn_full.astype(narrow)

    lowered, plane, gate_values, hidden = ffn_forward(
        count_b, normed_ffn, own_gate_up, down_weight
    )
    mixed, finish_pull = jax.vjp(finish, lowered, middle, modulated, norm_gains)
    grad_lowered, grad_middle, grad_modulated_last, grad_norm_last = finish_pull(
        cotangent.astype(wide)
    )
    grad_lowered_low = grad_lowered.astype(narrow)
    grad_normed_ffn, grad_gate_up, grad_down = ffn_backward(
        count_b, grad_lowered_low, own_gate_up, down_weight, gate_values, plane, hidden
    )
    share = width // (count_b * count_s)
    ffn_grads = (
        grad_gate_up.reshape(count_b, count_s, share, 2 * own_hidden),
        grad_down.reshape(count_s, own_hidden // count_s, width),
    )

    grad_attended, grad_tokens_post, grad_modulated_post, grad_norm_post = post_pull(
        (grad_middle, grad_normed_ffn)
    )
    grad_attended_low = grad_attended.astype(narrow)
    grad_projected, gain_sums, grad_gates, grad_pairs_low, text_gain_sum, early, *held = (
        attention_backward(
            count_b,
            count_s,
            size,
            lanes,
            scalars,
            grad_attended_low,
            full_output,
            saved,
            (raw_q, raw_k),
            rates,
            gains,
            (cosine, sine),
            text_kv,
            (total, cross_total),
            (grad_modulated_post + grad_modulated_last)[:, width:],
            head_gains[2:],
            text_pairs,
            ffn_grads,
        )
    )

    grad_normed, grad_words, grad_text, *held = end_exchange(
        count_b,
        count_s,
        grad_pairs_low,
        text_weight,
        words,
        grad_projected,
        own_projection,
        ffn_grads,
        held,
    )
    grad_tokens_pre, grad_modulated_pre, grad_norm_pre = pre_pull(grad_normed)
    grad_tokens = grad_tokens_pre + grad_tokens_post

    def place(values):
        return lax.dynamic_update_slice_in_dim(jnp.zeros((width,), wide), values, s * own, 0)

    gate_sums = lax.dynamic_update_slice_in_dim(
        jnp.zeros((heads,), wide),
        jnp.sum(grad_gates, axis=2).reshape(own_heads) * (1.0 - own_gates * own_gates),
        s * own_heads,
        0,
    )
    small = jnp.concatenate(
        [
            grad_norm_pre + grad_norm_post + grad_norm_last,
            jnp.stack(
                [
                    place(gain_sums[0]),
                    place(gain_sums[1]),
                    text_gain_sum[0],
                    jnp.zeros((width,), wide),
                ]
            ),
        ],
        axis=0,
    )
    own_clip = (jnp.arange(places, dtype=jnp.int32) == my_clip).astype(wide)
    row = jnp.concatenate(
        [
            jnp.pad(gate_sums, (0, 128 - heads)),
            jnp.pad(own_clip, (0, width - 128 - places)),
        ]
    )
    row = jnp.stack([grad_modulated_pre[0, :width], row], axis=0)
    (
        mod_share,
        down_share,
        text_share,
        output_share,
        proj_share,
        gate_share,
        null_share,
        grad_rows,
        own_sums,
    ) = final_sums(
        count_b,
        count_s,
        null_flags,
        grad_text,
        combined,
        grad_attended_low,
        normed,
        grad_projected,
        ffn_grads,
        held,
        grad_words,
        row,
        small.reshape(8, count_b, count_s, share).transpose(2, 1, 0, 3),
        early,
        lax.dynamic_slice_in_dim(cond_columns, s * share, share, 2),
    )
    null_share = lax.ppermute(
        null_share,
        ("bucket", "seq"),
        [(i * count_s + j, j * count_b + i) for i in range(count_b) for j in range(count_s)],
    )
    grad_words = grad_words.reshape(places, cap_local, text_width).astype(wide)
    grad_captions = jnp.where(is_null, 0.0, grad_words)

    return (
        mixed.astype(narrow),
        grad_tokens,
        grad_captions,
        null_share,
        mod_share,
        proj_share,
        text_share,
        output_share,
        gate_share,
        down_share,
        own_sums[:4],
        own_sums[4:7],
        jnp.sum(grad_rows[:, :, 1, :heads], axis=(0, 1)),
    )


def solution(mesh):
    whole = P(("bucket", "seq"), None)
    shard = P("bucket", None)
    return jax.shard_map(
        per_device,
        mesh=mesh,
        in_specs=(
            whole,
            shard,
            P("bucket", "seq", None),
            P("bucket"),
            P("bucket"),
            P("bucket"),
            P(),
            shard,
            shard,
            shard,
            shard,
            shard,
            shard,
            P(),
            P(),
            P(),
            whole,
        ),
        out_specs=(
            whole,
            whole,
            P("bucket", "seq", None),
            whole,
            whole,
            whole,
            whole,
            whole,
            whole,
            whole,
            P(None, ("bucket", "seq")),
            P(None, ("bucket", "seq")),
            P(),
        ),
        check_vma=False,
    )
```
